32 devices in a mesh: grp: 4 (over x, core), dev: 8 (over z, y).
Axes of the slice: x: 2, y: 2, z: 4, core: 2. Of those that a mesh axis runs over, the one named last changes fastest.
Arguments:
- residual: bfloat16 [4096, 2048], P(('grp', 'dev')), may hold values from -3 to 3
- queries: bfloat16 [4096, 1024], P(('grp', 'dev')), may hold values from -9 to 9
- keys: bfloat16 [4096, 256], P(('grp', 'dev')), may hold values from -6 to 6
- values: bfloat16 [4096, 256], P(('grp', 'dev')), may hold values from -18 to 18
- prefix_keys: bfloat16 [16, 512, 256], P('grp', 'dev'), may hold values from -6 to 6
- cached_prefix_values: bfloat16 [16, 512, 256], P('grp', 'dev'), may hold values from -18 to 18
- out_weight: bfloat16 [1024, 2048], replicated, may hold values from -0.1875 to 0.1875
- norm_gain: float32 [2048], replicated, may hold values from 0.25 to 1.75
- w_gate: bfloat16 [2048, 8192], P('grp', 'dev'), may hold values from -0.125 to 0.125
- w_up: bfloat16 [2048, 8192], P('grp', 'dev'), may hold values from -0.125 to 0.125
- w_down: bfloat16 [8192, 2048], P('dev', 'grp'), may hold values from -0.0625 to 0.0625
- suffix_lengths: int32 [4, 32], P('grp'), may hold values from 1 to 128, 1024 in all within a row
- request_group: int32 [4, 32], P('grp'), may hold values from 0 to 3, as said below
- placement_order: int32 [4, 32], P('grp'), may hold values from 0 to 31, each once within a row
Outputs:
- layer_out: bfloat16 [4096, 2048], P(('grp', 'dev'))
The draws below stay inside these ranges and needn't reach their ends.
Inputs may be any that keep to these rules, and one draw needn't show every extreme that they name: `suffix_lengths`: the 32 lengths of one row sum to 1024. `request_group`: each row names each of its 4 groups exactly 8 times. `placement_order`: each row is an ordering of its 32 requests.
All inputs are finite; a program needn't handle non-finite values.
Results may differ from the reference program's by a relative error of at most 0.012.
Values may be sent and summed in bfloat16 or wider, within the bound.
No kernel may reach another device: no remote copies, remote signals or barrier semaphores. Data moves between devices by JAX's collectives and lax.ppermute only.
A program may use at most 128 MiB of HBM per device.

```python
import math
import jax
import jax.numpy as jnp
import numpy as np
from jax import lax

D = 2048
FF = 8192
HEAD_SIZE = 64
QUERY_HEADS = 16
KEY_VALUE_HEADS = 4
G_ROW = 4
REQ_GRP = 8
TOK_DEV = 128
PRE_DEV = 64
REQ_ROW = 32
PREFIX_GROUPS = 16
ROW_TOKENS = 1024
SUFFIX_TOKENS = 4096
PREFIX_LENGTH = 512
N_GRP = 4
N_DEV = 8


def draw_queries(key, part):
    root_key = jax.random.fold_in(key, 11)
    return (1.5 * jax.random.truncated_normal(root_key, -6.0, 6.0, (SUFFIX_TOKENS, QUERY_HEADS * HEAD_SIZE), jnp.float32)).astype(jnp.bfloat16)


def draw_prefix_keys(key, part):
    root_key = jax.random.fold_in(key, 21)
    return jax.random.truncated_normal(root_key, -6.0, 6.0, (PREFIX_GROUPS, PREFIX_LENGTH, KEY_VALUE_HEADS * HEAD_SIZE), jnp.float32).astype(jnp.bfloat16)


def draw_request_group(key, part):
    row_keys = jax.random.split(jax.random.fold_in(key, 31), N_GRP)
    orders = jax.vmap(lambda row_key: jax.random.permutation(row_key, REQ_ROW))(row_keys)
    return (orders // REQ_GRP).astype(jnp.int32)


def steps_of(key, extent, pieces, least, high):
    def one(position, parts):
        heights = jax.random.uniform(jax.random.fold_in(jax.random.fold_in(key, 6), position), (parts,), jnp.float32, least / len(pieces), high / len(pieces))
        return jnp.repeat(jnp.exp(heights), extent[position] // parts).reshape((-1,) + (1,) * (len(extent) - position - 1))

    factor_of = one(*pieces[0])
    for cut in pieces[1:]:
        factor_of = factor_of * one(*cut)
    return factor_of


def split_up(count, total, bound, lean):
    weights = [(1 << 20) // math.isqrt(grade ** lean) + 1 for grade in range(2, count + 1)]
    rest, given = total - bound - (count - 1), [1] * (count - 1)
    while rest > 0:
        free = [i for i in range(count - 1) if given[i] < bound]
        mass, remaining = sum([weights[i] for i in free]), rest
        for i in free:
            extra = min(bound - given[i], max(1, remaining * weights[i] // mass), rest)
            given[i] = given[i] + extra
            rest = rest - extra
    return np.array([bound] + given)


def uneven_parts(own_key, number_of, total, reach, slope):
    if number_of == 2:
        one = jax.random.randint(own_key, (), max(1, total - reach), min(reach, total - 1) + 1)
        return jnp.stack([one, total - one])
    sizes = jnp.asarray(split_up(number_of, total, reach, slope), jnp.int32)
    pairs = (number_of - 1) // 2
    giver, taker = sizes[1:1 + 2 * pairs:2], sizes[2:2 + 2 * pairs:2]
    slack = jnp.minimum(giver - 1, reach - taker)
    moved = jax.random.randint(jax.random.fold_in(own_key, 1), (pairs,), 0, 1 << 20) % (slack + 1)
    sizes = sizes.at[1:1 + 2 * pairs:2].set(giver - moved).at[2:2 + 2 * pairs:2].set(taker + moved)
    return sizes[jax.random.permutation(jax.random.fold_in(own_key, 2), number_of)]


def noise(stream_key, extent, deviation, limit, cuts=(), held_as=jnp.bfloat16):
    entries = jax.random.normal(stream_key, extent, jnp.float32) * deviation
    if len(cuts) > 0:
        entries = steps_of(stream_key, extent, cuts, -0.22, 0.18) * entries
    return jnp.clip(entries, min=-limit, max=limit).astype(held_as)


def setup_inputs(seed: int = 0) -> dict:
    arg_keys = jax.random.split(jax.random.key(seed), 15)
    return {
        "residual": noise(arg_keys[0], (SUFFIX_TOKENS, D), 0.5, 3.0, ((0, 32),)),
        "queries": draw_queries(jax.random.fold_in(arg_keys[14], 71), 0),
        "keys": noise(arg_keys[2], (SUFFIX_TOKENS, KEY_VALUE_HEADS * HEAD_SIZE), 1.0, 6.0, ((0, 32),)),
        "values": noise(arg_keys[3], (SUFFIX_TOKENS, KEY_VALUE_HEADS * HEAD_SIZE), 3.0, 18.0, ((0, 32),)),
        "prefix_keys": draw_prefix_keys(jax.random.fold_in(arg_keys[14], 71), 0),
        "cached_prefix_values": noise(arg_keys[5], (PREFIX_GROUPS, PREFIX_LENGTH, KEY_VALUE_HEADS * HEAD_SIZE), 3.0, 18.0, ((0, 4), (1, 8))),
        "out_weight": noise(arg_keys[6], (QUERY_HEADS * HEAD_SIZE, D), (QUERY_HEADS * HEAD_SIZE) ** -0.5, 0.1875),
        "norm_gain": jnp.clip(1.0 + 0.15 * jax.random.normal(arg_keys[7], (D,), jnp.float32), 0.25, 1.75),
        "w_gate": noise(arg_keys[8], (D, FF), D ** -0.5, 0.125, ((0, 4), (1, 8))),
        "w_up": noise(arg_keys[9], (D, FF), D ** -0.5, 0.125, ((0, 4), (1, 8))),
        "w_down": noise(arg_keys[10], (FF, D), FF ** -0.5, 0.0625, ((0, 8), (1, 4))),
        "suffix_lengths": jax.vmap(lambda own: uneven_parts(own, REQ_ROW, ROW_TOKENS, TOK_DEV, 2))(jax.random.split(arg_keys[11], N_GRP)).reshape((N_GRP, REQ_ROW)).astype(jnp.int32),
        "request_group": draw_request_group(jax.random.fold_in(arg_keys[14], 71), 0),
        "placement_order": jax.vmap(lambda own: jax.random.permutation(own, REQ_ROW))(jax.random.split(arg_keys[13], N_GRP)).reshape((N_GRP, REQ_ROW)).astype(jnp.int32),
    }


NEG_FILL = -1e+30
EPSILON = 1e-05

def row_layout(lengths, group_map, packed_order):
    request_count = lengths.shape[0]
    picked = (packed_order[:, None] == jnp.arange(request_count, dtype=jnp.int32)[None, :]).astype(jnp.int32)
    packed_len = lax.optimization_barrier(jnp.sum(picked * lengths[None, :], axis=1))
    packed_group = lax.optimization_barrier(jnp.sum(picked * group_map[None, :], axis=1))
    ends_at = jnp.cumsum(packed_len).astype(jnp.int32)
    return (ends_at - packed_len, ends_at, packed_group)

def token_info(token_rows, starts_at, ends_at, packed_group):
    inside = ((token_rows[:, None] >= starts_at[None, :]) & (token_rows[:, None] < ends_at[None, :])).astype(jnp.int32)
    return (lax.optimization_barrier(jnp.sum(inside * packed_group[None, :], axis=1)), lax.optimization_barrier(jnp.sum(inside * starts_at[None, :], axis=1)))

def block_partial(rows_of_queries, allowed, rows_of_keys, rows_of_values):
    query_row_count = rows_of_queries.shape[0]
    key_row_count = rows_of_keys.shape[0]
    heads_of_queries = rows_of_queries.astype(jnp.float32).reshape(query_row_count, KEY_VALUE_HEADS, QUERY_HEADS // KEY_VALUE_HEADS, HEAD_SIZE)
    heads_of_keys = rows_of_keys.astype(jnp.float32).reshape(key_row_count, KEY_VALUE_HEADS, HEAD_SIZE)
    heads_of_values = rows_of_values.astype(jnp.float32).reshape(key_row_count, KEY_VALUE_HEADS, HEAD_SIZE)
    scores = jnp.einsum('nkrd,mkd->nkrm', heads_of_queries, heads_of_keys) * HEAD_SIZE ** (-0.5)
    scores = jnp.where(allowed[:, None, None, :], scores, NEG_FILL)
    maxima = lax.optimization_barrier(jnp.max(scores, axis=-1))
    weights = jnp.exp(scores - maxima[..., None])
    totals = lax.optimization_barrier(jnp.sum(weights, axis=-1))
    rounded = lax.optimization_barrier(weights.astype(jnp.bfloat16)).astype(jnp.float32)
    numerator = jnp.einsum('nkrm,mkd->nkrd', rounded, heads_of_values)
    return (numerator / totals[..., None], maxima, totals)

def merge_all(local_output, local_maximum, local_sum, block_outs, block_maxima, block_sums):
    highest = jnp.maximum(local_maximum, lax.optimization_barrier(jnp.max(block_maxima, axis=0)))
    own_scale = local_sum * jnp.exp(local_maximum - highest)
    scales = block_sums * jnp.exp(block_maxima - highest[None])
    numerator = own_scale[..., None] * local_output + lax.optimization_barrier(jnp.sum(scales[..., None] * block_outs.astype(jnp.float32), axis=0))
    return numerator / (own_scale + lax.optimization_barrier(jnp.sum(scales, axis=0)))[..., None]

def reference(residual, queries, keys, values, prefix_keys, cached_prefix_values, out_weight, norm_gain, w_gate, w_up, w_down, suffix_lengths, request_group, placement_order):
    key_value_width = KEY_VALUE_HEADS * HEAD_SIZE
    key_group = jnp.arange(G_ROW * PRE_DEV, dtype=jnp.int32) // PRE_DEV
    slice_width = FF // N_DEV

    def one_row(packed):
        row_res, row_q, row_k, row_v, row_pk, row_pv, lengths, group_map, packed_order = packed
        starts_at, ends_at, packed_group = row_layout(lengths, group_map, packed_order)
        token_rows = jnp.arange(ROW_TOKENS, dtype=jnp.int32)
        token_group, token_start = token_info(token_rows, starts_at, ends_at, packed_group)
        allowed = token_group[:, None] == key_group[None, :]
        owner_keys = row_pk.reshape(G_ROW, N_DEV, PRE_DEV, key_value_width).transpose(1, 0, 2, 3).reshape(N_DEV, G_ROW * PRE_DEV, key_value_width)
        owner_values = row_pv.reshape(G_ROW, N_DEV, PRE_DEV, key_value_width).transpose(1, 0, 2, 3).reshape(N_DEV, G_ROW * PRE_DEV, key_value_width)

        def owner_part(owner_pair):
            part_out, maxima, totals = block_partial(row_q, allowed, owner_pair[0], owner_pair[1])
            return (part_out.astype(jnp.bfloat16), maxima, totals)
        block_outs, block_maxima, block_sums = lax.map(owner_part, (owner_keys, owner_values))
        padded_k = jnp.concatenate([jnp.zeros((TOK_DEV, key_value_width), row_k.dtype), row_k], axis=0)
        padded_v = jnp.concatenate([jnp.zeros((TOK_DEV, key_value_width), row_v.dtype), row_v], axis=0)

        def suffix_part(device):
            first_row = (device * TOK_DEV).astype(jnp.int32)
            rows_of_queries = lax.dynamic_slice_in_dim(row_q, first_row, TOK_DEV, 0)
            rows_of_keys = lax.dynamic_slice_in_dim(padded_k, first_row, 2 * TOK_DEV, 0)
            rows_of_values = lax.dynamic_slice_in_dim(padded_v, first_row, 2 * TOK_DEV, 0)
            own_rows = first_row + jnp.arange(TOK_DEV, dtype=jnp.int32)
            window = first_row - TOK_DEV + jnp.arange(2 * TOK_DEV, dtype=jnp.int32)
            starts = lax.dynamic_slice_in_dim(token_start, first_row, TOK_DEV, 0)
            suffix_mask = (window[None, :] >= starts[:, None]) & (window[None, :] <= own_rows[:, None])
            return block_partial(rows_of_queries, suffix_mask, rows_of_keys, rows_of_values)
        local_output, local_maximum, local_sum = lax.map(suffix_part, jnp.arange(N_DEV, dtype=jnp.int32))
        local_output = local_output.reshape(ROW_TOKENS, KEY_VALUE_HEADS, QUERY_HEADS // KEY_VALUE_HEADS, HEAD_SIZE)
        local_maximum = local_maximum.reshape(ROW_TOKENS, KEY_VALUE_HEADS, QUERY_HEADS // KEY_VALUE_HEADS)
        local_sum = local_sum.reshape(ROW_TOKENS, KEY_VALUE_HEADS, QUERY_HEADS // KEY_VALUE_HEADS)
        merged = merge_all(local_output, local_maximum, local_sum, block_outs, block_maxima, block_sums)
        attention = merged.astype(jnp.bfloat16).reshape(ROW_TOKENS, QUERY_HEADS * HEAD_SIZE)
        hidden_state = row_res.astype(jnp.float32) + jnp.dot(attention, out_weight, preferred_element_type=jnp.float32)
        normed = (hidden_state * lax.rsqrt(lax.optimization_barrier(jnp.mean(hidden_state * hidden_state, axis=-1, keepdims=True)) + EPSILON) * norm_gain).astype(jnp.bfloat16)
        gate_value = jnp.dot(normed, w_gate, preferred_element_type=jnp.float32)
        up_value = jnp.dot(normed, w_up, preferred_element_type=jnp.float32)
        activation = (jax.nn.silu(gate_value) * up_value).astype(jnp.bfloat16)
        act_slices = activation.reshape(ROW_TOKENS, N_DEV, slice_width).transpose(1, 0, 2)
        down_slices = w_down.reshape(N_DEV, slice_width, D)

        def add_slice(running, slice_pair):
            slice_term = jnp.dot(slice_pair[0], slice_pair[1], preferred_element_type=jnp.float32)
            slice_term = lax.optimization_barrier(slice_term.astype(jnp.bfloat16)).astype(jnp.float32)
            return (running + slice_term, None)
        mlp_sum, unused_tail = lax.scan(add_slice, jnp.zeros((ROW_TOKENS, D), jnp.float32), (act_slices, down_slices))
        return (hidden_state + mlp_sum).astype(jnp.bfloat16)
    rows_out = lax.map(one_row, (residual.reshape(N_GRP, ROW_TOKENS, D), queries.reshape(N_GRP, ROW_TOKENS, QUERY_HEADS * HEAD_SIZE), keys.reshape(N_GRP, ROW_TOKENS, key_value_width), values.reshape(N_GRP, ROW_TOKENS, key_value_width), prefix_keys.reshape(N_GRP, G_ROW, PREFIX_LENGTH, key_value_width), cached_prefix_values.reshape(N_GRP, G_ROW, PREFIX_LENGTH, key_value_width), suffix_lengths, request_group, placement_order))
    return rows_out.reshape(SUFFIX_TOKENS, D)
```

```python
import functools
import math

import jax
import jax.numpy as jnp
from jax import lax
from jax.experimental import pallas as pl
from jax.experimental.pallas import tpu as pltpu
from jax.sharding import PartitionSpec as P

HEAD_SIZE = 64
NEG_FILL = -1e30
EPSILON = 1e-05
F32 = jnp.float32
BF16 = jnp.bfloat16
LANES = 2 * HEAD_SIZE


def row_layout(lengths, group_map, packed_order):
    request_count = lengths.shape[0]
    picked = (packed_order[:, None] == jnp.arange(request_count, dtype=jnp.int32)[None, :]).astype(
        jnp.int32
    )
    packed_len = jnp.sum(picked * lengths[None, :], axis=1)
    packed_group = jnp.sum(picked * group_map[None, :], axis=1)
    ends_at = jnp.cumsum(packed_len)
    return (ends_at - packed_len, ends_at, packed_group)


def token_info(token_rows, starts_at, ends_at, packed_group):
    inside = (
        (token_rows[:, None] >= starts_at[None, :]) & (token_rows[:, None] < ends_at[None, :])
    ).astype(jnp.int32)
    return (
        jnp.sum(inside * packed_group[None, :], axis=1),
        jnp.sum(inside * starts_at[None, :], axis=1),
    )


def dot(a, b, contract_b=0):
    return lax.dot_general(
        a, b, (((1,), (contract_b,)), ((), ())), preferred_element_type=F32
    )


def attend_body(first, pieces, refs):
    q_ref, refs = refs[0], refs[1:]
    if not first:
        old_max, old_sum, old_acc = refs[:3]
        refs = refs[3:]
    kv = refs[: 3 * pieces]
    new_max, new_sum, new_acc = refs[3 * pieces :]
    pairs, rows = q_ref.shape[0], q_ref.shape[1]
    half = rows // 2
    low = lax.broadcasted_iota(jnp.int32, (half, LANES), 1) < HEAD_SIZE

    def pick(even, odd):
        return jnp.where(low, even, odd)

    for j in range(pairs):
        q = q_ref[j]
        lanes = slice(j * LANES, (j + 1) * LANES)
        scores = []
        for i in range(pieces):
            k_ref, bias_ref = kv[3 * i], kv[3 * i + 2]
            s = dot(q, k_ref[:, lanes], 1)
            keys = s.shape[1]
            bias = bias_ref[...]
            s = s.reshape(rows // bias.shape[0], bias.shape[0], keys) + bias[None]
            scores.append(s.reshape(rows, keys))
        top = functools.reduce(
            jnp.maximum, [jnp.max(s, axis=1, keepdims=True) for s in scores]
        )
        if first:
            row_max = top
            pair_max = pick(row_max[:half], row_max[half:])
        else:
            old = old_max[j]
            pair_max = jnp.maximum(old, pick(top[:half], top[half:]))
            row_max = jnp.concatenate(
                [pair_max[:, :1], pair_max[:, HEAD_SIZE : HEAD_SIZE + 1]], axis=0
            )
        total = None
        for i in range(pieces):
            v_ref = kv[3 * i + 1]
            w = jnp.exp(scores[i] - row_max).astype(BF16)
            v = v_ref[:, lanes]
            v = jnp.concatenate([v, jnp.ones_like(v)], axis=1)
            part = dot(w, v)
            total = part if total is None else total + part
        acc = pick(total[:half, :LANES], total[half:, :LANES])
        summed = pick(total[:half, LANES:], total[half:, LANES:])
        if not first:
            scale = jnp.exp(old - pair_max)
            acc = acc + scale * old_acc[j]
            summed = summed + scale * old_sum[j]
        new_max[j] = pair_max
        new_sum[j] = summed
        new_acc[j] = acc


def attend(q, state, blocks):
    pairs, rows, lanes = q.shape
    first = state is None

    def kernel(*refs):
        attend_body(first, len(blocks), refs)

    shape = jax.ShapeDtypeStruct((pairs, rows // 2, lanes), F32)
    operands = [q] + ([] if first else list(state)) + [a for block in blocks for a in block]
    keys = sum(block[0].shape[0] for block in blocks)
    vmem = pl.BlockSpec(memory_space=pltpu.VMEM)
    return pl.pallas_call(
        kernel,
        out_shape=[shape] * 3,
        in_specs=[vmem] * len(operands),
        out_specs=[vmem] * 3,
        compiler_params=pltpu.CompilerParams(vmem_limit_bytes=48 * 2**20),
        cost_estimate=pl.CostEstimate(
            flops=pairs * rows * keys * lanes * 6,
            bytes_accessed=6 * pairs * rows * lanes * 2,
            transcendentals=pairs * rows * keys,
        ),
        name="attend",
    )(*operands)


def project_body(order_ref, sum_ref, acc_ref, weight_ref, residual_ref, gain_ref, hidden_ref, normed_ref, held):
    pairs, rows, lanes = acc_ref.shape
    tokens = residual_ref.shape[0]
    per = rows // tokens
    hidden = residual_ref[...].astype(F32)
    for j in range(pairs):
        out = (acc_ref[j] / sum_ref[j]).astype(BF16)
        for r in range(0, per, 2):
            left = jnp.concatenate(
                [out[r * tokens : (r + 1) * tokens], out[(r + 1) * tokens : (r + 2) * tokens]], axis=1
            )
            heads = [(2 * j) * per + r, (2 * j + 1) * per + r, (2 * j) * per + r + 1, (2 * j + 1) * per + r + 1]
            right = jnp.concatenate(
                [weight_ref[h * HEAD_SIZE : (h + 1) * HEAD_SIZE, :] for h in heads], axis=0
            )
            hidden = hidden + dot(left, right)
    hidden_ref[...] = hidden
    mean = jnp.mean(hidden * hidden, axis=1, keepdims=True)
    held[...] = hidden * lax.rsqrt(mean + EPSILON) * gain_ref[...]
    blocks = order_ref.shape[0]
    width = hidden.shape[1] // blocks
    for b in range(blocks):
        start = pl.multiple_of(order_ref[b] * width, width)
        normed_ref[:, b * width : (b + 1) * width] = held[:, pl.ds(start, width)].astype(BF16)


def project(order, state, out_weight, residual, gain):
    tokens, width = residual.shape
    vmem = pl.BlockSpec(memory_space=pltpu.VMEM)
    return pl.pallas_call(
        project_body,
        out_shape=[
            jax.ShapeDtypeStruct((tokens, width), F32),
            jax.ShapeDtypeStruct((tokens, width), BF16),
        ],
        in_specs=[pl.BlockSpec(memory_space=pltpu.SMEM)] + [vmem] * 5,
        out_specs=[vmem] * 2,
        scratch_shapes=[pltpu.VMEM((tokens, width), F32)],
        compiler_params=pltpu.CompilerParams(vmem_limit_bytes=48 * 2**20),
        cost_estimate=pl.CostEstimate(
            flops=2 * tokens * out_weight.size,
            bytes_accessed=out_weight.size * 2 + tokens * width * 8,
            transcendentals=0,
        ),
        name="project",
    )(order, state[1], state[2], out_weight, residual, gain)


def ffn_body(parts, blocks, tokens, refs):
    n_refs, refs = refs[:parts], refs[parts:]
    gates, refs = refs[:blocks], refs[blocks:]
    ups, refs = refs[:blocks], refs[blocks:]
    downs, refs = refs[:blocks], refs[blocks:]
    outs, total = refs[:parts], refs[parts]
    step, steps = pl.program_id(0), pl.num_programs(0)
    depth = gates[0].shape[0]
    gate = up = None
    for b in range(blocks):
        x = jnp.concatenate([n[:, b * depth : (b + 1) * depth] for n in n_refs], axis=0)
        g, u = dot(x, gates[b][...]), dot(x, ups[b][...])
        gate, up = (g, u) if gate is None else (gate + g, up + u)
    act = (gate / (1.0 + jnp.exp(-gate)) * up).astype(BF16)
    width = downs[0].shape[1]
    for b in range(blocks):
        term = dot(act, downs[b][...])
        cols = slice(b * width, (b + 1) * width)

        @pl.when(step == 0)
        def _():
            total[:, cols] = term

        @pl.when(step > 0)
        def _():
            total[:, cols] += term

    @pl.when(step == steps - 1)
    def _():
        for i in range(parts):
            outs[i][...] = total[i * tokens : (i + 1) * tokens, :].astype(BF16)


def ffn(normed, gates, ups, downs):
    parts, blocks = len(normed), len(gates)
    tokens, model = normed[0].shape
    depth, hidden = gates[0].shape
    width = downs[0].shape[1]
    tile = math.gcd(hidden, 256)

    def kernel(*refs):
        ffn_body(parts, blocks, tokens, refs)

    whole = pl.BlockSpec((tokens, model), lambda i: (0, 0))
    return pl.pallas_call(
        kernel,
        grid=(hidden // tile,),
        out_shape=[jax.ShapeDtypeStruct((tokens, model), BF16)] * parts,
        in_specs=[whole] * parts
        + [pl.BlockSpec((depth, tile), lambda i: (0, i))] * (2 * blocks)
        + [pl.BlockSpec((tile, width), lambda i: (i, 0))] * blocks,
        out_specs=[whole] * parts,
        scratch_shapes=[pltpu.VMEM((parts * tokens, model), F32)],
        compiler_params=pltpu.CompilerParams(vmem_limit_bytes=48 * 2**20),
        cost_estimate=pl.CostEstimate(
            flops=6 * parts * tokens * model * hidden,
            bytes_accessed=6 * model * hidden + 4 * parts * tokens * model,
            transcendentals=parts * tokens * hidden,
        ),
        name="ffn",
    )(*normed, *gates, *ups, *downs)


def shards(
    grps,
    devs,
    residual,
    queries,
    keys,
    values,
    prefix_keys,
    cached_prefix_values,
    out_weight,
    norm_gain,
    w_gate,
    w_up,
    w_down,
    suffix_lengths,
    request_group,
    placement_order,
):
    depth_z = math.gcd(devs, 4)
    depth_y = devs // depth_z
    cores = 2
    depth_x = grps // cores
    z_shift = [
        (z * depth_y + y, (z + 1) % depth_z * depth_y + y)
        for z in range(depth_z)
        for y in range(depth_y)
    ]

    def y_shift(by):
        return [
            (z * depth_y + y, z * depth_y + (y + by) % depth_y)
            for z in range(depth_z)
            for y in range(depth_y)
        ]

    x_shift = [
        (x * cores + c, (x + 1) % depth_x * cores + c) for x in range(depth_x) for c in range(cores)
    ]
    core_swap = [(x * cores + c, x * cores + 1 - c) for x in range(depth_x) for c in range(cores)]

    def spread(block):
        held = {}
        for zs in range(depth_z):
            if zs:
                block = lax.ppermute(block, "dev", z_shift)
            held[zs, 0] = block
            for ys in range(1, depth_y):
                held[zs, ys] = lax.ppermute(block, "dev", y_shift(ys))
        return held

    def collect(weight):
        blocks = []
        for xs in range(depth_x):
            if xs:
                weight = lax.ppermute(weight, "grp", x_shift)
            blocks += [weight, lax.ppermute(weight, "grp", core_swap)]
        return blocks

    tokens = queries.shape[0]
    width = keys.shape[1]
    groups, span = prefix_keys.shape[:2]
    pairs = width // LANES
    per = queries.shape[1] // width

    prefix = spread(
        jnp.stack([prefix_keys.reshape(-1, width), cached_prefix_values.reshape(-1, width)])
    )
    before = lax.ppermute(
        jnp.stack([keys, values]), "dev", [(i, i + 1) for i in range(devs - 1)]
    )
    gates, ups, downs = collect(w_gate), collect(w_up), collect(w_down)

    starts_at, ends_at, packed_group = row_layout(
        suffix_lengths[0], request_group[0], placement_order[0]
    )
    base_row = lax.axis_index("dev") * tokens
    own_rows = base_row + jnp.arange(tokens, dtype=jnp.int32)
    own_group, own_start = token_info(own_rows, starts_at, ends_at, packed_group)
    window = base_row - tokens + jnp.arange(2 * tokens, dtype=jnp.int32)
    suffix_bias = jnp.where(
        (window[None, :] >= own_start[:, None]) & (window[None, :] <= own_rows[:, None]), 0.0, NEG_FILL
    ).astype(F32)
    key_group = jnp.arange(groups * span, dtype=jnp.int32) // span
    prefix_bias = jnp.where(own_group[:, None] == key_group[None, :], 0.0, NEG_FILL).astype(F32)

    q = (queries * BF16(HEAD_SIZE ** (-0.5))).reshape(tokens, pairs, 2, per, HEAD_SIZE)
    q = q.transpose(1, 2, 3, 0, 4)
    empty = jnp.zeros_like(q[:, 0])
    q = jnp.stack(
        [
            jnp.concatenate([q[:, 0], empty], axis=-1),
            jnp.concatenate([empty, q[:, 1]], axis=-1),
        ],
        axis=1,
    ).reshape(pairs, 2 * per * tokens, LANES)

    state = attend(
        q,
        None,
        [
            (before[0], before[1], suffix_bias[:, :tokens]),
            (keys, values, suffix_bias[:, tokens:]),
            (prefix[0, 0][0], prefix[0, 0][1], prefix_bias),
        ],
    )
    for t in range(1, depth_z + depth_y - 1):
        arrived = [prefix[zs, t - zs] for zs in range(depth_z) if (zs, t - zs) in prefix]
        state = attend(q, state, [(b[0], b[1], prefix_bias) for b in arrived])

    me = lax.axis_index("grp")
    my_x, my_core = me // cores, me % cores
    order = jnp.stack(
        [
            (my_x + depth_x - xs) % depth_x * cores + (my_core + cs) % cores
            for xs in range(depth_x)
            for cs in range(cores)
        ]
    ).astype(jnp.int32)
    hidden_state, normed = project(order, state, out_weight, residual, norm_gain[None])

    chunks = spread(normed)
    terms = {}
    running = None
    for zs in list(range(1, depth_z)) + [0]:
        parts = ffn([chunks[zs, ys] for ys in range(depth_y)], gates, ups, downs)
        mine = parts[0].astype(F32)
        for ys in range(1, depth_y):
            mine = mine + lax.ppermute(parts[ys], "dev", y_shift(-ys)).astype(F32)
        if running is not None:
            mine = mine + lax.ppermute(running, "dev", z_shift).astype(F32)
        running = mine.astype(BF16)
    mlp_sum = mine
    block = mlp_sum.shape[1] // grps
    outcome = jnp.zeros_like(hidden_state)
    for b in range(grps):
        outcome = lax.dynamic_update_slice_in_dim(
            outcome, mlp_sum[:, b * block : (b + 1) * block], order[b] * block, 1
        )
    return (hidden_state + outcome).astype(BF16)


def solution(mesh):
    placed = (
        P(("grp", "dev"), None),
        P(("grp", "dev"), None),
        P(("grp", "dev"), None),
        P(("grp", "dev"), None),
        P("grp", "dev", None),
        P("grp", "dev", None),
        P(),
        P(),
        P("grp", "dev"),
        P("grp", "dev"),
        P("dev", "grp"),
        P("grp", None),
        P("grp", None),
        P("grp", None),
    )
    return jax.shard_map(
        functools.partial(shards, mesh.shape["grp"], mesh.shape["dev"]),
        mesh=mesh,
        in_specs=placed,
        out_specs=P(("grp", "dev"), None),
        check_vma=False,
    )
```

```python
import functools
import math

import jax
import jax.numpy as jnp
from jax import lax
from jax.experimental import pallas as pl
from jax.experimental.pallas import tpu as pltpu
from jax.sharding import PartitionSpec as P

HEAD_SIZE = 64
NEG_FILL = -1e30
EPSILON = 1e-05
F32 = jnp.float32
BF16 = jnp.bfloat16
LANES = 2 * HEAD_SIZE
CORES = 2


def dot(a, b, contract_b=0):
    return lax.dot_general(
        a, b, (((1,), (contract_b,)), ((), ())), preferred_element_type=F32
    )


def prepare_body(place_ref, lengths_ref, groups_ref, packing_ref, queries_ref, q_ref, suffix_ref, prefix_ref):
    tokens = queries_ref.shape[0]
    pairs, rows = q_ref.shape[0], q_ref.shape[1]
    per = rows // (2 * tokens)
    base = place_ref[0] * tokens
    span = prefix_ref.shape[1] // place_ref.shape[0]
    own = base + lax.broadcasted_iota(jnp.int32, (tokens, LANES), 0)

    def request(k, carry):
        start, group, first = carry
        j = packing_ref[0, k]
        end = start + lengths_ref[0, j]
        inside = (own >= start) & (own < end)
        return (
            end,
            jnp.where(inside, groups_ref[0, j], group),
            jnp.where(inside, start, first),
        )

    zero = jnp.zeros((tokens, LANES), jnp.int32)
    _, group, first = lax.fori_loop(0, lengths_ref.shape[1], request, (jnp.int32(0), zero, zero))
    for c in range(suffix_ref.shape[1] // LANES):
        key = base - tokens + c * LANES + lax.broadcasted_iota(jnp.int32, (tokens, LANES), 1)
        suffix_ref[:, c * LANES : (c + 1) * LANES] = jnp.where(
            (key >= first) & (key <= own), 0.0, NEG_FILL
        )
    for c in range(prefix_ref.shape[1] // LANES):
        key_group = lax.div(c * LANES + lax.broadcasted_iota(jnp.int32, (tokens, LANES), 1), span)
        prefix_ref[:, c * LANES : (c + 1) * LANES] = jnp.where(group == key_group, 0.0, NEG_FILL)
    low = lax.broadcasted_iota(jnp.int32, (tokens, LANES), 1) < HEAD_SIZE
    for j in range(pairs):
        for parity in range(2):
            for r in range(per):
                head = (2 * j + parity) * per + r
                block = head // 2
                q = queries_ref[:, block * LANES : (block + 1) * LANES].astype(F32) * HEAD_SIZE ** (-0.5)
                if head % 2 != parity:
                    q = pltpu.roll(q, HEAD_SIZE, 1)
                q = jnp.where(low == (parity == 0), q, 0.0)
                row = (parity * per + r) * tokens
                q_ref[j, row : row + tokens, :] = q.astype(BF16)


def prepare(place, groups, span, lengths, request_group, packing, queries, width):
    tokens = queries.shape[0]
    per = queries.shape[1] // width
    vmem = pl.BlockSpec(memory_space=pltpu.VMEM)
    smem = pl.BlockSpec(memory_space=pltpu.SMEM)
    return pl.pallas_call(
        prepare_body,
        out_shape=[
            jax.ShapeDtypeStruct((width // LANES, 2 * per * tokens, LANES), BF16),
            jax.ShapeDtypeStruct((tokens, 2 * tokens), F32),
            jax.ShapeDtypeStruct((tokens, groups * span), F32),
        ],
        in_specs=[smem] * 4 + [vmem],
        out_specs=[vmem] * 3,
        cost_estimate=pl.CostEstimate(flops=0, bytes_accessed=4 * 2**20, transcendentals=0),
        name="prepare",
    )(jnp.full((groups,), place, jnp.int32), lengths, request_group, packing, queries)


def attend_body(first, pieces, refs):
    q_ref, refs = refs[0], refs[1:]
    if not first:
        old_max, old_sum, old_acc = refs[:3]
        refs = refs[3:]
    kv = refs[: 3 * pieces]
    new_max, new_sum, new_acc = refs[-3:]
    pairs, rows = q_ref.shape[0], q_ref.shape[1]
    half = rows // 2
    low = lax.broadcasted_iota(jnp.int32, (half, LANES), 1) < HEAD_SIZE

    def pick(even, odd):
        return jnp.where(low, even, odd)

    for j in range(pairs):
        q = q_ref[j]
        lanes = slice(j * LANES, (j + 1) * LANES)
        scores = []
        for i in range(pieces):
            k_ref, bias_ref = kv[3 * i], kv[3 * i + 2]
            s = dot(q, k_ref[:, lanes], 1)
            keys = s.shape[1]
            bias = bias_ref[...]
            s = s.reshape(rows // bias.shape[0], bias.shape[0], keys) + bias[None]
            scores.append(s.reshape(rows, keys))
        top = functools.reduce(
            jnp.maximum, [jnp.max(s, axis=1, keepdims=True) for s in scores]
        )
        if first:
            row_max = top
            pair_max = pick(row_max[:half], row_max[half:])
        else:
            old = old_max[j]
            pair_max = jnp.maximum(old, pick(top[:half], top[half:]))
            row_max = jnp.concatenate(
                [pair_max[:, :1], pair_max[:, HEAD_SIZE : HEAD_SIZE + 1]], axis=0
            )
        total = None
        for i in range(pieces):
            v_ref = kv[3 * i + 1]
            w = jnp.exp(scores[i] - row_max).astype(BF16)
            v = v_ref[:, lanes]
            v = jnp.concatenate([v, jnp.ones_like(v)], axis=1)
            part = dot(w, v)
            total = part if total is None else total + part
        acc = pick(total[:half, :LANES], total[half:, :LANES])
        summed = pick(total[:half, LANES:], total[half:, LANES:])
        if not first:
            scale = jnp.exp(old - pair_max)
            acc = acc + scale * old_acc[j]
            summed = summed + scale * old_sum[j]
        new_max[j] = pair_max
        new_sum[j] = summed
        new_acc[j] = acc


def attend(q, state, separate, stacked, after=()):
    pairs, rows, lanes = q.shape
    first = state is None
    blocks = len(separate) + len(stacked)

    def kernel(*refs):
        lead = 1 + (0 if first else 3)
        head, tail = list(refs[:lead]), refs[lead:]
        for _ in separate:
            head += tail[:3]
            tail = tail[3:]
        for _ in stacked:
            head += [tail[0].at[0], tail[0].at[1], tail[1]]
            tail = tail[2:]
        attend_body(first, blocks, head + list(tail[-3:]))

    shape = jax.ShapeDtypeStruct((pairs, rows // 2, lanes), F32)
    operands = [q] + ([] if first else list(state))
    operands += [a for block in list(separate) + list(stacked) for a in block]
    keys = sum(block[-1].shape[1] for block in list(separate) + list(stacked))
    vmem = pl.BlockSpec(memory_space=pltpu.VMEM)
    return pl.pallas_call(
        kernel,
        out_shape=[shape] * 3,
        in_specs=[vmem] * len(operands) + [pl.BlockSpec(memory_space=pl.ANY)] * len(after),
        out_specs=[vmem] * 3,
        compiler_params=pltpu.CompilerParams(vmem_limit_bytes=28 * 2**20),
        cost_estimate=pl.CostEstimate(
            flops=pairs * rows * keys * lanes * 6,
            bytes_accessed=6 * pairs * rows * lanes * 2,
            transcendentals=pairs * rows * keys,
        ),
        name="attend",
    )(*operands, *after)


def block_owner(me, blocks, step):
    chips = blocks // CORES
    x, core = lax.div(me, CORES), lax.rem(me, CORES)
    x = lax.rem(x + chips - step // CORES, chips)
    return x * CORES + lax.rem(core + step % CORES, CORES)


def project_body(blocks, me_ref, sum_ref, acc_ref, weight_ref, residual_ref, gain_ref, *refs):
    hidden_ref, normed_ref, held = refs[-3:]
    pairs, rows, lanes = acc_ref.shape
    tokens = residual_ref.shape[0]
    per = rows // tokens
    hidden = residual_ref[...].astype(F32)
    for j in range(pairs):
        out = (acc_ref[j] / sum_ref[j]).astype(BF16)
        for r in range(0, per, 2):
            left = jnp.concatenate(
                [out[r * tokens : (r + 1) * tokens], out[(r + 1) * tokens : (r + 2) * tokens]], axis=1
            )
            heads = [(2 * j) * per + r, (2 * j + 1) * per + r, (2 * j) * per + r + 1, (2 * j + 1) * per + r + 1]
            right = jnp.concatenate(
                [weight_ref[h * HEAD_SIZE : (h + 1) * HEAD_SIZE, :] for h in heads], axis=0
            )
            hidden = hidden + dot(left, right)
    hidden_ref[...] = hidden
    mean = jnp.mean(hidden * hidden, axis=1, keepdims=True)
    held[...] = hidden * lax.rsqrt(mean + EPSILON) * gain_ref[...]
    width = hidden.shape[1] // blocks
    for b in range(blocks):
        start = pl.multiple_of(block_owner(me_ref[0], blocks, b) * width, width)
        normed_ref[:, b * width : (b + 1) * width] = held[:, pl.ds(start, width)].astype(BF16)


def project(me, blocks, state, out_weight, residual, gain, after=()):
    tokens, width = residual.shape
    vmem = pl.BlockSpec(memory_space=pltpu.VMEM)
    return pl.pallas_call(
        functools.partial(project_body, blocks),
        out_shape=[
            jax.ShapeDtypeStruct((tokens, width), F32),
            jax.ShapeDtypeStruct((tokens, width), BF16),
        ],
        in_specs=[pl.BlockSpec(memory_space=pltpu.SMEM)]
        + [vmem] * 5
        + [pl.BlockSpec(memory_space=pl.ANY)] * len(after),
        out_specs=[vmem] * 2,
        scratch_shapes=[pltpu.VMEM((tokens, width), F32)],
        compiler_params=pltpu.CompilerParams(vmem_limit_bytes=28 * 2**20),
        cost_estimate=pl.CostEstimate(
            flops=2 * tokens * out_weight.size,
            bytes_accessed=out_weight.size * 2 + tokens * width * 8,
            transcendentals=0,
        ),
        name="project",
    )(me, state[1], state[2], out_weight, residual, gain, *after)


def ffn_body(parts, blocks, tokens, refs):
    n_refs, refs = refs[:parts], refs[parts:]
    gates, refs = refs[:blocks], refs[blocks:]
    ups, refs = refs[:blocks], refs[blocks:]
    downs, refs = refs[:blocks], refs[blocks:]
    outs, x_ref, act_ref = refs[:parts], refs[parts], refs[parts + 1]
    for i in range(parts):
        x_ref[i * tokens : (i + 1) * tokens, :] = n_refs[i][...]
    depth, hidden = gates[0].shape
    tile = math.gcd(hidden, 256)

    @pl.loop(0, hidden // tile)
    def _(t):
        cols = pl.ds(pl.multiple_of(t * tile, tile), tile)
        gate = up = None
        for b in range(blocks):
            x = x_ref[:, b * depth : (b + 1) * depth]
            g, u = dot(x, gates[b][:, cols]), dot(x, ups[b][:, cols])
            gate, up = (g, u) if gate is None else (gate + g, up + u)
        act_ref[:, cols] = (gate / (1.0 + jnp.exp(-gate)) * up).astype(BF16)

    width = downs[0].shape[1]
    tile_out = math.gcd(width, 256)
    for b in range(blocks):

        @pl.loop(0, width // tile_out)
        def _(t):
            term = dot(act_ref[...], downs[b][:, pl.ds(pl.multiple_of(t * tile_out, tile_out), tile_out)])
            cols = pl.ds(pl.multiple_of(b * width + t * tile_out, tile_out), tile_out)
            for i in range(parts):
                outs[i][:, cols] = term[i * tokens : (i + 1) * tokens].astype(BF16)


def ffn(normed, gates, ups, downs):
    parts, blocks = len(normed), len(gates)
    tokens, model = normed[0].shape
    hidden = gates[0].shape[1]

    def kernel(*refs):
        ffn_body(parts, blocks, tokens, refs)

    vmem = pl.BlockSpec(memory_space=pltpu.VMEM)
    return pl.pallas_call(
        kernel,
        out_shape=[jax.ShapeDtypeStruct((tokens, model), BF16)] * parts,
        in_specs=[vmem] * (parts + 3 * blocks),
        out_specs=[vmem] * parts,
        scratch_shapes=[
            pltpu.VMEM((parts * tokens, model), BF16),
            pltpu.VMEM((parts * tokens, hidden), BF16),
        ],
        compiler_params=pltpu.CompilerParams(vmem_limit_bytes=28 * 2**20),
        cost_estimate=pl.CostEstimate(
            flops=6 * parts * tokens * model * hidden,
            bytes_accessed=6 * model * hidden + 4 * parts * tokens * model,
            transcendentals=parts * tokens * hidden,
        ),
        name="ffn",
    )(*normed, *gates, *ups, *downs)


def finish_body(blocks, me_ref, hidden_ref, *refs):
    terms, out_ref = refs[:-1], refs[-1]
    width = out_ref.shape[1] // blocks
    for b in range(blocks):
        cols = slice(b * width, (b + 1) * width)
        place = pl.ds(pl.multiple_of(block_owner(me_ref[0], blocks, b) * width, width), width)
        total = hidden_ref[:, place]
        for term in terms:
            total = total + term[:, cols].astype(F32)
        out_ref[:, place] = total.astype(BF16)


def finish(me, blocks, hidden_state, terms):
    vmem = pl.BlockSpec(memory_space=pltpu.VMEM)
    return pl.pallas_call(
        functools.partial(finish_body, blocks),
        out_shape=jax.ShapeDtypeStruct(hidden_state.shape, BF16),
        in_specs=[pl.BlockSpec(memory_space=pltpu.SMEM)] + [vmem] * (1 + len(terms)),
        out_specs=vmem,
        cost_estimate=pl.CostEstimate(
            flops=0, bytes_accessed=hidden_state.size * (6 + 2 * len(terms)), transcendentals=0
        ),
        name="finish",
    )(me, hidden_state, *terms)


def shards(
    grps,
    devs,
    residual,
    queries,
    keys,
    values,
    prefix_keys,
    cached_prefix_values,
    out_weight,
    norm_gain,
    w_gate,
    w_up,
    w_down,
    suffix_lengths,
    request_group,
    placement_order,
):
    depth_z = math.gcd(devs, 4)
    depth_y = devs // depth_z
    cores = CORES
    depth_x = grps // cores
    z_shift = [
        (z * depth_y + y, (z + 1) % depth_z * depth_y + y)
        for z in range(depth_z)
        for y in range(depth_y)
    ]

    def y_shift(by):
        return [
            (z * depth_y + y, z * depth_y + (y + by) % depth_y)
            for z in range(depth_z)
            for y in range(depth_y)
        ]

    x_shift = [
        (x * cores + c, (x + 1) % depth_x * cores + c) for x in range(depth_x) for c in range(cores)
    ]
    core_swap = [(x * cores + c, x * cores + 1 - c) for x in range(depth_x) for c in range(cores)]

    def spread(block):
        held = {}
        for zs in range(depth_z):
            if zs:
                block = lax.ppermute(block, "dev", z_shift)
            held[zs, 0] = block
            for ys in range(1, depth_y):
                held[zs, ys] = lax.ppermute(block, "dev", y_shift(ys))
        return held

    def along_x(weight):
        blocks = [weight]
        for _ in range(1, depth_x):
            blocks.append(lax.ppermute(blocks[-1], "grp", x_shift))
        return blocks

    def both_cores(blocks):
        return [b for block in blocks for b in (block, lax.ppermute(block, "grp", core_swap))]

    tokens = queries.shape[0]
    width = keys.shape[1]
    groups, span = prefix_keys.shape[:2]

    prefix = spread(
        jnp.stack([prefix_keys.reshape(-1, width), cached_prefix_values.reshape(-1, width)])
    )
    onward = [(i, i + 1) for i in range(devs - 1)]
    before_keys, before_values = (
        lax.ppermute(keys, "dev", onward),
        lax.ppermute(values, "dev", onward),
    )
    gate_rows, up_rows, down_cols = along_x(w_gate), along_x(w_up), along_x(w_down)
    gates, ups, downs = both_cores(gate_rows), both_cores(up_rows), both_cores(down_cols)

    q, suffix_mask, prefix_mask = prepare(
        lax.axis_index("dev"),
        groups,
        span,
        suffix_lengths,
        request_group,
        placement_order,
        queries,
        width,
    )
    state = attend(
        q,
        None,
        [
            (before_keys, before_values, suffix_mask[:, :tokens]),
            (keys, values, suffix_mask[:, tokens:]),
        ],
        [(prefix[0, 0], prefix_mask)],
    )
    for t in range(1, depth_z + depth_y - 1):
        arrived = [prefix[zs, t - zs] for zs in range(depth_z) if (zs, t - zs) in prefix]
        state = attend(
            q, state, [], [(b, prefix_mask) for b in arrived], after=gate_rows[1:] if t == 1 else ()
        )

    me = lax.axis_index("grp").astype(jnp.int32).reshape(1)
    hidden_state, normed = project(
        me, grps, state, out_weight, residual, norm_gain[None], after=up_rows[1:]
    )

    chunks = spread(normed)
    running = None
    for zs in list(range(1, depth_z)) + [0]:
        parts = ffn([chunks[zs, ys] for ys in range(depth_y)], gates, ups, downs)
        terms = [parts[0]] + [
            lax.ppermute(parts[ys], "dev", y_shift(-ys)) for ys in range(1, depth_y)
        ]
        if running is not None:
            terms.append(lax.ppermute(running, "dev", z_shift))
        if zs:
            running = functools.reduce(jnp.add, [term.astype(F32) for term in terms]).astype(BF16)
    return finish(me, grps, hidden_state, terms)


def solution(mesh):
    placed = (
        P(("grp", "dev"), None),
        P(("grp", "dev"), None),
        P(("grp", "dev"), None),
        P(("grp", "dev"), None),
        P("grp", "dev", None),
        P("grp", "dev", None),
        P(),
        P(),
        P("grp", "dev"),
        P("grp", "dev"),
        P("dev", "grp"),
        P("grp", None),
        P("grp", None),
        P("grp", None),
    )
    return jax.shard_map(
        functools.partial(shards, mesh.shape["grp"], mesh.shape["dev"]),
        mesh=mesh,
        in_specs=placed,
        out_specs=P(("grp", "dev"), None),
        check_vma=False,
    )
```

```python
import functools
import math

import jax
import jax.numpy as jnp
from jax import lax
from jax.experimental import pallas as pl
from jax.experimental.pallas import tpu as pltpu
from jax.sharding import PartitionSpec as P

HEAD_SIZE = 64
NEG_FILL = -1e30
EPSILON = 1e-05
F32 = jnp.float32
BF16 = jnp.bfloat16
LANES = 2 * HEAD_SIZE
CORES = 2
LIGHT = pl.CostEstimate(flops=0, bytes_accessed=1024, transcendentals=0)


def dot(a, b, contract_b=0):
    return lax.dot_general(
        a, b, (((1,), (contract_b,)), ((), ())), preferred_element_type=F32
    )


def prepare_body(
    span,
    place_ref,
    lengths_hbm,
    groups_hbm,
    packing_hbm,
    queries_hbm,
    keys_hbm,
    values_hbm,
    *refs,
):
    q_ref, before_ref, within_ref, prefix_ref, own_ref = refs[:5]
    lengths_ref, groups_ref, packing_ref, queries_ref, sems = refs[5:]
    copies = [
        pltpu.make_async_copy(source, target, sems.at[i])
        for i, (source, target) in enumerate(
            [
                (lengths_hbm, lengths_ref),
                (groups_hbm, groups_ref),
                (packing_hbm, packing_ref),
                (queries_hbm, queries_ref),
                (keys_hbm, own_ref.at[0]),
                (values_hbm, own_ref.at[1]),
            ]
        )
    ]
    for copy in copies:
        copy.start()
    for copy in copies[:4]:
        copy.wait()
    tokens = queries_ref.shape[0]
    pairs, rows = q_ref.shape[0], q_ref.shape[1]
    per = rows // (2 * tokens)
    base = place_ref[0] * tokens
    own = base + lax.broadcasted_iota(jnp.int32, (tokens, LANES), 0)

    def request(k, carry):
        start, group, first = carry
        j = packing_ref[0, k]
        end = start + lengths_ref[0, j]
        inside = (own >= start) & (own < end)
        return (
            end,
            jnp.where(inside, groups_ref[0, j], group),
            jnp.where(inside, start, first),
        )

    zero = jnp.zeros((tokens, LANES), jnp.int32)
    _, group, first = lax.fori_loop(0, lengths_ref.shape[1], request, (jnp.int32(0), zero, zero))
    for ref, back in ((before_ref, tokens), (within_ref, 0)):
        for c in range(0, tokens, LANES):
            key = base - back + c + lax.broadcasted_iota(jnp.int32, (tokens, LANES), 1)
            ref[:, c : c + LANES] = jnp.where((key >= first) & (key <= own), 0.0, NEG_FILL)
    for c in range(0, prefix_ref.shape[1], LANES):
        key_group = lax.div(c + lax.broadcasted_iota(jnp.int32, (tokens, LANES), 1), span)
        prefix_ref[:, c : c + LANES] = jnp.where(group == key_group, 0.0, NEG_FILL)
    low = lax.broadcasted_iota(jnp.int32, (tokens, LANES), 1) < HEAD_SIZE
    for j in range(pairs):
        for parity in range(2):
            for r in range(per):
                head = (2 * j + parity) * per + r
                block = head // 2
                q = queries_ref[:, block * LANES : (block + 1) * LANES].astype(F32) * HEAD_SIZE ** (-0.5)
                if head % 2 != parity:
                    q = pltpu.roll(q, HEAD_SIZE, 1)
                q = jnp.where(low == (parity == 0), q, 0.0)
                row = (parity * per + r) * tokens
                q_ref[j, row : row + tokens, :] = q.astype(BF16)
    for copy in copies[4:]:
        copy.wait()


def prepare(place, groups, span, lengths, request_group, packing, queries, keys, values):
    tokens, width = keys.shape
    per = queries.shape[1] // width
    vmem = pl.BlockSpec(memory_space=pltpu.VMEM)
    return pl.pallas_call(
        functools.partial(prepare_body, span),
        out_shape=[
            jax.ShapeDtypeStruct((width // LANES, 2 * per * tokens, LANES), BF16),
            jax.ShapeDtypeStruct((tokens, tokens), F32),
            jax.ShapeDtypeStruct((tokens, tokens), F32),
            jax.ShapeDtypeStruct((tokens, groups * span), F32),
            jax.ShapeDtypeStruct((2, tokens, width), BF16),
        ],
        in_specs=[pl.BlockSpec(memory_space=pltpu.SMEM)] + [pl.BlockSpec(memory_space=pltpu.HBM)] * 6,
        out_specs=[vmem] * 5,
        compiler_params=pltpu.CompilerParams(vmem_limit_bytes=51 * 2**20),
        scratch_shapes=[pltpu.SMEM(lengths.shape, jnp.int32)] * 3
        + [pltpu.VMEM(queries.shape, BF16), pltpu.SemaphoreType.DMA((6,))],
        cost_estimate=LIGHT,
        name="prepare",
    )(place, lengths, request_group, packing, queries, keys, values)


def attend_body(first, pieces, refs):
    q_ref, refs = refs[0], refs[1:]
    if not first:
        old_max, old_sum, old_acc = refs[:3]
        refs = refs[3:]
    kv = refs[: 3 * pieces]
    new_max, new_sum, new_acc = refs[-3:]
    pairs, rows = q_ref.shape[0], q_ref.shape[1]
    half = rows // 2
    low = lax.broadcasted_iota(jnp.int32, (half, LANES), 1) < HEAD_SIZE

    def pick(even, odd):
        return jnp.where(low, even, odd)

    for j in range(pairs):
        q = q_ref[j]
        lanes = slice(j * LANES, (j + 1) * LANES)
        scores = []
        for i in range(pieces):
            k_ref, bias_ref = kv[3 * i], kv[3 * i + 2]
            s = dot(q, k_ref[:, lanes], 1)
            keys = s.shape[1]
            bias = bias_ref[...]
            s = s.reshape(rows // bias.shape[0], bias.shape[0], keys) + bias[None]
            scores.append(s.reshape(rows, keys))
        top = functools.reduce(
            jnp.maximum, [jnp.max(s, axis=1, keepdims=True) for s in scores]
        )
        if first:
            row_max = top
            pair_max = pick(row_max[:half], row_max[half:])
        else:
            old = old_max[j]
            pair_max = jnp.maximum(old, pick(top[:half], top[half:]))
            row_max = jnp.concatenate(
                [pair_max[:, :1], pair_max[:, HEAD_SIZE : HEAD_SIZE + 1]], axis=0
            )
        total = None
        for i in range(pieces):
            v_ref = kv[3 * i + 1]
            w = jnp.exp(scores[i] - row_max).astype(BF16)
            v = v_ref[:, lanes]
            v = jnp.concatenate([v, jnp.ones_like(v)], axis=1)
            part = dot(w, v)
            total = part if total is None else total + part
        acc = pick(total[:half, :LANES], total[half:, :LANES])
        summed = pick(total[:half, LANES:], total[half:, LANES:])
        if not first:
            scale = jnp.exp(old - pair_max)
            acc = acc + scale * old_acc[j]
            summed = summed + scale * old_sum[j]
        new_max[j] = pair_max
        new_sum[j] = summed
        new_acc[j] = acc


def attend(q, state, blocks, after=()):
    pairs, rows, lanes = q.shape
    first = state is None

    def kernel(*refs):
        lead = 1 + (0 if first else 3)
        head, tail = list(refs[:lead]), refs[lead:]
        for _ in blocks:
            head += [tail[0].at[0], tail[0].at[1], tail[1]]
            tail = tail[2:]
        attend_body(first, len(blocks), head + list(tail[-3:]))

    shape = jax.ShapeDtypeStruct((pairs, rows // 2, lanes), F32)
    operands = [q] + ([] if first else list(state)) + [a for block in blocks for a in block]
    vmem = pl.BlockSpec(memory_space=pltpu.VMEM)
    return pl.pallas_call(
        kernel,
        out_shape=[shape] * 3,
        in_specs=[vmem] * len(operands) + [pl.BlockSpec(memory_space=pl.ANY)] * len(after),
        out_specs=[vmem] * 3,
        compiler_params=pltpu.CompilerParams(vmem_limit_bytes=28 * 2**20),
        cost_estimate=LIGHT,
        name="attend",
    )(*operands, *after)


def block_owner(me, blocks, step):
    chips = blocks // CORES
    x, core = lax.div(me, CORES), lax.rem(me, CORES)
    x = lax.rem(x + chips - step // CORES, chips)
    return x * CORES + lax.rem(core + step % CORES, CORES)


def project_body(sum_ref, acc_ref, weight_ref, residual_ref, gain_ref, *refs):
    hidden_ref, normed_ref = refs[-2:]
    pairs, rows, lanes = acc_ref.shape
    tokens = residual_ref.shape[0]
    per = rows // tokens
    hidden = residual_ref[...].astype(F32)
    for j in range(pairs):
        out = (acc_ref[j] / sum_ref[j]).astype(BF16)
        for r in range(0, per, 2):
            left = jnp.concatenate(
                [out[r * tokens : (r + 1) * tokens], out[(r + 1) * tokens : (r + 2) * tokens]], axis=1
            )
            heads = [(2 * j) * per + r, (2 * j + 1) * per + r, (2 * j) * per + r + 1, (2 * j + 1) * per + r + 1]
            right = jnp.concatenate(
                [weight_ref[h * HEAD_SIZE : (h + 1) * HEAD_SIZE, :] for h in heads], axis=0
            )
            hidden = hidden + dot(left, right)
    hidden_ref[...] = hidden
    mean = jnp.mean(hidden * hidden, axis=1, keepdims=True)
    normed_ref[...] = (hidden * lax.rsqrt(mean + EPSILON) * gain_ref[...]).astype(BF16)


def project(state, out_weight, residual, gain, after=()):
    tokens, width = residual.shape
    vmem = pl.BlockSpec(memory_space=pltpu.VMEM)
    return pl.pallas_call(
        project_body,
        out_shape=[
            jax.ShapeDtypeStruct((tokens, width), F32),
            jax.ShapeDtypeStruct((tokens, width), BF16),
        ],
        in_specs=[vmem] * 5 + [pl.BlockSpec(memory_space=pl.ANY)] * len(after),
        out_specs=[vmem] * 2,
        compiler_params=pltpu.CompilerParams(vmem_limit_bytes=28 * 2**20),
        cost_estimate=LIGHT,
        name="project",
    )(state[1], state[2], out_weight, residual, gain, *after)


def ffn_body(parts, blocks, tokens, refs):
    n_refs, (gate_ref, up_ref), refs = refs[:parts], refs[parts : parts + 2], refs[parts + 2 :]
    downs = refs[:blocks]
    outs, x_ref, act_ref = refs[-2 - parts : -2], refs[-2], refs[-1]
    for i in range(parts):
        x_ref[i * tokens : (i + 1) * tokens, :] = n_refs[i][...]
    hidden = gate_ref.shape[1]
    tile = math.gcd(hidden, 256)

    @pl.loop(0, hidden // tile)
    def _(t):
        cols = pl.ds(pl.multiple_of(t * tile, tile), tile)
        gate, up = dot(x_ref[...], gate_ref[:, cols]), dot(x_ref[...], up_ref[:, cols])
        act_ref[:, cols] = (gate / (1.0 + jnp.exp(-gate)) * up).astype(BF16)

    width = downs[0].shape[1]
    tile_out = math.gcd(width, 256)
    for b in range(blocks):

        @pl.loop(0, width // tile_out)
        def _(t):
            term = dot(act_ref[...], downs[b][:, pl.ds(pl.multiple_of(t * tile_out, tile_out), tile_out)])
            cols = pl.ds(pl.multiple_of(b * width + t * tile_out, tile_out), tile_out)
            for i in range(parts):
                outs[i][:, cols] = term[i * tokens : (i + 1) * tokens].astype(BF16)


def ffn(normed, gate, up, downs, after=()):
    parts, blocks = len(normed), len(downs)
    tokens, model = normed[0].shape
    hidden = gate.shape[1]

    def kernel(*refs):
        ffn_body(parts, blocks, tokens, refs)

    vmem = pl.BlockSpec(memory_space=pltpu.VMEM)
    return pl.pallas_call(
        kernel,
        out_shape=[jax.ShapeDtypeStruct((tokens, model), BF16)] * parts,
        in_specs=[vmem] * (parts + 2 + blocks) + [pl.BlockSpec(memory_space=pl.ANY)] * len(after),
        out_specs=[vmem] * parts,
        scratch_shapes=[
            pltpu.VMEM((parts * tokens, model), BF16),
            pltpu.VMEM((parts * tokens, hidden), BF16),
        ],
        compiler_params=pltpu.CompilerParams(vmem_limit_bytes=28 * 2**20),
        cost_estimate=LIGHT,
        name="ffn",
    )(*normed, gate, up, *downs, *after)


def finish_body(blocks, me_ref, hidden_ref, *refs):
    terms, out_ref = refs[:-1], refs[-1]
    width = out_ref.shape[1] // blocks
    for b in range(blocks):
        cols = slice(b * width, (b + 1) * width)
        place = pl.ds(pl.multiple_of(block_owner(me_ref[0], blocks, b) * width, width), width)
        total = hidden_ref[:, place]
        for term in terms:
            total = total + term[:, cols].astype(F32)
        out_ref[:, place] = total.astype(BF16)


def finish(me, blocks, hidden_state, terms):
    vmem = pl.BlockSpec(memory_space=pltpu.VMEM)
    return pl.pallas_call(
        functools.partial(finish_body, blocks),
        out_shape=jax.ShapeDtypeStruct(hidden_state.shape, BF16),
        in_specs=[pl.BlockSpec(memory_space=pltpu.SMEM)] + [vmem] * (1 + len(terms)),
        out_specs=vmem,
        cost_estimate=LIGHT,
        name="finish",
    )(me, hidden_state, *terms)


def tie(array, *others):
    return lax.optimization_barrier((array, *others))[0]


def shards(
    grps,
    devs,
    residual,
    queries,
    keys,
    values,
    prefix_keys,
    cached_prefix_values,
    out_weight,
    norm_gain,
    w_gate,
    w_up,
    w_down,
    suffix_lengths,
    request_group,
    placement_order,
):
    depth_z = math.gcd(devs, 4)
    depth_y = devs // depth_z
    cores = CORES
    depth_x = grps // cores
    def shift(by_z, by_y):
        return [
            (
                z * depth_y + y,
                (z + by_z) % depth_z * depth_y + (y + by_y) % depth_y,
            )
            for z in range(depth_z)
            for y in range(depth_y)
        ]

    x_shift = [
        (x * cores + c, (x + 1) % depth_x * cores + c) for x in range(depth_x) for c in range(cores)
    ]
    core_swap = [(x * cores + c, x * cores + 1 - c) for x in range(depth_x) for c in range(cores)]

    def along_y(block):
        return [block] + [lax.ppermute(block, "dev", shift(0, ys)) for ys in range(1, depth_y)]

    def along_x(weight):
        blocks = [weight]
        for _ in range(1, depth_x):
            blocks.append(lax.ppermute(blocks[-1], "grp", x_shift))
        return blocks

    def other_core(block, *others):
        return lax.ppermute(tie(block, *others), "grp", core_swap)

    tokens = queries.shape[0]
    width = keys.shape[1]
    groups, span = prefix_keys.shape[:2]

    place = lax.axis_index("dev").astype(jnp.int32).reshape(1)
    me = lax.axis_index("grp").astype(jnp.int32).reshape(1)
    prefix = jnp.stack([prefix_keys.reshape(-1, width), cached_prefix_values.reshape(-1, width)])
    forward = lax.ppermute(prefix, "dev", shift(1, 0))
    backward = lax.ppermute(prefix, "dev", shift(-1, 0))
    here = along_y(prefix)
    q, before_mask, within_mask, prefix_mask, own = prepare(
        place,
        groups,
        span,
        suffix_lengths,
        request_group,
        placement_order,
        queries,
        keys,
        values,
    )
    gate = lax.all_gather(w_gate, "grp", axis=0, tiled=True)
    up = lax.all_gather(w_up, "grp", axis=0, tiled=True)
    before = lax.ppermute(own, "dev", [(i, i + 1) for i in range(devs - 1)])
    forward, backward = tie(forward, q), tie(backward, q)
    late = along_y(forward)[1:] + along_y(backward)[1:]
    first = attend(
        q,
        None,
        [(before, before_mask), (own, within_mask)]
        + [(b, prefix_mask) for b in here + [forward, backward]],
    )
    down_cols = along_x(tie(w_down, first[0]))
    last = []
    for zs in range(2, depth_z - 1):
        forward = lax.ppermute(forward, "dev", shift(1, 0))
        late.append(forward)
        last += along_y(forward)[1:]
    state = attend(q, first, [(b, prefix_mask) for b in late])
    state = attend(q, state, [(b, prefix_mask) for b in last])
    hidden_state, normed = project(state, out_weight, tie(residual, gate), norm_gain[None])

    chunks = [along_y(normed)]
    arrived = normed
    for zs in range(1, depth_z):
        if zs > 1:
            arrived = tie(arrived, *chunks[zs - 2][1:])
        if zs == depth_z - 1:
            arrived = tie(arrived, *down_cols[1:])
        arrived = lax.ppermute(arrived, "dev", shift(1, 0))
        chunks.append(along_y(arrived))
    downs = [w_down, other_core(w_down, normed)]
    for cols in down_cols[1:]:
        downs += [cols, other_core(cols, chunks[2][0])]

    running = None
    for zs in list(range(1, depth_z)) + [0]:
        parts = ffn(chunks[zs], gate, up, downs)
        terms = [parts[0]] + [
            lax.ppermute(parts[ys], "dev", shift(0, -ys)) for ys in range(1, depth_y)
        ]
        if running is not None:
            terms.append(lax.ppermute(running, "dev", shift(1, 0)))
        if zs:
            running = functools.reduce(jnp.add, [term.astype(F32) for term in terms]).astype(BF16)
    return finish(me, grps, hidden_state, terms)


def solution(mesh):
    placed = (
        P(("grp", "dev"), None),
        P(("grp", "dev"), None),
        P(("grp", "dev"), None),
        P(("grp", "dev"), None),
        P("grp", "dev", None),
        P("grp", "dev", None),
        P(),
        P(),
        P("grp", "dev"),
        P("grp", "dev"),
        P("dev", "grp"),
        P("grp", None),
        P("grp", None),
        P("grp", None),
    )
    return jax.shard_map(
        functools.partial(shards, mesh.shape["grp"], mesh.shape["dev"]),
        mesh=mesh,
        in_specs=placed,
        out_specs=P(("grp", "dev"), None),
        check_vma=False,
    )
```

```python
import functools
import math

import jax
import jax.numpy as jnp
from jax import lax
from jax.experimental import pallas as pl
from jax.experimental.pallas import tpu as pltpu
from jax.sharding import PartitionSpec as P

HEAD_SIZE = 64
NEG_FILL = -1e30
EPSILON = 1e-05
F32 = jnp.float32
BF16 = jnp.bfloat16
LANES = 2 * HEAD_SIZE
CORES = 2


def cost(microseconds):
    return pl.CostEstimate(flops=0, bytes_accessed=int(microseconds * 3.5e6), transcendentals=0)


def dot(a, b, contract_b=0):
    return lax.dot_general(
        a, b, (((1,), (contract_b,)), ((), ())), preferred_element_type=F32
    )


def prepare_body(
    span,
    place_ref,
    lengths_hbm,
    groups_hbm,
    packing_hbm,
    queries_hbm,
    *refs,
):
    q_ref, before_ref, within_ref, prefix_ref = refs[:4]
    lengths_ref, groups_ref, packing_ref, queries_ref, sems = refs[4:]
    copies = [
        pltpu.make_async_copy(source, target, sems.at[i])
        for i, (source, target) in enumerate(
            [
                (lengths_hbm, lengths_ref),
                (groups_hbm, groups_ref),
                (packing_hbm, packing_ref),
                (queries_hbm, queries_ref),
            ]
        )
    ]
    for copy in copies:
        copy.start()
    for copy in copies:
        copy.wait()
    tokens = queries_ref.shape[0]
    pairs, rows = q_ref.shape[0], q_ref.shape[1]
    per = rows // (2 * tokens)
    base = place_ref[0] * tokens
    own = base + lax.broadcasted_iota(jnp.int32, (tokens, LANES), 0)

    def request(k, carry):
        start, group, first = carry
        j = packing_ref[0, k]
        end = start + lengths_ref[0, j]
        inside = (own >= start) & (own < end)
        return (
            end,
            jnp.where(inside, groups_ref[0, j], group),
            jnp.where(inside, start, first),
        )

    zero = jnp.zeros((tokens, LANES), jnp.int32)
    _, group, first = lax.fori_loop(0, lengths_ref.shape[1], request, (jnp.int32(0), zero, zero))
    for ref, back in ((before_ref, tokens), (within_ref, 0)):
        for c in range(0, tokens, LANES):
            key = base - back + c + lax.broadcasted_iota(jnp.int32, (tokens, LANES), 1)
            ref[:, c : c + LANES] = jnp.where((key >= first) & (key <= own), 0.0, NEG_FILL)
    for c in range(0, prefix_ref.shape[1], LANES):
        key_group = lax.div(c + lax.broadcasted_iota(jnp.int32, (tokens, LANES), 1), span)
        prefix_ref[:, c : c + LANES] = jnp.where(group == key_group, 0.0, NEG_FILL)
    low = lax.broadcasted_iota(jnp.int32, (tokens, LANES), 1) < HEAD_SIZE
    for j in range(pairs):
        for parity in range(2):
            for r in range(per):
                head = (2 * j + parity) * per + r
                block = head // 2
                q = queries_ref[:, block * LANES : (block + 1) * LANES].astype(F32) * HEAD_SIZE ** (-0.5)
                if head % 2 != parity:
                    q = pltpu.roll(q, HEAD_SIZE, 1)
                q = jnp.where(low == (parity == 0), q, 0.0)
                row = (parity * per + r) * tokens
                q_ref[j, row : row + tokens, :] = q.astype(BF16)


def prepare(place, groups, span, lengths, request_group, packing, queries, width):
    tokens = queries.shape[0]
    per = queries.shape[1] // width
    vmem = pl.BlockSpec(memory_space=pltpu.VMEM)
    return pl.pallas_call(
        functools.partial(prepare_body, span),
        out_shape=[
            jax.ShapeDtypeStruct((width // LANES, 2 * per * tokens, LANES), BF16),
            jax.ShapeDtypeStruct((tokens, tokens), F32),
            jax.ShapeDtypeStruct((tokens, tokens), F32),
            jax.ShapeDtypeStruct((tokens, groups * span), F32),
        ],
        in_specs=[pl.BlockSpec(memory_space=pltpu.SMEM)] + [pl.BlockSpec(memory_space=pltpu.HBM)] * 4,
        out_specs=[vmem] * 4,
        compiler_params=pltpu.CompilerParams(vmem_limit_bytes=51 * 2**20),
        scratch_shapes=[pltpu.SMEM(lengths.shape, jnp.int32)] * 3
        + [pltpu.VMEM(queries.shape, BF16), pltpu.SemaphoreType.DMA((4,))],
        cost_estimate=cost(3),
        name="prepare",
    )(place, lengths, request_group, packing, queries)


def attend_body(first, pieces, refs):
    q_ref, refs = refs[0], refs[1:]
    if not first:
        old_max, old_sum, old_acc = refs[:3]
        refs = refs[3:]
    kv = refs[: 3 * pieces]
    new_max, new_sum, new_acc = refs[-3:]
    pairs, rows = q_ref.shape[0], q_ref.shape[1]
    half = rows // 2
    low = lax.broadcasted_iota(jnp.int32, (half, LANES), 1) < HEAD_SIZE

    def pick(even, odd):
        return jnp.where(low, even, odd)

    for j in range(pairs):
        q = q_ref[j]
        lanes = slice(j * LANES, (j + 1) * LANES)
        scores = []
        for i in range(pieces):
            k_ref, bias_ref = kv[3 * i], kv[3 * i + 2]
            s = dot(q, k_ref[:, lanes], 1)
            keys = s.shape[1]
            bias = bias_ref[...]
            s = s.reshape(rows // bias.shape[0], bias.shape[0], keys) + bias[None]
            scores.append(s.reshape(rows, keys))
        top = functools.reduce(
            jnp.maximum, [jnp.max(s, axis=1, keepdims=True) for s in scores]
        )
        if first:
            row_max = top
            pair_max = pick(row_max[:half], row_max[half:])
        else:
            old = old_max[j]
            pair_max = jnp.maximum(old, pick(top[:half], top[half:]))
            row_max = jnp.concatenate(
                [pair_max[:, :1], pair_max[:, HEAD_SIZE : HEAD_SIZE + 1]], axis=0
            )
        total = None
        for i in range(pieces):
            v_ref = kv[3 * i + 1]
            w = jnp.exp(scores[i] - row_max).astype(BF16)
            v = v_ref[:, lanes]
            v = jnp.concatenate([v, jnp.ones_like(v)], axis=1)
            part = dot(w, v)
            total = part if total is None else total + part
        acc = pick(total[:half, :LANES], total[half:, :LANES])
        summed = pick(total[:half, LANES:], total[half:, LANES:])
        if not first:
            scale = jnp.exp(old - pair_max)
            acc = acc + scale * old_acc[j]
            summed = summed + scale * old_sum[j]
        new_max[j] = pair_max
        new_sum[j] = summed
        new_acc[j] = acc


def attend(q, state, blocks, after=()):
    pairs, rows, lanes = q.shape
    first = state is None

    def kernel(*refs):
        lead = 1 + (0 if first else 3)
        head, tail = list(refs[:lead]), refs[lead:]
        for _ in blocks:
            head += [tail[0].at[0], tail[0].at[1], tail[1]]
            tail = tail[2:]
        attend_body(first, len(blocks), head + list(tail[-3:]))

    shape = jax.ShapeDtypeStruct((pairs, rows // 2, lanes), F32)
    operands = [q] + ([] if first else list(state)) + [a for block in blocks for a in block]
    vmem = pl.BlockSpec(memory_space=pltpu.VMEM)
    return pl.pallas_call(
        kernel,
        out_shape=[shape] * 3,
        in_specs=[vmem] * len(operands) + [pl.BlockSpec(memory_space=pl.ANY)] * len(after),
        out_specs=[vmem] * 3,
        compiler_params=pltpu.CompilerParams(vmem_limit_bytes=28 * 2**20),
        cost_estimate=cost(1.1 * len(blocks)),
        name="attend",
    )(*operands, *after)


def block_owner(me, blocks, step):
    chips = blocks // CORES
    x, core = lax.div(me, CORES), lax.rem(me, CORES)
    x = lax.rem(x + chips - step // CORES, chips)
    return x * CORES + lax.rem(core + step % CORES, CORES)


def project_body(blocks, me_ref, sum_ref, acc_ref, weight_ref, residual_ref, gain_ref, *refs):
    hidden_ref, normed_ref, held = refs[-3:]
    pairs, rows, lanes = acc_ref.shape
    tokens = residual_ref.shape[0]
    per = rows // tokens
    hidden = residual_ref[...].astype(F32)
    for j in range(pairs):
        out = (acc_ref[j] / sum_ref[j]).astype(BF16)
        for r in range(0, per, 2):
            left = jnp.concatenate(
                [out[r * tokens : (r + 1) * tokens], out[(r + 1) * tokens : (r + 2) * tokens]], axis=1
            )
            heads = [(2 * j) * per + r, (2 * j + 1) * per + r, (2 * j) * per + r + 1, (2 * j + 1) * per + r + 1]
            right = jnp.concatenate(
                [weight_ref[h * HEAD_SIZE : (h + 1) * HEAD_SIZE, :] for h in heads], axis=0
            )
            hidden = hidden + dot(left, right)
    hidden_ref[...] = hidden
    mean = jnp.mean(hidden * hidden, axis=1, keepdims=True)
    held[...] = hidden * lax.rsqrt(mean + EPSILON) * gain_ref[...]
    width = hidden.shape[1] // blocks
    for b in range(blocks):
        start = pl.multiple_of(block_owner(me_ref[0], blocks, b) * width, width)
        normed_ref[:, b * width : (b + 1) * width] = held[:, pl.ds(start, width)].astype(BF16)


def project(me, blocks, state, out_weight, residual, gain, after=()):
    tokens, width = residual.shape
    vmem = pl.BlockSpec(memory_space=pltpu.VMEM)
    return pl.pallas_call(
        functools.partial(project_body, blocks),
        out_shape=[
            jax.ShapeDtypeStruct((tokens, width), F32),
            jax.ShapeDtypeStruct((tokens, width), BF16),
        ],
        in_specs=[pl.BlockSpec(memory_space=pltpu.SMEM)]
        + [vmem] * 5
        + [pl.BlockSpec(memory_space=pl.ANY)] * len(after),
        out_specs=[vmem] * 2,
        scratch_shapes=[pltpu.VMEM((tokens, width), F32)],
        compiler_params=pltpu.CompilerParams(vmem_limit_bytes=28 * 2**20),
        cost_estimate=cost(2),
        name="project",
    )(me, state[1], state[2], out_weight, residual, gain, *after)


def ffn_body(parts, blocks, tokens, refs):
    n_refs, refs = refs[:parts], refs[parts:]
    gates, ups, downs = refs[:blocks], refs[blocks : 2 * blocks], refs[2 * blocks : 3 * blocks]
    outs, x_ref, act_ref = refs[-2 - parts : -2], refs[-2], refs[-1]
    for i in range(parts):
        x_ref[i * tokens : (i + 1) * tokens, :] = n_refs[i][...]
    depth, hidden = gates[0].shape
    tile = math.gcd(hidden, 256)

    @pl.loop(0, hidden // tile)
    def _(t):
        cols = pl.ds(pl.multiple_of(t * tile, tile), tile)
        gate = up = None
        for b in range(blocks):
            x = x_ref[:, b * depth : (b + 1) * depth]
            g, u = dot(x, gates[b][:, cols]), dot(x, ups[b][:, cols])
            gate, up = (g, u) if gate is None else (gate + g, up + u)
        act_ref[:, cols] = (gate / (1.0 + jnp.exp(-gate)) * up).astype(BF16)

    width = downs[0].shape[1]
    tile_out = math.gcd(width, 256)
    for b in range(blocks):

        @pl.loop(0, width // tile_out)
        def _(t):
            term = dot(act_ref[...], downs[b][:, pl.ds(pl.multiple_of(t * tile_out, tile_out), tile_out)])
            cols = pl.ds(pl.multiple_of(b * width + t * tile_out, tile_out), tile_out)
            for i in range(parts):
                outs[i][:, cols] = term[i * tokens : (i + 1) * tokens].astype(BF16)


def ffn(normed, gates, ups, downs):
    parts, blocks = len(normed), len(gates)
    tokens, model = normed[0].shape
    hidden = gates[0].shape[1]

    def kernel(*refs):
        ffn_body(parts, blocks, tokens, refs)

    vmem = pl.BlockSpec(memory_space=pltpu.VMEM)
    return pl.pallas_call(
        kernel,
        out_shape=[jax.ShapeDtypeStruct((tokens, model), BF16)] * parts,
        in_specs=[vmem] * (parts + 3 * blocks),
        out_specs=[vmem] * parts,
        scratch_shapes=[
            pltpu.VMEM((parts * tokens, model), BF16),
            pltpu.VMEM((parts * tokens, hidden), BF16),
        ],
        compiler_params=pltpu.CompilerParams(vmem_limit_bytes=28 * 2**20),
        cost_estimate=cost(3.5 * parts),
        name="ffn",
    )(*normed, *gates, *ups, *downs)


def finish_body(blocks, me_ref, hidden_ref, *refs):
    terms, out_ref = refs[:-1], refs[-1]
    width = out_ref.shape[1] // blocks
    for b in range(blocks):
        cols = slice(b * width, (b + 1) * width)
        place = pl.ds(pl.multiple_of(block_owner(me_ref[0], blocks, b) * width, width), width)
        total = hidden_ref[:, place]
        for term in terms:
            total = total + term[:, cols].astype(F32)
        out_ref[:, place] = total.astype(BF16)


def finish(me, blocks, hidden_state, terms):
    vmem = pl.BlockSpec(memory_space=pltpu.VMEM)
    return pl.pallas_call(
        functools.partial(finish_body, blocks),
        out_shape=jax.ShapeDtypeStruct(hidden_state.shape, BF16),
        in_specs=[pl.BlockSpec(memory_space=pltpu.SMEM)] + [vmem] * (1 + len(terms)),
        out_specs=vmem,
        cost_estimate=cost(1),
        name="finish",
    )(me, hidden_state, *terms)


def tie(array, *others):
    return lax.optimization_barrier((array, *others))[0]


def shards(
    grps,
    devs,
    residual,
    queries,
    keys,
    values,
    prefix_keys,
    cached_prefix_values,
    out_weight,
    norm_gain,
    w_gate,
    w_up,
    w_down,
    suffix_lengths,
    request_group,
    placement_order,
):
    depth_z = math.gcd(devs, 4)
    depth_y = devs // depth_z
    cores = CORES
    depth_x = grps // cores
    def shift(by_z, by_y):
        return [
            (
                z * depth_y + y,
                (z + by_z) % depth_z * depth_y + (y + by_y) % depth_y,
            )
            for z in range(depth_z)
            for y in range(depth_y)
        ]

    x_shift = [
        (x * cores + c, (x + 1) % depth_x * cores + c) for x in range(depth_x) for c in range(cores)
    ]
    core_swap = [(x * cores + c, x * cores + 1 - c) for x in range(depth_x) for c in range(cores)]

    def along_y(block):
        return [block] + [lax.ppermute(block, "dev", shift(0, ys)) for ys in range(1, depth_y)]

    def along_x(weight, *others):
        blocks = [weight]
        for _ in range(1, depth_x):
            blocks.append(lax.ppermute(tie(blocks[-1], *others), "grp", x_shift))
        return blocks

    def other_core(block, *others):
        return lax.ppermute(tie(block, *others), "grp", core_swap)

    tokens = queries.shape[0]
    width = keys.shape[1]
    groups, span = prefix_keys.shape[:2]

    place = lax.axis_index("dev").astype(jnp.int32).reshape(1)
    me = lax.axis_index("grp").astype(jnp.int32).reshape(1)
    prefix = jnp.stack([prefix_keys.reshape(-1, width), cached_prefix_values.reshape(-1, width)])
    here = along_y(prefix)
    forward = lax.ppermute(prefix, "dev", shift(1, 0))
    backward = lax.ppermute(prefix, "dev", shift(-1, 0))
    own = jnp.stack([keys, values])
    before = lax.ppermute(own, "dev", [(i, i + 1) for i in range(devs - 1)])
    gate_rows = along_x(w_gate)
    q, before_mask, within_mask, prefix_mask = prepare(
        place,
        groups,
        span,
        suffix_lengths,
        request_group,
        placement_order,
        queries,
        width,
    )
    forward, backward = tie(forward, q, before, *here), tie(backward, q, before, *here)
    late = along_y(forward)[1:] + along_y(backward)[1:]
    first = state = attend(
        q,
        None,
        [(before, before_mask), (own, within_mask)]
        + [(b, prefix_mask) for b in here + [forward, backward]],
    )
    last = []
    for zs in range(2, depth_z - 1):
        forward = lax.ppermute(forward, "dev", shift(1, 0))
        late.append(forward)
        last += along_y(tie(forward, first[0]))[1:]
    state = attend(tie(q, *gate_rows[1:]), state, [(b, prefix_mask) for b in late])
    up_rows = along_x(w_up, *gate_rows[1:], *late)
    gate_swap, up_swap = other_core(w_gate, *late, first[0]), other_core(w_up, state[0])
    state = attend(q, state, [(b, prefix_mask) for b in last])
    hidden_state, normed = project(
        me, grps, state, out_weight, tie(residual, gate_swap), norm_gain[None]
    )

    gates, ups, downs = [w_gate, gate_swap], [w_up, up_swap], [w_down]
    for gate in gate_rows[1:]:
        gates += [gate, other_core(gate, normed)]
    chunks = [along_y(normed)]
    chunks.append(along_y(lax.ppermute(normed, "dev", shift(1, 0))))
    down_cols = along_x(w_down, *up_rows[1:], chunks[1][0])
    downs.append(other_core(w_down, chunks[1][0]))
    for up in up_rows[1:]:
        ups += [up, other_core(up, chunks[1][0])]
    ready = chunks[0][1:] + gates[3:] + [up_swap]
    for zs in range(2, depth_z):
        chunks.append(along_y(lax.ppermute(tie(chunks[-1][0], *ready), "dev", shift(1, 0))))
        ready = chunks[-2][1:] + downs[1:] + ups[3:]
    for down in down_cols[1:]:
        downs += [down, other_core(down, chunks[-1][0], *chunks[-2][1:])]

    parts = ffn(chunks[1] + chunks[0], gates, ups, downs)
    chunks[2][0] = tie(chunks[2][0], *chunks[-1][1:])
    done = {1: parts[:depth_y], 0: parts[depth_y:]}
    running = None
    for zs in list(range(1, depth_z)) + [0]:
        parts = done[zs] if zs in done else ffn(chunks[zs], gates, ups, downs)
        if zs == 0:
            parts = [parts[0]] + [tie(part, running) for part in parts[1:]]
        terms = [parts[0]] + [
            lax.ppermute(parts[ys], "dev", shift(0, -ys)) for ys in range(1, depth_y)
        ]
        if running is not None:
            terms.append(lax.ppermute(running, "dev", shift(1, 0)))
        if zs:
            running = functools.reduce(jnp.add, [term.astype(F32) for term in terms]).astype(BF16)
    return finish(me, grps, hidden_state, terms)


def solution(mesh):
    placed = (
        P(("grp", "dev"), None),
        P(("grp", "dev"), None),
        P(("grp", "dev"), None),
        P(("grp", "dev"), None),
        P("grp", "dev", None),
        P("grp", "dev", None),
        P(),
        P(),
        P("grp", "dev"),
        P("grp", "dev"),
        P("dev", "grp"),
        P("grp", None),
        P("grp", None),
        P("grp", None),
    )
    return jax.shard_map(
        functools.partial(shards, mesh.shape["grp"], mesh.shape["dev"]),
        mesh=mesh,
        in_specs=placed,
        out_specs=P(("grp", "dev"), None),
        check_vma=False,
    )
```

```python
import functools
import math

import jax
import jax.numpy as jnp
from jax import lax
from jax.experimental import pallas as pl
from jax.experimental.pallas import tpu as pltpu
from jax.sharding import PartitionSpec as P

HEAD_SIZE = 64
NEG_FILL = -1e30
EPSILON = 1e-05
F32 = jnp.float32
BF16 = jnp.bfloat16
LANES = 2 * HEAD_SIZE
CORES = 2


def cost(microseconds):
    return pl.CostEstimate(flops=0, bytes_accessed=int(microseconds * 3.5e6), transcendentals=0)


def dot(a, b, contract_b=0):
    return lax.dot_general(
        a, b, (((1,), (contract_b,)), ((), ())), preferred_element_type=F32
    )


def prepare_body(
    span,
    place_ref,
    lengths_hbm,
    groups_hbm,
    packing_hbm,
    queries_hbm,
    *refs,
):
    q_ref, before_ref, within_ref, prefix_ref = refs[:4]
    lengths_ref, groups_ref, packing_ref, queries_ref, sems = refs[4:]
    copies = [
        pltpu.make_async_copy(source, target, sems.at[i])
        for i, (source, target) in enumerate(
            [
                (lengths_hbm, lengths_ref),
                (groups_hbm, groups_ref),
                (packing_hbm, packing_ref),
                (queries_hbm, queries_ref),
            ]
        )
    ]
    for copy in copies:
        copy.start()
    for copy in copies:
        copy.wait()
    tokens = queries_ref.shape[0]
    pairs, rows = q_ref.shape[0], q_ref.shape[1]
    per = rows // (2 * tokens)
    base = place_ref[0] * tokens
    own = base + lax.broadcasted_iota(jnp.int32, (tokens, LANES), 0)

    def request(k, carry):
        start, group, first = carry
        j = packing_ref[0, k]
        end = start + lengths_ref[0, j]
        inside = (own >= start) & (own < end)
        return (
            end,
            jnp.where(inside, groups_ref[0, j], group),
            jnp.where(inside, start, first),
        )

    zero = jnp.zeros((tokens, LANES), jnp.int32)
    _, group, first = lax.fori_loop(0, lengths_ref.shape[1], request, (jnp.int32(0), zero, zero))
    for ref, back in ((before_ref, tokens), (within_ref, 0)):
        for c in range(0, tokens, LANES):
            key = base - back + c + lax.broadcasted_iota(jnp.int32, (tokens, LANES), 1)
            ref[:, c : c + LANES] = jnp.where((key >= first) & (key <= own), 0.0, NEG_FILL)
    for c in range(0, prefix_ref.shape[1], LANES):
        key_group = lax.div(c + lax.broadcasted_iota(jnp.int32, (tokens, LANES), 1), span)
        prefix_ref[:, c : c + LANES] = jnp.where(group == key_group, 0.0, NEG_FILL)
    low = lax.broadcasted_iota(jnp.int32, (tokens, LANES), 1) < HEAD_SIZE
    for j in range(pairs):
        for parity in range(2):
            for r in range(per):
                head = (2 * j + parity) * per + r
                block = head // 2
                q = queries_ref[:, block * LANES : (block + 1) * LANES].astype(F32) * HEAD_SIZE ** (-0.5)
                if head % 2 != parity:
                    q = pltpu.roll(q, HEAD_SIZE, 1)
                q = jnp.where(low == (parity == 0), q, 0.0)
                row = (parity * per + r) * tokens
                q_ref[j, row : row + tokens, :] = q.astype(BF16)


def prepare(place, groups, span, lengths, request_group, packing, queries, width):
    tokens = queries.shape[0]
    per = queries.shape[1] // width
    vmem = pl.BlockSpec(memory_space=pltpu.VMEM)
    return pl.pallas_call(
        functools.partial(prepare_body, span),
        out_shape=[
            jax.ShapeDtypeStruct((width // LANES, 2 * per * tokens, LANES), BF16),
            jax.ShapeDtypeStruct((tokens, tokens), F32),
            jax.ShapeDtypeStruct((tokens, tokens), F32),
            jax.ShapeDtypeStruct((tokens, groups * span), F32),
        ],
        in_specs=[pl.BlockSpec(memory_space=pltpu.SMEM)] + [pl.BlockSpec(memory_space=pltpu.HBM)] * 4,
        out_specs=[vmem] * 4,
        compiler_params=pltpu.CompilerParams(vmem_limit_bytes=8 * 2**20),
        scratch_shapes=[pltpu.SMEM(lengths.shape, jnp.int32)] * 3
        + [pltpu.VMEM(queries.shape, BF16), pltpu.SemaphoreType.DMA((4,))],
        cost_estimate=cost(3),
        name="prepare",
    )(place, lengths, request_group, packing, queries)


def attend_body(first, pieces, refs):
    q_ref, refs = refs[0], refs[1:]
    if not first:
        old_max, old_sum, old_acc = refs[:3]
        refs = refs[3:]
    kv = refs[: 3 * pieces]
    new_max, new_sum, new_acc = refs[-3:]
    pairs, rows = q_ref.shape[0], q_ref.shape[1]
    half = rows // 2
    low = lax.broadcasted_iota(jnp.int32, (half, LANES), 1) < HEAD_SIZE

    def pick(even, odd):
        return jnp.where(low, even, odd)

    for j in range(pairs):
        q = q_ref[j]
        lanes = slice(j * LANES, (j + 1) * LANES)
        scores = []
        for i in range(pieces):
            k_ref, bias_ref = kv[3 * i], kv[3 * i + 2]
            s = dot(q, k_ref[:, lanes], 1)
            keys = s.shape[1]
            bias = bias_ref[...]
            s = s.reshape(rows // bias.shape[0], bias.shape[0], keys) + bias[None]
            scores.append(s.reshape(rows, keys))
        top = functools.reduce(
            jnp.maximum, [jnp.max(s, axis=1, keepdims=True) for s in scores]
        )
        if first:
            row_max = top
            pair_max = pick(row_max[:half], row_max[half:])
        else:
            old = old_max[j]
            pair_max = jnp.maximum(old, pick(top[:half], top[half:]))
            row_max = jnp.concatenate(
                [pair_max[:, :1], pair_max[:, HEAD_SIZE : HEAD_SIZE + 1]], axis=0
            )
        total = None
        for i in range(pieces):
            v_ref = kv[3 * i + 1]
            w = jnp.exp(scores[i] - row_max).astype(BF16)
            v = v_ref[:, lanes]
            v = jnp.concatenate([v, jnp.ones_like(v)], axis=1)
            part = dot(w, v)
            total = part if total is None else total + part
        acc = pick(total[:half, :LANES], total[half:, :LANES])
        summed = pick(total[:half, LANES:], total[half:, LANES:])
        if not first:
            scale = jnp.exp(old - pair_max)
            acc = acc + scale * old_acc[j]
            summed = summed + scale * old_sum[j]
        new_max[j] = pair_max
        new_sum[j] = summed
        new_acc[j] = acc


def block_refs(refs, count):
    return [r for i in range(count) for r in (refs[2 * i].at[0], refs[2 * i].at[1], refs[2 * i + 1])]


def attend(q, state, blocks):
    pairs, rows, lanes = q.shape
    first = state is None

    def kernel(*refs):
        lead = 1 + (0 if first else 3)
        attend_body(first, len(blocks), [*refs[:lead], *block_refs(refs[lead:], len(blocks)), *refs[-3:]])

    shape = jax.ShapeDtypeStruct((pairs, rows // 2, lanes), F32)
    operands = [q] + ([] if first else list(state)) + [a for block in blocks for a in block]
    vmem = pl.BlockSpec(memory_space=pltpu.VMEM)
    return pl.pallas_call(
        kernel,
        out_shape=[shape] * 3,
        in_specs=[vmem] * len(operands),
        out_specs=[vmem] * 3,
        compiler_params=pltpu.CompilerParams(vmem_limit_bytes=20 * 2**20),
        cost_estimate=cost(1.1 * len(blocks)),
        name="attend",
    )(*operands)


def block_owner(me, blocks, step):
    chips = blocks // CORES
    x, core = lax.div(me, CORES), lax.rem(me, CORES)
    x = lax.rem(x + chips - step // CORES, chips)
    return x * CORES + lax.rem(core + step % CORES, CORES)


def project_body(
    blocks, me_ref, sum_ref, acc_ref, weight_ref, residual_ref, gain_ref, hidden_ref, normed_ref, held
):
    pairs, rows, lanes = acc_ref.shape
    tokens = residual_ref.shape[0]
    per = rows // tokens
    hidden = residual_ref[...].astype(F32)
    for j in range(pairs):
        out = (acc_ref[j] / sum_ref[j]).astype(BF16)
        for r in range(0, per, 2):
            left = jnp.concatenate(
                [out[r * tokens : (r + 1) * tokens], out[(r + 1) * tokens : (r + 2) * tokens]], axis=1
            )
            heads = [(2 * j) * per + r, (2 * j + 1) * per + r, (2 * j) * per + r + 1, (2 * j + 1) * per + r + 1]
            right = jnp.concatenate(
                [weight_ref[h * HEAD_SIZE : (h + 1) * HEAD_SIZE, :] for h in heads], axis=0
            )
            hidden = hidden + dot(left, right)
    hidden_ref[...] = hidden
    mean = jnp.mean(hidden * hidden, axis=1, keepdims=True)
    held[...] = hidden * lax.rsqrt(mean + EPSILON) * gain_ref[...]
    width = hidden.shape[1] // blocks
    for b in range(blocks):
        start = pl.multiple_of(block_owner(me_ref[0], blocks, b) * width, width)
        normed_ref[:, b * width : (b + 1) * width] = held[:, pl.ds(start, width)].astype(BF16)


def attend_project(q, state, blocks, me, columns, out_weight, residual, gain):
    pairs, rows, lanes = q.shape
    tokens, width = residual.shape
    count = len(blocks)

    def kernel(*refs):
        mine, (me_ref, weight_ref, residual_ref, gain_ref) = refs[: 4 + 2 * count], refs[4 + 2 * count : 8 + 2 * count]
        hidden_ref, normed_ref, held, top, total, acc = refs[-6:]
        attend_body(False, count, [*mine[:4], *block_refs(mine[4:], count), top, total, acc])
        project_body(
            columns, me_ref, total, acc, weight_ref, residual_ref, gain_ref, hidden_ref, normed_ref, held
        )

    operands = [q, *state] + [a for block in blocks for a in block]
    vmem = pl.BlockSpec(memory_space=pltpu.VMEM)
    return pl.pallas_call(
        kernel,
        out_shape=[
            jax.ShapeDtypeStruct((tokens, width), F32),
            jax.ShapeDtypeStruct((tokens, width), BF16),
        ],
        in_specs=[vmem] * len(operands) + [pl.BlockSpec(memory_space=pltpu.SMEM)] + [vmem] * 3,
        out_specs=[vmem] * 2,
        scratch_shapes=[pltpu.VMEM((tokens, width), F32)]
        + [pltpu.VMEM((pairs, rows // 2, lanes), F32)] * 3,
        compiler_params=pltpu.CompilerParams(vmem_limit_bytes=20 * 2**20),
        cost_estimate=cost(1.1 * count + 2),
        name="attend_project",
    )(*operands, me, out_weight, residual, gain)


def rise_body(parts, blocks, refs):
    n_refs, gates, ups = refs[:parts], refs[parts : parts + blocks], refs[parts + blocks : parts + 2 * blocks]
    act_ref, x_ref = refs[-2:]
    tokens = n_refs[0].shape[0]
    for i in range(parts):
        x_ref[i * tokens : (i + 1) * tokens, :] = n_refs[i][...]
    depth, hidden = gates[0].shape
    tile = math.gcd(hidden, 256)

    @pl.loop(0, hidden // tile)
    def _(t):
        cols = pl.ds(pl.multiple_of(t * tile, tile), tile)
        gate = up = None
        for b in range(blocks):
            x = x_ref[:, b * depth : (b + 1) * depth]
            g, u = dot(x, gates[b][:, cols]), dot(x, ups[b][:, cols])
            gate, up = (g, u) if gate is None else (gate + g, up + u)
        act_ref[:, cols] = (gate / (1.0 + jnp.exp(-gate)) * up).astype(BF16)


def rise(normed, gates, ups):
    parts, blocks = len(normed), len(gates)
    tokens, model = normed[0].shape
    hidden = gates[0].shape[1]

    def kernel(*refs):
        rise_body(parts, blocks, refs)

    vmem = pl.BlockSpec(memory_space=pltpu.VMEM)
    return pl.pallas_call(
        kernel,
        out_shape=jax.ShapeDtypeStruct((parts * tokens, hidden), BF16),
        in_specs=[vmem] * (parts + 2 * blocks),
        out_specs=vmem,
        scratch_shapes=[pltpu.VMEM((parts * tokens, model), BF16)],
        compiler_params=pltpu.CompilerParams(vmem_limit_bytes=12 * 2**20),
        cost_estimate=cost(2 * parts),
        name="rise",
    )(*normed, *gates, *ups)


def fall_body(parts, blocks, refs):
    act_ref, downs, outs = refs[0], refs[1 : 1 + blocks], refs[1 + blocks :]
    tokens, width = outs[0].shape[0], downs[0].shape[1]
    tile = math.gcd(width, 256)
    for b in range(blocks):

        @pl.loop(0, width // tile)
        def _(t):
            term = dot(act_ref[...], downs[b][:, pl.ds(pl.multiple_of(t * tile, tile), tile)])
            cols = pl.ds(pl.multiple_of(b * width + t * tile, tile), tile)
            for i in range(parts):
                outs[i][:, cols] = term[i * tokens : (i + 1) * tokens].astype(BF16)


def fall(act, parts, downs):
    blocks = len(downs)
    shape = jax.ShapeDtypeStruct((act.shape[0] // parts, blocks * downs[0].shape[1]), BF16)

    def kernel(*refs):
        fall_body(parts, blocks, refs)

    vmem = pl.BlockSpec(memory_space=pltpu.VMEM)
    return pl.pallas_call(
        kernel,
        out_shape=[shape] * parts,
        in_specs=[vmem] * (1 + blocks),
        out_specs=[vmem] * parts,
        compiler_params=pltpu.CompilerParams(vmem_limit_bytes=12 * 2**20),
        cost_estimate=cost(parts),
        name="fall",
    )(act, *downs)


def finish_body(blocks, me_ref, hidden_ref, *refs):
    terms, out_ref = refs[:-1], refs[-1]
    width = out_ref.shape[1] // blocks
    for b in range(blocks):
        cols = slice(b * width, (b + 1) * width)
        place = pl.ds(pl.multiple_of(block_owner(me_ref[0], blocks, b) * width, width), width)
        total = hidden_ref[:, place]
        for term in terms:
            total = total + term[:, cols].astype(F32)
        out_ref[:, place] = total.astype(BF16)


def finish(me, blocks, hidden_state, terms):
    vmem = pl.BlockSpec(memory_space=pltpu.VMEM)
    return pl.pallas_call(
        functools.partial(finish_body, blocks),
        out_shape=jax.ShapeDtypeStruct(hidden_state.shape, BF16),
        in_specs=[pl.BlockSpec(memory_space=pltpu.SMEM)] + [vmem] * (1 + len(terms)),
        out_specs=vmem,
        compiler_params=pltpu.CompilerParams(vmem_limit_bytes=8 * 2**20),
        cost_estimate=cost(1),
        name="finish",
    )(me, hidden_state, *terms)


def tie(array, *others):
    return lax.optimization_barrier((array, *others))[0]


def shards(
    grps,
    devs,
    residual,
    queries,
    keys,
    values,
    prefix_keys,
    cached_prefix_values,
    out_weight,
    norm_gain,
    w_gate,
    w_up,
    w_down,
    suffix_lengths,
    request_group,
    placement_order,
):
    depth_z = math.gcd(devs, 4)
    depth_y = devs // depth_z
    cores = CORES
    depth_x = grps // cores
    def shift(by_z, by_y):
        return [
            (
                z * depth_y + y,
                (z + by_z) % depth_z * depth_y + (y + by_y) % depth_y,
            )
            for z in range(depth_z)
            for y in range(depth_y)
        ]

    x_shift = [
        (x * cores + c, (x + 1) % depth_x * cores + c) for x in range(depth_x) for c in range(cores)
    ]
    core_swap = [(x * cores + c, x * cores + 1 - c) for x in range(depth_x) for c in range(cores)]

    def along_y(block):
        return [block] + [lax.ppermute(block, "dev", shift(0, ys)) for ys in range(1, depth_y)]

    def along_x(weight, *others):
        blocks = [weight]
        for _ in range(1, depth_x):
            blocks.append(lax.ppermute(tie(blocks[-1], *others), "grp", x_shift))
        return blocks

    def other_core(block, *others):
        return lax.ppermute(tie(block, *others), "grp", core_swap)

    tokens = queries.shape[0]
    width = keys.shape[1]
    groups, span = prefix_keys.shape[:2]

    place = lax.axis_index("dev").astype(jnp.int32).reshape(1)
    me = lax.axis_index("grp").astype(jnp.int32).reshape(1)
    prefix = jnp.stack([prefix_keys.reshape(-1, width), cached_prefix_values.reshape(-1, width)])
    here = along_y(prefix)
    forward = lax.ppermute(prefix, "dev", shift(1, 0))
    backward = lax.ppermute(prefix, "dev", shift(-1, 0))
    own = jnp.stack([keys, values])
    before = lax.ppermute(own, "dev", [(i, i + 1) for i in range(devs - 1)])
    gate_rows = along_x(w_gate)
    q, before_mask, within_mask, prefix_mask = prepare(
        place,
        groups,
        span,
        suffix_lengths,
        request_group,
        placement_order,
        queries,
        width,
    )
    forward, backward = tie(forward, q, before, *here), tie(backward, q, before, *here)
    late = along_y(forward)[1:] + along_y(backward)[1:]
    first = state = attend(
        q,
        None,
        [(before, before_mask), (own, within_mask)]
        + [(b, prefix_mask) for b in here + [forward, backward]],
    )
    last = []
    for zs in range(2, depth_z - 1):
        forward = lax.ppermute(forward, "dev", shift(1, 0))
        late.append(forward)
        last += along_y(tie(forward, first[0]))[1:]
    state = attend(tie(q, *gate_rows[1:]), state, [(b, prefix_mask) for b in late])
    up_rows = along_x(w_up, *gate_rows[1:], *late)
    gate_swap, up_swap = other_core(w_gate, *late, first[0]), other_core(w_up, state[0])
    hidden_state, normed = attend_project(
        q,
        state,
        [(b, prefix_mask) for b in last],
        me,
        grps,
        out_weight,
        tie(residual, gate_swap),
        norm_gain[None],
    )

    gates, ups, downs = [w_gate, gate_swap], [w_up, up_swap], [w_down]
    for gate in gate_rows[1:]:
        gates += [gate, other_core(gate, normed)]
    chunks = [along_y(normed)]
    down_cols = along_x(w_down, *up_rows[1:], normed)
    chunks.append(along_y(lax.ppermute(normed, "dev", shift(1, 0))))
    for up in up_rows[1:]:
        ups += [up, other_core(up, normed, *chunks[0][1:])]
    downs.append(other_core(w_down, chunks[1][0]))
    ready = chunks[0][1:] + gates[3:] + [up_swap]
    acts = {}
    for zs in range(2, depth_z):
        chunks.append(along_y(lax.ppermute(tie(chunks[-1][0], *ready), "dev", shift(1, 0))))
        ready = chunks[-2][1:] + downs[1:] + [acts.setdefault(0, rise(chunks[0], gates, ups))]
    acts[1] = rise(chunks[1], gates, ups)
    for down in down_cols[1:]:
        downs += [down, other_core(down, chunks[-1][0], *chunks[-2][1:], acts[1])]
    chunks[2][0] = tie(chunks[2][0], *chunks[-1][1:])

    running = None
    for zs in list(range(1, depth_z)) + [0]:
        act = acts[zs] if zs in acts else rise(chunks[zs], gates, ups)
        parts = fall(act, depth_y, downs)
        if zs == 0:
            parts = [parts[0]] + [tie(part, running) for part in parts[1:]]
        terms = [parts[0]] + [
            lax.ppermute(parts[ys], "dev", shift(0, -ys)) for ys in range(1, depth_y)
        ]
        if running is not None:
            terms.append(lax.ppermute(running, "dev", shift(1, 0)))
        if zs:
            running = functools.reduce(jnp.add, [term.astype(F32) for term in terms]).astype(BF16)
    return finish(me, grps, hidden_state, terms)


def solution(mesh):
    placed = (
        P(("grp", "dev"), None),
        P(("grp", "dev"), None),
        P(("grp", "dev"), None),
        P(("grp", "dev"), None),
        P("grp", "dev", None),
        P("grp", "dev", None),
        P(),
        P(),
        P("grp", "dev"),
        P("grp", "dev"),
        P("dev", "grp"),
        P("grp", None),
        P("grp", None),
        P("grp", None),
    )
    return jax.shard_map(
        functools.partial(shards, mesh.shape["grp"], mesh.shape["dev"]),
        mesh=mesh,
        in_specs=placed,
        out_specs=P(("grp", "dev"), None),
        check_vma=False,
    )
```

```python
import functools
import math

import jax
import jax.numpy as jnp
from jax import lax
from jax.experimental import pallas as pl
from jax.experimental.pallas import tpu as pltpu
from jax.sharding import PartitionSpec as P

HEAD_SIZE = 64
NEG_FILL = -1e30
EPSILON = 1e-05
F32 = jnp.float32
BF16 = jnp.bfloat16
LANES = 2 * HEAD_SIZE
CORES = 2


def cost(microseconds):
    return pl.CostEstimate(flops=0, bytes_accessed=int(microseconds * 3.5e6), transcendentals=0)


def dot(a, b, contract_b=0):
    return lax.dot_general(
        a, b, (((1,), (contract_b,)), ((), ())), preferred_element_type=F32
    )


def prepare_body(
    span,
    lengths_hbm,
    groups_hbm,
    packing_hbm,
    queries_hbm,
    *refs,
):
    q_ref, before_ref, within_ref, prefix_ref = refs[:4]
    lengths_ref, groups_ref, packing_ref, queries_ref, sems = refs[4:]
    copies = [
        pltpu.make_async_copy(source, target, sems.at[i])
        for i, (source, target) in enumerate(
            [
                (lengths_hbm, lengths_ref),
                (groups_hbm, groups_ref),
                (packing_hbm, packing_ref),
                (queries_hbm, queries_ref),
            ]
        )
    ]
    for copy in copies:
        copy.start()
    for copy in copies:
        copy.wait()
    tokens = queries_ref.shape[0]
    pairs, rows = q_ref.shape[0], q_ref.shape[1]
    per = rows // (2 * tokens)
    base = lax.axis_index("dev") * tokens
    own = base + lax.broadcasted_iota(jnp.int32, (tokens, LANES), 0)

    def request(k, carry):
        start, group, first = carry
        j = packing_ref[0, k]
        end = start + lengths_ref[0, j]
        inside = (own >= start) & (own < end)
        return (
            end,
            jnp.where(inside, groups_ref[0, j], group),
            jnp.where(inside, start, first),
        )

    zero = jnp.zeros((tokens, LANES), jnp.int32)
    _, group, first = lax.fori_loop(0, lengths_ref.shape[1], request, (jnp.int32(0), zero, zero))
    for ref, back in ((before_ref, tokens), (within_ref, 0)):
        for c in range(0, tokens, LANES):
            key = base - back + c + lax.broadcasted_iota(jnp.int32, (tokens, LANES), 1)
            ref[:, c : c + LANES] = jnp.where((key >= first) & (key <= own), 0.0, NEG_FILL)
    for c in range(0, prefix_ref.shape[1], LANES):
        key_group = lax.div(c + lax.broadcasted_iota(jnp.int32, (tokens, LANES), 1), span)
        prefix_ref[:, c : c + LANES] = jnp.where(group == key_group, 0.0, NEG_FILL)
    low = lax.broadcasted_iota(jnp.int32, (tokens, LANES), 1) < HEAD_SIZE
    for j in range(pairs):
        for parity in range(2):
            for r in range(per):
                head = (2 * j + parity) * per + r
                block = head // 2
                q = queries_ref[:, block * LANES : (block + 1) * LANES].astype(F32) * HEAD_SIZE ** (-0.5)
                if head % 2 != parity:
                    q = pltpu.roll(q, HEAD_SIZE, 1)
                q = jnp.where(low == (parity == 0), q, 0.0)
                row = (parity * per + r) * tokens
                q_ref[j, row : row + tokens, :] = q.astype(BF16)


def prepare(groups, span, lengths, request_group, packing, queries, width):
    tokens = queries.shape[0]
    per = queries.shape[1] // width
    vmem = pl.BlockSpec(memory_space=pltpu.VMEM)
    return pl.pallas_call(
        functools.partial(prepare_body, span),
        out_shape=[
            jax.ShapeDtypeStruct((width // LANES, 2 * per * tokens, LANES), BF16),
            jax.ShapeDtypeStruct((tokens, tokens), F32),
            jax.ShapeDtypeStruct((tokens, tokens), F32),
            jax.ShapeDtypeStruct((tokens, groups * span), F32),
        ],
        in_specs=[pl.BlockSpec(memory_space=pltpu.HBM)] * 4,
        out_specs=[vmem] * 4,
        compiler_params=pltpu.CompilerParams(vmem_limit_bytes=8 * 2**20),
        scratch_shapes=[pltpu.SMEM(lengths.shape, jnp.int32)] * 3
        + [pltpu.VMEM(queries.shape, BF16), pltpu.SemaphoreType.DMA((4,))],
        cost_estimate=cost(3),
        name="prepare",
    )(lengths, request_group, packing, queries)


def attend_body(first, pieces, refs):
    q_ref, refs = refs[0], refs[1:]
    if not first:
        old_max, old_sum, old_acc = refs[:3]
        refs = refs[3:]
    kv = refs[: 3 * pieces]
    new_max, new_sum, new_acc = refs[-3:]
    pairs, rows = q_ref.shape[0], q_ref.shape[1]
    half = rows // 2
    low = lax.broadcasted_iota(jnp.int32, (half, LANES), 1) < HEAD_SIZE

    def pick(even, odd):
        return jnp.where(low, even, odd)

    for j in range(pairs):
        q = q_ref[j]
        lanes = slice(j * LANES, (j + 1) * LANES)
        scores = []
        for i in range(pieces):
            k_ref, bias_ref = kv[3 * i], kv[3 * i + 2]
            s = dot(q, k_ref[:, lanes], 1)
            keys = s.shape[1]
            bias = bias_ref[...]
            s = s.reshape(rows // bias.shape[0], bias.shape[0], keys) + bias[None]
            scores.append(s.reshape(rows, keys))
        top = functools.reduce(
            jnp.maximum, [jnp.max(s, axis=1, keepdims=True) for s in scores]
        )
        if first:
            row_max = top
            pair_max = pick(row_max[:half], row_max[half:])
        else:
            old = old_max[j]
            pair_max = jnp.maximum(old, pick(top[:half], top[half:]))
            row_max = jnp.concatenate(
                [pair_max[:, :1], pair_max[:, HEAD_SIZE : HEAD_SIZE + 1]], axis=0
            )
        total = None
        for i in range(pieces):
            v_ref = kv[3 * i + 1]
            w = jnp.exp(scores[i] - row_max).astype(BF16)
            v = v_ref[:, lanes]
            v = jnp.concatenate([v, jnp.ones_like(v)], axis=1)
            part = dot(w, v)
            total = part if total is None else total + part
        acc = pick(total[:half, :LANES], total[half:, :LANES])
        summed = pick(total[:half, LANES:], total[half:, LANES:])
        if not first:
            scale = jnp.exp(old - pair_max)
            acc = acc + scale * old_acc[j]
            summed = summed + scale * old_sum[j]
        new_max[j] = pair_max
        new_sum[j] = summed
        new_acc[j] = acc


def block_refs(refs, count):
    return [r for i in range(count) for r in (refs[2 * i].at[0], refs[2 * i].at[1], refs[2 * i + 1])]


def attend(q, state, blocks):
    pairs, rows, lanes = q.shape
    first = state is None

    def kernel(*refs):
        lead = 1 + (0 if first else 3)
        attend_body(first, len(blocks), [*refs[:lead], *block_refs(refs[lead:], len(blocks)), *refs[-3:]])

    shape = jax.ShapeDtypeStruct((pairs, rows // 2, lanes), F32)
    operands = [q] + ([] if first else list(state)) + [a for block in blocks for a in block]
    vmem = pl.BlockSpec(memory_space=pltpu.VMEM)
    return pl.pallas_call(
        kernel,
        out_shape=[shape] * 3,
        in_specs=[vmem] * len(operands),
        out_specs=[vmem] * 3,
        compiler_params=pltpu.CompilerParams(vmem_limit_bytes=20 * 2**20),
        cost_estimate=cost(1.1 * len(blocks)),
        name="attend",
    )(*operands)


def block_owner(blocks, step):
    chips = blocks // CORES
    me = lax.axis_index("grp")
    x, core = lax.div(me, CORES), lax.rem(me, CORES)
    x = lax.rem(x + chips - step // CORES, chips)
    return x * CORES + lax.rem(core + step % CORES, CORES)


def project_body(
    blocks, sum_ref, acc_ref, weight_ref, residual_ref, gain_ref, hidden_ref, normed_ref, held
):
    pairs, rows, lanes = acc_ref.shape
    tokens = residual_ref.shape[0]
    per = rows // tokens
    hidden = residual_ref[...].astype(F32)
    for j in range(pairs):
        out = (acc_ref[j] / sum_ref[j]).astype(BF16)
        for r in range(0, per, 2):
            left = jnp.concatenate(
                [out[r * tokens : (r + 1) * tokens], out[(r + 1) * tokens : (r + 2) * tokens]], axis=1
            )
            heads = [(2 * j) * per + r, (2 * j + 1) * per + r, (2 * j) * per + r + 1, (2 * j + 1) * per + r + 1]
            right = jnp.concatenate(
                [weight_ref[h * HEAD_SIZE : (h + 1) * HEAD_SIZE, :] for h in heads], axis=0
            )
            hidden = hidden + dot(left, right)
    hidden_ref[...] = hidden
    mean = jnp.mean(hidden * hidden, axis=1, keepdims=True)
    held[...] = hidden * lax.rsqrt(mean + EPSILON) * gain_ref[...]
    width = hidden.shape[1] // blocks
    for b in range(blocks):
        start = pl.multiple_of(block_owner(blocks, b) * width, width)
        normed_ref[:, b * width : (b + 1) * width] = held[:, pl.ds(start, width)].astype(BF16)


def attend_project(q, state, blocks, columns, out_weight, residual, gain):
    pairs, rows, lanes = q.shape
    tokens, width = residual.shape
    count = len(blocks)

    def kernel(*refs):
        mine, (weight_ref, residual_ref, gain_ref) = refs[: 4 + 2 * count], refs[4 + 2 * count : 7 + 2 * count]
        hidden_ref, normed_ref, held, top, total, acc = refs[-6:]
        attend_body(False, count, [*mine[:4], *block_refs(mine[4:], count), top, total, acc])
        project_body(
            columns, total, acc, weight_ref, residual_ref, gain_ref, hidden_ref, normed_ref, held
        )

    operands = [q, *state] + [a for block in blocks for a in block]
    vmem = pl.BlockSpec(memory_space=pltpu.VMEM)
    return pl.pallas_call(
        kernel,
        out_shape=[
            jax.ShapeDtypeStruct((tokens, width), F32),
            jax.ShapeDtypeStruct((tokens, width), BF16),
        ],
        in_specs=[vmem] * (len(operands) + 3),
        out_specs=[vmem] * 2,
        scratch_shapes=[pltpu.VMEM((tokens, width), F32)]
        + [pltpu.VMEM((pairs, rows // 2, lanes), F32)] * 3,
        compiler_params=pltpu.CompilerParams(vmem_limit_bytes=20 * 2**20),
        cost_estimate=cost(1.1 * count + 2),
        name="attend_project",
    )(*operands, out_weight, residual, gain)


def rise_body(parts, blocks, refs):
    n_refs, gates, ups = refs[:parts], refs[parts : parts + blocks], refs[parts + blocks : parts + 2 * blocks]
    act_ref, x_ref = refs[-2:]
    tokens = n_refs[0].shape[0]
    for i in range(parts):
        x_ref[i * tokens : (i + 1) * tokens, :] = n_refs[i][...]
    depth, hidden = gates[0].shape
    tile = math.gcd(hidden, 256)

    @pl.loop(0, hidden // tile)
    def _(t):
        cols = pl.ds(pl.multiple_of(t * tile, tile), tile)
        gate = up = None
        for b in range(blocks):
            x = x_ref[:, b * depth : (b + 1) * depth]
            g, u = dot(x, gates[b][:, cols]), dot(x, ups[b][:, cols])
            gate, up = (g, u) if gate is None else (gate + g, up + u)
        act_ref[:, cols] = (gate / (1.0 + jnp.exp(-gate)) * up).astype(BF16)


def rise(normed, gates, ups):
    parts, blocks = len(normed), len(gates)
    tokens, model = normed[0].shape
    hidden = gates[0].shape[1]

    def kernel(*refs):
        rise_body(parts, blocks, refs)

    vmem = pl.BlockSpec(memory_space=pltpu.VMEM)
    return pl.pallas_call(
        kernel,
        out_shape=jax.ShapeDtypeStruct((parts * tokens, hidden), BF16),
        in_specs=[vmem] * (parts + 2 * blocks),
        out_specs=vmem,
        scratch_shapes=[pltpu.VMEM((parts * tokens, model), BF16)],
        compiler_params=pltpu.CompilerParams(vmem_limit_bytes=12 * 2**20),
        cost_estimate=cost(2 * parts),
        name="rise",
    )(*normed, *gates, *ups)


def fall_body(parts, blocks, refs):
    act_ref, downs, outs = refs[0], refs[1 : 1 + blocks], refs[1 + blocks :]
    tokens, width = outs[0].shape[0], downs[0].shape[1]
    tile = math.gcd(width, 256)
    for b in range(blocks):

        @pl.loop(0, width // tile)
        def _(t):
            term = dot(act_ref[...], downs[b][:, pl.ds(pl.multiple_of(t * tile, tile), tile)])
            cols = pl.ds(pl.multiple_of(b * width + t * tile, tile), tile)
            for i in range(parts):
                outs[i][:, cols] = term[i * tokens : (i + 1) * tokens].astype(BF16)


def fall(act, parts, downs):
    blocks = len(downs)
    shape = jax.ShapeDtypeStruct((act.shape[0] // parts, blocks * downs[0].shape[1]), BF16)

    def kernel(*refs):
        fall_body(parts, blocks, refs)

    vmem = pl.BlockSpec(memory_space=pltpu.VMEM)
    return pl.pallas_call(
        kernel,
        out_shape=[shape] * parts,
        in_specs=[vmem] * (1 + blocks),
        out_specs=[vmem] * parts,
        compiler_params=pltpu.CompilerParams(vmem_limit_bytes=12 * 2**20),
        cost_estimate=cost(parts),
        name="fall",
    )(act, *downs)


def finish_body(blocks, hidden_ref, *refs):
    terms, out_ref = refs[:-1], refs[-1]
    width = out_ref.shape[1] // blocks
    for b in range(blocks):
        cols = slice(b * width, (b + 1) * width)
        place = pl.ds(pl.multiple_of(block_owner(blocks, b) * width, width), width)
        total = hidden_ref[:, place]
        for term in terms:
            total = total + term[:, cols].astype(F32)
        out_ref[:, place] = total.astype(BF16)


def finish(blocks, hidden_state, terms):
    vmem = pl.BlockSpec(memory_space=pltpu.VMEM)
    return pl.pallas_call(
        functools.partial(finish_body, blocks),
        out_shape=jax.ShapeDtypeStruct(hidden_state.shape, BF16),
        in_specs=[vmem] * (1 + len(terms)),
        out_specs=vmem,
        compiler_params=pltpu.CompilerParams(vmem_limit_bytes=8 * 2**20),
        cost_estimate=cost(1),
        name="finish",
    )(hidden_state, *terms)


def tie(array, *others):
    return lax.optimization_barrier((array, *others))[0]


def shards(
    grps,
    devs,
    residual,
    queries,
    keys,
    values,
    prefix_keys,
    cached_prefix_values,
    out_weight,
    norm_gain,
    w_gate,
    w_up,
    w_down,
    suffix_lengths,
    request_group,
    placement_order,
):
    depth_z = math.gcd(devs, 4)
    depth_y = devs // depth_z
    cores = CORES
    depth_x = grps // cores
    ring = list(range(0, depth_z, 2)) + list(range(1, depth_z, 2))[::-1]

    def shift(by_z, by_y):
        return [
            (
                ring[i] * depth_y + y,
                ring[(i + by_z) % depth_z] * depth_y + (y + by_y) % depth_y,
            )
            for i in range(depth_z)
            for y in range(depth_y)
        ]

    x_shift = [
        (x * cores + c, (x + 1) % depth_x * cores + c) for x in range(depth_x) for c in range(cores)
    ]
    core_swap = [(x * cores + c, x * cores + 1 - c) for x in range(depth_x) for c in range(cores)]

    def along_y(block):
        return [block] + [lax.ppermute(block, "dev", shift(0, ys)) for ys in range(1, depth_y)]

    def along_x(weight, *others):
        blocks = [weight]
        for _ in range(1, depth_x):
            blocks.append(lax.ppermute(tie(blocks[-1], *others), "grp", x_shift))
        return blocks

    def other_core(block, *others):
        return lax.ppermute(tie(block, *others), "grp", core_swap)

    tokens = queries.shape[0]
    width = keys.shape[1]
    groups, span = prefix_keys.shape[:2]

    prefix = jnp.stack([prefix_keys.reshape(-1, width), cached_prefix_values.reshape(-1, width)])
    here = along_y(prefix)
    forward = lax.ppermute(prefix, "dev", shift(1, 0))
    backward = lax.ppermute(prefix, "dev", shift(-1, 0))
    own = jnp.stack([keys, values])
    before = lax.ppermute(own, "dev", [(i, i + 1) for i in range(devs - 1)])
    gate_rows = along_x(w_gate)
    q, before_mask, within_mask, prefix_mask = prepare(
        groups,
        span,
        suffix_lengths,
        request_group,
        placement_order,
        queries,
        width,
    )
    forward, backward = tie(forward, q, before, *here), tie(backward, q, before, *here)
    late = along_y(forward)[1:] + along_y(backward)[1:]
    first = state = attend(
        q,
        None,
        [(before, before_mask), (own, within_mask)]
        + [(b, prefix_mask) for b in here + [forward, backward]],
    )
    last = []
    for zs in range(2, depth_z - 1):
        forward = lax.ppermute(forward, "dev", shift(1, 0))
        late.append(forward)
        last += along_y(tie(forward, first[0]))[1:]
    state = attend(tie(q, *gate_rows[1:]), state, [(b, prefix_mask) for b in late])
    up_rows = along_x(w_up, *gate_rows[1:], *late)
    gate_swap, up_swap = other_core(w_gate, *late, first[0]), other_core(w_up, state[0])
    hidden_state, normed = attend_project(
        q,
        state,
        [(b, prefix_mask) for b in last],
        grps,
        out_weight,
        tie(residual, gate_swap),
        norm_gain[None],
    )

    gates, ups, downs = [w_gate, gate_swap], [w_up, up_swap], [w_down]
    for gate in gate_rows[1:]:
        gates += [gate, other_core(gate, normed)]
    chunks = [along_y(normed)]
    down_cols = along_x(w_down, *up_rows[1:], normed)
    chunks.append(along_y(lax.ppermute(normed, "dev", shift(1, 0))))
    for up in up_rows[1:]:
        ups += [up, other_core(up, normed, *chunks[0][1:])]
    downs.append(other_core(w_down, chunks[1][0]))
    ready = chunks[0][1:] + gates[3:] + [up_swap]
    acts = {}
    for zs in range(2, depth_z):
        chunks.append(along_y(lax.ppermute(tie(chunks[-1][0], *ready), "dev", shift(1, 0))))
        ready = chunks[-2][1:] + downs[1:] + [acts.setdefault(0, rise(chunks[0], gates, ups))]
    acts[1] = rise(chunks[1], gates, ups)
    for down in down_cols[1:]:
        downs += [down, other_core(down, chunks[-1][0], *chunks[-2][1:], acts[1])]
    chunks[2][0] = tie(chunks[2][0], *chunks[-1][1:])

    running = None
    for zs in list(range(1, depth_z)) + [0]:
        act = acts[zs] if zs in acts else rise(chunks[zs], gates, ups)
        parts = fall(act, depth_y, downs)
        if zs == 0:
            parts = [parts[0]] + [tie(part, running) for part in parts[1:]]
        terms = [parts[0]] + [
            lax.ppermute(parts[ys], "dev", shift(0, -ys)) for ys in range(1, depth_y)
        ]
        if running is not None:
            terms.append(lax.ppermute(running, "dev", shift(1, 0)))
        if zs:
            running = functools.reduce(jnp.add, [term.astype(F32) for term in terms]).astype(BF16)
    return finish(grps, hidden_state, terms)


def solution(mesh):
    placed = (
        P(("grp", "dev"), None),
        P(("grp", "dev"), None),
        P(("grp", "dev"), None),
        P(("grp", "dev"), None),
        P("grp", "dev", None),
        P("grp", "dev", None),
        P(),
        P(),
        P("grp", "dev"),
        P("grp", "dev"),
        P("dev", "grp"),
        P("grp", None),
        P("grp", None),
        P("grp", None),
    )
    return jax.shard_map(
        functools.partial(shards, mesh.shape["grp"], mesh.shape["dev"]),
        mesh=mesh,
        in_specs=placed,
        out_specs=P(("grp", "dev"), None),
        check_vma=False,
    )
```

```python
import functools
import math

import jax
import jax.numpy as jnp
from jax import lax
from jax.experimental import pallas as pl
from jax.experimental.pallas import tpu as pltpu
from jax.sharding import PartitionSpec as P

HEAD_SIZE = 64
NEG_FILL = -1e30
EPSILON = 1e-05
F32 = jnp.float32
BF16 = jnp.bfloat16
LANES = 2 * HEAD_SIZE
CORES = 2
HALVES = 2


def cost(microseconds):
    return pl.CostEstimate(flops=0, bytes_accessed=int(microseconds * 3.5e6), transcendentals=0)


def dot(a, b, contract_b=0):
    return lax.dot_general(
        a, b, (((1,), (contract_b,)), ((), ())), preferred_element_type=F32
    )


def prepare_body(
    span,
    lengths_hbm,
    groups_hbm,
    packing_hbm,
    queries_hbm,
    *refs,
):
    q_ref, before_ref, within_ref, prefix_ref = refs[:4]
    lengths_ref, groups_ref, packing_ref, queries_ref, sems = refs[4:]
    copies = [
        pltpu.make_async_copy(source, target, sems.at[i])
        for i, (source, target) in enumerate(
            [
                (lengths_hbm, lengths_ref),
                (groups_hbm, groups_ref),
                (packing_hbm, packing_ref),
                (queries_hbm, queries_ref),
            ]
        )
    ]
    for copy in copies:
        copy.start()
    for copy in copies:
        copy.wait()
    tokens = queries_ref.shape[0]
    pairs, rows = q_ref.shape[0], q_ref.shape[1]
    per = rows // (2 * tokens)
    base = lax.axis_index("dev") * tokens
    own = base + lax.broadcasted_iota(jnp.int32, (tokens, LANES), 0)

    def request(k, carry):
        start, group, first = carry
        j = packing_ref[0, k]
        end = start + lengths_ref[0, j]
        inside = (own >= start) & (own < end)
        return (
            end,
            jnp.where(inside, groups_ref[0, j], group),
            jnp.where(inside, start, first),
        )

    zero = jnp.zeros((tokens, LANES), jnp.int32)
    _, group, first = lax.fori_loop(0, lengths_ref.shape[1], request, (jnp.int32(0), zero, zero))
    for ref, back in ((before_ref, tokens), (within_ref, 0)):
        for c in range(0, tokens, LANES):
            key = base - back + c + lax.broadcasted_iota(jnp.int32, (tokens, LANES), 1)
            ref[:, c : c + LANES] = jnp.where((key >= first) & (key <= own), 0.0, NEG_FILL)
    for c in range(0, prefix_ref.shape[1], LANES):
        key_group = lax.div(c + lax.broadcasted_iota(jnp.int32, (tokens, LANES), 1), span)
        prefix_ref[:, c : c + LANES] = jnp.where(group == key_group, 0.0, NEG_FILL)
    low = lax.broadcasted_iota(jnp.int32, (tokens, LANES), 1) < HEAD_SIZE
    for j in range(pairs):
        for parity in range(2):
            for r in range(per):
                head = (2 * j + parity) * per + r
                block = head // 2
                q = queries_ref[:, block * LANES : (block + 1) * LANES].astype(F32) * HEAD_SIZE ** (-0.5)
                if head % 2 != parity:
                    q = pltpu.roll(q, HEAD_SIZE, 1)
                q = jnp.where(low == (parity == 0), q, 0.0)
                row = (parity * per + r) * tokens
                q_ref[j, row : row + tokens, :] = q.astype(BF16)


def prepare(groups, span, lengths, request_group, packing, queries, width):
    tokens = queries.shape[0]
    per = queries.shape[1] // width
    vmem = pl.BlockSpec(memory_space=pltpu.VMEM)
    return pl.pallas_call(
        functools.partial(prepare_body, span),
        out_shape=[
            jax.ShapeDtypeStruct((width // LANES, 2 * per * tokens, LANES), BF16),
            jax.ShapeDtypeStruct((tokens, tokens), F32),
            jax.ShapeDtypeStruct((tokens, tokens), F32),
            jax.ShapeDtypeStruct((tokens, groups * span), F32),
        ],
        in_specs=[pl.BlockSpec(memory_space=pltpu.HBM)] * 4,
        out_specs=[vmem] * 4,
        compiler_params=pltpu.CompilerParams(vmem_limit_bytes=8 * 2**20),
        scratch_shapes=[pltpu.SMEM(lengths.shape, jnp.int32)] * 3
        + [pltpu.VMEM(queries.shape, BF16), pltpu.SemaphoreType.DMA((4,))],
        cost_estimate=cost(3),
        name="prepare",
    )(lengths, request_group, packing, queries)


def attend_body(first, pieces, refs):
    q_ref, refs = refs[0], refs[1:]
    if not first:
        old_max, old_sum, old_acc = refs[:3]
        refs = refs[3:]
    kv = refs[: 3 * pieces]
    new_max, new_sum, new_acc = refs[-3:]
    pairs, rows = q_ref.shape[0], q_ref.shape[1]
    half = rows // 2
    low = lax.broadcasted_iota(jnp.int32, (half, LANES), 1) < HEAD_SIZE

    def pick(even, odd):
        return jnp.where(low, even, odd)

    for j in range(pairs):
        q = q_ref[j]
        lanes = slice(j * LANES, (j + 1) * LANES)
        scores = []
        for i in range(pieces):
            k_ref, bias_ref = kv[3 * i], kv[3 * i + 2]
            s = dot(q, k_ref[:, lanes], 1)
            keys = s.shape[1]
            bias = bias_ref[...]
            s = s.reshape(rows // bias.shape[0], bias.shape[0], keys) + bias[None]
            scores.append(s.reshape(rows, keys))
        top = functools.reduce(
            jnp.maximum, [jnp.max(s, axis=1, keepdims=True) for s in scores]
        )
        if first:
            row_max = top
            pair_max = pick(row_max[:half], row_max[half:])
        else:
            old = old_max[j]
            pair_max = jnp.maximum(old, pick(top[:half], top[half:]))
            row_max = jnp.concatenate(
                [pair_max[:, :1], pair_max[:, HEAD_SIZE : HEAD_SIZE + 1]], axis=0
            )
        total = None
        for i in range(pieces):
            v_ref = kv[3 * i + 1]
            w = jnp.exp(scores[i] - row_max).astype(BF16)
            v = v_ref[:, lanes]
            v = jnp.concatenate([v, jnp.ones_like(v)], axis=1)
            part = dot(w, v)
            total = part if total is None else total + part
        acc = pick(total[:half, :LANES], total[half:, :LANES])
        summed = pick(total[:half, LANES:], total[half:, LANES:])
        if not first:
            scale = jnp.exp(old - pair_max)
            acc = acc + scale * old_acc[j]
            summed = summed + scale * old_sum[j]
        new_max[j] = pair_max
        new_sum[j] = summed
        new_acc[j] = acc


def block_refs(refs, count):
    return [r for i in range(count) for r in (refs[2 * i].at[0], refs[2 * i].at[1], refs[2 * i + 1])]


def attend(q, state, blocks):
    pairs, rows, lanes = q.shape
    first = state is None

    def kernel(*refs):
        lead = 1 + (0 if first else 3)
        attend_body(first, len(blocks), [*refs[:lead], *block_refs(refs[lead:], len(blocks)), *refs[-3:]])

    shape = jax.ShapeDtypeStruct((pairs, rows // 2, lanes), F32)
    operands = [q] + ([] if first else list(state)) + [a for block in blocks for a in block]
    vmem = pl.BlockSpec(memory_space=pltpu.VMEM)
    return pl.pallas_call(
        kernel,
        out_shape=[shape] * 3,
        in_specs=[vmem] * len(operands),
        out_specs=[vmem] * 3,
        compiler_params=pltpu.CompilerParams(vmem_limit_bytes=20 * 2**20),
        cost_estimate=cost(1.1 * len(blocks)),
        name="attend",
    )(*operands)


def block_owner(blocks, step):
    chips = blocks // CORES
    me = lax.axis_index("grp")
    x, core = lax.div(me, CORES), lax.rem(me, CORES)
    x = lax.rem(x + chips - step // CORES, chips)
    return x * CORES + lax.rem(core + step % CORES, CORES)


def project_body(
    blocks, sum_ref, acc_ref, weight_ref, residual_ref, gain_ref, hidden_ref, normed_refs, held
):
    pairs, rows, lanes = acc_ref.shape
    tokens = residual_ref.shape[0]
    per = rows // tokens
    hidden = residual_ref[...].astype(F32)
    for j in range(pairs):
        out = (acc_ref[j] / sum_ref[j]).astype(BF16)
        for r in range(0, per, 2):
            left = jnp.concatenate(
                [out[r * tokens : (r + 1) * tokens], out[(r + 1) * tokens : (r + 2) * tokens]], axis=1
            )
            heads = [(2 * j) * per + r, (2 * j + 1) * per + r, (2 * j) * per + r + 1, (2 * j + 1) * per + r + 1]
            right = jnp.concatenate(
                [weight_ref[h * HEAD_SIZE : (h + 1) * HEAD_SIZE, :] for h in heads], axis=0
            )
            hidden = hidden + dot(left, right)
    hidden_ref[...] = hidden
    mean = jnp.mean(hidden * hidden, axis=1, keepdims=True)
    held[...] = hidden * lax.rsqrt(mean + EPSILON) * gain_ref[...]
    width = hidden.shape[1] // blocks
    for b in range(blocks):
        start = pl.multiple_of(block_owner(blocks, b) * width, width)
        half, place = divmod(b, blocks // HALVES)
        normed_refs[half][:, place * width : (place + 1) * width] = held[:, pl.ds(start, width)].astype(BF16)


def attend_project(q, state, blocks, columns, out_weight, residual, gain):
    pairs, rows, lanes = q.shape
    tokens, width = residual.shape
    count = len(blocks)

    def kernel(*refs):
        mine, (weight_ref, residual_ref, gain_ref) = refs[: 4 + 2 * count], refs[4 + 2 * count : 7 + 2 * count]
        hidden_ref, *normed_refs = refs[7 + 2 * count : 8 + 2 * count + HALVES]
        held, top, total, acc = refs[-4:]
        attend_body(False, count, [*mine[:4], *block_refs(mine[4:], count), top, total, acc])
        project_body(
            columns, total, acc, weight_ref, residual_ref, gain_ref, hidden_ref, normed_refs, held
        )

    operands = [q, *state] + [a for block in blocks for a in block]
    vmem = pl.BlockSpec(memory_space=pltpu.VMEM)
    return pl.pallas_call(
        kernel,
        out_shape=[
            jax.ShapeDtypeStruct((tokens, width), F32),
        ]
        + [jax.ShapeDtypeStruct((tokens, width // HALVES), BF16)] * HALVES,
        in_specs=[vmem] * (len(operands) + 3),
        out_specs=[vmem] * (1 + HALVES),
        scratch_shapes=[pltpu.VMEM((tokens, width), F32)]
        + [pltpu.VMEM((pairs, rows // 2, lanes), F32)] * 3,
        compiler_params=pltpu.CompilerParams(vmem_limit_bytes=20 * 2**20),
        cost_estimate=cost(1.1 * count + 2),
        name="attend_project",
    )(*operands, out_weight, residual, gain)


def rise_body(parts, blocks, refs):
    pieces = parts * HALVES
    n_refs, gates, ups = refs[:pieces], refs[pieces : pieces + blocks], refs[pieces + blocks : pieces + 2 * blocks]
    act_ref, x_ref = refs[-2:]
    tokens, width = n_refs[0].shape
    for i in range(parts):
        for half in range(HALVES):
            x_ref[i * tokens : (i + 1) * tokens, half * width : (half + 1) * width] = n_refs[i * HALVES + half][...]
    depth, hidden = gates[0].shape
    tile = math.gcd(hidden, 256)

    @pl.loop(0, hidden // tile)
    def _(t):
        cols = pl.ds(pl.multiple_of(t * tile, tile), tile)
        gate = up = None
        for b in range(blocks):
            x = x_ref[:, b * depth : (b + 1) * depth]
            g, u = dot(x, gates[b][:, cols]), dot(x, ups[b][:, cols])
            gate, up = (g, u) if gate is None else (gate + g, up + u)
        act_ref[:, cols] = (gate / (1.0 + jnp.exp(-gate)) * up).astype(BF16)


def rise(normed, gates, ups):
    parts, blocks = len(normed), len(gates)
    tokens, width = normed[0][0].shape
    hidden = gates[0].shape[1]

    def kernel(*refs):
        rise_body(parts, blocks, refs)

    vmem = pl.BlockSpec(memory_space=pltpu.VMEM)
    return pl.pallas_call(
        kernel,
        out_shape=jax.ShapeDtypeStruct((parts * tokens, hidden), BF16),
        in_specs=[vmem] * (parts * HALVES + 2 * blocks),
        out_specs=vmem,
        scratch_shapes=[pltpu.VMEM((parts * tokens, HALVES * width), BF16)],
        compiler_params=pltpu.CompilerParams(vmem_limit_bytes=12 * 2**20),
        cost_estimate=cost(1.5 * parts),
        name="rise",
    )(*[half for chunk in normed for half in chunk], *gates, *ups)


def fall_body(parts, blocks, refs):
    act_ref, downs, outs = refs[0], refs[1 : 1 + blocks], refs[1 + blocks :]
    tokens, width = outs[0].shape[0], downs[0].shape[1]
    tile = math.gcd(width, 256)
    for b in range(blocks):

        @pl.loop(0, width // tile)
        def _(t):
            term = dot(act_ref[...], downs[b][:, pl.ds(pl.multiple_of(t * tile, tile), tile)])
            cols = pl.ds(pl.multiple_of(b * width + t * tile, tile), tile)
            for i in range(parts):
                outs[i][:, cols] = term[i * tokens : (i + 1) * tokens].astype(BF16)


def fall(act, parts, downs):
    blocks = len(downs)
    shape = jax.ShapeDtypeStruct((act.shape[0] // parts, blocks * downs[0].shape[1]), BF16)

    def kernel(*refs):
        fall_body(parts, blocks, refs)

    vmem = pl.BlockSpec(memory_space=pltpu.VMEM)
    return pl.pallas_call(
        kernel,
        out_shape=[shape] * parts,
        in_specs=[vmem] * (1 + blocks),
        out_specs=[vmem] * parts,
        compiler_params=pltpu.CompilerParams(vmem_limit_bytes=12 * 2**20),
        cost_estimate=cost(0.6 * parts),
        name="fall",
    )(act, *downs)


def finish_body(blocks, hidden_ref, *refs):
    terms, out_ref = refs[:-1], refs[-1]
    each = len(terms) // HALVES
    width = out_ref.shape[1] // blocks
    for b in range(blocks):
        half, column = divmod(b, blocks // HALVES)
        place = pl.ds(pl.multiple_of(block_owner(blocks, b) * width, width), width)
        total = hidden_ref[:, place]
        for term in terms[half * each : (half + 1) * each]:
            total = total + term[:, column * width : (column + 1) * width].astype(F32)
        out_ref[:, place] = total.astype(BF16)


def finish(blocks, hidden_state, terms):
    vmem = pl.BlockSpec(memory_space=pltpu.VMEM)
    operands = [hidden_state] + [term for half in terms for term in half]
    return pl.pallas_call(
        functools.partial(finish_body, blocks),
        out_shape=jax.ShapeDtypeStruct(hidden_state.shape, BF16),
        in_specs=[vmem] * len(operands),
        out_specs=vmem,
        compiler_params=pltpu.CompilerParams(vmem_limit_bytes=8 * 2**20),
        cost_estimate=cost(1),
        name="finish",
    )(*operands)


def tie(array, *others):
    return lax.optimization_barrier((array, *others))[0] if others else array


def shards(
    grps,
    devs,
    residual,
    queries,
    keys,
    values,
    prefix_keys,
    cached_prefix_values,
    out_weight,
    norm_gain,
    w_gate,
    w_up,
    w_down,
    suffix_lengths,
    request_group,
    placement_order,
):
    depth_z = math.gcd(devs, 4)
    depth_y = devs // depth_z
    cores = CORES
    depth_x = grps // cores
    ring = list(range(0, depth_z, 2)) + list(range(1, depth_z, 2))[::-1]

    def shift(by_z, by_y):
        return [
            (
                ring[i] * depth_y + y,
                ring[(i + by_z) % depth_z] * depth_y + (y + by_y) % depth_y,
            )
            for i in range(depth_z)
            for y in range(depth_y)
        ]

    x_shift = [
        (x * cores + c, (x + 1) % depth_x * cores + c) for x in range(depth_x) for c in range(cores)
    ]
    core_swap = [(x * cores + c, x * cores + 1 - c) for x in range(depth_x) for c in range(cores)]

    def round_z(block, *others):
        return lax.ppermute(tie(block, *others), "dev", shift(1, 0))

    def along_y(block, *others):
        return [lax.ppermute(tie(block, *others), "dev", shift(0, ys)) for ys in range(1, depth_y)]

    def along_x(weight, *others):
        blocks = [weight]
        for _ in range(1, depth_x):
            blocks.append(lax.ppermute(tie(blocks[-1], *others), "grp", x_shift))
        return blocks

    def other_core(block, *others):
        return lax.ppermute(tie(block, *others), "grp", core_swap)

    tokens = queries.shape[0]
    width = keys.shape[1]
    groups, span = prefix_keys.shape[:2]

    prefix = jnp.stack([prefix_keys.reshape(-1, width), cached_prefix_values.reshape(-1, width)])
    other = along_y(prefix)
    arriving = round_z(prefix)
    own = jnp.stack([keys, values])
    before = lax.ppermute(own, "dev", [(i, i + 1) for i in range(devs - 1)])
    gate_rows = along_x(w_gate)
    q, before_mask, within_mask, prefix_mask = prepare(
        groups,
        span,
        suffix_lengths,
        request_group,
        placement_order,
        queries,
        width,
    )
    blocks = [(before, before_mask), (own, within_mask), (prefix, prefix_mask)]
    ready, state = [q, before], None
    for zs in range(1, depth_z):
        if zs == depth_z - 1:
            ready += [gate_swap, *gate_rows[1:]]
        here = tie(arriving, *other, *ready)
        if zs < depth_z - 1:
            arriving = round_z(here)
        blocks += [(b, prefix_mask) for b in other + [here]]
        other = along_y(here)
        state = attend(q, state, blocks)
        blocks, ready = [], [state[0]]
        if zs == 1:
            gate_swap = other_core(w_gate, here)
        elif zs == 2:
            up_swap = other_core(w_up, here)
    down_swap = other_core(w_down, here)
    up_rows = along_x(w_up, *gate_rows[1:], here)
    gates = [w_gate, gate_swap]
    for gate in gate_rows[1:]:
        gates += [gate, other_core(gate, here)]
    hidden_state, *normed = attend_project(
        q,
        state,
        [(b, prefix_mask) for b in other],
        grps,
        out_weight,
        tie(residual, up_swap, down_swap, *gates[2:]),
        norm_gain[None],
    )

    arrived, across = [normed], [[along_y(half) for half in normed]]
    ups, downs, acts = [w_up, up_swap], [w_down, down_swap], {}
    for zs in range(1, depth_z):
        waits = across[zs - 2] if zs > 1 else [[] for _ in normed]
        arrived.append([round_z(half, *wait) for half, wait in zip(arrived[-1], waits)])
        if zs == 1:
            for up in up_rows[1:]:
                ups += [up, other_core(up, *arrived[1], *[b for c in across[0] for b in c])]
            down_cols = along_x(w_down, *ups[3:])
        late = arrived[zs - 1][1:] if zs > 1 else []
        if zs == depth_z - 1:
            acts[1] = rise([arrived[1]] + [list(c) for c in zip(*across[1])], gates, ups)
            late = [*late, acts[1]]
        across.append([along_y(half, *late) for half in arrived[zs]])
    chunks = [[a] + [list(c) for c in zip(*b)] for a, b in zip(arrived, across)]
    for down in down_cols[1:]:
        downs += [down, other_core(down, *arrived[-1], *[b for c in across[-2] for b in c])]
    chunks[2][0] = [tie(half, *[b for c in across[-1] for b in c]) for half in chunks[2][0]]

    running, terms = [None] * HALVES, [None] * HALVES
    each = len(downs) // HALVES
    for zs in list(range(1, depth_z)) + [0]:
        act = acts[zs] if zs in acts else rise(chunks[zs], gates, ups)
        for half in range(HALVES):
            parts = fall(act, depth_y, downs[half * each : (half + 1) * each])
            if zs == 0:
                parts = [parts[0]] + [tie(part, running[half]) for part in parts[1:]]
            terms[half] = [parts[0]] + [
                lax.ppermute(parts[ys], "dev", shift(0, -ys)) for ys in range(1, depth_y)
            ]
            if running[half] is not None:
                terms[half].append(round_z(running[half]))
            if zs:
                running[half] = functools.reduce(
                    jnp.add, [term.astype(F32) for term in terms[half]]
                ).astype(BF16)
    return finish(grps, hidden_state, terms)


def solution(mesh):
    placed = (
        P(("grp", "dev"), None),
        P(("grp", "dev"), None),
        P(("grp", "dev"), None),
        P(("grp", "dev"), None),
        P("grp", "dev", None),
        P("grp", "dev", None),
        P(),
        P(),
        P("grp", "dev"),
        P("grp", "dev"),
        P("dev", "grp"),
        P("grp", None),
        P("grp", None),
        P("grp", None),
    )
    return jax.shard_map(
        functools.partial(shards, mesh.shape["grp"], mesh.shape["dev"]),
        mesh=mesh,
        in_specs=placed,
        out_specs=P(("grp", "dev"), None),
        check_vma=False,
    )
```

```python
import functools
import math

import jax
import jax.numpy as jnp
from jax import lax
from jax.experimental import pallas as pl
from jax.experimental.pallas import tpu as pltpu
from jax.sharding import PartitionSpec as P

HEAD_SIZE = 64
NEG_FILL = -1e30
EPSILON = 1e-05
F32 = jnp.float32
BF16 = jnp.bfloat16
LANES = 2 * HEAD_SIZE
CORES = 2
HALVES = 2


def cost(microseconds):
    return pl.CostEstimate(flops=0, bytes_accessed=int(microseconds * 3.5e6), transcendentals=0)


def dot(a, b, contract_b=0):
    return lax.dot_general(
        a, b, (((1,), (contract_b,)), ((), ())), preferred_element_type=F32
    )


def prepare_body(
    span,
    lengths_hbm,
    groups_hbm,
    packing_hbm,
    queries_hbm,
    *refs,
):
    q_ref, before_ref, within_ref, prefix_ref = refs[:4]
    lengths_ref, groups_ref, packing_ref, queries_ref, sems = refs[4:]
    copies = [
        pltpu.make_async_copy(source, target, sems.at[i])
        for i, (source, target) in enumerate(
            [
                (lengths_hbm, lengths_ref),
                (groups_hbm, groups_ref),
                (packing_hbm, packing_ref),
                (queries_hbm, queries_ref),
            ]
        )
    ]
    for copy in copies:
        copy.start()
    for copy in copies:
        copy.wait()
    tokens = queries_ref.shape[0]
    pairs, rows = q_ref.shape[0], q_ref.shape[1]
    per = rows // (2 * tokens)
    base = lax.axis_index("dev") * tokens
    own = base + lax.broadcasted_iota(jnp.int32, (tokens, LANES), 0)

    def request(k, carry):
        start, group, first = carry
        j = packing_ref[0, k]
        end = start + lengths_ref[0, j]
        inside = (own >= start) & (own < end)
        return (
            end,
            jnp.where(inside, groups_ref[0, j], group),
            jnp.where(inside, start, first),
        )

    zero = jnp.zeros((tokens, LANES), jnp.int32)
    _, group, first = lax.fori_loop(0, lengths_ref.shape[1], request, (jnp.int32(0), zero, zero))
    for ref, back in ((before_ref, tokens), (within_ref, 0)):
        for c in range(0, tokens, LANES):
            key = base - back + c + lax.broadcasted_iota(jnp.int32, (tokens, LANES), 1)
            ref[:, c : c + LANES] = jnp.where((key >= first) & (key <= own), 0.0, NEG_FILL)
    for c in range(0, prefix_ref.shape[1], LANES):
        key_group = lax.div(c + lax.broadcasted_iota(jnp.int32, (tokens, LANES), 1), span)
        prefix_ref[:, c : c + LANES] = jnp.where(group == key_group, 0.0, NEG_FILL)
    low = lax.broadcasted_iota(jnp.int32, (tokens, LANES), 1) < HEAD_SIZE
    for j in range(pairs):
        for parity in range(2):
            for r in range(per):
                head = (2 * j + parity) * per + r
                block = head // 2
                q = queries_ref[:, block * LANES : (block + 1) * LANES].astype(F32) * HEAD_SIZE ** (-0.5)
                if head % 2 != parity:
                    q = pltpu.roll(q, HEAD_SIZE, 1)
                q = jnp.where(low == (parity == 0), q, 0.0)
                row = (parity * per + r) * tokens
                q_ref[j, row : row + tokens, :] = q.astype(BF16)


def prepare(groups, span, lengths, request_group, packing, queries, width):
    tokens = queries.shape[0]
    per = queries.shape[1] // width
    vmem = pl.BlockSpec(memory_space=pltpu.VMEM)
    return pl.pallas_call(
        functools.partial(prepare_body, span),
        out_shape=[
            jax.ShapeDtypeStruct((width // LANES, 2 * per * tokens, LANES), BF16),
            jax.ShapeDtypeStruct((tokens, tokens), F32),
            jax.ShapeDtypeStruct((tokens, tokens), F32),
            jax.ShapeDtypeStruct((tokens, groups * span), F32),
        ],
        in_specs=[pl.BlockSpec(memory_space=pltpu.HBM)] * 4,
        out_specs=[vmem] * 4,
        compiler_params=pltpu.CompilerParams(vmem_limit_bytes=8 * 2**20),
        scratch_shapes=[pltpu.SMEM(lengths.shape, jnp.int32)] * 3
        + [pltpu.VMEM(queries.shape, BF16), pltpu.SemaphoreType.DMA((4,))],
        cost_estimate=cost(3),
        name="prepare",
    )(lengths, request_group, packing, queries)


def attend_body(first, pieces, refs):
    q_ref, refs = refs[0], refs[1:]
    if not first:
        old_max, old_sum, old_acc = refs[:3]
        refs = refs[3:]
    kv = refs[: 3 * pieces]
    new_max, new_sum, new_acc = refs[-3:]
    pairs, rows = q_ref.shape[0], q_ref.shape[1]
    half = rows // 2
    low = lax.broadcasted_iota(jnp.int32, (half, LANES), 1) < HEAD_SIZE

    def pick(even, odd):
        return jnp.where(low, even, odd)

    for j in range(pairs):
        q = q_ref[j]
        lanes = slice(j * LANES, (j + 1) * LANES)
        scores = []
        for i in range(pieces):
            k_ref, bias_ref = kv[3 * i], kv[3 * i + 2]
            s = dot(q, k_ref[:, lanes], 1)
            keys = s.shape[1]
            bias = bias_ref[...]
            s = s.reshape(rows // bias.shape[0], bias.shape[0], keys) + bias[None]
            scores.append(s.reshape(rows, keys))
        top = functools.reduce(
            jnp.maximum, [jnp.max(s, axis=1, keepdims=True) for s in scores]
        )
        if first:
            row_max = top
            pair_max = pick(row_max[:half], row_max[half:])
        else:
            old = old_max[j]
            pair_max = jnp.maximum(old, pick(top[:half], top[half:]))
            row_max = jnp.concatenate(
                [pair_max[:, :1], pair_max[:, HEAD_SIZE : HEAD_SIZE + 1]], axis=0
            )
        total = None
        for i in range(pieces):
            v_ref = kv[3 * i + 1]
            w = jnp.exp(scores[i] - row_max).astype(BF16)
            v = v_ref[:, lanes]
            v = jnp.concatenate([v, jnp.ones_like(v)], axis=1)
            part = dot(w, v)
            total = part if total is None else total + part
        acc = pick(total[:half, :LANES], total[half:, :LANES])
        summed = pick(total[:half, LANES:], total[half:, LANES:])
        if not first:
            scale = jnp.exp(old - pair_max)
            acc = acc + scale * old_acc[j]
            summed = summed + scale * old_sum[j]
        new_max[j] = pair_max
        new_sum[j] = summed
        new_acc[j] = acc


def block_refs(refs, count):
    return [r for i in range(count) for r in (refs[2 * i].at[0], refs[2 * i].at[1], refs[2 * i + 1])]


def attend(q, state, blocks):
    pairs, rows, lanes = q.shape
    first = state is None

    def kernel(*refs):
        lead = 1 + (0 if first else 3)
        attend_body(first, len(blocks), [*refs[:lead], *block_refs(refs[lead:], len(blocks)), *refs[-3:]])

    shape = jax.ShapeDtypeStruct((pairs, rows // 2, lanes), F32)
    operands = [q] + ([] if first else list(state)) + [a for block in blocks for a in block]
    vmem = pl.BlockSpec(memory_space=pltpu.VMEM)
    return pl.pallas_call(
        kernel,
        out_shape=[shape] * 3,
        in_specs=[vmem] * len(operands),
        out_specs=[vmem] * 3,
        compiler_params=pltpu.CompilerParams(vmem_limit_bytes=20 * 2**20),
        cost_estimate=cost(1.1 * len(blocks)),
        name="attend",
    )(*operands)


def block_owner(blocks, step):
    chips = blocks // CORES
    me = lax.axis_index("grp")
    x, core = lax.div(me, CORES), lax.rem(me, CORES)
    x = lax.rem(x + chips - step // CORES, chips)
    return x * CORES + lax.rem(core + step % CORES, CORES)


def project_body(
    blocks, sum_ref, acc_ref, weight_ref, residual_ref, gain_ref, hidden_ref, normed_refs, held
):
    pairs, rows, lanes = acc_ref.shape
    tokens = residual_ref.shape[0]
    per = rows // tokens
    hidden = residual_ref[...].astype(F32)
    for j in range(pairs):
        out = (acc_ref[j] / sum_ref[j]).astype(BF16)
        for r in range(0, per, 2):
            left = jnp.concatenate(
                [out[r * tokens : (r + 1) * tokens], out[(r + 1) * tokens : (r + 2) * tokens]], axis=1
            )
            heads = [(2 * j) * per + r, (2 * j + 1) * per + r, (2 * j) * per + r + 1, (2 * j + 1) * per + r + 1]
            right = jnp.concatenate(
                [weight_ref[h * HEAD_SIZE : (h + 1) * HEAD_SIZE, :] for h in heads], axis=0
            )
            hidden = hidden + dot(left, right)
    hidden_ref[...] = hidden
    mean = jnp.mean(hidden * hidden, axis=1, keepdims=True)
    held[...] = hidden * lax.rsqrt(mean + EPSILON) * gain_ref[...]
    width = hidden.shape[1] // blocks
    for b in range(blocks):
        start = pl.multiple_of(block_owner(blocks, b) * width, width)
        half, place = divmod(b, blocks // HALVES)
        normed_refs[half][:, place * width : (place + 1) * width] = held[:, pl.ds(start, width)].astype(BF16)


def attend_project(q, state, blocks, columns, out_weight, residual, gain):
    pairs, rows, lanes = q.shape
    tokens, width = residual.shape
    count = len(blocks)

    def kernel(*refs):
        mine, (weight_ref, residual_ref, gain_ref) = refs[: 4 + 2 * count], refs[4 + 2 * count : 7 + 2 * count]
        hidden_ref, *normed_refs = refs[7 + 2 * count : 8 + 2 * count + HALVES]
        held, top, total, acc = refs[-4:]
        attend_body(False, count, [*mine[:4], *block_refs(mine[4:], count), top, total, acc])
        project_body(
            columns, total, acc, weight_ref, residual_ref, gain_ref, hidden_ref, normed_refs, held
        )

    operands = [q, *state] + [a for block in blocks for a in block]
    vmem = pl.BlockSpec(memory_space=pltpu.VMEM)
    return pl.pallas_call(
        kernel,
        out_shape=[
            jax.ShapeDtypeStruct((tokens, width), F32),
        ]
        + [jax.ShapeDtypeStruct((tokens, width // HALVES), BF16)] * HALVES,
        in_specs=[vmem] * (len(operands) + 3),
        out_specs=[vmem] * (1 + HALVES),
        scratch_shapes=[pltpu.VMEM((tokens, width), F32)]
        + [pltpu.VMEM((pairs, rows // 2, lanes), F32)] * 3,
        compiler_params=pltpu.CompilerParams(vmem_limit_bytes=20 * 2**20),
        cost_estimate=cost(1.1 * count + 2),
        name="attend_project",
    )(*operands, out_weight, residual, gain)


def rise_body(parts, blocks, refs):
    pieces = parts * HALVES
    n_refs, gates, ups = refs[:pieces], refs[pieces : pieces + blocks], refs[pieces + blocks : pieces + 2 * blocks]
    act_ref, x_ref = refs[-2:]
    tokens, width = n_refs[0].shape
    for i in range(parts):
        for half in range(HALVES):
            x_ref[i * tokens : (i + 1) * tokens, half * width : (half + 1) * width] = n_refs[i * HALVES + half][...]
    depth, hidden = gates[0].shape
    tile = math.gcd(hidden, 256)

    @pl.loop(0, hidden // tile)
    def _(t):
        cols = pl.ds(pl.multiple_of(t * tile, tile), tile)
        gate = up = None
        for b in range(blocks):
            x = x_ref[:, b * depth : (b + 1) * depth]
            g, u = dot(x, gates[b][:, cols]), dot(x, ups[b][:, cols])
            gate, up = (g, u) if gate is None else (gate + g, up + u)
        act_ref[:, cols] = (gate / (1.0 + jnp.exp(-gate)) * up).astype(BF16)


def rise(normed, gates, ups):
    parts, blocks = len(normed), len(gates)
    tokens, width = normed[0][0].shape
    hidden = gates[0].shape[1]

    def kernel(*refs):
        rise_body(parts, blocks, refs)

    vmem = pl.BlockSpec(memory_space=pltpu.VMEM)
    return pl.pallas_call(
        kernel,
        out_shape=jax.ShapeDtypeStruct((parts * tokens, hidden), BF16),
        in_specs=[vmem] * (parts * HALVES + 2 * blocks),
        out_specs=vmem,
        scratch_shapes=[pltpu.VMEM((parts * tokens, HALVES * width), BF16)],
        compiler_params=pltpu.CompilerParams(vmem_limit_bytes=12 * 2**20),
        cost_estimate=cost(1.5 * parts),
        name="rise",
    )(*[half for chunk in normed for half in chunk], *gates, *ups)


def fall_body(parts, blocks, refs):
    act_ref, downs, outs = refs[0], refs[1 : 1 + blocks], refs[1 + blocks :]
    tokens, width = outs[0].shape[0], downs[0].shape[1]
    tile = math.gcd(width, 256)
    for b in range(blocks):

        @pl.loop(0, width // tile)
        def _(t):
            term = dot(act_ref[...], downs[b][:, pl.ds(pl.multiple_of(t * tile, tile), tile)])
            cols = pl.ds(pl.multiple_of(b * width + t * tile, tile), tile)
            for i in range(parts):
                outs[i][:, cols] = term[i * tokens : (i + 1) * tokens].astype(BF16)


def fall(act, parts, downs):
    blocks = len(downs)
    shape = jax.ShapeDtypeStruct((act.shape[0] // parts, blocks * downs[0].shape[1]), BF16)

    def kernel(*refs):
        fall_body(parts, blocks, refs)

    vmem = pl.BlockSpec(memory_space=pltpu.VMEM)
    return pl.pallas_call(
        kernel,
        out_shape=[shape] * parts,
        in_specs=[vmem] * (1 + blocks),
        out_specs=[vmem] * parts,
        compiler_params=pltpu.CompilerParams(vmem_limit_bytes=12 * 2**20),
        cost_estimate=cost(0.6 * parts),
        name="fall",
    )(act, *downs)


def finish_body(blocks, hidden_ref, *refs):
    terms, out_ref = refs[:-1], refs[-1]
    each = len(terms) // HALVES
    width = out_ref.shape[1] // blocks
    for b in range(blocks):
        half, column = divmod(b, blocks // HALVES)
        place = pl.ds(pl.multiple_of(block_owner(blocks, b) * width, width), width)
        total = hidden_ref[:, place]
        for term in terms[half * each : (half + 1) * each]:
            total = total + term[:, column * width : (column + 1) * width].astype(F32)
        out_ref[:, place] = total.astype(BF16)


def finish(blocks, hidden_state, terms):
    vmem = pl.BlockSpec(memory_space=pltpu.VMEM)
    operands = [hidden_state] + [term for half in terms for term in half]
    return pl.pallas_call(
        functools.partial(finish_body, blocks),
        out_shape=jax.ShapeDtypeStruct(hidden_state.shape, BF16),
        in_specs=[vmem] * len(operands),
        out_specs=vmem,
        compiler_params=pltpu.CompilerParams(vmem_limit_bytes=8 * 2**20),
        cost_estimate=cost(1),
        name="finish",
    )(*operands)


def tie(array, *others):
    return lax.optimization_barrier((array, *others))[0] if others else array


def shards(
    grps,
    devs,
    residual,
    queries,
    keys,
    values,
    prefix_keys,
    cached_prefix_values,
    out_weight,
    norm_gain,
    w_gate,
    w_up,
    w_down,
    suffix_lengths,
    request_group,
    placement_order,
):
    depth_z = math.gcd(devs, 4)
    depth_y = devs // depth_z
    cores = CORES
    depth_x = grps // cores
    ring = list(range(0, depth_z, 2)) + list(range(1, depth_z, 2))[::-1]

    def shift(by_z, by_y):
        return [
            (
                ring[i] * depth_y + y,
                ring[(i + by_z) % depth_z] * depth_y + (y + by_y) % depth_y,
            )
            for i in range(depth_z)
            for y in range(depth_y)
        ]

    x_shift = [
        (x * cores + c, (x + 1) % depth_x * cores + c) for x in range(depth_x) for c in range(cores)
    ]
    core_swap = [(x * cores + c, x * cores + 1 - c) for x in range(depth_x) for c in range(cores)]

    def round_z(block, *others):
        return lax.ppermute(tie(block, *others), "dev", shift(1, 0))

    def along_y(block, *others):
        return [lax.ppermute(tie(block, *others), "dev", shift(0, ys)) for ys in range(1, depth_y)]

    def along_x(weight, *others):
        blocks = [weight]
        for _ in range(1, depth_x):
            blocks.append(lax.ppermute(tie(blocks[-1], *others), "grp", x_shift))
        return blocks

    def other_core(block, *others):
        return lax.ppermute(tie(block, *others), "grp", core_swap)

    tokens = queries.shape[0]
    width = keys.shape[1]
    groups, span = prefix_keys.shape[:2]

    prefix = jnp.stack([prefix_keys.reshape(-1, width), cached_prefix_values.reshape(-1, width)])
    other = along_y(prefix)
    arriving = round_z(prefix)
    own = jnp.stack([keys, values])
    before = lax.ppermute(own, "dev", [(i, i + 1) for i in range(devs - 1)])
    gate_rows = along_x(w_gate)
    q, before_mask, within_mask, prefix_mask = prepare(
        groups,
        span,
        suffix_lengths,
        request_group,
        placement_order,
        queries,
        width,
    )
    blocks = [(before, before_mask), (own, within_mask), (prefix, prefix_mask)]
    ready, state = [], None
    for zs in range(1, depth_z):
        if zs == depth_z - 1:
            ready += [gate_swap, *gate_rows[1:]]
        here = tie(arriving, *other, *ready)
        if zs < depth_z - 1:
            arriving = round_z(here)
        blocks += [(b, prefix_mask) for b in other + [here]]
        other = along_y(here)
        state = attend(q, state, blocks)
        blocks, ready = [], [state[0]]
        if zs == 1:
            gate_swap = other_core(w_gate, here)
        elif zs == 2:
            up_swap = other_core(w_up, here)
    down_swap = other_core(w_down, here)
    up_rows = along_x(w_up, *gate_rows[1:], here)
    gates = [w_gate, gate_swap]
    for gate in gate_rows[1:]:
        gates += [gate, other_core(gate, here)]
    hidden_state, *normed = attend_project(
        q,
        state,
        [(b, prefix_mask) for b in other],
        grps,
        out_weight,
        tie(residual, up_swap, down_swap, *gates[2:]),
        norm_gain[None],
    )

    arrived, across = [normed], [[along_y(half) for half in normed]]
    ups, downs, acts = [w_up, up_swap], [w_down, down_swap], {}
    for zs in range(1, depth_z):
        before = [b for c in across[zs - 2] for b in c] if zs > 1 else []
        waits = [before for _ in normed]
        if zs == depth_z - 1:
            down_cols = along_x(w_down, *ups[3:], *arrived[2], *[b for c in across[1] for b in c])
        if zs == depth_z - 1:
            acts[1] = rise([arrived[1]] + [list(c) for c in zip(*across[1])], gates, ups)
            acts[0] = rise([arrived[0]] + [list(c) for c in zip(*across[0])], gates, ups)
        arrived.append([round_z(half, *wait) for half, wait in zip(arrived[-1], waits)])
        if zs == 1:
            for up in up_rows[1:]:
                ups += [up, other_core(up, *arrived[1], *[b for c in across[0] for b in c])]
        late = arrived[zs][1:] + [b for c in across[-1] for b in c]
        if zs == depth_z - 1:
            late += [acts[1]]
        across.append([along_y(half, *late) for half in arrived[zs]])
    chunks = [[a] + [list(c) for c in zip(*b)] for a, b in zip(arrived, across)]
    each = grps // HALVES
    fallen = {}
    acts[2] = rise(chunks[2], gates, ups)
    soon = [b for c in across[-1] for b in c] + [acts[2]]
    if each <= len(downs):
        fallen[1, 0] = fall(acts[1], depth_y, downs[:each])
        soon.append(fallen[1, 0][0])
    for down in down_cols[1:]:
        downs += [down, other_core(down, *soon)]

    running, terms = [None] * HALVES, [None] * HALVES
    for zs in list(range(1, depth_z)) + [0]:
        act = acts[zs] if zs in acts else rise(chunks[zs], gates, ups)
        for half in range(HALVES):
            if (zs, half) in fallen:
                parts = fallen[zs, half]
            else:
                parts = fall(act, depth_y, downs[half * each : (half + 1) * each])
            if zs == 0:
                parts = [parts[0]] + [tie(part, running[half]) for part in parts[1:]]
            terms[half] = [parts[0]] + [
                lax.ppermute(parts[ys], "dev", shift(0, -ys)) for ys in range(1, depth_y)
            ]
            if running[half] is not None:
                terms[half].append(round_z(running[half]))
            if zs:
                running[half] = functools.reduce(
                    jnp.add, [term.astype(F32) for term in terms[half]]
                ).astype(BF16)
    return finish(grps, hidden_state, terms)


def solution(mesh):
    placed = (
        P(("grp", "dev"), None),
        P(("grp", "dev"), None),
        P(("grp", "dev"), None),
        P(("grp", "dev"), None),
        P("grp", "dev", None),
        P("grp", "dev", None),
        P(),
        P(),
        P("grp", "dev"),
        P("grp", "dev"),
        P("dev", "grp"),
        P("grp", None),
        P("grp", None),
        P("grp", None),
    )
    return jax.shard_map(
        functools.partial(shards, mesh.shape["grp"], mesh.shape["dev"]),
        mesh=mesh,
        in_specs=placed,
        out_specs=P(("grp", "dev"), None),
        check_vma=False,
    )
```

```python
import functools
import math

import jax
import jax.numpy as jnp
from jax import lax
from jax.experimental import pallas as pl
from jax.experimental.pallas import tpu as pltpu
from jax.sharding import PartitionSpec as P

HEAD_SIZE = 64
NEG_FILL = -1e30
EPSILON = 1e-05
F32 = jnp.float32
BF16 = jnp.bfloat16
LANES = 2 * HEAD_SIZE
CORES = 2
HALVES = 2


def cost(microseconds):
    return pl.CostEstimate(flops=0, bytes_accessed=int(microseconds * 3.5e6), transcendentals=0)


def dot(a, b, contract_b=0):
    return lax.dot_general(
        a, b, (((1,), (contract_b,)), ((), ())), preferred_element_type=F32
    )


def prepare_body(
    span,
    lengths_hbm,
    groups_hbm,
    packing_hbm,
    queries_hbm,
    *refs,
):
    q_ref, before_ref, within_ref, prefix_ref = refs[:4]
    lengths_ref, groups_ref, packing_ref, queries_ref, sems = refs[4:]
    copies = [
        pltpu.make_async_copy(source, target, sems.at[i])
        for i, (source, target) in enumerate(
            [
                (lengths_hbm, lengths_ref),
                (groups_hbm, groups_ref),
                (packing_hbm, packing_ref),
                (queries_hbm, queries_ref),
            ]
        )
    ]
    for copy in copies:
        copy.start()
    for copy in copies:
        copy.wait()
    tokens = queries_ref.shape[0]
    pairs, rows = q_ref.shape[0], q_ref.shape[1]
    per = rows // (2 * tokens)
    base = lax.axis_index("dev") * tokens
    own = base + lax.broadcasted_iota(jnp.int32, (tokens, LANES), 0)

    def request(k, carry):
        start, group, first = carry
        j = packing_ref[0, k]
        end = start + lengths_ref[0, j]
        inside = (own >= start) & (own < end)
        return (
            end,
            jnp.where(inside, groups_ref[0, j], group),
            jnp.where(inside, start, first),
        )

    zero = jnp.zeros((tokens, LANES), jnp.int32)
    _, group, first = lax.fori_loop(0, lengths_ref.shape[1], request, (jnp.int32(0), zero, zero))
    for ref, back in ((before_ref, tokens), (within_ref, 0)):
        for c in range(0, tokens, LANES):
            key = base - back + c + lax.broadcasted_iota(jnp.int32, (tokens, LANES), 1)
            ref[:, c : c + LANES] = jnp.where((key >= first) & (key <= own), 0.0, NEG_FILL)
    for c in range(0, prefix_ref.shape[1], LANES):
        key_group = lax.div(c + lax.broadcasted_iota(jnp.int32, (tokens, LANES), 1), span)
        prefix_ref[:, c : c + LANES] = jnp.where(group == key_group, 0.0, NEG_FILL)
    low = lax.broadcasted_iota(jnp.int32, (tokens, LANES), 1) < HEAD_SIZE
    for j in range(pairs):
        for parity in range(2):
            for r in range(per):
                head = (2 * j + parity) * per + r
                block = head // 2
                q = queries_ref[:, block * LANES : (block + 1) * LANES].astype(F32) * HEAD_SIZE ** (-0.5)
                if head % 2 != parity:
                    q = pltpu.roll(q, HEAD_SIZE, 1)
                q = jnp.where(low == (parity == 0), q, 0.0)
                row = (parity * per + r) * tokens
                q_ref[j, row : row + tokens, :] = q.astype(BF16)


def prepare(groups, span, lengths, request_group, packing, queries, width):
    tokens = queries.shape[0]
    per = queries.shape[1] // width
    vmem = pl.BlockSpec(memory_space=pltpu.VMEM)
    return pl.pallas_call(
        functools.partial(prepare_body, span),
        out_shape=[
            jax.ShapeDtypeStruct((width // LANES, 2 * per * tokens, LANES), BF16),
            jax.ShapeDtypeStruct((tokens, tokens), F32),
            jax.ShapeDtypeStruct((tokens, tokens), F32),
            jax.ShapeDtypeStruct((tokens, groups * span), F32),
        ],
        in_specs=[pl.BlockSpec(memory_space=pltpu.HBM)] * 4,
        out_specs=[vmem] * 4,
        compiler_params=pltpu.CompilerParams(vmem_limit_bytes=8 * 2**20),
        scratch_shapes=[pltpu.SMEM(lengths.shape, jnp.int32)] * 3
        + [pltpu.VMEM(queries.shape, BF16), pltpu.SemaphoreType.DMA((4,))],
        cost_estimate=cost(3),
        name="prepare",
    )(lengths, request_group, packing, queries)


def attend_body(first, pieces, refs):
    q_ref, refs = refs[0], refs[1:]
    if not first:
        old_max, old_sum, old_acc = refs[:3]
        refs = refs[3:]
    kv = refs[: 3 * pieces]
    new_max, new_sum, new_acc = refs[-3:]
    pairs, rows = q_ref.shape[0], q_ref.shape[1]
    half = rows // 2
    low = lax.broadcasted_iota(jnp.int32, (half, LANES), 1) < HEAD_SIZE

    def pick(even, odd):
        return jnp.where(low, even, odd)

    for j in range(pairs):
        q = q_ref[j]
        lanes = slice(j * LANES, (j + 1) * LANES)
        scores = []
        for i in range(pieces):
            k_ref, bias_ref = kv[3 * i], kv[3 * i + 2]
            s = dot(q, k_ref[:, lanes], 1)
            keys = s.shape[1]
            bias = bias_ref[...]
            s = s.reshape(rows // bias.shape[0], bias.shape[0], keys) + bias[None]
            scores.append(s.reshape(rows, keys))
        top = functools.reduce(
            jnp.maximum, [jnp.max(s, axis=1, keepdims=True) for s in scores]
        )
        if first:
            row_max = top
            pair_max = pick(row_max[:half], row_max[half:])
        else:
            old = old_max[j]
            pair_max = jnp.maximum(old, pick(top[:half], top[half:]))
            row_max = jnp.concatenate(
                [pair_max[:, :1], pair_max[:, HEAD_SIZE : HEAD_SIZE + 1]], axis=0
            )
        total = None
        for i in range(pieces):
            v_ref = kv[3 * i + 1]
            w = jnp.exp(scores[i] - row_max).astype(BF16)
            v = v_ref[:, lanes]
            v = jnp.concatenate([v, jnp.ones_like(v)], axis=1)
            part = dot(w, v)
            total = part if total is None else total + part
        acc = pick(total[:half, :LANES], total[half:, :LANES])
        summed = pick(total[:half, LANES:], total[half:, LANES:])
        if not first:
            scale = jnp.exp(old - pair_max)
            acc = acc + scale * old_acc[j]
            summed = summed + scale * old_sum[j]
        new_max[j] = pair_max
        new_sum[j] = summed
        new_acc[j] = acc


def block_refs(refs, count):
    return [r for i in range(count) for r in (refs[2 * i].at[0], refs[2 * i].at[1], refs[2 * i + 1])]


def attend(q, state, blocks):
    pairs, rows, lanes = q.shape
    first = state is None

    def kernel(*refs):
        lead = 1 + (0 if first else 3)
        attend_body(first, len(blocks), [*refs[:lead], *block_refs(refs[lead:], len(blocks)), *refs[-3:]])

    shape = jax.ShapeDtypeStruct((pairs, rows // 2, lanes), F32)
    operands = [q] + ([] if first else list(state)) + [a for block in blocks for a in block]
    vmem = pl.BlockSpec(memory_space=pltpu.VMEM)
    return pl.pallas_call(
        kernel,
        out_shape=[shape] * 3,
        in_specs=[vmem] * len(operands),
        out_specs=[vmem] * 3,
        compiler_params=pltpu.CompilerParams(vmem_limit_bytes=20 * 2**20),
        cost_estimate=cost(1.1 * len(blocks)),
        name="attend",
    )(*operands)


def block_owner(blocks, step):
    chips = blocks // CORES
    me = lax.axis_index("grp")
    x, core = lax.div(me, CORES), lax.rem(me, CORES)
    x = lax.rem(x + chips - step // CORES, chips)
    return x * CORES + lax.rem(core + step % CORES, CORES)


def project_body(
    blocks, sum_ref, acc_ref, weight_ref, residual_ref, gain_ref, hidden_ref, normed_refs, held
):
    pairs, rows, lanes = acc_ref.shape
    tokens = residual_ref.shape[0]
    per = rows // tokens
    hidden = residual_ref[...].astype(F32)
    for j in range(pairs):
        out = (acc_ref[j] / sum_ref[j]).astype(BF16)
        for r in range(0, per, 2):
            left = jnp.concatenate(
                [out[r * tokens : (r + 1) * tokens], out[(r + 1) * tokens : (r + 2) * tokens]], axis=1
            )
            heads = [(2 * j) * per + r, (2 * j + 1) * per + r, (2 * j) * per + r + 1, (2 * j + 1) * per + r + 1]
            right = jnp.concatenate(
                [weight_ref[h * HEAD_SIZE : (h + 1) * HEAD_SIZE, :] for h in heads], axis=0
            )
            hidden = hidden + dot(left, right)
    hidden_ref[...] = hidden
    mean = jnp.mean(hidden * hidden, axis=1, keepdims=True)
    held[...] = hidden * lax.rsqrt(mean + EPSILON) * gain_ref[...]
    width = hidden.shape[1] // blocks
    for b in range(blocks):
        start = pl.multiple_of(block_owner(blocks, b) * width, width)
        half, place = divmod(b, blocks // HALVES)
        normed_refs[half][:, place * width : (place + 1) * width] = held[:, pl.ds(start, width)].astype(BF16)


def attend_project(q, state, blocks, columns, out_weight, residual, gain):
    pairs, rows, lanes = q.shape
    tokens, width = residual.shape
    count = len(blocks)

    def kernel(*refs):
        mine, (weight_ref, residual_ref, gain_ref) = refs[: 4 + 2 * count], refs[4 + 2 * count : 7 + 2 * count]
        hidden_ref, *normed_refs = refs[7 + 2 * count : 8 + 2 * count + HALVES]
        held, top, total, acc = refs[-4:]
        attend_body(False, count, [*mine[:4], *block_refs(mine[4:], count), top, total, acc])
        project_body(
            columns, total, acc, weight_ref, residual_ref, gain_ref, hidden_ref, normed_refs, held
        )

    operands = [q, *state] + [a for block in blocks for a in block]
    vmem = pl.BlockSpec(memory_space=pltpu.VMEM)
    return pl.pallas_call(
        kernel,
        out_shape=[
            jax.ShapeDtypeStruct((tokens, width), F32),
        ]
        + [jax.ShapeDtypeStruct((tokens, width // HALVES), BF16)] * HALVES,
        in_specs=[vmem] * (len(operands) + 3),
        out_specs=[vmem] * (1 + HALVES),
        scratch_shapes=[pltpu.VMEM((tokens, width), F32)]
        + [pltpu.VMEM((pairs, rows // 2, lanes), F32)] * 3,
        compiler_params=pltpu.CompilerParams(vmem_limit_bytes=20 * 2**20),
        cost_estimate=cost(1.1 * count + 2),
        name="attend_project",
    )(*operands, out_weight, residual, gain)


def rise_body(parts, blocks, refs):
    pieces = parts * HALVES
    n_refs, gates, ups = refs[:pieces], refs[pieces : pieces + blocks], refs[pieces + blocks : pieces + 2 * blocks]
    act_ref, x_ref = refs[-2:]
    tokens, width = n_refs[0].shape
    for i in range(parts):
        for half in range(HALVES):
            x_ref[i * tokens : (i + 1) * tokens, half * width : (half + 1) * width] = n_refs[i * HALVES + half][...]
    depth, hidden = gates[0].shape
    tile = math.gcd(hidden, 256)

    @pl.loop(0, hidden // tile)
    def _(t):
        cols = pl.ds(pl.multiple_of(t * tile, tile), tile)
        gate = up = None
        for b in range(blocks):
            x = x_ref[:, b * depth : (b + 1) * depth]
            g, u = dot(x, gates[b][:, cols]), dot(x, ups[b][:, cols])
            gate, up = (g, u) if gate is None else (gate + g, up + u)
        act_ref[:, cols] = (gate / (1.0 + jnp.exp(-gate)) * up).astype(BF16)


def rise(normed, gates, ups):
    parts, blocks = len(normed), len(gates)
    tokens, width = normed[0][0].shape
    hidden = gates[0].shape[1]

    def kernel(*refs):
        rise_body(parts, blocks, refs)

    vmem = pl.BlockSpec(memory_space=pltpu.VMEM)
    return pl.pallas_call(
        kernel,
        out_shape=jax.ShapeDtypeStruct((parts * tokens, hidden), BF16),
        in_specs=[vmem] * (parts * HALVES + 2 * blocks),
        out_specs=vmem,
        scratch_shapes=[pltpu.VMEM((parts * tokens, HALVES * width), BF16)],
        compiler_params=pltpu.CompilerParams(vmem_limit_bytes=12 * 2**20),
        cost_estimate=cost(1.5 * parts),
        name="rise",
    )(*[half for chunk in normed for half in chunk], *gates, *ups)


def fall_body(parts, blocks, refs):
    act_ref, downs, outs = refs[0], refs[1 : 1 + blocks], refs[1 + blocks :]
    tokens, width = outs[0].shape[0], downs[0].shape[1]
    tile = math.gcd(width, 256)
    for b in range(blocks):

        @pl.loop(0, width // tile)
        def _(t):
            term = dot(act_ref[...], downs[b][:, pl.ds(pl.multiple_of(t * tile, tile), tile)])
            cols = pl.ds(pl.multiple_of(b * width + t * tile, tile), tile)
            for i in range(parts):
                outs[i][:, cols] = term[i * tokens : (i + 1) * tokens].astype(BF16)


def fall(act, parts, downs):
    blocks = len(downs)
    shape = jax.ShapeDtypeStruct((act.shape[0] // parts, blocks * downs[0].shape[1]), BF16)

    def kernel(*refs):
        fall_body(parts, blocks, refs)

    vmem = pl.BlockSpec(memory_space=pltpu.VMEM)
    return pl.pallas_call(
        kernel,
        out_shape=[shape] * parts,
        in_specs=[vmem] * (1 + blocks),
        out_specs=[vmem] * parts,
        compiler_params=pltpu.CompilerParams(vmem_limit_bytes=12 * 2**20),
        cost_estimate=cost(0.6 * parts),
        name="fall",
    )(act, *downs)


def finish_body(blocks, hidden_ref, *refs):
    terms, out_ref = refs[:-1], refs[-1]
    each = len(terms) // HALVES
    width = out_ref.shape[1] // blocks
    for b in range(blocks):
        half, column = divmod(b, blocks // HALVES)
        place = pl.ds(pl.multiple_of(block_owner(blocks, b) * width, width), width)
        total = hidden_ref[:, place]
        for term in terms[half * each : (half + 1) * each]:
            total = total + term[:, column * width : (column + 1) * width].astype(F32)
        out_ref[:, place] = total.astype(BF16)


def finish(blocks, hidden_state, terms):
    vmem = pl.BlockSpec(memory_space=pltpu.VMEM)
    operands = [hidden_state] + [term for half in terms for term in half]
    return pl.pallas_call(
        functools.partial(finish_body, blocks),
        out_shape=jax.ShapeDtypeStruct(hidden_state.shape, BF16),
        in_specs=[vmem] * len(operands),
        out_specs=vmem,
        compiler_params=pltpu.CompilerParams(vmem_limit_bytes=8 * 2**20),
        cost_estimate=cost(1),
        name="finish",
    )(*operands)


def tie(array, *others):
    return lax.optimization_barrier((array, *others))[0] if others else array


def shards(
    grps,
    devs,
    residual,
    queries,
    keys,
    values,
    prefix_keys,
    cached_prefix_values,
    out_weight,
    norm_gain,
    w_gate,
    w_up,
    w_down,
    suffix_lengths,
    request_group,
    placement_order,
):
    depth_z = math.gcd(devs, 4)
    depth_y = devs // depth_z
    cores = CORES
    depth_x = grps // cores
    ring = list(range(0, depth_z, 2)) + list(range(1, depth_z, 2))[::-1]

    def shift(by_z, by_y):
        return [
            (
                ring[i] * depth_y + y,
                ring[(i + by_z) % depth_z] * depth_y + (y + by_y) % depth_y,
            )
            for i in range(depth_z)
            for y in range(depth_y)
        ]

    x_shift = [
        (x * cores + c, (x + 1) % depth_x * cores + c) for x in range(depth_x) for c in range(cores)
    ]
    core_swap = [(x * cores + c, x * cores + 1 - c) for x in range(depth_x) for c in range(cores)]

    def round_z(block, *others):
        return lax.ppermute(tie(block, *others), "dev", shift(1, 0))

    def along_y(block, *others):
        return [lax.ppermute(tie(block, *others), "dev", shift(0, ys)) for ys in range(1, depth_y)]

    def along_x(weight, *others):
        blocks = [weight]
        for _ in range(1, depth_x):
            blocks.append(lax.ppermute(tie(blocks[-1], *others), "grp", x_shift))
        return blocks

    def other_core(block, *others):
        return lax.ppermute(tie(block, *others), "grp", core_swap)

    tokens = queries.shape[0]
    width = keys.shape[1]
    groups, span = prefix_keys.shape[:2]

    prefix = jnp.stack([prefix_keys.reshape(-1, width), cached_prefix_values.reshape(-1, width)])
    other = along_y(prefix)
    arriving = round_z(prefix)
    own = jnp.stack([keys, values])
    before = lax.ppermute(own, "dev", [(i, i + 1) for i in range(devs - 1)])
    gate_rows = along_x(w_gate)
    q, before_mask, within_mask, prefix_mask = prepare(
        groups,
        span,
        suffix_lengths,
        request_group,
        placement_order,
        tie(queries, *other),
        width,
    )
    blocks = [(before, before_mask), (own, within_mask), (prefix, prefix_mask)]
    blocks += [(b, prefix_mask) for b in other]
    here, late = arriving, []
    for zs in range(1, depth_z):
        across = along_y(here)
        if zs < depth_z - 1:
            late += [here, *across]
            if zs == 1:
                blocks += [(b, prefix_mask) for b in late]
                gate_swap, late = other_core(w_gate, here), []
            elif zs == 2:
                up_swap = other_core(w_up, here)
            here = round_z(tie(here, q) if zs == 2 else here)
            if zs == depth_z - 2:
                state = attend(q, None, blocks)
                here = tie(here, state[0])
    state = attend(
        tie(q, gate_swap, *gate_rows[1:]), state, [(b, prefix_mask) for b in late + [here]]
    )
    down_swap = other_core(w_down, state[0])
    up_rows = along_x(w_up, *gate_rows[1:], state[0])
    gates = [w_gate, gate_swap]
    for gate in gate_rows[1:]:
        gates += [gate, other_core(gate, state[0])]
    hidden_state, *normed = attend_project(
        q,
        state,
        [(b, prefix_mask) for b in across],
        grps,
        out_weight,
        tie(residual, up_swap, down_swap, *gates[2:]),
        norm_gain[None],
    )

    arrived, across = [normed], [[along_y(half) for half in normed]]
    ups, downs, acts = [w_up, up_swap], [w_down, down_swap], {}
    for zs in range(1, depth_z):
        waits = across[zs - 2] if zs > 1 else [[] for _ in normed]
        arrived.append([round_z(half, *wait) for half, wait in zip(arrived[-1], waits)])
        if zs == 1:
            for up in up_rows[1:]:
                ups += [up, other_core(up, *arrived[1], *[b for c in across[0] for b in c])]
        elif zs == depth_z - 1:
            down_cols = along_x(w_down, *ups[3:], *arrived[2], *[b for c in across[1] for b in c])
            acts[1] = rise([arrived[1]] + [list(c) for c in zip(*across[1])], gates, ups)
        late = arrived[zs - 1][1:] if zs > 1 else []
        across.append([along_y(half, *late) for half in arrived[zs]])
    chunks = [[a] + [list(c) for c in zip(*b)] for a, b in zip(arrived, across)]
    each = grps // HALVES
    fallen = {}
    acts[2] = rise(chunks[2], gates, ups)
    soon = [b for c in across[-1] for b in c] + [acts[2]]
    if each <= len(downs):
        fallen[1, 0] = fall(acts[1], depth_y, downs[:each])
        soon.append(fallen[1, 0][0])
    for down in down_cols[1:]:
        downs += [down, other_core(down, *soon)]

    running, terms = [None] * HALVES, [None] * HALVES
    for zs in list(range(1, depth_z)) + [0]:
        act = acts[zs] if zs in acts else rise(chunks[zs], gates, ups)
        for half in range(HALVES):
            if (zs, half) in fallen:
                parts = fallen[zs, half]
            else:
                parts = fall(act, depth_y, downs[half * each : (half + 1) * each])
            if zs == 0:
                parts = [parts[0]] + [tie(part, running[half]) for part in parts[1:]]
            terms[half] = [parts[0]] + [
                lax.ppermute(parts[ys], "dev", shift(0, -ys)) for ys in range(1, depth_y)
            ]
            if running[half] is not None:
                terms[half].append(round_z(running[half]))
            if zs:
                running[half] = functools.reduce(
                    jnp.add, [term.astype(F32) for term in terms[half]]
                ).astype(BF16)
    return finish(grps, hidden_state, terms)


def solution(mesh):
    placed = (
        P(("grp", "dev"), None),
        P(("grp", "dev"), None),
        P(("grp", "dev"), None),
        P(("grp", "dev"), None),
        P("grp", "dev", None),
        P("grp", "dev", None),
        P(),
        P(),
        P("grp", "dev"),
        P("grp", "dev"),
        P("dev", "grp"),
        P("grp", None),
        P("grp", None),
        P("grp", None),
    )
    return jax.shard_map(
        functools.partial(shards, mesh.shape["grp"], mesh.shape["dev"]),
        mesh=mesh,
        in_specs=placed,
        out_specs=P(("grp", "dev"), None),
        check_vma=False,
    )
```

```python
import functools
import math

import jax
import jax.numpy as jnp
from jax import lax
from jax.experimental import pallas as pl
from jax.experimental.pallas import tpu as pltpu
from jax.sharding import PartitionSpec as P

HEAD_SIZE = 64
NEG_FILL = -1e30
EPSILON = 1e-05
F32 = jnp.float32
BF16 = jnp.bfloat16
LANES = 2 * HEAD_SIZE
CORES = 2
HALVES = 2


def cost(microseconds):
    return pl.CostEstimate(flops=0, bytes_accessed=int(microseconds * 3.5e6), transcendentals=0)


def dot(a, b, contract_b=0):
    return lax.dot_general(
        a, b, (((1,), (contract_b,)), ((), ())), preferred_element_type=F32
    )


def prepare_body(
    span,
    lengths_hbm,
    groups_hbm,
    packing_hbm,
    queries_hbm,
    *refs,
):
    q_ref, before_ref, within_ref, prefix_ref = refs[:4]
    lengths_ref, groups_ref, packing_ref, queries_ref, sems = refs[4:]
    copies = [
        pltpu.make_async_copy(source, target, sems.at[i])
        for i, (source, target) in enumerate(
            [
                (lengths_hbm, lengths_ref),
                (groups_hbm, groups_ref),
                (packing_hbm, packing_ref),
                (queries_hbm, queries_ref),
            ]
        )
    ]
    for copy in copies:
        copy.start()
    for copy in copies:
        copy.wait()
    tokens = queries_ref.shape[0]
    pairs, rows = q_ref.shape[0], q_ref.shape[1]
    per = rows // (2 * tokens)
    base = lax.axis_index("dev") * tokens
    own = base + lax.broadcasted_iota(jnp.int32, (tokens, LANES), 0)

    def request(k, carry):
        start, group, first = carry
        j = packing_ref[0, k]
        end = start + lengths_ref[0, j]
        inside = (own >= start) & (own < end)
        return (
            end,
            jnp.where(inside, groups_ref[0, j], group),
            jnp.where(inside, start, first),
        )

    zero = jnp.zeros((tokens, LANES), jnp.int32)
    _, group, first = lax.fori_loop(0, lengths_ref.shape[1], request, (jnp.int32(0), zero, zero))
    for ref, back in ((before_ref, tokens), (within_ref, 0)):
        for c in range(0, tokens, LANES):
            key = base - back + c + lax.broadcasted_iota(jnp.int32, (tokens, LANES), 1)
            ref[:, c : c + LANES] = jnp.where((key >= first) & (key <= own), 0.0, NEG_FILL)
    for c in range(0, prefix_ref.shape[1], LANES):
        key_group = lax.div(c + lax.broadcasted_iota(jnp.int32, (tokens, LANES), 1), span)
        prefix_ref[:, c : c + LANES] = jnp.where(group == key_group, 0.0, NEG_FILL)
    low = lax.broadcasted_iota(jnp.int32, (tokens, LANES), 1) < HEAD_SIZE
    for j in range(pairs):
        for parity in range(2):
            for r in range(per):
                head = (2 * j + parity) * per + r
                block = head // 2
                q = queries_ref[:, block * LANES : (block + 1) * LANES].astype(F32) * HEAD_SIZE ** (-0.5)
                if head % 2 != parity:
                    q = pltpu.roll(q, HEAD_SIZE, 1)
                q = jnp.where(low == (parity == 0), q, 0.0)
                row = (parity * per + r) * tokens
                q_ref[j, row : row + tokens, :] = q.astype(BF16)


def prepare(groups, span, lengths, request_group, packing, queries, width):
    tokens = queries.shape[0]
    per = queries.shape[1] // width
    vmem = pl.BlockSpec(memory_space=pltpu.VMEM)
    return pl.pallas_call(
        functools.partial(prepare_body, span),
        out_shape=[
            jax.ShapeDtypeStruct((width // LANES, 2 * per * tokens, LANES), BF16),
            jax.ShapeDtypeStruct((tokens, tokens), F32),
            jax.ShapeDtypeStruct((tokens, tokens), F32),
            jax.ShapeDtypeStruct((tokens, groups * span), F32),
        ],
        in_specs=[pl.BlockSpec(memory_space=pltpu.HBM)] * 4,
        out_specs=[vmem] * 4,
        compiler_params=pltpu.CompilerParams(vmem_limit_bytes=8 * 2**20),
        scratch_shapes=[pltpu.SMEM(lengths.shape, jnp.int32)] * 3
        + [pltpu.VMEM(queries.shape, BF16), pltpu.SemaphoreType.DMA((4,))],
        cost_estimate=cost(3),
        name="prepare",
    )(lengths, request_group, packing, queries)


def attend_body(first, pieces, refs):
    q_ref, refs = refs[0], refs[1:]
    if not first:
        old_max, old_sum, old_acc = refs[:3]
        refs = refs[3:]
    kv = refs[: 3 * pieces]
    new_max, new_sum, new_acc = refs[-3:]
    pairs, rows = q_ref.shape[0], q_ref.shape[1]
    half = rows // 2
    low = lax.broadcasted_iota(jnp.int32, (half, LANES), 1) < HEAD_SIZE

    def pick(even, odd):
        return jnp.where(low, even, odd)

    for j in range(pairs):
        q = q_ref[j]
        lanes = slice(j * LANES, (j + 1) * LANES)
        scores = []
        for i in range(pieces):
            k_ref, bias_ref = kv[3 * i], kv[3 * i + 2]
            s = dot(q, k_ref[:, lanes], 1)
            keys = s.shape[1]
            bias = bias_ref[...]
            s = s.reshape(rows // bias.shape[0], bias.shape[0], keys) + bias[None]
            scores.append(s.reshape(rows, keys))
        top = functools.reduce(
            jnp.maximum, [jnp.max(s, axis=1, keepdims=True) for s in scores]
        )
        if first:
            row_max = top
            pair_max = pick(row_max[:half], row_max[half:])
        else:
            old = old_max[j]
            pair_max = jnp.maximum(old, pick(top[:half], top[half:]))
            row_max = jnp.concatenate(
                [pair_max[:, :1], pair_max[:, HEAD_SIZE : HEAD_SIZE + 1]], axis=0
            )
        total = None
        for i in range(pieces):
            v_ref = kv[3 * i + 1]
            w = jnp.exp(scores[i] - row_max).astype(BF16)
            v = v_ref[:, lanes]
            v = jnp.concatenate([v, jnp.ones_like(v)], axis=1)
            part = dot(w, v)
            total = part if total is None else total + part
        acc = pick(total[:half, :LANES], total[half:, :LANES])
        summed = pick(total[:half, LANES:], total[half:, LANES:])
        if not first:
            scale = jnp.exp(old - pair_max)
            acc = acc + scale * old_acc[j]
            summed = summed + scale * old_sum[j]
        new_max[j] = pair_max
        new_sum[j] = summed
        new_acc[j] = acc


def block_refs(refs, count):
    return [r for i in range(count) for r in (refs[2 * i].at[0], refs[2 * i].at[1], refs[2 * i + 1])]


def attend(q, state, blocks):
    pairs, rows, lanes = q.shape
    first = state is None

    def kernel(*refs):
        lead = 1 + (0 if first else 3)
        attend_body(first, len(blocks), [*refs[:lead], *block_refs(refs[lead:], len(blocks)), *refs[-3:]])

    shape = jax.ShapeDtypeStruct((pairs, rows // 2, lanes), F32)
    operands = [q] + ([] if first else list(state)) + [a for block in blocks for a in block]
    vmem = pl.BlockSpec(memory_space=pltpu.VMEM)
    return pl.pallas_call(
        kernel,
        out_shape=[shape] * 3,
        in_specs=[vmem] * len(operands),
        out_specs=[vmem] * 3,
        compiler_params=pltpu.CompilerParams(vmem_limit_bytes=(8 + 3 * len(blocks)) * 2**20),
        cost_estimate=cost(1.1 * len(blocks)),
        name="attend",
    )(*operands)


def block_owner(blocks, step):
    chips = blocks // CORES
    me = lax.axis_index("grp")
    x, core = lax.div(me, CORES), lax.rem(me, CORES)
    x = lax.rem(x + chips - step // CORES, chips)
    return x * CORES + lax.rem(core + step % CORES, CORES)


def project_body(
    blocks, sum_ref, acc_ref, weight_ref, residual_ref, gain_ref, hidden_ref, normed_refs, held
):
    pairs, rows, lanes = acc_ref.shape
    tokens = residual_ref.shape[0]
    per = rows // tokens
    hidden = residual_ref[...].astype(F32)
    for j in range(pairs):
        out = (acc_ref[j] / sum_ref[j]).astype(BF16)
        for r in range(0, per, 2):
            left = jnp.concatenate(
                [out[r * tokens : (r + 1) * tokens], out[(r + 1) * tokens : (r + 2) * tokens]], axis=1
            )
            heads = [(2 * j) * per + r, (2 * j + 1) * per + r, (2 * j) * per + r + 1, (2 * j + 1) * per + r + 1]
            right = jnp.concatenate(
                [weight_ref[h * HEAD_SIZE : (h + 1) * HEAD_SIZE, :] for h in heads], axis=0
            )
            hidden = hidden + dot(left, right)
    hidden_ref[...] = hidden
    mean = jnp.mean(hidden * hidden, axis=1, keepdims=True)
    held[...] = hidden * lax.rsqrt(mean + EPSILON) * gain_ref[...]
    width = hidden.shape[1] // blocks
    for b in range(blocks):
        start = pl.multiple_of(block_owner(blocks, b) * width, width)
        half, place = divmod(b, blocks // HALVES)
        normed_refs[half][:, place * width : (place + 1) * width] = held[:, pl.ds(start, width)].astype(BF16)


def attend_project(q, state, blocks, columns, out_weight, residual, gain):
    pairs, rows, lanes = q.shape
    tokens, width = residual.shape
    count = len(blocks)

    def kernel(*refs):
        mine, (weight_ref, residual_ref, gain_ref) = refs[: 4 + 2 * count], refs[4 + 2 * count : 7 + 2 * count]
        hidden_ref, *normed_refs = refs[7 + 2 * count : 8 + 2 * count + HALVES]
        held, top, total, acc = refs[-4:]
        attend_body(False, count, [*mine[:4], *block_refs(mine[4:], count), top, total, acc])
        project_body(
            columns, total, acc, weight_ref, residual_ref, gain_ref, hidden_ref, normed_refs, held
        )

    operands = [q, *state] + [a for block in blocks for a in block]
    vmem = pl.BlockSpec(memory_space=pltpu.VMEM)
    return pl.pallas_call(
        kernel,
        out_shape=[
            jax.ShapeDtypeStruct((tokens, width), F32),
        ]
        + [jax.ShapeDtypeStruct((tokens, width // HALVES), BF16)] * HALVES,
        in_specs=[vmem] * (len(operands) + 3),
        out_specs=[vmem] * (1 + HALVES),
        scratch_shapes=[pltpu.VMEM((tokens, width), F32)]
        + [pltpu.VMEM((pairs, rows // 2, lanes), F32)] * 3,
        compiler_params=pltpu.CompilerParams(vmem_limit_bytes=20 * 2**20),
        cost_estimate=cost(1.1 * count + 2),
        name="attend_project",
    )(*operands, out_weight, residual, gain)


def rise_body(parts, blocks, refs):
    pieces = parts * HALVES
    n_refs, gates, ups = refs[:pieces], refs[pieces : pieces + blocks], refs[pieces + blocks : pieces + 2 * blocks]
    act_ref, x_ref = refs[-2:]
    tokens, width = n_refs[0].shape
    for i in range(parts):
        for half in range(HALVES):
            x_ref[i * tokens : (i + 1) * tokens, half * width : (half + 1) * width] = n_refs[i * HALVES + half][...]
    depth, hidden = gates[0].shape
    tile = math.gcd(hidden, 256)

    @pl.loop(0, hidden // tile)
    def _(t):
        cols = pl.ds(pl.multiple_of(t * tile, tile), tile)
        gate = up = None
        for b in range(blocks):
            x = x_ref[:, b * depth : (b + 1) * depth]
            g, u = dot(x, gates[b][:, cols]), dot(x, ups[b][:, cols])
            gate, up = (g, u) if gate is None else (gate + g, up + u)
        act_ref[:, cols] = (gate / (1.0 + jnp.exp(-gate)) * up).astype(BF16)


def rise(normed, gates, ups):
    parts, blocks = len(normed), len(gates)
    tokens, width = normed[0][0].shape
    hidden = gates[0].shape[1]

    def kernel(*refs):
        rise_body(parts, blocks, refs)

    vmem = pl.BlockSpec(memory_space=pltpu.VMEM)
    return pl.pallas_call(
        kernel,
        out_shape=jax.ShapeDtypeStruct((parts * tokens, hidden), BF16),
        in_specs=[vmem] * (parts * HALVES + 2 * blocks),
        out_specs=vmem,
        scratch_shapes=[pltpu.VMEM((parts * tokens, HALVES * width), BF16)],
        compiler_params=pltpu.CompilerParams(vmem_limit_bytes=12 * 2**20),
        cost_estimate=cost(1.5 * parts),
        name="rise",
    )(*[half for chunk in normed for half in chunk], *gates, *ups)


def fall_body(parts, blocks, refs):
    act_ref, downs, outs = refs[0], refs[1 : 1 + blocks], refs[1 + blocks :]
    tokens, width = outs[0].shape[0], downs[0].shape[1]
    tile = math.gcd(width, 256)
    for b in range(blocks):

        @pl.loop(0, width // tile)
        def _(t):
            term = dot(act_ref[...], downs[b][:, pl.ds(pl.multiple_of(t * tile, tile), tile)])
            cols = pl.ds(pl.multiple_of(b * width + t * tile, tile), tile)
            for i in range(parts):
                outs[i][:, cols] = term[i * tokens : (i + 1) * tokens].astype(BF16)


def fall(act, parts, downs):
    blocks = len(downs)
    shape = jax.ShapeDtypeStruct((act.shape[0] // parts, blocks * downs[0].shape[1]), BF16)

    def kernel(*refs):
        fall_body(parts, blocks, refs)

    vmem = pl.BlockSpec(memory_space=pltpu.VMEM)
    return pl.pallas_call(
        kernel,
        out_shape=[shape] * parts,
        in_specs=[vmem] * (1 + blocks),
        out_specs=[vmem] * parts,
        compiler_params=pltpu.CompilerParams(vmem_limit_bytes=12 * 2**20),
        cost_estimate=cost(0.6 * parts),
        name="fall",
    )(act, *downs)


def finish_body(blocks, hidden_ref, *refs):
    terms, out_ref = refs[:-1], refs[-1]
    each = len(terms) // HALVES
    width = out_ref.shape[1] // blocks
    for b in range(blocks):
        half, column = divmod(b, blocks // HALVES)
        place = pl.ds(pl.multiple_of(block_owner(blocks, b) * width, width), width)
        total = hidden_ref[:, place]
        for term in terms[half * each : (half + 1) * each]:
            total = total + term[:, column * width : (column + 1) * width].astype(F32)
        out_ref[:, place] = total.astype(BF16)


def finish(blocks, hidden_state, terms):
    vmem = pl.BlockSpec(memory_space=pltpu.VMEM)
    operands = [hidden_state] + [term for half in terms for term in half]
    return pl.pallas_call(
        functools.partial(finish_body, blocks),
        out_shape=jax.ShapeDtypeStruct(hidden_state.shape, BF16),
        in_specs=[vmem] * len(operands),
        out_specs=vmem,
        compiler_params=pltpu.CompilerParams(vmem_limit_bytes=8 * 2**20),
        cost_estimate=cost(1),
        name="finish",
    )(*operands)


def tie(array, *others):
    return lax.optimization_barrier((array, *others))[0] if others else array


def shards(
    grps,
    devs,
    residual,
    queries,
    keys,
    values,
    prefix_keys,
    cached_prefix_values,
    out_weight,
    norm_gain,
    w_gate,
    w_up,
    w_down,
    suffix_lengths,
    request_group,
    placement_order,
):
    depth_z = math.gcd(devs, 4)
    depth_y = devs // depth_z
    cores = CORES
    depth_x = grps // cores
    ring = list(range(0, depth_z, 2)) + list(range(1, depth_z, 2))[::-1]

    def shift(by_z, by_y):
        return [
            (
                ring[i] * depth_y + y,
                ring[(i + by_z) % depth_z] * depth_y + (y + by_y) % depth_y,
            )
            for i in range(depth_z)
            for y in range(depth_y)
        ]

    x_shift = [
        (x * cores + c, (x + 1) % depth_x * cores + c) for x in range(depth_x) for c in range(cores)
    ]
    core_swap = [(x * cores + c, x * cores + 1 - c) for x in range(depth_x) for c in range(cores)]

    def round_z(block, *others):
        return lax.ppermute(tie(block, *others), "dev", shift(1, 0))

    def along_y(block, *others):
        return [lax.ppermute(tie(block, *others), "dev", shift(0, ys)) for ys in range(1, depth_y)]

    def along_x(weight, *others):
        blocks = [weight]
        for _ in range(1, depth_x):
            blocks.append(lax.ppermute(tie(blocks[-1], *others), "grp", x_shift))
        return blocks

    def other_core(block, *others):
        return lax.ppermute(tie(block, *others), "grp", core_swap)

    tokens = queries.shape[0]
    width = keys.shape[1]
    groups, span = prefix_keys.shape[:2]

    prefix = jnp.stack([prefix_keys.reshape(-1, width), cached_prefix_values.reshape(-1, width)])
    other = along_y(prefix)
    arriving = round_z(prefix)
    own = jnp.stack([keys, values])
    before = lax.ppermute(own, "dev", [(i, i + 1) for i in range(devs - 1)])
    gate_rows = along_x(w_gate)
    q, before_mask, within_mask, prefix_mask = prepare(
        groups,
        span,
        suffix_lengths,
        request_group,
        placement_order,
        queries,
        width,
    )
    blocks = [(before, before_mask), (own, within_mask), (prefix, prefix_mask)]
    ready, state = [], None
    for zs in range(1, depth_z):
        if zs == depth_z - 1:
            state = attend(q, None, blocks)
            blocks, ready = [], [state[0], gate_swap, *gate_rows[1:]]
        here = tie(arriving, *other, *ready)
        if zs < depth_z - 1:
            arriving, ready = round_z(here), [q, before]
        blocks += [(b, prefix_mask) for b in other + [here]]
        other = along_y(here)
        if zs == 1:
            gate_swap = other_core(w_gate, here)
        elif zs == 2:
            up_swap = other_core(w_up, here)
    state = attend(q, state, blocks)
    down_swap = other_core(w_down, here)
    up_rows = along_x(w_up, *gate_rows[1:], here)
    gates = [w_gate, gate_swap]
    for gate in gate_rows[1:]:
        gates += [gate, other_core(gate, here)]
    hidden_state, *normed = attend_project(
        q,
        state,
        [(b, prefix_mask) for b in other],
        grps,
        out_weight,
        tie(residual, up_swap, down_swap, *gates[2:]),
        norm_gain[None],
    )

    arrived, across = [normed], [[along_y(half) for half in normed]]
    ups, downs, acts = [w_up, up_swap], [w_down, down_swap], {}
    for zs in range(1, depth_z):
        waits = across[zs - 2] if zs > 1 else [[] for _ in normed]
        arrived.append([round_z(half, *wait) for half, wait in zip(arrived[-1], waits)])
        across.append([along_y(half, *arrived[zs][1:]) for half in arrived[zs]])
        if zs == depth_z - 2:
            for up in up_rows[1:]:
                ups += [up, other_core(up, *arrived[zs], *across[zs - 1][0])]
            down_cols = along_x(w_down, *up_rows[1:], *arrived[zs], *[b for c in across[zs - 1] for b in c])
    acts[1] = rise([arrived[1]] + [list(c) for c in zip(*across[1])], gates, ups)
    chunks = [[a] + [list(c) for c in zip(*b)] for a, b in zip(arrived, across)]
    each = grps // HALVES
    fallen = {}
    acts[2] = rise(chunks[2], gates, ups)
    soon = [b for c in across[-1] for b in c] + [acts[2]]
    if each <= len(downs):
        fallen[1, 0] = fall(acts[1], depth_y, downs[:each])
        soon.append(fallen[1, 0][0])
    for down in down_cols[1:]:
        downs += [down, other_core(down, *soon)]

    running, terms = [None] * HALVES, [None] * HALVES
    for zs in list(range(1, depth_z)) + [0]:
        act = acts[zs] if zs in acts else rise(chunks[zs], gates, ups)
        for half in range(HALVES):
            if (zs, half) in fallen:
                parts = fallen[zs, half]
            else:
                parts = fall(act, depth_y, downs[half * each : (half + 1) * each])
            if zs == 0:
                parts = [parts[0]] + [tie(part, running[half]) for part in parts[1:]]
            terms[half] = [parts[0]] + [
                lax.ppermute(parts[ys], "dev", shift(0, -ys)) for ys in range(1, depth_y)
            ]
            if running[half] is not None:
                terms[half].append(round_z(running[half]))
            if zs:
                running[half] = functools.reduce(
                    jnp.add, [term.astype(F32) for term in terms[half]]
                ).astype(BF16)
    return finish(grps, hidden_state, terms)


def solution(mesh):
    placed = (
        P(("grp", "dev"), None),
        P(("grp", "dev"), None),
        P(("grp", "dev"), None),
        P(("grp", "dev"), None),
        P("grp", "dev", None),
        P("grp", "dev", None),
        P(),
        P(),
        P("grp", "dev"),
        P("grp", "dev"),
        P("dev", "grp"),
        P("grp", None),
        P("grp", None),
        P("grp", None),
    )
    return jax.shard_map(
        functools.partial(shards, mesh.shape["grp"], mesh.shape["dev"]),
        mesh=mesh,
        in_specs=placed,
        out_specs=P(("grp", "dev"), None),
        check_vma=False,
    )
```

```python
import functools
import math

import jax
import jax.numpy as jnp
from jax import lax
from jax.experimental import pallas as pl
from jax.experimental.pallas import tpu as pltpu
from jax.sharding import PartitionSpec as P

HEAD_SIZE = 64
NEG_FILL = -1e30
EPSILON = 1e-05
F32 = jnp.float32
BF16 = jnp.bfloat16
LANES = 2 * HEAD_SIZE
CORES = 2
HALVES = 2


def cost(microseconds):
    return pl.CostEstimate(flops=0, bytes_accessed=int(microseconds * 3.5e6), transcendentals=0)


def dot(a, b, contract_b=0):
    return lax.dot_general(
        a, b, (((1,), (contract_b,)), ((), ())), preferred_element_type=F32
    )


def prepare_body(
    span,
    lengths_hbm,
    groups_hbm,
    packing_hbm,
    queries_hbm,
    *refs,
):
    q_ref, before_ref, within_ref, prefix_ref = refs[:4]
    lengths_ref, groups_ref, packing_ref, queries_ref, sems = refs[4:]
    copies = [
        pltpu.make_async_copy(source, target, sems.at[i])
        for i, (source, target) in enumerate(
            [
                (lengths_hbm, lengths_ref),
                (groups_hbm, groups_ref),
                (packing_hbm, packing_ref),
                (queries_hbm, queries_ref),
            ]
        )
    ]
    for copy in copies:
        copy.start()
    for copy in copies:
        copy.wait()
    tokens = queries_ref.shape[0]
    pairs, rows = q_ref.shape[0], q_ref.shape[1]
    per = rows // (2 * tokens)
    base = lax.axis_index("dev") * tokens
    own = base + lax.broadcasted_iota(jnp.int32, (tokens, LANES), 0)

    def request(k, carry):
        start, group, first = carry
        j = packing_ref[0, k]
        end = start + lengths_ref[0, j]
        inside = (own >= start) & (own < end)
        return (
            end,
            jnp.where(inside, groups_ref[0, j], group),
            jnp.where(inside, start, first),
        )

    zero = jnp.zeros((tokens, LANES), jnp.int32)
    _, group, first = lax.fori_loop(0, lengths_ref.shape[1], request, (jnp.int32(0), zero, zero))
    for ref, back in ((before_ref, tokens), (within_ref, 0)):
        for c in range(0, tokens, LANES):
            key = base - back + c + lax.broadcasted_iota(jnp.int32, (tokens, LANES), 1)
            ref[:, c : c + LANES] = jnp.where((key >= first) & (key <= own), 0.0, NEG_FILL)
    for c in range(0, prefix_ref.shape[1], LANES):
        key_group = lax.div(c + lax.broadcasted_iota(jnp.int32, (tokens, LANES), 1), span)
        prefix_ref[:, c : c + LANES] = jnp.where(group == key_group, 0.0, NEG_FILL)
    low = lax.broadcasted_iota(jnp.int32, (tokens, LANES), 1) < HEAD_SIZE
    for j in range(pairs):
        for parity in range(2):
            for r in range(per):
                head = (2 * j + parity) * per + r
                block = head // 2
                q = queries_ref[:, block * LANES : (block + 1) * LANES].astype(F32) * HEAD_SIZE ** (-0.5)
                if head % 2 != parity:
                    q = pltpu.roll(q, HEAD_SIZE, 1)
                q = jnp.where(low == (parity == 0), q, 0.0)
                row = (parity * per + r) * tokens
                q_ref[j, row : row + tokens, :] = q.astype(BF16)


def prepare(groups, span, lengths, request_group, packing, queries, width):
    tokens = queries.shape[0]
    per = queries.shape[1] // width
    vmem = pl.BlockSpec(memory_space=pltpu.VMEM)
    return pl.pallas_call(
        functools.partial(prepare_body, span),
        out_shape=[
            jax.ShapeDtypeStruct((width // LANES, 2 * per * tokens, LANES), BF16),
            jax.ShapeDtypeStruct((tokens, tokens), F32),
            jax.ShapeDtypeStruct((tokens, tokens), F32),
            jax.ShapeDtypeStruct((tokens, groups * span), F32),
        ],
        in_specs=[pl.BlockSpec(memory_space=pltpu.HBM)] * 4,
        out_specs=[vmem] * 4,
        compiler_params=pltpu.CompilerParams(vmem_limit_bytes=8 * 2**20),
        scratch_shapes=[pltpu.SMEM(lengths.shape, jnp.int32)] * 3
        + [pltpu.VMEM(queries.shape, BF16), pltpu.SemaphoreType.DMA((4,))],
        cost_estimate=cost(3),
        name="prepare",
    )(lengths, request_group, packing, queries)


def attend_body(first, pieces, refs):
    q_ref, refs = refs[0], refs[1:]
    if not first:
        old_max, old_sum, old_acc = refs[:3]
        refs = refs[3:]
    kv = refs[: 3 * pieces]
    new_max, new_sum, new_acc = refs[-3:]
    pairs, rows = q_ref.shape[0], q_ref.shape[1]
    half = rows // 2
    low = lax.broadcasted_iota(jnp.int32, (half, LANES), 1) < HEAD_SIZE

    def pick(even, odd):
        return jnp.where(low, even, odd)

    for j in range(pairs):
        q = q_ref[j]
        lanes = slice(j * LANES, (j + 1) * LANES)
        scores = []
        for i in range(pieces):
            k_ref, bias_ref = kv[3 * i], kv[3 * i + 2]
            s = dot(q, k_ref[:, lanes], 1)
            keys = s.shape[1]
            bias = bias_ref[...]
            s = s.reshape(rows // bias.shape[0], bias.shape[0], keys) + bias[None]
            scores.append(s.reshape(rows, keys))
        top = functools.reduce(
            jnp.maximum, [jnp.max(s, axis=1, keepdims=True) for s in scores]
        )
        if first:
            row_max = top
            pair_max = pick(row_max[:half], row_max[half:])
        else:
            old = old_max[j]
            pair_max = jnp.maximum(old, pick(top[:half], top[half:]))
            row_max = jnp.concatenate(
                [pair_max[:, :1], pair_max[:, HEAD_SIZE : HEAD_SIZE + 1]], axis=0
            )
        total = None
        for i in range(pieces):
            v_ref = kv[3 * i + 1]
            w = jnp.exp(scores[i] - row_max).astype(BF16)
            v = v_ref[:, lanes]
            v = jnp.concatenate([v, jnp.ones_like(v)], axis=1)
            part = dot(w, v)
            total = part if total is None else total + part
        acc = pick(total[:half, :LANES], total[half:, :LANES])
        summed = pick(total[:half, LANES:], total[half:, LANES:])
        if not first:
            scale = jnp.exp(old - pair_max)
            acc = acc + scale * old_acc[j]
            summed = summed + scale * old_sum[j]
        new_max[j] = pair_max
        new_sum[j] = summed
        new_acc[j] = acc


def block_refs(refs, count):
    return [r for i in range(count) for r in (refs[2 * i].at[0], refs[2 * i].at[1], refs[2 * i + 1])]


def attend(q, state, blocks):
    pairs, rows, lanes = q.shape
    first = state is None

    def kernel(*refs):
        lead = 1 + (0 if first else 3)
        attend_body(first, len(blocks), [*refs[:lead], *block_refs(refs[lead:], len(blocks)), *refs[-3:]])

    shape = jax.ShapeDtypeStruct((pairs, rows // 2, lanes), F32)
    operands = [q] + ([] if first else list(state)) + [a for block in blocks for a in block]
    vmem = pl.BlockSpec(memory_space=pltpu.VMEM)
    return pl.pallas_call(
        kernel,
        out_shape=[shape] * 3,
        in_specs=[vmem] * len(operands),
        out_specs=[vmem] * 3,
        compiler_params=pltpu.CompilerParams(vmem_limit_bytes=(8 + 3 * len(blocks)) * 2**20),
        cost_estimate=cost(1.1 * len(blocks)),
        name="attend",
    )(*operands)


def block_owner(blocks, step):
    chips = blocks // CORES
    me = lax.axis_index("grp")
    x, core = lax.div(me, CORES), lax.rem(me, CORES)
    x = lax.rem(x + chips - step // CORES, chips)
    return x * CORES + lax.rem(core + step % CORES, CORES)


def project_body(
    blocks, sum_ref, acc_ref, weight_ref, residual_ref, gain_ref, hidden_ref, normed_refs, held
):
    pairs, rows, lanes = acc_ref.shape
    tokens = residual_ref.shape[0]
    per = rows // tokens
    hidden = residual_ref[...].astype(F32)
    for j in range(pairs):
        out = (acc_ref[j] / sum_ref[j]).astype(BF16)
        for r in range(0, per, 2):
            left = jnp.concatenate(
                [out[r * tokens : (r + 1) * tokens], out[(r + 1) * tokens : (r + 2) * tokens]], axis=1
            )
            heads = [(2 * j) * per + r, (2 * j + 1) * per + r, (2 * j) * per + r + 1, (2 * j + 1) * per + r + 1]
            right = jnp.concatenate(
                [weight_ref[h * HEAD_SIZE : (h + 1) * HEAD_SIZE, :] for h in heads], axis=0
            )
            hidden = hidden + dot(left, right)
    hidden_ref[...] = hidden
    mean = jnp.mean(hidden * hidden, axis=1, keepdims=True)
    held[...] = hidden * lax.rsqrt(mean + EPSILON) * gain_ref[...]
    width = hidden.shape[1] // blocks
    for b in range(blocks):
        start = pl.multiple_of(block_owner(blocks, b) * width, width)
        half, place = divmod(b, blocks // HALVES)
        normed_refs[half][:, place * width : (place + 1) * width] = held[:, pl.ds(start, width)].astype(BF16)


def attend_project(q, state, blocks, columns, out_weight, residual, gain):
    pairs, rows, lanes = q.shape
    tokens, width = residual.shape
    count = len(blocks)

    def kernel(*refs):
        mine, (weight_ref, residual_ref, gain_ref) = refs[: 4 + 2 * count], refs[4 + 2 * count : 7 + 2 * count]
        hidden_ref, *normed_refs = refs[7 + 2 * count : 8 + 2 * count + HALVES]
        held, top, total, acc = refs[-4:]
        attend_body(False, count, [*mine[:4], *block_refs(mine[4:], count), top, total, acc])
        project_body(
            columns, total, acc, weight_ref, residual_ref, gain_ref, hidden_ref, normed_refs, held
        )

    operands = [q, *state] + [a for block in blocks for a in block]
    vmem = pl.BlockSpec(memory_space=pltpu.VMEM)
    return pl.pallas_call(
        kernel,
        out_shape=[
            jax.ShapeDtypeStruct((tokens, width), F32),
        ]
        + [jax.ShapeDtypeStruct((tokens, width // HALVES), BF16)] * HALVES,
        in_specs=[vmem] * (len(operands) + 3),
        out_specs=[vmem] * (1 + HALVES),
        scratch_shapes=[pltpu.VMEM((tokens, width), F32)]
        + [pltpu.VMEM((pairs, rows // 2, lanes), F32)] * 3,
        compiler_params=pltpu.CompilerParams(vmem_limit_bytes=20 * 2**20),
        cost_estimate=cost(1.1 * count + 2),
        name="attend_project",
    )(*operands, out_weight, residual, gain)


def rise_body(parts, blocks, refs):
    pieces = parts * HALVES
    n_refs, gates, ups = refs[:pieces], refs[pieces : pieces + blocks], refs[pieces + blocks : pieces + 2 * blocks]
    act_ref, x_ref = refs[-2:]
    tokens, width = n_refs[0].shape
    for i in range(parts):
        for half in range(HALVES):
            x_ref[i * tokens : (i + 1) * tokens, half * width : (half + 1) * width] = n_refs[i * HALVES + half][...]
    depth, hidden = gates[0].shape
    tile = math.gcd(hidden, 256)

    @pl.loop(0, hidden // tile)
    def _(t):
        cols = pl.ds(pl.multiple_of(t * tile, tile), tile)
        gate = up = None
        for b in range(blocks):
            x = x_ref[:, b * depth : (b + 1) * depth]
            g, u = dot(x, gates[b][:, cols]), dot(x, ups[b][:, cols])
            gate, up = (g, u) if gate is None else (gate + g, up + u)
        act_ref[:, cols] = (gate / (1.0 + jnp.exp(-gate)) * up).astype(BF16)


def rise(normed, gates, ups):
    parts, blocks = len(normed), len(gates)
    tokens, width = normed[0][0].shape
    hidden = gates[0].shape[1]

    def kernel(*refs):
        rise_body(parts, blocks, refs)

    vmem = pl.BlockSpec(memory_space=pltpu.VMEM)
    return pl.pallas_call(
        kernel,
        out_shape=jax.ShapeDtypeStruct((parts * tokens, hidden), BF16),
        in_specs=[vmem] * (parts * HALVES + 2 * blocks),
        out_specs=vmem,
        scratch_shapes=[pltpu.VMEM((parts * tokens, HALVES * width), BF16)],
        compiler_params=pltpu.CompilerParams(vmem_limit_bytes=12 * 2**20),
        cost_estimate=cost(1.5 * parts),
        name="rise",
    )(*[half for chunk in normed for half in chunk], *gates, *ups)


def fall_body(blocks, refs):
    act_ref, downs, outs = refs[0], refs[1 : 1 + blocks], refs[1 + blocks :]
    rows, width = outs[0].shape[0], downs[0].shape[1]
    tile = math.gcd(width, 256)
    for b in range(blocks):

        @pl.loop(0, width // tile)
        def _(t):
            term = dot(act_ref[...], downs[b][:, pl.ds(pl.multiple_of(t * tile, tile), tile)])
            cols = pl.ds(pl.multiple_of(b * width + t * tile, tile), tile)
            for i, out in enumerate(outs):
                out[:, cols] = term[i * rows : (i + 1) * rows].astype(BF16)


def fall(act, parts, downs):
    blocks = len(downs)
    shape = jax.ShapeDtypeStruct((act.shape[0] // parts, blocks * downs[0].shape[1]), BF16)

    def kernel(*refs):
        fall_body(blocks, refs)

    vmem = pl.BlockSpec(memory_space=pltpu.VMEM)
    return pl.pallas_call(
        kernel,
        out_shape=[shape] * parts,
        in_specs=[vmem] * (1 + blocks),
        out_specs=[vmem] * parts,
        compiler_params=pltpu.CompilerParams(vmem_limit_bytes=12 * 2**20),
        cost_estimate=cost(1.2),
        name="fall",
    )(act, *downs)


def finish_body(blocks, hidden_ref, *refs):
    terms, out_ref = refs[:-1], refs[-1]
    each = len(terms) // HALVES
    width = out_ref.shape[1] // blocks
    for b in range(blocks):
        half, column = divmod(b, blocks // HALVES)
        place = pl.ds(pl.multiple_of(block_owner(blocks, b) * width, width), width)
        total = hidden_ref[:, place]
        for term in terms[half * each : (half + 1) * each]:
            total = total + term[:, column * width : (column + 1) * width].astype(F32)
        out_ref[:, place] = total.astype(BF16)


def finish(blocks, hidden_state, terms):
    vmem = pl.BlockSpec(memory_space=pltpu.VMEM)
    operands = [hidden_state] + [term for half in terms for term in half]
    return pl.pallas_call(
        functools.partial(finish_body, blocks),
        out_shape=jax.ShapeDtypeStruct(hidden_state.shape, BF16),
        in_specs=[vmem] * len(operands),
        out_specs=vmem,
        compiler_params=pltpu.CompilerParams(vmem_limit_bytes=8 * 2**20),
        cost_estimate=cost(1),
        name="finish",
    )(*operands)


def tie(array, *others):
    return lax.optimization_barrier((array, *others))[0] if others else array


def shards(
    grps,
    devs,
    residual,
    queries,
    keys,
    values,
    prefix_keys,
    cached_prefix_values,
    out_weight,
    norm_gain,
    w_gate,
    w_up,
    w_down,
    suffix_lengths,
    request_group,
    placement_order,
):
    depth_z = math.gcd(devs, 4)
    depth_y = devs // depth_z
    cores = CORES
    depth_x = grps // cores
    ring = list(range(0, depth_z, 2)) + list(range(1, depth_z, 2))[::-1]

    def shift(by_z, by_y):
        return [
            (
                ring[i] * depth_y + y,
                ring[(i + by_z) % depth_z] * depth_y + (y + by_y) % depth_y,
            )
            for i in range(depth_z)
            for y in range(depth_y)
        ]

    x_shift = [
        (x * cores + c, (x + 1) % depth_x * cores + c) for x in range(depth_x) for c in range(cores)
    ]
    core_swap = [(x * cores + c, x * cores + 1 - c) for x in range(depth_x) for c in range(cores)]

    def round_z(block, *others):
        return lax.ppermute(tie(block, *others), "dev", shift(1, 0))

    def along_y(block, *others):
        return [lax.ppermute(tie(block, *others), "dev", shift(0, ys)) for ys in range(1, depth_y)]

    def along_x(weight, *others):
        blocks = [weight]
        for _ in range(1, depth_x):
            blocks.append(lax.ppermute(tie(blocks[-1], *others), "grp", x_shift))
        return blocks

    def other_core(block, *others):
        return lax.ppermute(tie(block, *others), "grp", core_swap)

    tokens = queries.shape[0]
    width = keys.shape[1]
    groups, span = prefix_keys.shape[:2]

    prefix = jnp.stack([prefix_keys.reshape(-1, width), cached_prefix_values.reshape(-1, width)])
    other = along_y(prefix)
    arriving = round_z(prefix)
    own = jnp.stack([keys, values])
    before = lax.ppermute(own, "dev", [(i, i + 1) for i in range(devs - 1)])
    gate_rows = along_x(w_gate)
    q, before_mask, within_mask, prefix_mask = prepare(
        groups,
        span,
        suffix_lengths,
        request_group,
        placement_order,
        queries,
        width,
    )
    blocks = [(before, before_mask), (own, within_mask), (prefix, prefix_mask)]
    ready, state = [], None
    for zs in range(1, depth_z):
        if zs == depth_z - 1:
            state = attend(q, None, blocks)
            blocks, ready = [], [state[0], gate_swap, *gate_rows[1:]]
        here = tie(arriving, *other, *ready)
        if zs < depth_z - 1:
            arriving, ready = round_z(here), [q, before]
        blocks += [(b, prefix_mask) for b in other + [here]]
        other = along_y(here)
        if zs == 1:
            gate_swap = other_core(w_gate, here)
        elif zs == 2:
            up_swap = other_core(w_up, here)
    state = attend(q, state, blocks)
    down_swap = other_core(w_down, here)
    up_rows = along_x(w_up, *gate_rows[1:], here)
    gates = [w_gate, gate_swap]
    for gate in gate_rows[1:]:
        gates += [gate, other_core(gate, here)]
    hidden_state, *normed = attend_project(
        q,
        state,
        [(b, prefix_mask) for b in other],
        grps,
        out_weight,
        tie(residual, up_swap, down_swap, *gates[2:]),
        norm_gain[None],
    )

    arrived, across = [normed], [[along_y(half) for half in normed]]
    ups, downs, acts = [w_up, up_swap], [w_down, down_swap], {}
    for zs in range(1, depth_z):
        waits = across[zs - 2] if zs > 1 else [[] for _ in normed]
        arrived.append([round_z(half, *wait) for half, wait in zip(arrived[-1], waits)])
        late = arrived[zs][1:]
        if zs == depth_z - 1:
            acts[1] = rise([arrived[1]] + [list(c) for c in zip(*across[1])], gates, ups)
            late = [*late, acts[1]]
        across.append([along_y(half, *late) for half in arrived[zs]])
        if zs == depth_z - 2:
            for up in up_rows[1:]:
                ups += [up, other_core(up, *arrived[zs], *[b for c in across[zs - 1] for b in c])]
            down_cols = along_x(w_down, *up_rows[1:], *arrived[zs], *[b for c in across[zs - 1] for b in c])
    chunks = [[a] + [list(c) for c in zip(*b)] for a, b in zip(arrived, across)]
    each = grps // HALVES
    acts[2] = rise(chunks[2], gates, ups)
    acts[0] = rise(chunks[0], gates, ups)
    soon = [b for c in across[-1] for b in c] + [acts[2], acts[0]]
    sent = [None] * HALVES
    if each <= len(downs):
        sent[0] = round_z(
            fall(acts[1], 1, downs[:each])[0], *arrived[-1], *[b for c in across[-2] for b in c]
        )
        soon.append(sent[0])
    for down in down_cols[1:]:
        downs += [down, other_core(down, *soon)]

    terms = [None] * HALVES
    for zs in list(range(1, depth_z)) + [0]:
        act = acts[zs] if zs in acts else rise(chunks[zs], gates, ups)
        for half in range(HALVES):
            weights = downs[half * each : (half + 1) * each]
            if zs == 1:
                if sent[half] is None:
                    sent[half] = round_z(fall(act, 1, weights)[0])
                continue
            parts = fall(act, depth_y, weights)
            if zs == 2:
                came = [sent[half][i * tokens : (i + 1) * tokens] for i in range(depth_y)]
                parts = [
                    (part.astype(F32) + share.astype(F32)).astype(BF16) if i else part
                    for i, (part, share) in enumerate(zip(parts, came))
                ]
                terms[half] = [parts[0], came[0]]
            else:
                terms[half] = [parts[0], round_z(sent[half])]
            if zs == 0:
                parts = [tie(part, sent[half]) for part in parts]
            terms[half] += [
                lax.ppermute(parts[ys], "dev", shift(0, -ys)) for ys in range(1, depth_y)
            ]
            if zs:
                sent[half] = functools.reduce(
                    jnp.add, [term.astype(F32) for term in terms[half]]
                ).astype(BF16)
    return finish(grps, hidden_state, terms)


def solution(mesh):
    placed = (
        P(("grp", "dev"), None),
        P(("grp", "dev"), None),
        P(("grp", "dev"), None),
        P(("grp", "dev"), None),
        P("grp", "dev", None),
        P("grp", "dev", None),
        P(),
        P(),
        P("grp", "dev"),
        P("grp", "dev"),
        P("dev", "grp"),
        P("grp", None),
        P("grp", None),
        P("grp", None),
    )
    return jax.shard_map(
        functools.partial(shards, mesh.shape["grp"], mesh.shape["dev"]),
        mesh=mesh,
        in_specs=placed,
        out_specs=P(("grp", "dev"), None),
        check_vma=False,
    )
```

```python
import functools
import math

import jax
import jax.numpy as jnp
from jax import lax
from jax.experimental import pallas as pl
from jax.experimental.pallas import tpu as pltpu
from jax.sharding import PartitionSpec as P

HEAD_SIZE = 64
NEG_FILL = -1e30
EPSILON = 1e-05
F32 = jnp.float32
BF16 = jnp.bfloat16
LANES = 2 * HEAD_SIZE
CORES = 2
HALVES = 2


def cost(microseconds):
    return pl.CostEstimate(flops=0, bytes_accessed=int(microseconds * 3.5e6), transcendentals=0)


def dot(a, b, contract_b=0):
    return lax.dot_general(
        a, b, (((1,), (contract_b,)), ((), ())), preferred_element_type=F32
    )


def prepare_body(
    span,
    lengths_hbm,
    groups_hbm,
    packing_hbm,
    queries_hbm,
    *refs,
):
    q_ref, before_ref, within_ref, prefix_ref = refs[:4]
    lengths_ref, groups_ref, packing_ref, queries_ref, sems = refs[4:]
    copies = [
        pltpu.make_async_copy(source, target, sems.at[i])
        for i, (source, target) in enumerate(
            [
                (lengths_hbm, lengths_ref),
                (groups_hbm, groups_ref),
                (packing_hbm, packing_ref),
                (queries_hbm, queries_ref),
            ]
        )
    ]
    for copy in copies:
        copy.start()
    for copy in copies:
        copy.wait()
    tokens = queries_ref.shape[0]
    pairs, rows = q_ref.shape[0], q_ref.shape[1]
    per = rows // (2 * tokens)
    base = lax.axis_index("dev") * tokens
    own = base + lax.broadcasted_iota(jnp.int32, (tokens, LANES), 0)

    def request(k, carry):
        start, group, first = carry
        j = packing_ref[0, k]
        end = start + lengths_ref[0, j]
        inside = (own >= start) & (own < end)
        return (
            end,
            jnp.where(inside, groups_ref[0, j], group),
            jnp.where(inside, start, first),
        )

    zero = jnp.zeros((tokens, LANES), jnp.int32)
    _, group, first = lax.fori_loop(0, lengths_ref.shape[1], request, (jnp.int32(0), zero, zero))
    for ref, back in ((before_ref, tokens), (within_ref, 0)):
        for c in range(0, tokens, LANES):
            key = base - back + c + lax.broadcasted_iota(jnp.int32, (tokens, LANES), 1)
            ref[:, c : c + LANES] = jnp.where((key >= first) & (key <= own), 0.0, NEG_FILL)
    for c in range(0, prefix_ref.shape[1], LANES):
        key_group = lax.div(c + lax.broadcasted_iota(jnp.int32, (tokens, LANES), 1), span)
        prefix_ref[:, c : c + LANES] = jnp.where(group == key_group, 0.0, NEG_FILL)
    low = lax.broadcasted_iota(jnp.int32, (tokens, LANES), 1) < HEAD_SIZE
    for j in range(pairs):
        for parity in range(2):
            for r in range(per):
                head = (2 * j + parity) * per + r
                block = head // 2
                q = queries_ref[:, block * LANES : (block + 1) * LANES].astype(F32) * HEAD_SIZE ** (-0.5)
                if head % 2 != parity:
                    q = pltpu.roll(q, HEAD_SIZE, 1)
                q = jnp.where(low == (parity == 0), q, 0.0)
                row = (parity * per + r) * tokens
                q_ref[j, row : row + tokens, :] = q.astype(BF16)


def prepare(groups, span, lengths, request_group, packing, queries, width):
    tokens = queries.shape[0]
    per = queries.shape[1] // width
    vmem = pl.BlockSpec(memory_space=pltpu.VMEM)
    return pl.pallas_call(
        functools.partial(prepare_body, span),
        out_shape=[
            jax.ShapeDtypeStruct((width // LANES, 2 * per * tokens, LANES), BF16),
            jax.ShapeDtypeStruct((tokens, tokens), F32),
            jax.ShapeDtypeStruct((tokens, tokens), F32),
            jax.ShapeDtypeStruct((tokens, groups * span), F32),
        ],
        in_specs=[pl.BlockSpec(memory_space=pltpu.HBM)] * 4,
        out_specs=[vmem] * 4,
        compiler_params=pltpu.CompilerParams(vmem_limit_bytes=8 * 2**20),
        scratch_shapes=[pltpu.SMEM(lengths.shape, jnp.int32)] * 3
        + [pltpu.VMEM(queries.shape, BF16), pltpu.SemaphoreType.DMA((4,))],
        cost_estimate=cost(3),
        name="prepare",
    )(lengths, request_group, packing, queries)


def attend_body(first, pieces, refs):
    q_ref, refs = refs[0], refs[1:]
    if not first:
        old_max, old_sum, old_acc = refs[:3]
        refs = refs[3:]
    kv = refs[: 3 * pieces]
    new_max, new_sum, new_acc = refs[-3:]
    pairs, rows = q_ref.shape[0], q_ref.shape[1]
    half = rows // 2
    low = lax.broadcasted_iota(jnp.int32, (half, LANES), 1) < HEAD_SIZE

    def pick(even, odd):
        return jnp.where(low, even, odd)

    for j in range(pairs):
        q = q_ref[j]
        lanes = slice(j * LANES, (j + 1) * LANES)
        scores = []
        for i in range(pieces):
            k_ref, bias_ref = kv[3 * i], kv[3 * i + 2]
            s = dot(q, k_ref[:, lanes], 1)
            keys = s.shape[1]
            bias = bias_ref[...]
            s = s.reshape(rows // bias.shape[0], bias.shape[0], keys) + bias[None]
            scores.append(s.reshape(rows, keys))
        top = functools.reduce(
            jnp.maximum, [jnp.max(s, axis=1, keepdims=True) for s in scores]
        )
        if first:
            row_max = top
            pair_max = pick(row_max[:half], row_max[half:])
        else:
            old = old_max[j]
            pair_max = jnp.maximum(old, pick(top[:half], top[half:]))
            row_max = jnp.concatenate(
                [pair_max[:, :1], pair_max[:, HEAD_SIZE : HEAD_SIZE + 1]], axis=0
            )
        total = None
        for i in range(pieces):
            v_ref = kv[3 * i + 1]
            w = jnp.exp(scores[i] - row_max).astype(BF16)
            v = v_ref[:, lanes]
            v = jnp.concatenate([v, jnp.ones_like(v)], axis=1)
            part = dot(w, v)
            total = part if total is None else total + part
        acc = pick(total[:half, :LANES], total[half:, :LANES])
        summed = pick(total[:half, LANES:], total[half:, LANES:])
        if not first:
            scale = jnp.exp(old - pair_max)
            acc = acc + scale * old_acc[j]
            summed = summed + scale * old_sum[j]
        new_max[j] = pair_max
        new_sum[j] = summed
        new_acc[j] = acc


def block_refs(refs, count):
    return [r for i in range(count) for r in (refs[2 * i].at[0], refs[2 * i].at[1], refs[2 * i + 1])]


def attend(q, state, blocks):
    pairs, rows, lanes = q.shape
    first = state is None

    def kernel(*refs):
        lead = 1 + (0 if first else 3)
        attend_body(first, len(blocks), [*refs[:lead], *block_refs(refs[lead:], len(blocks)), *refs[-3:]])

    shape = jax.ShapeDtypeStruct((pairs, rows // 2, lanes), F32)
    operands = [q] + ([] if first else list(state)) + [a for block in blocks for a in block]
    vmem = pl.BlockSpec(memory_space=pltpu.VMEM)
    return pl.pallas_call(
        kernel,
        out_shape=[shape] * 3,
        in_specs=[vmem] * len(operands),
        out_specs=[vmem] * 3,
        compiler_params=pltpu.CompilerParams(vmem_limit_bytes=(8 + 3 * len(blocks)) * 2**20),
        cost_estimate=cost(1.1 * len(blocks)),
        name="attend",
    )(*operands)


def block_owner(blocks, step):
    chips = blocks // CORES
    me = lax.axis_index("grp")
    x, core = lax.div(me, CORES), lax.rem(me, CORES)
    x = lax.rem(x + chips - step // CORES, chips)
    return x * CORES + lax.rem(core + step % CORES, CORES)


def project_body(
    blocks, sum_ref, acc_ref, weight_ref, residual_ref, gain_ref, hidden_ref, normed_refs, held
):
    pairs, rows, lanes = acc_ref.shape
    tokens = residual_ref.shape[0]
    per = rows // tokens
    hidden = residual_ref[...].astype(F32)
    for j in range(pairs):
        out = (acc_ref[j] / sum_ref[j]).astype(BF16)
        for r in range(0, per, 2):
            left = jnp.concatenate(
                [out[r * tokens : (r + 1) * tokens], out[(r + 1) * tokens : (r + 2) * tokens]], axis=1
            )
            heads = [(2 * j) * per + r, (2 * j + 1) * per + r, (2 * j) * per + r + 1, (2 * j + 1) * per + r + 1]
            right = jnp.concatenate(
                [weight_ref[h * HEAD_SIZE : (h + 1) * HEAD_SIZE, :] for h in heads], axis=0
            )
            hidden = hidden + dot(left, right)
    hidden_ref[...] = hidden
    mean = jnp.mean(hidden * hidden, axis=1, keepdims=True)
    held[...] = hidden * lax.rsqrt(mean + EPSILON) * gain_ref[...]
    width = hidden.shape[1] // blocks
    for b in range(blocks):
        start = pl.multiple_of(block_owner(blocks, b) * width, width)
        half, place = divmod(b, blocks // HALVES)
        normed_refs[half][:, place * width : (place + 1) * width] = held[:, pl.ds(start, width)].astype(BF16)


def attend_project(q, state, blocks, columns, out_weight, residual, gain):
    pairs, rows, lanes = q.shape
    tokens, width = residual.shape
    count = len(blocks)

    def kernel(*refs):
        mine, (weight_ref, residual_ref, gain_ref) = refs[: 4 + 2 * count], refs[4 + 2 * count : 7 + 2 * count]
        hidden_ref, *normed_refs = refs[7 + 2 * count : 8 + 2 * count + HALVES]
        held, top, total, acc = refs[-4:]
        attend_body(False, count, [*mine[:4], *block_refs(mine[4:], count), top, total, acc])
        project_body(
            columns, total, acc, weight_ref, residual_ref, gain_ref, hidden_ref, normed_refs, held
        )

    operands = [q, *state] + [a for block in blocks for a in block]
    vmem = pl.BlockSpec(memory_space=pltpu.VMEM)
    return pl.pallas_call(
        kernel,
        out_shape=[
            jax.ShapeDtypeStruct((tokens, width), F32),
        ]
        + [jax.ShapeDtypeStruct((tokens, width // HALVES), BF16)] * HALVES,
        in_specs=[vmem] * (len(operands) + 3),
        out_specs=[vmem] * (1 + HALVES),
        scratch_shapes=[pltpu.VMEM((tokens, width), F32)]
        + [pltpu.VMEM((pairs, rows // 2, lanes), F32)] * 3,
        compiler_params=pltpu.CompilerParams(vmem_limit_bytes=20 * 2**20),
        cost_estimate=cost(1.1 * count + 2),
        name="attend_project",
    )(*operands, out_weight, residual, gain)


def rise_body(parts, blocks, refs):
    pieces = parts * HALVES
    n_refs, gates, ups = refs[:pieces], refs[pieces : pieces + blocks], refs[pieces + blocks : pieces + 2 * blocks]
    act_ref, x_ref = refs[-2:]
    tokens, width = n_refs[0].shape
    for i in range(parts):
        for half in range(HALVES):
            x_ref[i * tokens : (i + 1) * tokens, half * width : (half + 1) * width] = n_refs[i * HALVES + half][...]
    depth, hidden = gates[0].shape
    tile = math.gcd(hidden, 256)

    @pl.loop(0, hidden // tile)
    def _(t):
        cols = pl.ds(pl.multiple_of(t * tile, tile), tile)
        gate = up = None
        for b in range(blocks):
            x = x_ref[:, b * depth : (b + 1) * depth]
            g, u = dot(x, gates[b][:, cols]), dot(x, ups[b][:, cols])
            gate, up = (g, u) if gate is None else (gate + g, up + u)
        act_ref[:, cols] = (gate / (1.0 + jnp.exp(-gate)) * up).astype(BF16)


def rise(normed, gates, ups):
    parts, blocks = len(normed), len(gates)
    tokens, width = normed[0][0].shape
    hidden = gates[0].shape[1]

    def kernel(*refs):
        rise_body(parts, blocks, refs)

    vmem = pl.BlockSpec(memory_space=pltpu.VMEM)
    return pl.pallas_call(
        kernel,
        out_shape=jax.ShapeDtypeStruct((parts * tokens, hidden), BF16),
        in_specs=[vmem] * (parts * HALVES + 2 * blocks),
        out_specs=vmem,
        scratch_shapes=[pltpu.VMEM((parts * tokens, HALVES * width), BF16)],
        compiler_params=pltpu.CompilerParams(vmem_limit_bytes=12 * 2**20),
        cost_estimate=cost(1.5 * parts),
        name="rise",
    )(*[half for chunk in normed for half in chunk], *gates, *ups)


def fall_body(blocks, refs):
    act_ref, downs, outs = refs[0], refs[1 : 1 + blocks], refs[1 + blocks :]
    rows, width = outs[0].shape[0], downs[0].shape[1]
    tile = math.gcd(width, 256)
    for b in range(blocks):

        @pl.loop(0, width // tile)
        def _(t):
            term = dot(act_ref[...], downs[b][:, pl.ds(pl.multiple_of(t * tile, tile), tile)])
            cols = pl.ds(pl.multiple_of(b * width + t * tile, tile), tile)
            for i, out in enumerate(outs):
                out[:, cols] = term[i * rows : (i + 1) * rows].astype(BF16)


def fall(act, parts, downs):
    blocks = len(downs)
    shape = jax.ShapeDtypeStruct((act.shape[0] // parts, blocks * downs[0].shape[1]), BF16)

    def kernel(*refs):
        fall_body(blocks, refs)

    vmem = pl.BlockSpec(memory_space=pltpu.VMEM)
    return pl.pallas_call(
        kernel,
        out_shape=[shape] * parts,
        in_specs=[vmem] * (1 + blocks),
        out_specs=[vmem] * parts,
        compiler_params=pltpu.CompilerParams(vmem_limit_bytes=12 * 2**20),
        cost_estimate=cost(1.2),
        name="fall",
    )(act, *downs)


def finish_body(blocks, hidden_ref, *refs):
    terms, out_ref = refs[:-1], refs[-1]
    each = len(terms) // HALVES
    width = out_ref.shape[1] // blocks
    for b in range(blocks):
        half, column = divmod(b, blocks // HALVES)
        place = pl.ds(pl.multiple_of(block_owner(blocks, b) * width, width), width)
        total = hidden_ref[:, place]
        for term in terms[half * each : (half + 1) * each]:
            total = total + term[:, column * width : (column + 1) * width].astype(F32)
        out_ref[:, place] = total.astype(BF16)


def finish(blocks, hidden_state, terms):
    vmem = pl.BlockSpec(memory_space=pltpu.VMEM)
    operands = [hidden_state] + [term for half in terms for term in half]
    return pl.pallas_call(
        functools.partial(finish_body, blocks),
        out_shape=jax.ShapeDtypeStruct(hidden_state.shape, BF16),
        in_specs=[vmem] * len(operands),
        out_specs=vmem,
        compiler_params=pltpu.CompilerParams(vmem_limit_bytes=8 * 2**20),
        cost_estimate=cost(1),
        name="finish",
    )(*operands)


def tie(array, *others):
    return lax.optimization_barrier((array, *others))[0] if others else array


def shards(
    grps,
    devs,
    residual,
    queries,
    keys,
    values,
    prefix_keys,
    cached_prefix_values,
    out_weight,
    norm_gain,
    w_gate,
    w_up,
    w_down,
    suffix_lengths,
    request_group,
    placement_order,
):
    depth_z = math.gcd(devs, 4)
    depth_y = devs // depth_z
    cores = CORES
    depth_x = grps // cores
    ring = list(range(0, depth_z, 2)) + list(range(1, depth_z, 2))[::-1]

    def shift(by_z, by_y):
        return [
            (
                ring[i] * depth_y + y,
                ring[(i + by_z) % depth_z] * depth_y + (y + by_y) % depth_y,
            )
            for i in range(depth_z)
            for y in range(depth_y)
        ]

    x_shift = [
        (x * cores + c, (x + 1) % depth_x * cores + c) for x in range(depth_x) for c in range(cores)
    ]
    core_swap = [(x * cores + c, x * cores + 1 - c) for x in range(depth_x) for c in range(cores)]

    def round_z(block, *others):
        return lax.ppermute(tie(block, *others), "dev", shift(1, 0))

    def along_y(block, *others):
        return [lax.ppermute(tie(block, *others), "dev", shift(0, ys)) for ys in range(1, depth_y)]

    def along_x(weight, *others):
        blocks = [weight]
        for _ in range(1, depth_x):
            blocks.append(lax.ppermute(tie(blocks[-1], *others), "grp", x_shift))
        return blocks

    def other_core(block, *others):
        return lax.ppermute(tie(block, *others), "grp", core_swap)

    tokens = queries.shape[0]
    width = keys.shape[1]
    groups, span = prefix_keys.shape[:2]

    prefix = jnp.stack([prefix_keys.reshape(-1, width), cached_prefix_values.reshape(-1, width)])
    other = along_y(prefix)
    arriving = round_z(prefix)
    own = jnp.stack([keys, values])
    before = lax.ppermute(own, "dev", [(i, i + 1) for i in range(devs - 1)])
    gate_rows = along_x(w_gate)
    q, before_mask, within_mask, prefix_mask = prepare(
        groups,
        span,
        suffix_lengths,
        request_group,
        placement_order,
        queries,
        width,
    )
    blocks = [(before, before_mask), (own, within_mask), (prefix, prefix_mask)]
    ready, state = [], None
    for zs in range(1, depth_z):
        if zs == depth_z - 1:
            state = attend(q, None, blocks)
            blocks, ready = [], [state[0], gate_swap, *gate_rows[1:]]
        here = tie(arriving, *other, *ready)
        if zs < depth_z - 1:
            arriving, ready = round_z(here), [q, before]
        blocks += [(b, prefix_mask) for b in other + [here]]
        other = along_y(here)
        if zs == 1:
            gate_swap = other_core(w_gate, here)
        elif zs == 2:
            up_swap = other_core(w_up, here)
    state = attend(q, state, blocks)
    down_swap = other_core(w_down, here)
    up_rows = along_x(w_up, *gate_rows[1:], here)
    gates = [w_gate, gate_swap]
    for gate in gate_rows[1:]:
        gates += [gate, other_core(gate, here)]
    hidden_state, *normed = attend_project(
        q,
        state,
        [(b, prefix_mask) for b in other],
        grps,
        out_weight,
        tie(residual, up_swap, down_swap, *gates[2:]),
        norm_gain[None],
    )

    arrived, across = [normed], [[along_y(half) for half in normed]]
    ups, downs, acts = [w_up, up_swap], [w_down, down_swap], {}
    for zs in range(1, depth_z):
        waits = across[zs - 2] if zs > 1 else [[] for _ in normed]
        arrived.append([round_z(half, *wait) for half, wait in zip(arrived[-1], waits)])
        late = arrived[zs][1:]
        if zs == depth_z - 1:
            acts[1] = rise([arrived[1]] + [list(c) for c in zip(*across[1])], gates, ups)
            late = [*late, acts[1]]
        across.append([along_y(half, *late) for half in arrived[zs]])
        if zs == depth_z - 2:
            for up in up_rows[1:]:
                ups += [up, other_core(up, *arrived[zs], *[b for c in across[zs - 1] for b in c])]
            down_cols = along_x(w_down, *up_rows[1:], *arrived[zs], *[b for c in across[zs - 1] for b in c])
    chunks = [[a] + [list(c) for c in zip(*b)] for a, b in zip(arrived, across)]
    each = grps // HALVES
    acts[2] = rise(chunks[2], gates, ups)
    acts[0] = rise(chunks[0], gates, ups)
    soon = [b for c in across[-1] for b in c] + [acts[2], acts[0]]
    fallen = {}
    sent = [None] * HALVES
    if each <= len(downs):
        sent[0] = round_z(
            fall(acts[1], 1, downs[:each])[0], *arrived[-1], *[b for c in across[-2] for b in c]
        )
        came = [sent[0][i * tokens : (i + 1) * tokens] for i in range(depth_y)]
        fallen[2, 0] = [
            (part.astype(F32) + share.astype(F32)).astype(BF16) if i else part
            for i, (part, share) in enumerate(zip(fall(acts[2], depth_y, downs[:each]), came))
        ]
        soon += fallen[2, 0]
    for down in down_cols[1:]:
        downs += [down, other_core(down, *soon)]

    terms = [None] * HALVES
    for zs in list(range(1, depth_z)) + [0]:
        act = acts[zs] if zs in acts else rise(chunks[zs], gates, ups)
        for half in range(HALVES):
            if zs == 1 and sent[half] is not None:
                continue
            parts = fallen.get((zs, half))
            if parts is not None:
                terms[half] = [parts[0], came[0]]
            else:
                parts = fall(act, depth_y, downs[half * each : (half + 1) * each])
                terms[half] = [parts[0]] + ([round_z(sent[half])] if zs != 1 else [])
            if zs == 0:
                parts = [tie(part, sent[half]) for part in parts]
            terms[half] += [
                lax.ppermute(parts[ys], "dev", shift(0, -ys)) for ys in range(1, depth_y)
            ]
            if zs:
                sent[half] = functools.reduce(
                    jnp.add, [term.astype(F32) for term in terms[half]]
                ).astype(BF16)
    return finish(grps, hidden_state, terms)


def solution(mesh):
    placed = (
        P(("grp", "dev"), None),
        P(("grp", "dev"), None),
        P(("grp", "dev"), None),
        P(("grp", "dev"), None),
        P("grp", "dev", None),
        P("grp", "dev", None),
        P(),
        P(),
        P("grp", "dev"),
        P("grp", "dev"),
        P("dev", "grp"),
        P("grp", None),
        P("grp", None),
        P("grp", None),
    )
    return jax.shard_map(
        functools.partial(shards, mesh.shape["grp"], mesh.shape["dev"]),
        mesh=mesh,
        in_specs=placed,
        out_specs=P(("grp", "dev"), None),
        check_vma=False,
    )
```

```python
import functools
import math

import jax
import jax.numpy as jnp
from jax import lax
from jax.experimental import pallas as pl
from jax.experimental.pallas import tpu as pltpu
from jax.sharding import PartitionSpec as P

HEAD_SIZE = 64
NEG_FILL = -1e30
EPSILON = 1e-05
F32 = jnp.float32
BF16 = jnp.bfloat16
LANES = 2 * HEAD_SIZE
CORES = 2
HALVES = 2


def cost(microseconds):
    return pl.CostEstimate(flops=0, bytes_accessed=int(microseconds * 3.5e6), transcendentals=0)


def dot(a, b, contract_b=0):
    return lax.dot_general(
        a, b, (((1,), (contract_b,)), ((), ())), preferred_element_type=F32
    )


def prepare_body(
    span,
    lengths_hbm,
    groups_hbm,
    packing_hbm,
    queries_hbm,
    *refs,
):
    q_ref, before_ref, within_ref, prefix_ref = refs[:4]
    lengths_ref, groups_ref, packing_ref, queries_ref, sems = refs[4:]
    copies = [
        pltpu.make_async_copy(source, target, sems.at[i])
        for i, (source, target) in enumerate(
            [
                (lengths_hbm, lengths_ref),
                (groups_hbm, groups_ref),
                (packing_hbm, packing_ref),
                (queries_hbm, queries_ref),
            ]
        )
    ]
    for copy in copies:
        copy.start()
    for copy in copies:
        copy.wait()
    tokens = queries_ref.shape[0]
    pairs, rows = q_ref.shape[0], q_ref.shape[1]
    per = rows // (2 * tokens)
    base = lax.axis_index("dev") * tokens
    own = base + lax.broadcasted_iota(jnp.int32, (tokens, LANES), 0)

    def request(k, carry):
        start, group, first = carry
        j = packing_ref[0, k]
        end = start + lengths_ref[0, j]
        inside = (own >= start) & (own < end)
        return (
            end,
            jnp.where(inside, groups_ref[0, j], group),
            jnp.where(inside, start, first),
        )

    zero = jnp.zeros((tokens, LANES), jnp.int32)
    _, group, first = lax.fori_loop(0, lengths_ref.shape[1], request, (jnp.int32(0), zero, zero))
    for ref, back in ((before_ref, tokens), (within_ref, 0)):
        for c in range(0, tokens, LANES):
            key = base - back + c + lax.broadcasted_iota(jnp.int32, (tokens, LANES), 1)
            ref[:, c : c + LANES] = jnp.where((key >= first) & (key <= own), 0.0, NEG_FILL)
    for c in range(0, prefix_ref.shape[1], LANES):
        key_group = lax.div(c + lax.broadcasted_iota(jnp.int32, (tokens, LANES), 1), span)
        prefix_ref[:, c : c + LANES] = jnp.where(group == key_group, 0.0, NEG_FILL)
    low = lax.broadcasted_iota(jnp.int32, (tokens, LANES), 1) < HEAD_SIZE
    for j in range(pairs):
        for parity in range(2):
            for r in range(per):
                head = (2 * j + parity) * per + r
                block = head // 2
                q = queries_ref[:, block * LANES : (block + 1) * LANES].astype(F32) * HEAD_SIZE ** (-0.5)
                if head % 2 != parity:
                    q = pltpu.roll(q, HEAD_SIZE, 1)
                q = jnp.where(low == (parity == 0), q, 0.0)
                row = (parity * per + r) * tokens
                q_ref[j, row : row + tokens, :] = q.astype(BF16)


def prepare(groups, span, lengths, request_group, packing, queries, width):
    tokens = queries.shape[0]
    per = queries.shape[1] // width
    vmem = pl.BlockSpec(memory_space=pltpu.VMEM)
    return pl.pallas_call(
        functools.partial(prepare_body, span),
        out_shape=[
            jax.ShapeDtypeStruct((width // LANES, 2 * per * tokens, LANES), BF16),
            jax.ShapeDtypeStruct((tokens, tokens), F32),
            jax.ShapeDtypeStruct((tokens, tokens), F32),
            jax.ShapeDtypeStruct((tokens, groups * span), F32),
        ],
        in_specs=[pl.BlockSpec(memory_space=pltpu.HBM)] * 4,
        out_specs=[vmem] * 4,
        compiler_params=pltpu.CompilerParams(vmem_limit_bytes=8 * 2**20),
        scratch_shapes=[pltpu.SMEM(lengths.shape, jnp.int32)] * 3
        + [pltpu.VMEM(queries.shape, BF16), pltpu.SemaphoreType.DMA((4,))],
        cost_estimate=cost(3),
        name="prepare",
    )(lengths, request_group, packing, queries)


def attend_body(first, pieces, refs):
    q_ref, refs = refs[0], refs[1:]
    if not first:
        old_max, old_sum, old_acc = refs[:3]
        refs = refs[3:]
    kv = refs[: 3 * pieces]
    new_max, new_sum, new_acc = refs[-3:]
    pairs, rows = q_ref.shape[0], q_ref.shape[1]
    half = rows // 2
    low = lax.broadcasted_iota(jnp.int32, (half, LANES), 1) < HEAD_SIZE

    def pick(even, odd):
        return jnp.where(low, even, odd)

    for j in range(pairs):
        q = q_ref[j]
        lanes = slice(j * LANES, (j + 1) * LANES)
        scores = []
        for i in range(pieces):
            k_ref, bias_ref = kv[3 * i], kv[3 * i + 2]
            s = dot(q, k_ref[:, lanes], 1)
            keys = s.shape[1]
            bias = bias_ref[...]
            s = s.reshape(rows // bias.shape[0], bias.shape[0], keys) + bias[None]
            scores.append(s.reshape(rows, keys))
        top = functools.reduce(
            jnp.maximum, [jnp.max(s, axis=1, keepdims=True) for s in scores]
        )
        if first:
            row_max = top
            pair_max = pick(row_max[:half], row_max[half:])
        else:
            old = old_max[j]
            pair_max = jnp.maximum(old, pick(top[:half], top[half:]))
            row_max = jnp.concatenate(
                [pair_max[:, :1], pair_max[:, HEAD_SIZE : HEAD_SIZE + 1]], axis=0
            )
        total = None
        for i in range(pieces):
            v_ref = kv[3 * i + 1]
            w = jnp.exp(scores[i] - row_max).astype(BF16)
            v = v_ref[:, lanes]
            v = jnp.concatenate([v, jnp.ones_like(v)], axis=1)
            part = dot(w, v)
            total = part if total is None else total + part
        acc = pick(total[:half, :LANES], total[half:, :LANES])
        summed = pick(total[:half, LANES:], total[half:, LANES:])
        if not first:
            scale = jnp.exp(old - pair_max)
            acc = acc + scale * old_acc[j]
            summed = summed + scale * old_sum[j]
        new_max[j] = pair_max
        new_sum[j] = summed
        new_acc[j] = acc


def block_refs(refs, count):
    return [r for i in range(count) for r in (refs[2 * i].at[0], refs[2 * i].at[1], refs[2 * i + 1])]


def attend(q, state, blocks):
    pairs, rows, lanes = q.shape
    first = state is None

    def kernel(*refs):
        lead = 1 + (0 if first else 3)
        attend_body(first, len(blocks), [*refs[:lead], *block_refs(refs[lead:], len(blocks)), *refs[-3:]])

    shape = jax.ShapeDtypeStruct((pairs, rows // 2, lanes), F32)
    operands = [q] + ([] if first else list(state)) + [a for block in blocks for a in block]
    vmem = pl.BlockSpec(memory_space=pltpu.VMEM)
    return pl.pallas_call(
        kernel,
        out_shape=[shape] * 3,
        in_specs=[vmem] * len(operands),
        out_specs=[vmem] * 3,
        compiler_params=pltpu.CompilerParams(vmem_limit_bytes=(8 + 3 * len(blocks)) * 2**20),
        cost_estimate=cost(1.1 * len(blocks)),
        name="attend",
    )(*operands)


def block_owner(blocks, step):
    chips = blocks // CORES
    me = lax.axis_index("grp")
    x, core = lax.div(me, CORES), lax.rem(me, CORES)
    x = lax.rem(x + chips - step // CORES, chips)
    return x * CORES + lax.rem(core + step % CORES, CORES)


def project_body(
    blocks, sum_ref, acc_ref, weight_ref, residual_ref, gain_ref, hidden_ref, normed_refs, held
):
    pairs, rows, lanes = acc_ref.shape
    tokens = residual_ref.shape[0]
    per = rows // tokens
    hidden = residual_ref[...].astype(F32)
    for j in range(pairs):
        out = (acc_ref[j] / sum_ref[j]).astype(BF16)
        for r in range(0, per, 2):
            left = jnp.concatenate(
                [out[r * tokens : (r + 1) * tokens], out[(r + 1) * tokens : (r + 2) * tokens]], axis=1
            )
            heads = [(2 * j) * per + r, (2 * j + 1) * per + r, (2 * j) * per + r + 1, (2 * j + 1) * per + r + 1]
            right = jnp.concatenate(
                [weight_ref[h * HEAD_SIZE : (h + 1) * HEAD_SIZE, :] for h in heads], axis=0
            )
            hidden = hidden + dot(left, right)
    hidden_ref[...] = hidden
    mean = jnp.mean(hidden * hidden, axis=1, keepdims=True)
    held[...] = hidden * lax.rsqrt(mean + EPSILON) * gain_ref[...]
    width = hidden.shape[1] // blocks
    for b in range(blocks):
        start = pl.multiple_of(block_owner(blocks, b) * width, width)
        half, place = divmod(b, blocks // HALVES)
        normed_refs[half][:, place * width : (place + 1) * width] = held[:, pl.ds(start, width)].astype(BF16)


def attend_project(q, state, blocks, columns, out_weight, residual, gain):
    pairs, rows, lanes = q.shape
    tokens, width = residual.shape
    count = len(blocks)

    def kernel(*refs):
        mine, (weight_ref, residual_ref, gain_ref) = refs[: 4 + 2 * count], refs[4 + 2 * count : 7 + 2 * count]
        hidden_ref, *normed_refs = refs[7 + 2 * count : 8 + 2 * count + HALVES]
        held, top, total, acc = refs[-4:]
        attend_body(False, count, [*mine[:4], *block_refs(mine[4:], count), top, total, acc])
        project_body(
            columns, total, acc, weight_ref, residual_ref, gain_ref, hidden_ref, normed_refs, held
        )

    operands = [q, *state] + [a for block in blocks for a in block]
    vmem = pl.BlockSpec(memory_space=pltpu.VMEM)
    return pl.pallas_call(
        kernel,
        out_shape=[
            jax.ShapeDtypeStruct((tokens, width), F32),
        ]
        + [jax.ShapeDtypeStruct((tokens, width // HALVES), BF16)] * HALVES,
        in_specs=[vmem] * (len(operands) + 3),
        out_specs=[vmem] * (1 + HALVES),
        scratch_shapes=[pltpu.VMEM((tokens, width), F32)]
        + [pltpu.VMEM((pairs, rows // 2, lanes), F32)] * 3,
        compiler_params=pltpu.CompilerParams(vmem_limit_bytes=20 * 2**20),
        cost_estimate=cost(1.1 * count + 2),
        name="attend_project",
    )(*operands, out_weight, residual, gain)


def rise_body(parts, blocks, refs):
    pieces = parts * HALVES
    n_refs, gates, ups = refs[:pieces], refs[pieces : pieces + blocks], refs[pieces + blocks : pieces + 2 * blocks]
    act_ref, x_ref = refs[-2:]
    tokens, width = n_refs[0].shape
    for i in range(parts):
        for half in range(HALVES):
            x_ref[i * tokens : (i + 1) * tokens, half * width : (half + 1) * width] = n_refs[i * HALVES + half][...]
    depth, hidden = gates[0].shape
    tile = math.gcd(hidden, 256)

    @pl.loop(0, hidden // tile)
    def _(t):
        cols = pl.ds(pl.multiple_of(t * tile, tile), tile)
        gate = up = None
        for b in range(blocks):
            x = x_ref[:, b * depth : (b + 1) * depth]
            g, u = dot(x, gates[b][:, cols]), dot(x, ups[b][:, cols])
            gate, up = (g, u) if gate is None else (gate + g, up + u)
        act_ref[:, cols] = (gate / (1.0 + jnp.exp(-gate)) * up).astype(BF16)


def rise(normed, gates, ups):
    parts, blocks = len(normed), len(gates)
    tokens, width = normed[0][0].shape
    hidden = gates[0].shape[1]

    def kernel(*refs):
        rise_body(parts, blocks, refs)

    vmem = pl.BlockSpec(memory_space=pltpu.VMEM)
    return pl.pallas_call(
        kernel,
        out_shape=jax.ShapeDtypeStruct((parts * tokens, hidden), BF16),
        in_specs=[vmem] * (parts * HALVES + 2 * blocks),
        out_specs=vmem,
        scratch_shapes=[pltpu.VMEM((parts * tokens, HALVES * width), BF16)],
        compiler_params=pltpu.CompilerParams(vmem_limit_bytes=12 * 2**20),
        cost_estimate=cost(1.5 * parts),
        name="rise",
    )(*[half for chunk in normed for half in chunk], *gates, *ups)


def fall_body(blocks, refs):
    act_ref, downs, outs = refs[0], refs[1 : 1 + blocks], refs[1 + blocks :]
    rows, width = outs[0].shape[0], downs[0].shape[1]
    tile = math.gcd(width, 256)
    for b in range(blocks):

        @pl.loop(0, width // tile)
        def _(t):
            term = dot(act_ref[...], downs[b][:, pl.ds(pl.multiple_of(t * tile, tile), tile)])
            cols = pl.ds(pl.multiple_of(b * width + t * tile, tile), tile)
            for i, out in enumerate(outs):
                out[:, cols] = term[i * rows : (i + 1) * rows].astype(BF16)


def fall(act, parts, downs):
    blocks = len(downs)
    shape = jax.ShapeDtypeStruct((act.shape[0] // parts, blocks * downs[0].shape[1]), BF16)

    def kernel(*refs):
        fall_body(blocks, refs)

    vmem = pl.BlockSpec(memory_space=pltpu.VMEM)
    return pl.pallas_call(
        kernel,
        out_shape=[shape] * parts,
        in_specs=[vmem] * (1 + blocks),
        out_specs=[vmem] * parts,
        compiler_params=pltpu.CompilerParams(vmem_limit_bytes=12 * 2**20),
        cost_estimate=cost(1.2),
        name="fall",
    )(act, *downs)


def finish_body(blocks, hidden_ref, *refs):
    terms, out_ref = refs[:-1], refs[-1]
    each = len(terms) // HALVES
    width = out_ref.shape[1] // blocks
    for b in range(blocks):
        half, column = divmod(b, blocks // HALVES)
        place = pl.ds(pl.multiple_of(block_owner(blocks, b) * width, width), width)
        total = hidden_ref[:, place]
        for term in terms[half * each : (half + 1) * each]:
            total = total + term[:, column * width : (column + 1) * width].astype(F32)
        out_ref[:, place] = total.astype(BF16)


def finish(blocks, hidden_state, terms):
    vmem = pl.BlockSpec(memory_space=pltpu.VMEM)
    operands = [hidden_state] + [term for half in terms for term in half]
    return pl.pallas_call(
        functools.partial(finish_body, blocks),
        out_shape=jax.ShapeDtypeStruct(hidden_state.shape, BF16),
        in_specs=[vmem] * len(operands),
        out_specs=vmem,
        compiler_params=pltpu.CompilerParams(vmem_limit_bytes=8 * 2**20),
        cost_estimate=cost(1),
        name="finish",
    )(*operands)


def tie(array, *others):
    return lax.optimization_barrier((array, *others))[0] if others else array


def shards(
    grps,
    devs,
    residual,
    queries,
    keys,
    values,
    prefix_keys,
    cached_prefix_values,
    out_weight,
    norm_gain,
    w_gate,
    w_up,
    w_down,
    suffix_lengths,
    request_group,
    placement_order,
):
    depth_z = math.gcd(devs, 4)
    depth_y = devs // depth_z
    cores = CORES
    depth_x = grps // cores
    ring = list(range(0, depth_z, 2)) + list(range(1, depth_z, 2))[::-1]

    def shift(by_z, by_y):
        return [
            (
                ring[i] * depth_y + y,
                ring[(i + by_z) % depth_z] * depth_y + (y + by_y) % depth_y,
            )
            for i in range(depth_z)
            for y in range(depth_y)
        ]

    x_shift = [
        (x * cores + c, (x + 1) % depth_x * cores + c) for x in range(depth_x) for c in range(cores)
    ]
    core_swap = [(x * cores + c, x * cores + 1 - c) for x in range(depth_x) for c in range(cores)]

    def round_z(block, *others):
        return lax.ppermute(tie(block, *others), "dev", shift(1, 0))

    def along_y(block, *others):
        return [lax.ppermute(tie(block, *others), "dev", shift(0, ys)) for ys in range(1, depth_y)]

    def along_x(weight, *others):
        blocks = [weight]
        for _ in range(1, depth_x):
            blocks.append(lax.ppermute(tie(blocks[-1], *others), "grp", x_shift))
        return blocks

    def other_core(block, *others):
        return lax.ppermute(tie(block, *others), "grp", core_swap)

    tokens = queries.shape[0]
    width = keys.shape[1]
    groups, span = prefix_keys.shape[:2]

    prefix = jnp.stack([prefix_keys.reshape(-1, width), cached_prefix_values.reshape(-1, width)])
    other = along_y(prefix)
    arriving = round_z(prefix)
    own = jnp.stack([keys, values])
    before = lax.ppermute(own, "dev", [(i, i + 1) for i in range(devs - 1)])
    gate_rows = along_x(w_gate)
    q, before_mask, within_mask, prefix_mask = prepare(
        groups,
        span,
        suffix_lengths,
        request_group,
        placement_order,
        queries,
        width,
    )
    blocks = [(before, before_mask), (own, within_mask), (prefix, prefix_mask)]
    ready, state = [], None
    for zs in range(1, depth_z):
        if zs == depth_z - 1:
            state = attend(q, None, blocks)
            blocks, ready = [], [state[0], gate_swap, *gate_rows[1:]]
        here = tie(arriving, *other, *ready)
        if zs < depth_z - 1:
            arriving, ready = round_z(here), [q, before]
        blocks += [(b, prefix_mask) for b in other + [here]]
        other = along_y(here)
        if zs == 1:
            gate_swap = other_core(w_gate, here)
        elif zs == 2:
            up_swap = other_core(w_up, here)
    state = attend(q, state, blocks)
    down_swap = other_core(w_down, here)
    up_rows = along_x(w_up, *gate_rows[1:], here)
    gates = [w_gate, gate_swap]
    for gate in gate_rows[1:]:
        gates += [gate, other_core(gate, here)]
    hidden_state, *normed = attend_project(
        q,
        state,
        [(b, prefix_mask) for b in other],
        grps,
        out_weight,
        tie(residual, up_swap, down_swap, *gates[2:]),
        norm_gain[None],
    )

    arrived, across = [normed], [[along_y(half) for half in normed]]
    ups, downs, acts = [w_up, up_swap], [w_down, down_swap], {}
    for zs in range(1, depth_z):
        waits = across[zs - 2] if zs > 1 else [[] for _ in normed]
        arrived.append([round_z(half, *wait) for half, wait in zip(arrived[-1], waits)])
        late = arrived[zs][1:]
        if zs == depth_z - 1:
            acts[1] = rise([arrived[1]] + [list(c) for c in zip(*across[1])], gates, ups)
            late = [*late, acts[1]]
        across.append([along_y(half, *late) for half in arrived[zs]])
        if zs == depth_z - 2:
            for up in up_rows[1:]:
                ups += [up, other_core(up, *arrived[zs], *[b for c in across[zs - 1] for b in c])]
            down_cols = along_x(w_down, *up_rows[1:], *arrived[zs], *[b for c in across[zs - 1] for b in c])
    chunks = [[a] + [list(c) for c in zip(*b)] for a, b in zip(arrived, across)]
    each = grps // HALVES
    acts[2] = rise(chunks[2], gates, ups)
    acts[0] = rise(chunks[0], gates, ups)
    soon = [b for c in across[-1] for b in c] + [acts[2], acts[0]]
    sent = [None] * HALVES
    if each <= len(downs):
        sent[0] = round_z(
            fall(acts[1], 1, downs[:each])[0], *arrived[-1], *[b for c in across[-2] for b in c]
        )
        second = fall(acts[2], 1, downs[:each])[0]
        second = (second.astype(F32) + sent[0].astype(F32)).astype(BF16)
        soon.append(second)
        sent[0] = round_z(second)
    for down in down_cols[1:]:
        downs += [down, other_core(down, *soon)]

    terms = [None] * HALVES
    for zs in list(range(1, depth_z)) + [0]:
        act = acts[zs] if zs in acts else rise(chunks[zs], gates, ups)
        for half in range(HALVES):
            joint = sent[half] is not None and sent[half].shape[0] > tokens
            if joint and zs < depth_z - 1:
                continue
            parts = fall(act, depth_y, downs[half * each : (half + 1) * each])
            if joint:
                came = [sent[half][i * tokens : (i + 1) * tokens] for i in range(depth_y)]
                parts = [
                    (part.astype(F32) + share.astype(F32)).astype(BF16) if i else part
                    for i, (part, share) in enumerate(zip(parts, came))
                ]
                terms[half] = [parts[0], came[0]]
            else:
                terms[half] = [parts[0]] + ([round_z(sent[half])] if zs != 1 else [])
            if zs == 0:
                parts = [tie(part, sent[half]) for part in parts]
            terms[half] += [
                lax.ppermute(parts[ys], "dev", shift(0, -ys)) for ys in range(1, depth_y)
            ]
            if zs:
                sent[half] = functools.reduce(
                    jnp.add, [term.astype(F32) for term in terms[half]]
                ).astype(BF16)
    return finish(grps, hidden_state, terms)


def solution(mesh):
    placed = (
        P(("grp", "dev"), None),
        P(("grp", "dev"), None),
        P(("grp", "dev"), None),
        P(("grp", "dev"), None),
        P("grp", "dev", None),
        P("grp", "dev", None),
        P(),
        P(),
        P("grp", "dev"),
        P("grp", "dev"),
        P("dev", "grp"),
        P("grp", None),
        P("grp", None),
        P("grp", None),
    )
    return jax.shard_map(
        functools.partial(shards, mesh.shape["grp"], mesh.shape["dev"]),
        mesh=mesh,
        in_specs=placed,
        out_specs=P(("grp", "dev"), None),
        check_vma=False,
    )
```

```python
import functools
import math

import jax
import jax.numpy as jnp
from jax import lax
from jax.experimental import pallas as pl
from jax.experimental.pallas import tpu as pltpu
from jax.sharding import PartitionSpec as P

HEAD_SIZE = 64
NEG_FILL = -1e30
EPSILON = 1e-05
F32 = jnp.float32
BF16 = jnp.bfloat16
LANES = 2 * HEAD_SIZE
CORES = 2
HALVES = 2


def cost(microseconds):
    return pl.CostEstimate(flops=0, bytes_accessed=int(microseconds * 3.5e6), transcendentals=0)


def dot(a, b, contract_b=0):
    return lax.dot_general(
        a, b, (((1,), (contract_b,)), ((), ())), preferred_element_type=F32
    )


def prepare_body(
    span,
    lengths_hbm,
    groups_hbm,
    packing_hbm,
    queries_hbm,
    *refs,
):
    q_ref, before_ref, within_ref, prefix_ref = refs[:4]
    lengths_ref, groups_ref, packing_ref, queries_ref, sems = refs[4:]
    copies = [
        pltpu.make_async_copy(source, target, sems.at[i])
        for i, (source, target) in enumerate(
            [
                (lengths_hbm, lengths_ref),
                (groups_hbm, groups_ref),
                (packing_hbm, packing_ref),
                (queries_hbm, queries_ref),
            ]
        )
    ]
    for copy in copies:
        copy.start()
    for copy in copies:
        copy.wait()
    tokens = queries_ref.shape[0]
    pairs, rows = q_ref.shape[0], q_ref.shape[1]
    per = rows // (2 * tokens)
    base = lax.axis_index("dev") * tokens
    own = base + lax.broadcasted_iota(jnp.int32, (tokens, LANES), 0)

    def request(k, carry):
        start, group, first = carry
        j = packing_ref[0, k]
        end = start + lengths_ref[0, j]
        inside = (own >= start) & (own < end)
        return (
            end,
            jnp.where(inside, groups_ref[0, j], group),
            jnp.where(inside, start, first),
        )

    zero = jnp.zeros((tokens, LANES), jnp.int32)
    _, group, first = lax.fori_loop(0, lengths_ref.shape[1], request, (jnp.int32(0), zero, zero))
    for ref, back in ((before_ref, tokens), (within_ref, 0)):
        for c in range(0, tokens, LANES):
            key = base - back + c + lax.broadcasted_iota(jnp.int32, (tokens, LANES), 1)
            ref[:, c : c + LANES] = jnp.where((key >= first) & (key <= own), 0.0, NEG_FILL)
    for c in range(0, prefix_ref.shape[1], LANES):
        key_group = lax.div(c + lax.broadcasted_iota(jnp.int32, (tokens, LANES), 1), span)
        prefix_ref[:, c : c + LANES] = jnp.where(group == key_group, 0.0, NEG_FILL)
    low = lax.broadcasted_iota(jnp.int32, (tokens, LANES), 1) < HEAD_SIZE
    for j in range(pairs):
        for parity in range(2):
            for r in range(per):
                head = (2 * j + parity) * per + r
                block = head // 2
                q = queries_ref[:, block * LANES : (block + 1) * LANES].astype(F32) * HEAD_SIZE ** (-0.5)
                if head % 2 != parity:
                    q = pltpu.roll(q, HEAD_SIZE, 1)
                q = jnp.where(low == (parity == 0), q, 0.0)
                row = (parity * per + r) * tokens
                q_ref[j, row : row + tokens, :] = q.astype(BF16)


def prepare(groups, span, lengths, request_group, packing, queries, width):
    tokens = queries.shape[0]
    per = queries.shape[1] // width
    vmem = pl.BlockSpec(memory_space=pltpu.VMEM)
    return pl.pallas_call(
        functools.partial(prepare_body, span),
        out_shape=[
            jax.ShapeDtypeStruct((width // LANES, 2 * per * tokens, LANES), BF16),
            jax.ShapeDtypeStruct((tokens, tokens), F32),
            jax.ShapeDtypeStruct((tokens, tokens), F32),
            jax.ShapeDtypeStruct((tokens, groups * span), F32),
        ],
        in_specs=[pl.BlockSpec(memory_space=pltpu.HBM)] * 4,
        out_specs=[vmem] * 4,
        compiler_params=pltpu.CompilerParams(vmem_limit_bytes=8 * 2**20),
        scratch_shapes=[pltpu.SMEM(lengths.shape, jnp.int32)] * 3
        + [pltpu.VMEM(queries.shape, BF16), pltpu.SemaphoreType.DMA((4,))],
        cost_estimate=cost(3),
        name="prepare",
    )(lengths, request_group, packing, queries)


def attend_body(first, pieces, refs):
    q_ref, refs = refs[0], refs[1:]
    if not first:
        old_max, old_sum, old_acc = refs[:3]
        refs = refs[3:]
    kv = refs[: 3 * pieces]
    new_max, new_sum, new_acc = refs[-3:]
    pairs, rows = q_ref.shape[0], q_ref.shape[1]
    half = rows // 2
    low = lax.broadcasted_iota(jnp.int32, (half, LANES), 1) < HEAD_SIZE

    def pick(even, odd):
        return jnp.where(low, even, odd)

    for j in range(pairs):
        q = q_ref[j]
        lanes = slice(j * LANES, (j + 1) * LANES)
        scores = []
        for i in range(pieces):
            k_ref, bias_ref = kv[3 * i], kv[3 * i + 2]
            s = dot(q, k_ref[:, lanes], 1)
            keys = s.shape[1]
            bias = bias_ref[...]
            s = s.reshape(rows // bias.shape[0], bias.shape[0], keys) + bias[None]
            scores.append(s.reshape(rows, keys))
        top = functools.reduce(
            jnp.maximum, [jnp.max(s, axis=1, keepdims=True) for s in scores]
        )
        if first:
            row_max = top
            pair_max = pick(row_max[:half], row_max[half:])
        else:
            old = old_max[j]
            pair_max = jnp.maximum(old, pick(top[:half], top[half:]))
            row_max = jnp.concatenate(
                [pair_max[:, :1], pair_max[:, HEAD_SIZE : HEAD_SIZE + 1]], axis=0
            )
        total = None
        for i in range(pieces):
            v_ref = kv[3 * i + 1]
            w = jnp.exp(scores[i] - row_max).astype(BF16)
            v = v_ref[:, lanes]
            v = jnp.concatenate([v, jnp.ones_like(v)], axis=1)
            part = dot(w, v)
            total = part if total is None else total + part
        acc = pick(total[:half, :LANES], total[half:, :LANES])
        summed = pick(total[:half, LANES:], total[half:, LANES:])
        if not first:
            scale = jnp.exp(old - pair_max)
            acc = acc + scale * old_acc[j]
            summed = summed + scale * old_sum[j]
        new_max[j] = pair_max
        new_sum[j] = summed
        new_acc[j] = acc


def block_refs(refs, count):
    return [r for i in range(count) for r in (refs[2 * i].at[0], refs[2 * i].at[1], refs[2 * i + 1])]


def attend(q, state, blocks):
    pairs, rows, lanes = q.shape
    first = state is None

    def kernel(*refs):
        lead = 1 + (0 if first else 3)
        attend_body(first, len(blocks), [*refs[:lead], *block_refs(refs[lead:], len(blocks)), *refs[-3:]])

    shape = jax.ShapeDtypeStruct((pairs, rows // 2, lanes), F32)
    operands = [q] + ([] if first else list(state)) + [a for block in blocks for a in block]
    vmem = pl.BlockSpec(memory_space=pltpu.VMEM)
    return pl.pallas_call(
        kernel,
        out_shape=[shape] * 3,
        in_specs=[vmem] * len(operands),
        out_specs=[vmem] * 3,
        compiler_params=pltpu.CompilerParams(vmem_limit_bytes=(8 + 3 * len(blocks)) * 2**20),
        cost_estimate=cost(1.1 * len(blocks)),
        name="attend",
    )(*operands)


def block_owner(blocks, step):
    chips = blocks // CORES
    me = lax.axis_index("grp")
    x, core = lax.div(me, CORES), lax.rem(me, CORES)
    x = lax.rem(x + chips - step // CORES, chips)
    return x * CORES + lax.rem(core + step % CORES, CORES)


def project_body(
    blocks, sum_ref, acc_ref, weight_ref, residual_ref, gain_ref, hidden_ref, normed_refs, held
):
    pairs, rows, lanes = acc_ref.shape
    tokens = residual_ref.shape[0]
    per = rows // tokens
    hidden = residual_ref[...].astype(F32)
    for j in range(pairs):
        out = (acc_ref[j] / sum_ref[j]).astype(BF16)
        for r in range(0, per, 2):
            left = jnp.concatenate(
                [out[r * tokens : (r + 1) * tokens], out[(r + 1) * tokens : (r + 2) * tokens]], axis=1
            )
            heads = [(2 * j) * per + r, (2 * j + 1) * per + r, (2 * j) * per + r + 1, (2 * j + 1) * per + r + 1]
            right = jnp.concatenate(
                [weight_ref[h * HEAD_SIZE : (h + 1) * HEAD_SIZE, :] for h in heads], axis=0
            )
            hidden = hidden + dot(left, right)
    hidden_ref[...] = hidden
    mean = jnp.mean(hidden * hidden, axis=1, keepdims=True)
    held[...] = hidden * lax.rsqrt(mean + EPSILON) * gain_ref[...]
    width = hidden.shape[1] // blocks
    for b in range(blocks):
        start = pl.multiple_of(block_owner(blocks, b) * width, width)
        half, place = divmod(b, blocks // HALVES)
        normed_refs[half][:, place * width : (place + 1) * width] = held[:, pl.ds(start, width)].astype(BF16)


def attend_project(q, state, blocks, columns, out_weight, residual, gain):
    pairs, rows, lanes = q.shape
    tokens, width = residual.shape
    count = len(blocks)

    def kernel(*refs):
        mine, (weight_ref, residual_ref, gain_ref) = refs[: 4 + 2 * count], refs[4 + 2 * count : 7 + 2 * count]
        hidden_ref, *normed_refs = refs[7 + 2 * count : 8 + 2 * count + HALVES]
        held, top, total, acc = refs[-4:]
        attend_body(False, count, [*mine[:4], *block_refs(mine[4:], count), top, total, acc])
        project_body(
            columns, total, acc, weight_ref, residual_ref, gain_ref, hidden_ref, normed_refs, held
        )

    operands = [q, *state] + [a for block in blocks for a in block]
    vmem = pl.BlockSpec(memory_space=pltpu.VMEM)
    return pl.pallas_call(
        kernel,
        out_shape=[
            jax.ShapeDtypeStruct((tokens, width), F32),
        ]
        + [jax.ShapeDtypeStruct((tokens, width // HALVES), BF16)] * HALVES,
        in_specs=[vmem] * (len(operands) + 3),
        out_specs=[vmem] * (1 + HALVES),
        scratch_shapes=[pltpu.VMEM((tokens, width), F32)]
        + [pltpu.VMEM((pairs, rows // 2, lanes), F32)] * 3,
        compiler_params=pltpu.CompilerParams(vmem_limit_bytes=20 * 2**20),
        cost_estimate=cost(1.1 * count + 2),
        name="attend_project",
    )(*operands, out_weight, residual, gain)


def rise_body(parts, blocks, refs):
    pieces = parts * HALVES
    n_refs, gates, ups = refs[:pieces], refs[pieces : pieces + blocks], refs[pieces + blocks : pieces + 2 * blocks]
    act_ref, x_ref = refs[-2:]
    tokens, width = n_refs[0].shape
    for i in range(parts):
        for half in range(HALVES):
            x_ref[i * tokens : (i + 1) * tokens, half * width : (half + 1) * width] = n_refs[i * HALVES + half][...]
    depth, hidden = gates[0].shape
    tile = math.gcd(hidden, 256)

    @pl.loop(0, hidden // tile)
    def _(t):
        cols = pl.ds(pl.multiple_of(t * tile, tile), tile)
        gate = up = None
        for b in range(blocks):
            x = x_ref[:, b * depth : (b + 1) * depth]
            g, u = dot(x, gates[b][:, cols]), dot(x, ups[b][:, cols])
            gate, up = (g, u) if gate is None else (gate + g, up + u)
        act_ref[:, cols] = (gate / (1.0 + jnp.exp(-gate)) * up).astype(BF16)


def rise(normed, gates, ups):
    parts, blocks = len(normed), len(gates)
    tokens, width = normed[0][0].shape
    hidden = gates[0].shape[1]

    def kernel(*refs):
        rise_body(parts, blocks, refs)

    vmem = pl.BlockSpec(memory_space=pltpu.VMEM)
    return pl.pallas_call(
        kernel,
        out_shape=jax.ShapeDtypeStruct((parts * tokens, hidden), BF16),
        in_specs=[vmem] * (parts * HALVES + 2 * blocks),
        out_specs=vmem,
        scratch_shapes=[pltpu.VMEM((parts * tokens, HALVES * width), BF16)],
        compiler_params=pltpu.CompilerParams(vmem_limit_bytes=12 * 2**20),
        cost_estimate=cost(1.5 * parts),
        name="rise",
    )(*[half for chunk in normed for half in chunk], *gates, *ups)


def fall_body(blocks, refs):
    act_ref, downs, outs = refs[0], refs[1 : 1 + blocks], refs[1 + blocks :]
    rows, width = outs[0].shape[0], downs[0].shape[1]
    tile = math.gcd(width, 256)
    for b in range(blocks):

        @pl.loop(0, width // tile)
        def _(t):
            term = dot(act_ref[...], downs[b][:, pl.ds(pl.multiple_of(t * tile, tile), tile)])
            cols = pl.ds(pl.multiple_of(b * width + t * tile, tile), tile)
            for i, out in enumerate(outs):
                out[:, cols] = term[i * rows : (i + 1) * rows].astype(BF16)


def fall(act, parts, downs):
    blocks = len(downs)
    shape = jax.ShapeDtypeStruct((act.shape[0] // parts, blocks * downs[0].shape[1]), BF16)

    def kernel(*refs):
        fall_body(blocks, refs)

    vmem = pl.BlockSpec(memory_space=pltpu.VMEM)
    return pl.pallas_call(
        kernel,
        out_shape=[shape] * parts,
        in_specs=[vmem] * (1 + blocks),
        out_specs=[vmem] * parts,
        compiler_params=pltpu.CompilerParams(vmem_limit_bytes=12 * 2**20),
        cost_estimate=cost(1.2),
        name="fall",
    )(act, *downs)


def finish_body(blocks, hidden_ref, *refs):
    terms, out_ref = refs[:-1], refs[-1]
    each = len(terms) // HALVES
    width = out_ref.shape[1] // blocks
    for b in range(blocks):
        half, column = divmod(b, blocks // HALVES)
        place = pl.ds(pl.multiple_of(block_owner(blocks, b) * width, width), width)
        total = hidden_ref[:, place]
        for term in terms[half * each : (half + 1) * each]:
            total = total + term[:, column * width : (column + 1) * width].astype(F32)
        out_ref[:, place] = total.astype(BF16)


def finish(blocks, hidden_state, terms):
    vmem = pl.BlockSpec(memory_space=pltpu.VMEM)
    operands = [hidden_state] + [term for half in terms for term in half]
    return pl.pallas_call(
        functools.partial(finish_body, blocks),
        out_shape=jax.ShapeDtypeStruct(hidden_state.shape, BF16),
        in_specs=[vmem] * len(operands),
        out_specs=vmem,
        compiler_params=pltpu.CompilerParams(vmem_limit_bytes=8 * 2**20),
        cost_estimate=cost(1),
        name="finish",
    )(*operands)


def tie(array, *others):
    return lax.optimization_barrier((array, *others))[0] if others else array


def shards(
    grps,
    devs,
    residual,
    queries,
    keys,
    values,
    prefix_keys,
    cached_prefix_values,
    out_weight,
    norm_gain,
    w_gate,
    w_up,
    w_down,
    suffix_lengths,
    request_group,
    placement_order,
):
    depth_z = math.gcd(devs, 4)
    depth_y = devs // depth_z
    cores = CORES
    depth_x = grps // cores
    ring = list(range(0, depth_z, 2)) + list(range(1, depth_z, 2))[::-1]

    def shift(by_z, by_y):
        return [
            (
                ring[i] * depth_y + y,
                ring[(i + by_z) % depth_z] * depth_y + (y + by_y) % depth_y,
            )
            for i in range(depth_z)
            for y in range(depth_y)
        ]

    x_shift = [
        (x * cores + c, (x + 1) % depth_x * cores + c) for x in range(depth_x) for c in range(cores)
    ]
    core_swap = [(x * cores + c, x * cores + 1 - c) for x in range(depth_x) for c in range(cores)]

    def round_z(block, *others):
        return lax.ppermute(tie(block, *others), "dev", shift(1, 0))

    def along_y(block, *others):
        return [lax.ppermute(tie(block, *others), "dev", shift(0, ys)) for ys in range(1, depth_y)]

    def along_x(weight, *others):
        blocks = [weight]
        for _ in range(1, depth_x):
            blocks.append(lax.ppermute(tie(blocks[-1], *others), "grp", x_shift))
        return blocks

    def other_core(block, *others):
        return lax.ppermute(tie(block, *others), "grp", core_swap)

    tokens = queries.shape[0]
    width = keys.shape[1]
    groups, span = prefix_keys.shape[:2]

    prefix = jnp.stack([prefix_keys.reshape(-1, width), cached_prefix_values.reshape(-1, width)])
    other = along_y(prefix)
    arriving = round_z(prefix)
    own = jnp.stack([keys, values])
    before = lax.ppermute(own, "dev", [(i, i + 1) for i in range(devs - 1)])
    gate_rows = along_x(w_gate)
    q, before_mask, within_mask, prefix_mask = prepare(
        groups,
        span,
        suffix_lengths,
        request_group,
        placement_order,
        queries,
        width,
    )
    blocks = [(before, before_mask), (own, within_mask), (prefix, prefix_mask)]
    ready, state = [], None
    for zs in range(1, depth_z):
        if zs == depth_z - 1:
            state = attend(q, None, blocks)
            blocks, ready = [], [state[0], gate_swap, *gate_rows[1:]]
        here = tie(arriving, *other, *ready)
        if zs < depth_z - 1:
            arriving, ready = round_z(here), [q, before]
        blocks += [(b, prefix_mask) for b in other + [here]]
        other = along_y(here)
        if zs == 1:
            gate_swap = other_core(w_gate, here)
        elif zs == 2:
            up_swap = other_core(w_up, here)
    state = attend(q, state, blocks)
    down_swap = other_core(w_down, here)
    up_rows = along_x(w_up, *gate_rows[1:], here)
    gates = [w_gate, gate_swap]
    for gate in gate_rows[1:]:
        gates += [gate, other_core(gate, here)]
    hidden_state, *normed = attend_project(
        q,
        state,
        [(b, prefix_mask) for b in other],
        grps,
        out_weight,
        tie(residual, up_swap, down_swap, *gates[2:]),
        norm_gain[None],
    )

    arrived, across = [normed], [[along_y(half) for half in normed]]
    ups, downs, acts = [w_up, up_swap], [w_down, down_swap], {}
    for zs in range(1, depth_z):
        waits = across[zs - 2] if zs > 1 else [[] for _ in normed]
        arrived.append([round_z(half, *wait) for half, wait in zip(arrived[-1], waits)])
        late = arrived[zs][1:]
        if zs == depth_z - 1:
            acts[1] = rise([arrived[1]] + [list(c) for c in zip(*across[1])], gates, ups)
            late = [*late, acts[1]]
        across.append([along_y(half, *late) for half in arrived[zs]])
        if zs == depth_z - 2:
            for up in up_rows[1:]:
                ups += [up, other_core(up, *arrived[zs], *[b for c in across[zs - 1] for b in c])]
            down_cols = along_x(w_down, *up_rows[1:], *arrived[zs], *[b for c in across[zs - 1] for b in c])
    chunks = [[a] + [list(c) for c in zip(*b)] for a, b in zip(arrived, across)]
    each = grps // HALVES
    acts[2] = rise(chunks[2], gates, ups)
    acts[0] = rise(chunks[0], gates, ups)
    soon = [b for c in across[-1] for b in c] + [acts[2], acts[0]]
    sent = [None] * HALVES
    if each <= len(downs):
        sent[0] = round_z(
            fall(acts[1], 1, downs[:each])[0], *arrived[-1], *[b for c in across[-2] for b in c]
        )
        second = fall(acts[2], 1, downs[:each])[0]
        second = (second.astype(F32) + sent[0].astype(F32)).astype(BF16)
        soon.append(second)
        sent[0] = round_z(second)
    final = depth_z - 1
    for down in down_cols[1:]:
        downs += [down, other_core(down, *soon)]

    terms, fallen = [None] * HALVES, {}
    acts[final] = rise(chunks[final], gates, ups)
    fallen[final, 0] = fall(acts[final], depth_y, downs[:each])
    filler = fallen[final, 0][0]
    for zs in list(range(1, depth_z)) + [0]:
        act = acts[zs]
        for half in range(HALVES):
            joint = sent[half] is not None and sent[half].shape[0] > tokens
            if joint and zs < depth_z - 1:
                continue
            parts = fallen.pop((zs, half), None)
            if parts is None:
                parts = fall(act, depth_y, downs[half * each : (half + 1) * each])
            if joint:
                came = [sent[half][i * tokens : (i + 1) * tokens] for i in range(depth_y)]
                parts = [
                    (part.astype(F32) + share.astype(F32)).astype(BF16) if i else part
                    for i, (part, share) in enumerate(zip(parts, came))
                ]
                terms[half] = [parts[0], came[0]]
            else:
                terms[half] = [parts[0]] + ([round_z(sent[half])] if zs != 1 else [])
            if zs == 0:
                parts = [tie(part, sent[0]) for part in parts]
            terms[half] += [
                lax.ppermute(parts[ys], "dev", shift(0, -ys)) for ys in range(1, depth_y)
            ]
            if zs == 1:
                terms[half][0] = tie(terms[half][0], filler)
            if zs:
                sent[half] = functools.reduce(
                    jnp.add, [term.astype(F32) for term in terms[half]]
                ).astype(BF16)
    return finish(grps, hidden_state, terms)


def solution(mesh):
    placed = (
        P(("grp", "dev"), None),
        P(("grp", "dev"), None),
        P(("grp", "dev"), None),
        P(("grp", "dev"), None),
        P("grp", "dev", None),
        P("grp", "dev", None),
        P(),
        P(),
        P("grp", "dev"),
        P("grp", "dev"),
        P("dev", "grp"),
        P("grp", None),
        P("grp", None),
        P("grp", None),
    )
    return jax.shard_map(
        functools.partial(shards, mesh.shape["grp"], mesh.shape["dev"]),
        mesh=mesh,
        in_specs=placed,
        out_specs=P(("grp", "dev"), None),
        check_vma=False,
    )
```

```python
import functools
import math

import jax
import jax.numpy as jnp
from jax import lax
from jax.experimental import pallas as pl
from jax.experimental.pallas import tpu as pltpu
from jax.sharding import PartitionSpec as P

HEAD_SIZE = 64
NEG_FILL = -1e30
EPSILON = 1e-05
F32 = jnp.float32
BF16 = jnp.bfloat16
LANES = 2 * HEAD_SIZE
CORES = 2
HALVES = 2


def cost(microseconds):
    return pl.CostEstimate(flops=0, bytes_accessed=int(microseconds * 3.5e6), transcendentals=0)


def dot(a, b, contract_b=0):
    return lax.dot_general(
        a, b, (((1,), (contract_b,)), ((), ())), preferred_element_type=F32
    )


def prepare_body(
    span,
    lengths_hbm,
    groups_hbm,
    packing_hbm,
    queries_hbm,
    *refs,
):
    q_ref, before_ref, within_ref, prefix_ref = refs[:4]
    lengths_ref, groups_ref, packing_ref, queries_ref, sems = refs[4:]
    copies = [
        pltpu.make_async_copy(source, target, sems.at[i])
        for i, (source, target) in enumerate(
            [
                (lengths_hbm, lengths_ref),
                (groups_hbm, groups_ref),
                (packing_hbm, packing_ref),
                (queries_hbm, queries_ref),
            ]
        )
    ]
    for copy in copies:
        copy.start()
    for copy in copies:
        copy.wait()
    tokens = queries_ref.shape[0]
    pairs, rows = q_ref.shape[0], q_ref.shape[1]
    per = rows // (2 * tokens)
    base = lax.axis_index("dev") * tokens
    own = base + lax.broadcasted_iota(jnp.int32, (tokens, LANES), 0)

    def request(k, carry):
        start, group, first = carry
        j = packing_ref[0, k]
        end = start + lengths_ref[0, j]
        inside = (own >= start) & (own < end)
        return (
            end,
            jnp.where(inside, groups_ref[0, j], group),
            jnp.where(inside, start, first),
        )

    zero = jnp.zeros((tokens, LANES), jnp.int32)
    _, group, first = lax.fori_loop(0, lengths_ref.shape[1], request, (jnp.int32(0), zero, zero))
    for ref, back in ((before_ref, tokens), (within_ref, 0)):
        for c in range(0, tokens, LANES):
            key = base - back + c + lax.broadcasted_iota(jnp.int32, (tokens, LANES), 1)
            ref[:, c : c + LANES] = jnp.where((key >= first) & (key <= own), 0.0, NEG_FILL)
    for c in range(0, prefix_ref.shape[1], LANES):
        key_group = lax.div(c + lax.broadcasted_iota(jnp.int32, (tokens, LANES), 1), span)
        prefix_ref[:, c : c + LANES] = jnp.where(group == key_group, 0.0, NEG_FILL)
    low = lax.broadcasted_iota(jnp.int32, (tokens, LANES), 1) < HEAD_SIZE
    for j in range(pairs):
        for parity in range(2):
            for r in range(per):
                head = (2 * j + parity) * per + r
                block = head // 2
                q = queries_ref[:, block * LANES : (block + 1) * LANES].astype(F32) * HEAD_SIZE ** (-0.5)
                if head % 2 != parity:
                    q = pltpu.roll(q, HEAD_SIZE, 1)
                q = jnp.where(low == (parity == 0), q, 0.0)
                row = (parity * per + r) * tokens
                q_ref[j, row : row + tokens, :] = q.astype(BF16)


def prepare(groups, span, lengths, request_group, packing, queries, width):
    tokens = queries.shape[0]
    per = queries.shape[1] // width
    vmem = pl.BlockSpec(memory_space=pltpu.VMEM)
    return pl.pallas_call(
        functools.partial(prepare_body, span),
        out_shape=[
            jax.ShapeDtypeStruct((width // LANES, 2 * per * tokens, LANES), BF16),
            jax.ShapeDtypeStruct((tokens, tokens), F32),
            jax.ShapeDtypeStruct((tokens, tokens), F32),
            jax.ShapeDtypeStruct((tokens, groups * span), F32),
        ],
        in_specs=[pl.BlockSpec(memory_space=pltpu.HBM)] * 4,
        out_specs=[vmem] * 4,
        compiler_params=pltpu.CompilerParams(vmem_limit_bytes=8 * 2**20),
        scratch_shapes=[pltpu.SMEM(lengths.shape, jnp.int32)] * 3
        + [pltpu.VMEM(queries.shape, BF16), pltpu.SemaphoreType.DMA((4,))],
        cost_estimate=cost(3),
        name="prepare",
    )(lengths, request_group, packing, queries)


def attend_body(first, pieces, refs):
    q_ref, refs = refs[0], refs[1:]
    if not first:
        old_max, old_sum, old_acc = refs[:3]
        refs = refs[3:]
    kv = refs[: 3 * pieces]
    new_max, new_sum, new_acc = refs[-3:]
    pairs, rows = q_ref.shape[0], q_ref.shape[1]
    half = rows // 2
    low = lax.broadcasted_iota(jnp.int32, (half, LANES), 1) < HEAD_SIZE

    def pick(even, odd):
        return jnp.where(low, even, odd)

    for j in range(pairs):
        q = q_ref[j]
        lanes = slice(j * LANES, (j + 1) * LANES)
        scores = []
        for i in range(pieces):
            k_ref, bias_ref = kv[3 * i], kv[3 * i + 2]
            s = dot(q, k_ref[:, lanes], 1)
            keys = s.shape[1]
            bias = bias_ref[...]
            s = s.reshape(rows // bias.shape[0], bias.shape[0], keys) + bias[None]
            scores.append(s.reshape(rows, keys))
        top = functools.reduce(
            jnp.maximum, [jnp.max(s, axis=1, keepdims=True) for s in scores]
        )
        if first:
            row_max = top
            pair_max = pick(row_max[:half], row_max[half:])
        else:
            old = old_max[j]
            pair_max = jnp.maximum(old, pick(top[:half], top[half:]))
            row_max = jnp.concatenate(
                [pair_max[:, :1], pair_max[:, HEAD_SIZE : HEAD_SIZE + 1]], axis=0
            )
        total = None
        for i in range(pieces):
            v_ref = kv[3 * i + 1]
            w = jnp.exp(scores[i] - row_max).astype(BF16)
            v = v_ref[:, lanes]
            v = jnp.concatenate([v, jnp.ones_like(v)], axis=1)
            part = dot(w, v)
            total = part if total is None else total + part
        acc = pick(total[:half, :LANES], total[half:, :LANES])
        summed = pick(total[:half, LANES:], total[half:, LANES:])
        if not first:
            scale = jnp.exp(old - pair_max)
            acc = acc + scale * old_acc[j]
            summed = summed + scale * old_sum[j]
        new_max[j] = pair_max
        new_sum[j] = summed
        new_acc[j] = acc


def block_refs(refs, count):
    return [r for i in range(count) for r in (refs[2 * i].at[0], refs[2 * i].at[1], refs[2 * i + 1])]


def attend(q, state, blocks):
    pairs, rows, lanes = q.shape
    first = state is None

    def kernel(*refs):
        lead = 1 + (0 if first else 3)
        attend_body(first, len(blocks), [*refs[:lead], *block_refs(refs[lead:], len(blocks)), *refs[-3:]])

    shape = jax.ShapeDtypeStruct((pairs, rows // 2, lanes), F32)
    operands = [q] + ([] if first else list(state)) + [a for block in blocks for a in block]
    vmem = pl.BlockSpec(memory_space=pltpu.VMEM)
    return pl.pallas_call(
        kernel,
        out_shape=[shape] * 3,
        in_specs=[vmem] * len(operands),
        out_specs=[vmem] * 3,
        compiler_params=pltpu.CompilerParams(vmem_limit_bytes=(8 + 3 * len(blocks)) * 2**20),
        cost_estimate=cost(1.1 * len(blocks)),
        name="attend",
    )(*operands)


def block_owner(blocks, step):
    chips = blocks // CORES
    me = lax.axis_index("grp")
    x, core = lax.div(me, CORES), lax.rem(me, CORES)
    x = lax.rem(x + chips - step // CORES, chips)
    return x * CORES + lax.rem(core + step % CORES, CORES)


def project_body(
    blocks, sum_ref, acc_ref, weight_ref, residual_ref, gain_ref, hidden_ref, normed_refs, held
):
    pairs, rows, lanes = acc_ref.shape
    tokens = residual_ref.shape[0]
    per = rows // tokens
    hidden = residual_ref[...].astype(F32)
    for j in range(pairs):
        out = (acc_ref[j] / sum_ref[j]).astype(BF16)
        for r in range(0, per, 2):
            left = jnp.concatenate(
                [out[r * tokens : (r + 1) * tokens], out[(r + 1) * tokens : (r + 2) * tokens]], axis=1
            )
            heads = [(2 * j) * per + r, (2 * j + 1) * per + r, (2 * j) * per + r + 1, (2 * j + 1) * per + r + 1]
            right = jnp.concatenate(
                [weight_ref[h * HEAD_SIZE : (h + 1) * HEAD_SIZE, :] for h in heads], axis=0
            )
            hidden = hidden + dot(left, right)
    hidden_ref[...] = hidden
    mean = jnp.mean(hidden * hidden, axis=1, keepdims=True)
    held[...] = hidden * lax.rsqrt(mean + EPSILON) * gain_ref[...]
    width = hidden.shape[1] // blocks
    for b in range(blocks):
        start = pl.multiple_of(block_owner(blocks, b) * width, width)
        half, place = divmod(b, blocks // HALVES)
        normed_refs[half][:, place * width : (place + 1) * width] = held[:, pl.ds(start, width)].astype(BF16)


def attend_project(q, state, blocks, columns, out_weight, residual, gain):
    pairs, rows, lanes = q.shape
    tokens, width = residual.shape
    count = len(blocks)

    def kernel(*refs):
        mine, (weight_ref, residual_ref, gain_ref) = refs[: 4 + 2 * count], refs[4 + 2 * count : 7 + 2 * count]
        hidden_ref, *normed_refs = refs[7 + 2 * count : 8 + 2 * count + HALVES]
        held, top, total, acc = refs[-4:]
        attend_body(False, count, [*mine[:4], *block_refs(mine[4:], count), top, total, acc])
        project_body(
            columns, total, acc, weight_ref, residual_ref, gain_ref, hidden_ref, normed_refs, held
        )

    operands = [q, *state] + [a for block in blocks for a in block]
    vmem = pl.BlockSpec(memory_space=pltpu.VMEM)
    return pl.pallas_call(
        kernel,
        out_shape=[
            jax.ShapeDtypeStruct((tokens, width), F32),
        ]
        + [jax.ShapeDtypeStruct((tokens, width // HALVES), BF16)] * HALVES,
        in_specs=[vmem] * (len(operands) + 3),
        out_specs=[vmem] * (1 + HALVES),
        scratch_shapes=[pltpu.VMEM((tokens, width), F32)]
        + [pltpu.VMEM((pairs, rows // 2, lanes), F32)] * 3,
        compiler_params=pltpu.CompilerParams(vmem_limit_bytes=20 * 2**20),
        cost_estimate=cost(1.1 * count + 2),
        name="attend_project",
    )(*operands, out_weight, residual, gain)


def rise_body(parts, blocks, refs):
    pieces = parts * HALVES
    n_refs, gates, ups = refs[:pieces], refs[pieces : pieces + blocks], refs[pieces + blocks : pieces + 2 * blocks]
    act_ref, x_ref = refs[-2:]
    tokens, width = n_refs[0].shape
    for i in range(parts):
        for half in range(HALVES):
            x_ref[i * tokens : (i + 1) * tokens, half * width : (half + 1) * width] = n_refs[i * HALVES + half][...]
    depth, hidden = gates[0].shape
    tile = math.gcd(hidden, 256)

    @pl.loop(0, hidden // tile)
    def _(t):
        cols = pl.ds(pl.multiple_of(t * tile, tile), tile)
        gate = up = None
        for b in range(blocks):
            x = x_ref[:, b * depth : (b + 1) * depth]
            g, u = dot(x, gates[b][:, cols]), dot(x, ups[b][:, cols])
            gate, up = (g, u) if gate is None else (gate + g, up + u)
        act_ref[:, cols] = (gate / (1.0 + jnp.exp(-gate)) * up).astype(BF16)


def rise(normed, gates, ups):
    parts, blocks = len(normed), len(gates)
    tokens, width = normed[0][0].shape
    hidden = gates[0].shape[1]

    def kernel(*refs):
        rise_body(parts, blocks, refs)

    vmem = pl.BlockSpec(memory_space=pltpu.VMEM)
    return pl.pallas_call(
        kernel,
        out_shape=jax.ShapeDtypeStruct((parts * tokens, hidden), BF16),
        in_specs=[vmem] * (parts * HALVES + 2 * blocks),
        out_specs=vmem,
        scratch_shapes=[pltpu.VMEM((parts * tokens, HALVES * width), BF16)],
        compiler_params=pltpu.CompilerParams(vmem_limit_bytes=12 * 2**20),
        cost_estimate=cost(1.5 * parts),
        name="rise",
    )(*[half for chunk in normed for half in chunk], *gates, *ups)


def fall_body(blocks, refs):
    act_ref, downs, outs = refs[0], refs[1 : 1 + blocks], refs[1 + blocks :]
    rows, width = outs[0].shape[0], downs[0].shape[1]
    tile = math.gcd(width, 256)
    for b in range(blocks):

        @pl.loop(0, width // tile)
        def _(t):
            term = dot(act_ref[...], downs[b][:, pl.ds(pl.multiple_of(t * tile, tile), tile)])
            cols = pl.ds(pl.multiple_of(b * width + t * tile, tile), tile)
            for i, out in enumerate(outs):
                out[:, cols] = term[i * rows : (i + 1) * rows].astype(BF16)


def fall(act, parts, downs):
    blocks = len(downs)
    shape = jax.ShapeDtypeStruct((act.shape[0] // parts, blocks * downs[0].shape[1]), BF16)

    def kernel(*refs):
        fall_body(blocks, refs)

    vmem = pl.BlockSpec(memory_space=pltpu.VMEM)
    return pl.pallas_call(
        kernel,
        out_shape=[shape] * parts,
        in_specs=[vmem] * (1 + blocks),
        out_specs=[vmem] * parts,
        compiler_params=pltpu.CompilerParams(vmem_limit_bytes=12 * 2**20),
        cost_estimate=cost(1.2),
        name="fall",
    )(act, *downs)


def finish_body(blocks, hidden_ref, *refs):
    terms, out_ref = refs[:-1], refs[-1]
    each = len(terms) // HALVES
    width = out_ref.shape[1] // blocks
    for b in range(blocks):
        half, column = divmod(b, blocks // HALVES)
        place = pl.ds(pl.multiple_of(block_owner(blocks, b) * width, width), width)
        total = hidden_ref[:, place]
        for term in terms[half * each : (half + 1) * each]:
            total = total + term[:, column * width : (column + 1) * width].astype(F32)
        out_ref[:, place] = total.astype(BF16)


def finish(blocks, hidden_state, terms):
    vmem = pl.BlockSpec(memory_space=pltpu.VMEM)
    operands = [hidden_state] + [term for half in terms for term in half]
    return pl.pallas_call(
        functools.partial(finish_body, blocks),
        out_shape=jax.ShapeDtypeStruct(hidden_state.shape, BF16),
        in_specs=[vmem] * len(operands),
        out_specs=vmem,
        compiler_params=pltpu.CompilerParams(vmem_limit_bytes=8 * 2**20),
        cost_estimate=cost(1),
        name="finish",
    )(*operands)


def tie(array, *others):
    return lax.optimization_barrier((array, *others))[0] if others else array


def shards(
    grps,
    devs,
    residual,
    queries,
    keys,
    values,
    prefix_keys,
    cached_prefix_values,
    out_weight,
    norm_gain,
    w_gate,
    w_up,
    w_down,
    suffix_lengths,
    request_group,
    placement_order,
):
    depth_z = math.gcd(devs, 4)
    depth_y = devs // depth_z
    cores = CORES
    depth_x = grps // cores
    ring = list(range(0, depth_z, 2)) + list(range(1, depth_z, 2))[::-1]

    def shift(by_z, by_y):
        return [
            (
                ring[i] * depth_y + y,
                ring[(i + by_z) % depth_z] * depth_y + (y + by_y) % depth_y,
            )
            for i in range(depth_z)
            for y in range(depth_y)
        ]

    x_shift = [
        (x * cores + c, (x + 1) % depth_x * cores + c) for x in range(depth_x) for c in range(cores)
    ]
    core_swap = [(x * cores + c, x * cores + 1 - c) for x in range(depth_x) for c in range(cores)]

    def round_z(block, *others):
        return lax.ppermute(tie(block, *others), "dev", shift(1, 0))

    def along_y(block, *others):
        return [lax.ppermute(tie(block, *others), "dev", shift(0, ys)) for ys in range(1, depth_y)]

    def along_x(weight, *others):
        blocks = [weight]
        for _ in range(1, depth_x):
            blocks.append(lax.ppermute(tie(blocks[-1], *others), "grp", x_shift))
        return blocks

    def other_core(block, *others):
        return lax.ppermute(tie(block, *others), "grp", core_swap)

    tokens = queries.shape[0]
    width = keys.shape[1]
    groups, span = prefix_keys.shape[:2]

    prefix = jnp.stack([prefix_keys.reshape(-1, width), cached_prefix_values.reshape(-1, width)])
    other = along_y(prefix)
    arriving = round_z(prefix)
    own = jnp.stack([keys, values])
    before = lax.ppermute(own, "dev", [(i, i + 1) for i in range(devs - 1)])
    gate_rows = along_x(w_gate)
    q, before_mask, within_mask, prefix_mask = prepare(
        groups,
        span,
        suffix_lengths,
        request_group,
        placement_order,
        queries,
        width,
    )
    blocks = [(before, before_mask), (own, within_mask), (prefix, prefix_mask)]
    ready, state = [], None
    for zs in range(1, depth_z):
        if zs == depth_z - 1:
            state = attend(q, None, blocks)
            blocks, ready = [], [state[0], gate_swap, *gate_rows[1:]]
        here = tie(arriving, *other, *ready)
        if zs < depth_z - 1:
            arriving, ready = round_z(here), [q, before]
        blocks += [(b, prefix_mask) for b in other + [here]]
        other = along_y(here)
        if zs == 1:
            gate_swap = other_core(w_gate, here)
        elif zs == 2:
            up_swap = other_core(w_up, here)
    state = attend(q, state, blocks)
    down_swap = other_core(w_down, here)
    up_rows = along_x(w_up, *gate_rows[1:], here)
    gates = [w_gate, gate_swap]
    for gate in gate_rows[1:]:
        gates += [gate, other_core(gate, here)]
    hidden_state, *normed = attend_project(
        q,
        state,
        [(b, prefix_mask) for b in other],
        grps,
        out_weight,
        tie(residual, up_swap, down_swap, *gates[2:]),
        norm_gain[None],
    )

    arrived, across = [normed], [[along_y(half) for half in normed]]
    ups, downs, acts = [w_up, up_swap], [w_down, down_swap], {}
    for zs in range(1, depth_z):
        waits = across[zs - 2] if zs > 1 else [[] for _ in normed]
        arrived.append([round_z(half, *wait) for half, wait in zip(arrived[-1], waits)])
        late = arrived[zs][1:]
        if zs == depth_z - 1:
            acts[1] = rise([arrived[1]] + [list(c) for c in zip(*across[1])], gates, ups)
            late = [*late, acts[1]]
        across.append([along_y(half, *late) for half in arrived[zs]])
        if zs == depth_z - 2:
            for up in up_rows[1:]:
                ups += [up, other_core(up, *arrived[zs], *[b for c in across[zs - 1] for b in c])]
            down_cols = along_x(w_down, *up_rows[1:], *arrived[zs], *[b for c in across[zs - 1] for b in c])
    chunks = [[a] + [list(c) for c in zip(*b)] for a, b in zip(arrived, across)]
    each = grps // HALVES
    acts[2] = rise(chunks[2], gates, ups)
    acts[0] = rise(chunks[0], gates, ups)
    soon = [b for c in across[-1] for b in c] + [acts[2], acts[0]]
    sent = [None] * HALVES
    fallen = {}
    if each <= len(downs):
        sent[0] = round_z(
            fall(acts[1], 1, downs[:each])[0], *arrived[-1], *[b for c in across[-2] for b in c]
        )
        second = fall(acts[2], 1, downs[:each])[0]
        second = (second.astype(F32) + sent[0].astype(F32)).astype(BF16)
        fallen[0, 0] = fall(acts[0], depth_y, downs[:each])
        soon += [second, fallen[0, 0][0]]
        sent[0] = round_z(second)
    final = depth_z - 1
    for down in down_cols[1:]:
        downs += [down, other_core(down, *soon)]

    def over_y(parts):
        return [lax.ppermute(parts[ys], "dev", shift(0, -ys)) for ys in range(1, depth_y)]

    terms = [None] * HALVES
    fallen[2, 1] = fall(acts[2], depth_y, downs[each:])
    if (0, 0) not in fallen:
        fallen[0, 0] = fall(acts[0], depth_y, downs[:each])
    joined = {(0, 0): over_y(fallen[0, 0])}
    chunks[final][0][0] = tie(chunks[final][0][0], fallen[2, 1][0], *joined[0, 0])
    acts[final] = rise(chunks[final], gates, ups)
    fallen[final, 0] = fall(acts[final], depth_y, downs[:each])
    filler = fallen[final, 0][0]
    for zs in list(range(1, depth_z)) + [0]:
        act = acts[zs]
        for half in range(HALVES):
            joint = sent[half] is not None and sent[half].shape[0] > tokens
            if joint and zs < depth_z - 1:
                continue
            parts = fallen.pop((zs, half), None)
            if parts is None:
                parts = fall(act, depth_y, downs[half * each : (half + 1) * each])
            if joint:
                came = [sent[half][i * tokens : (i + 1) * tokens] for i in range(depth_y)]
                parts = [
                    (part.astype(F32) + share.astype(F32)).astype(BF16) if i else part
                    for i, (part, share) in enumerate(zip(parts, came))
                ]
                terms[half] = [parts[0], came[0]]
            else:
                terms[half] = [parts[0]] + ([round_z(sent[half])] if zs != 1 else [])
            if zs == 0:
                parts = [tie(part, sent[0]) for part in parts]
            terms[half] += joined[zs, half] if (zs, half) in joined else over_y(parts)
            if zs == 1:
                terms[half][0] = tie(terms[half][0], filler)
            if zs:
                sent[half] = functools.reduce(
                    jnp.add, [term.astype(F32) for term in terms[half]]
                ).astype(BF16)
    return finish(grps, hidden_state, terms)


def solution(mesh):
    placed = (
        P(("grp", "dev"), None),
        P(("grp", "dev"), None),
        P(("grp", "dev"), None),
        P(("grp", "dev"), None),
        P("grp", "dev", None),
        P("grp", "dev", None),
        P(),
        P(),
        P("grp", "dev"),
        P("grp", "dev"),
        P("dev", "grp"),
        P("grp", None),
        P("grp", None),
        P("grp", None),
    )
    return jax.shard_map(
        functools.partial(shards, mesh.shape["grp"], mesh.shape["dev"]),
        mesh=mesh,
        in_specs=placed,
        out_specs=P(("grp", "dev"), None),
        check_vma=False,
    )
```

```python
import functools
import math

import jax
import jax.numpy as jnp
from jax import lax
from jax.experimental import pallas as pl
from jax.experimental.pallas import tpu as pltpu
from jax.sharding import PartitionSpec as P

HEAD_SIZE = 64
NEG_FILL = -1e30
EPSILON = 1e-05
F32 = jnp.float32
BF16 = jnp.bfloat16
LANES = 2 * HEAD_SIZE
CORES = 2
HALVES = 2


def cost(microseconds):
    return pl.CostEstimate(flops=0, bytes_accessed=int(microseconds * 3.5e6), transcendentals=0)


def dot(a, b, contract_b=0):
    return lax.dot_general(
        a, b, (((1,), (contract_b,)), ((), ())), preferred_element_type=F32
    )


def prepare_body(
    span,
    layout_hbm,
    queries_hbm,
    *refs,
):
    q_ref, before_ref, within_ref, prefix_ref = refs[:4]
    layout_ref, queries_ref, sems = refs[4:]
    copies = [
        pltpu.make_async_copy(source, target, sems.at[i])
        for i, (source, target) in enumerate(
            [
                (layout_hbm, layout_ref),
                (queries_hbm, queries_ref),
            ]
        )
    ]
    for copy in copies:
        copy.start()
    for copy in copies:
        copy.wait()
    tokens = queries_ref.shape[0]
    pairs, rows = q_ref.shape[0], q_ref.shape[1]
    per = rows // (2 * tokens)
    base = lax.axis_index("dev") * tokens
    own = base + lax.broadcasted_iota(jnp.int32, (tokens, LANES), 0)

    def request(k, carry):
        start, group, first = carry
        j = layout_ref[2, k]
        end = start + layout_ref[0, j]
        inside = (own >= start) & (own < end)
        return (
            end,
            jnp.where(inside, layout_ref[1, j], group),
            jnp.where(inside, start, first),
        )

    zero = jnp.zeros((tokens, LANES), jnp.int32)
    _, group, first = lax.fori_loop(0, layout_ref.shape[1], request, (jnp.int32(0), zero, zero))
    for ref, back in ((before_ref, tokens), (within_ref, 0)):
        for c in range(0, tokens, LANES):
            key = base - back + c + lax.broadcasted_iota(jnp.int32, (tokens, LANES), 1)
            ref[:, c : c + LANES] = jnp.where((key >= first) & (key <= own), 0.0, NEG_FILL)
    for c in range(0, prefix_ref.shape[1], LANES):
        key_group = lax.div(c + lax.broadcasted_iota(jnp.int32, (tokens, LANES), 1), span)
        prefix_ref[:, c : c + LANES] = jnp.where(group == key_group, 0.0, NEG_FILL)
    low = lax.broadcasted_iota(jnp.int32, (tokens, LANES), 1) < HEAD_SIZE
    for j in range(pairs):
        for parity in range(2):
            for r in range(per):
                head = (2 * j + parity) * per + r
                block = head // 2
                q = queries_ref[:, block * LANES : (block + 1) * LANES].astype(F32) * HEAD_SIZE ** (-0.5)
                if head % 2 != parity:
                    q = pltpu.roll(q, HEAD_SIZE, 1)
                q = jnp.where(low == (parity == 0), q, 0.0)
                row = (parity * per + r) * tokens
                q_ref[j, row : row + tokens, :] = q.astype(BF16)


def prepare(groups, span, lengths, request_group, packing, queries, width):
    tokens = queries.shape[0]
    layout = jnp.concatenate([lengths, request_group, packing], axis=0)
    per = queries.shape[1] // width
    vmem = pl.BlockSpec(memory_space=pltpu.VMEM)
    return pl.pallas_call(
        functools.partial(prepare_body, span),
        out_shape=[
            jax.ShapeDtypeStruct((width // LANES, 2 * per * tokens, LANES), BF16),
            jax.ShapeDtypeStruct((tokens, tokens), F32),
            jax.ShapeDtypeStruct((tokens, tokens), F32),
            jax.ShapeDtypeStruct((tokens, groups * span), F32),
        ],
        in_specs=[pl.BlockSpec(memory_space=pltpu.HBM)] * 2,
        out_specs=[vmem] * 4,
        compiler_params=pltpu.CompilerParams(vmem_limit_bytes=8 * 2**20),
        scratch_shapes=[
            pltpu.SMEM(layout.shape, jnp.int32),
            pltpu.VMEM(queries.shape, BF16),
            pltpu.SemaphoreType.DMA((2,)),
        ],
        cost_estimate=cost(3),
        name="prepare",
    )(layout, queries)


def attend_body(first, pieces, refs):
    q_ref, refs = refs[0], refs[1:]
    if not first:
        old_max, old_sum, old_acc = refs[:3]
        refs = refs[3:]
    kv = refs[: 3 * pieces]
    new_max, new_sum, new_acc = refs[-3:]
    pairs, rows = q_ref.shape[0], q_ref.shape[1]
    half = rows // 2
    low = lax.broadcasted_iota(jnp.int32, (half, LANES), 1) < HEAD_SIZE

    def pick(even, odd):
        return jnp.where(low, even, odd)

    for j in range(pairs):
        q = q_ref[j]
        lanes = slice(j * LANES, (j + 1) * LANES)
        scores = []
        for i in range(pieces):
            k_ref, bias_ref = kv[3 * i], kv[3 * i + 2]
            s = dot(q, k_ref[:, lanes], 1)
            keys = s.shape[1]
            bias = bias_ref[...]
            s = s.reshape(rows // bias.shape[0], bias.shape[0], keys) + bias[None]
            scores.append(s.reshape(rows, keys))
        top = functools.reduce(
            jnp.maximum, [jnp.max(s, axis=1, keepdims=True) for s in scores]
        )
        if first:
            row_max = top
            pair_max = pick(row_max[:half], row_max[half:])
        else:
            old = old_max[j]
            pair_max = jnp.maximum(old, pick(top[:half], top[half:]))
            row_max = jnp.concatenate(
                [pair_max[:, :1], pair_max[:, HEAD_SIZE : HEAD_SIZE + 1]], axis=0
            )
        total = None
        for i in range(pieces):
            v_ref = kv[3 * i + 1]
            w = jnp.exp(scores[i] - row_max).astype(BF16)
            v = v_ref[:, lanes]
            v = jnp.concatenate([v, jnp.ones_like(v)], axis=1)
            part = dot(w, v)
            total = part if total is None else total + part
        acc = pick(total[:half, :LANES], total[half:, :LANES])
        summed = pick(total[:half, LANES:], total[half:, LANES:])
        if not first:
            scale = jnp.exp(old - pair_max)
            acc = acc + scale * old_acc[j]
            summed = summed + scale * old_sum[j]
        new_max[j] = pair_max
        new_sum[j] = summed
        new_acc[j] = acc


def block_refs(refs, count):
    return [r for i in range(count) for r in (refs[2 * i].at[0], refs[2 * i].at[1], refs[2 * i + 1])]


def attend(q, state, blocks):
    pairs, rows, lanes = q.shape
    first = state is None

    def kernel(*refs):
        lead = 1 + (0 if first else 3)
        attend_body(first, len(blocks), [*refs[:lead], *block_refs(refs[lead:], len(blocks)), *refs[-3:]])

    shape = jax.ShapeDtypeStruct((pairs, rows // 2, lanes), F32)
    operands = [q] + ([] if first else list(state)) + [a for block in blocks for a in block]
    vmem = pl.BlockSpec(memory_space=pltpu.VMEM)
    return pl.pallas_call(
        kernel,
        out_shape=[shape] * 3,
        in_specs=[vmem] * len(operands),
        out_specs=[vmem] * 3,
        compiler_params=pltpu.CompilerParams(vmem_limit_bytes=(8 + 3 * len(blocks)) * 2**20),
        cost_estimate=cost(1.1 * len(blocks)),
        name="attend",
    )(*operands)


def block_owner(blocks, step):
    chips = blocks // CORES
    me = lax.axis_index("grp")
    x, core = lax.div(me, CORES), lax.rem(me, CORES)
    x = lax.rem(x + chips - step // CORES, chips)
    return x * CORES + lax.rem(core + step % CORES, CORES)


def project_body(
    blocks, sum_ref, acc_ref, weight_ref, residual_ref, gain_ref, hidden_ref, normed_refs, held
):
    pairs, rows, lanes = acc_ref.shape
    tokens = residual_ref.shape[0]
    per = rows // tokens
    hidden = residual_ref[...].astype(F32)
    for j in range(pairs):
        out = (acc_ref[j] / sum_ref[j]).astype(BF16)
        for r in range(0, per, 2):
            left = jnp.concatenate(
                [out[r * tokens : (r + 1) * tokens], out[(r + 1) * tokens : (r + 2) * tokens]], axis=1
            )
            heads = [(2 * j) * per + r, (2 * j + 1) * per + r, (2 * j) * per + r + 1, (2 * j + 1) * per + r + 1]
            right = jnp.concatenate(
                [weight_ref[h * HEAD_SIZE : (h + 1) * HEAD_SIZE, :] for h in heads], axis=0
            )
            hidden = hidden + dot(left, right)
    hidden_ref[...] = hidden
    mean = jnp.mean(hidden * hidden, axis=1, keepdims=True)
    held[...] = hidden * lax.rsqrt(mean + EPSILON) * gain_ref[...]
    width = hidden.shape[1] // blocks
    for b in range(blocks):
        start = pl.multiple_of(block_owner(blocks, b) * width, width)
        half, place = divmod(b, blocks // HALVES)
        normed_refs[half][:, place * width : (place + 1) * width] = held[:, pl.ds(start, width)].astype(BF16)


def attend_project(q, state, blocks, columns, out_weight, residual, gain):
    pairs, rows, lanes = q.shape
    tokens, width = residual.shape
    count = len(blocks)

    def kernel(*refs):
        mine, (weight_ref, residual_ref, gain_ref) = refs[: 4 + 2 * count], refs[4 + 2 * count : 7 + 2 * count]
        hidden_ref, *normed_refs = refs[7 + 2 * count : 8 + 2 * count + HALVES]
        held, top, total, acc = refs[-4:]
        attend_body(False, count, [*mine[:4], *block_refs(mine[4:], count), top, total, acc])
        project_body(
            columns, total, acc, weight_ref, residual_ref, gain_ref, hidden_ref, normed_refs, held
        )

    operands = [q, *state] + [a for block in blocks for a in block]
    vmem = pl.BlockSpec(memory_space=pltpu.VMEM)
    return pl.pallas_call(
        kernel,
        out_shape=[
            jax.ShapeDtypeStruct((tokens, width), F32),
        ]
        + [jax.ShapeDtypeStruct((tokens, width // HALVES), BF16)] * HALVES,
        in_specs=[vmem] * (len(operands) + 3),
        out_specs=[vmem] * (1 + HALVES),
        scratch_shapes=[pltpu.VMEM((tokens, width), F32)]
        + [pltpu.VMEM((pairs, rows // 2, lanes), F32)] * 3,
        compiler_params=pltpu.CompilerParams(vmem_limit_bytes=20 * 2**20),
        cost_estimate=cost(1.1 * count + 2),
        name="attend_project",
    )(*operands, out_weight, residual, gain)


def rise_body(parts, blocks, refs):
    pieces = parts * HALVES
    n_refs, gates, ups = refs[:pieces], refs[pieces : pieces + blocks], refs[pieces + blocks : pieces + 2 * blocks]
    act_ref, x_ref = refs[-2:]
    tokens, width = n_refs[0].shape
    for i in range(parts):
        for half in range(HALVES):
            x_ref[i * tokens : (i + 1) * tokens, half * width : (half + 1) * width] = n_refs[i * HALVES + half][...]
    depth, hidden = gates[0].shape
    tile = math.gcd(hidden, 256)

    @pl.loop(0, hidden // tile)
    def _(t):
        cols = pl.ds(pl.multiple_of(t * tile, tile), tile)
        gate = up = None
        for b in range(blocks):
            x = x_ref[:, b * depth : (b + 1) * depth]
            g, u = dot(x, gates[b][:, cols]), dot(x, ups[b][:, cols])
            gate, up = (g, u) if gate is None else (gate + g, up + u)
        act_ref[:, cols] = (gate / (1.0 + jnp.exp(-gate)) * up).astype(BF16)


def rise(normed, gates, ups):
    parts, blocks = len(normed), len(gates)
    tokens, width = normed[0][0].shape
    hidden = gates[0].shape[1]

    def kernel(*refs):
        rise_body(parts, blocks, refs)

    vmem = pl.BlockSpec(memory_space=pltpu.VMEM)
    return pl.pallas_call(
        kernel,
        out_shape=jax.ShapeDtypeStruct((parts * tokens, hidden), BF16),
        in_specs=[vmem] * (parts * HALVES + 2 * blocks),
        out_specs=vmem,
        scratch_shapes=[pltpu.VMEM((parts * tokens, HALVES * width), BF16)],
        compiler_params=pltpu.CompilerParams(vmem_limit_bytes=12 * 2**20),
        cost_estimate=cost(1.5 * parts),
        name="rise",
    )(*[half for chunk in normed for half in chunk], *gates, *ups)


def fall_body(blocks, refs):
    act_ref, downs, outs = refs[0], refs[1 : 1 + blocks], refs[1 + blocks :]
    rows, width = outs[0].shape[0], downs[0].shape[1]
    tile = math.gcd(width, 256)
    for b in range(blocks):

        @pl.loop(0, width // tile)
        def _(t):
            term = dot(act_ref[...], downs[b][:, pl.ds(pl.multiple_of(t * tile, tile), tile)])
            cols = pl.ds(pl.multiple_of(b * width + t * tile, tile), tile)
            for i, out in enumerate(outs):
                out[:, cols] = term[i * rows : (i + 1) * rows].astype(BF16)


def fall(act, parts, downs):
    blocks = len(downs)
    shape = jax.ShapeDtypeStruct((act.shape[0] // parts, blocks * downs[0].shape[1]), BF16)

    def kernel(*refs):
        fall_body(blocks, refs)

    vmem = pl.BlockSpec(memory_space=pltpu.VMEM)
    return pl.pallas_call(
        kernel,
        out_shape=[shape] * parts,
        in_specs=[vmem] * (1 + blocks),
        out_specs=[vmem] * parts,
        compiler_params=pltpu.CompilerParams(vmem_limit_bytes=12 * 2**20),
        cost_estimate=cost(1.2),
        name="fall",
    )(act, *downs)


def finish_body(blocks, hidden_ref, *refs):
    terms, out_ref = refs[:-1], refs[-1]
    each = len(terms) // HALVES
    width = out_ref.shape[1] // blocks
    for b in range(blocks):
        half, column = divmod(b, blocks // HALVES)
        place = pl.ds(pl.multiple_of(block_owner(blocks, b) * width, width), width)
        total = hidden_ref[:, place]
        for term in terms[half * each : (half + 1) * each]:
            total = total + term[:, column * width : (column + 1) * width].astype(F32)
        out_ref[:, place] = total.astype(BF16)


def finish(blocks, hidden_state, terms):
    vmem = pl.BlockSpec(memory_space=pltpu.VMEM)
    operands = [hidden_state] + [term for half in terms for term in half]
    return pl.pallas_call(
        functools.partial(finish_body, blocks),
        out_shape=jax.ShapeDtypeStruct(hidden_state.shape, BF16),
        in_specs=[vmem] * len(operands),
        out_specs=vmem,
        compiler_params=pltpu.CompilerParams(vmem_limit_bytes=8 * 2**20),
        cost_estimate=cost(1),
        name="finish",
    )(*operands)


def tie(array, *others):
    return lax.optimization_barrier((array, *others))[0] if others else array


def shards(
    grps,
    devs,
    residual,
    queries,
    keys,
    values,
    prefix_keys,
    cached_prefix_values,
    out_weight,
    norm_gain,
    w_gate,
    w_up,
    w_down,
    suffix_lengths,
    request_group,
    placement_order,
):
    depth_z = math.gcd(devs, 4)
    depth_y = devs // depth_z
    cores = CORES
    depth_x = grps // cores
    ring = list(range(0, depth_z, 2)) + list(range(1, depth_z, 2))[::-1]

    def shift(by_z, by_y):
        return [
            (
                ring[i] * depth_y + y,
                ring[(i + by_z) % depth_z] * depth_y + (y + by_y) % depth_y,
            )
            for i in range(depth_z)
            for y in range(depth_y)
        ]

    x_shift = [
        (x * cores + c, (x + 1) % depth_x * cores + c) for x in range(depth_x) for c in range(cores)
    ]
    core_swap = [(x * cores + c, x * cores + 1 - c) for x in range(depth_x) for c in range(cores)]

    def round_z(block, *others):
        return lax.ppermute(tie(block, *others), "dev", shift(1, 0))

    def along_y(block, *others):
        return [lax.ppermute(tie(block, *others), "dev", shift(0, ys)) for ys in range(1, depth_y)]

    def along_x(weight, *others):
        blocks = [weight]
        for _ in range(1, depth_x):
            blocks.append(lax.ppermute(tie(blocks[-1], *others), "grp", x_shift))
        return blocks

    def other_core(block, *others):
        return lax.ppermute(tie(block, *others), "grp", core_swap)

    tokens = queries.shape[0]
    width = keys.shape[1]
    groups, span = prefix_keys.shape[:2]

    prefix = jnp.stack([prefix_keys.reshape(-1, width), cached_prefix_values.reshape(-1, width)])
    other = along_y(prefix)
    arriving = round_z(prefix)
    own = jnp.stack([keys, values])
    before = lax.ppermute(own, "dev", [(i, i + 1) for i in range(devs - 1)])
    gate_rows = along_x(w_gate)
    q, before_mask, within_mask, prefix_mask = prepare(
        groups,
        span,
        suffix_lengths,
        request_group,
        placement_order,
        queries,
        width,
    )
    blocks = [(before, before_mask), (own, within_mask), (prefix, prefix_mask)]
    ready, state = [], None
    for zs in range(1, depth_z):
        if zs == depth_z - 1:
            state = attend(q, None, blocks)
            blocks, ready = [], [state[0], gate_swap, *gate_rows[1:]]
        here = tie(arriving, *other, *ready)
        if zs < depth_z - 1:
            arriving, ready = round_z(here), [before]
        blocks += [(b, prefix_mask) for b in other + [here]]
        other = along_y(here)
        if zs == 1:
            gate_swap = other_core(w_gate, here)
        elif zs == 2:
            up_swap = other_core(w_up, here)
    state = attend(q, state, blocks)
    down_swap = other_core(w_down, here)
    up_rows = along_x(w_up, *gate_rows[1:], here)
    gates = [w_gate, gate_swap]
    for gate in gate_rows[1:]:
        gates += [gate, other_core(gate, here)]
    hidden_state, *normed = attend_project(
        q,
        state,
        [(b, prefix_mask) for b in other],
        grps,
        out_weight,
        tie(residual, up_swap, down_swap, *gates[2:]),
        norm_gain[None],
    )

    arrived, across = [normed], [[along_y(half) for half in normed]]
    ups, downs, acts = [w_up, up_swap], [w_down, down_swap], {}
    for zs in range(1, depth_z):
        waits = across[zs - 2] if zs > 1 else [[] for _ in normed]
        arrived.append([round_z(half, *wait) for half, wait in zip(arrived[-1], waits)])
        late = arrived[zs][1:]
        if zs == depth_z - 1:
            acts[1] = rise([arrived[1]] + [list(c) for c in zip(*across[1])], gates, ups)
            late = [*late, acts[1]]
        across.append([along_y(half, *late) for half in arrived[zs]])
        if zs == depth_z - 2:
            for up in up_rows[1:]:
                ups += [up, other_core(up, *arrived[zs], *[b for c in across[zs - 1] for b in c])]
            down_cols = along_x(w_down, *up_rows[1:], *arrived[zs], *[b for c in across[zs - 1] for b in c])
    chunks = [[a] + [list(c) for c in zip(*b)] for a, b in zip(arrived, across)]
    each = grps // HALVES
    acts[2] = rise(chunks[2], gates, ups)
    acts[0] = rise(chunks[0], gates, ups)
    soon = [b for c in across[-1] for b in c] + [acts[2], acts[0]]
    sent = [None] * HALVES
    if each <= len(downs):
        sent[0] = round_z(
            fall(acts[1], 1, downs[:each])[0], *arrived[-1], *[b for c in across[-2] for b in c]
        )
        second = fall(acts[2], 1, downs[:each])[0]
        second = (second.astype(F32) + sent[0].astype(F32)).astype(BF16)
        soon.append(second)
        sent[0] = round_z(second)
    final = depth_z - 1
    for down in down_cols[1:]:
        downs += [down, other_core(down, *soon)]

    terms, fallen = [None] * HALVES, {}
    acts[final] = rise(chunks[final], gates, ups)
    fallen[final, 0] = fall(acts[final], depth_y, downs[:each])
    filler = fallen[final, 0][0]
    for zs in list(range(1, depth_z)) + [0]:
        act = acts[zs]
        for half in range(HALVES):
            joint = sent[half] is not None and sent[half].shape[0] > tokens
            if joint and zs < depth_z - 1:
                continue
            parts = fallen.pop((zs, half), None)
            if parts is None:
                parts = fall(act, depth_y, downs[half * each : (half + 1) * each])
            if joint:
                came = [sent[half][i * tokens : (i + 1) * tokens] for i in range(depth_y)]
                parts = [
                    (part.astype(F32) + share.astype(F32)).astype(BF16) if i else part
                    for i, (part, share) in enumerate(zip(parts, came))
                ]
                terms[half] = [parts[0], came[0]]
            else:
                terms[half] = [parts[0]] + ([round_z(sent[half])] if zs != 1 else [])
            if zs == 0:
                parts = [tie(part, sent[0]) for part in parts]
            terms[half] += [
                lax.ppermute(parts[ys], "dev", shift(0, -ys)) for ys in range(1, depth_y)
            ]
            if zs == 1:
                terms[half][0] = tie(terms[half][0], filler)
            if zs:
                sent[half] = functools.reduce(
                    jnp.add, [term.astype(F32) for term in terms[half]]
                ).astype(BF16)
    return finish(grps, hidden_state, terms)


def solution(mesh):
    placed = (
        P(("grp", "dev"), None),
        P(("grp", "dev"), None),
        P(("grp", "dev"), None),
        P(("grp", "dev"), None),
        P("grp", "dev", None),
        P("grp", "dev", None),
        P(),
        P(),
        P("grp", "dev"),
        P("grp", "dev"),
        P("dev", "grp"),
        P("grp", None),
        P("grp", None),
        P("grp", None),
    )
    return jax.shard_map(
        functools.partial(shards, mesh.shape["grp"], mesh.shape["dev"]),
        mesh=mesh,
        in_specs=placed,
        out_specs=P(("grp", "dev"), None),
        check_vma=False,
    )
```

```python
import functools
import math

import jax
import jax.numpy as jnp
from jax import lax
from jax.experimental import pallas as pl
from jax.experimental.pallas import tpu as pltpu
from jax.sharding import PartitionSpec as P

HEAD_SIZE = 64
NEG_FILL = -1e30
EPSILON = 1e-05
F32 = jnp.float32
BF16 = jnp.bfloat16
LANES = 2 * HEAD_SIZE
CORES = 2
HALVES = 2


def cost(microseconds):
    return pl.CostEstimate(flops=0, bytes_accessed=int(microseconds * 3.5e6), transcendentals=0)


def dot(a, b, contract_b=0):
    return lax.dot_general(
        a, b, (((1,), (contract_b,)), ((), ())), preferred_element_type=F32
    )


def prepare_body(
    span,
    layout_hbm,
    queries_hbm,
    *refs,
):
    q_ref, before_ref, within_ref, prefix_ref = refs[:4]
    layout_ref, queries_ref, sems = refs[4:]
    copies = [
        pltpu.make_async_copy(source, target, sems.at[i])
        for i, (source, target) in enumerate(
            [
                (layout_hbm, layout_ref),
                (queries_hbm, queries_ref),
            ]
        )
    ]
    for copy in copies:
        copy.start()
    for copy in copies:
        copy.wait()
    tokens = queries_ref.shape[0]
    pairs, rows = q_ref.shape[0], q_ref.shape[1]
    per = rows // (2 * tokens)
    base = lax.axis_index("dev") * tokens
    own = base + lax.broadcasted_iota(jnp.int32, (tokens, LANES), 0)

    def request(k, carry):
        start, group, first = carry
        j = layout_ref[2, k]
        end = start + layout_ref[0, j]
        inside = (own >= start) & (own < end)
        return (
            end,
            jnp.where(inside, layout_ref[1, j], group),
            jnp.where(inside, start, first),
        )

    zero = jnp.zeros((tokens, LANES), jnp.int32)
    _, group, first = lax.fori_loop(0, layout_ref.shape[1], request, (jnp.int32(0), zero, zero))
    for ref, back in ((before_ref, tokens), (within_ref, 0)):
        for c in range(0, tokens, LANES):
            key = base - back + c + lax.broadcasted_iota(jnp.int32, (tokens, LANES), 1)
            ref[:, c : c + LANES] = jnp.where((key >= first) & (key <= own), 0.0, NEG_FILL)
    for c in range(0, prefix_ref.shape[1], LANES):
        key_group = lax.div(c + lax.broadcasted_iota(jnp.int32, (tokens, LANES), 1), span)
        prefix_ref[:, c : c + LANES] = jnp.where(group == key_group, 0.0, NEG_FILL)
    low = lax.broadcasted_iota(jnp.int32, (tokens, LANES), 1) < HEAD_SIZE
    for j in range(pairs):
        for parity in range(2):
            for r in range(per):
                head = (2 * j + parity) * per + r
                block = head // 2
                q = queries_ref[:, block * LANES : (block + 1) * LANES].astype(F32) * HEAD_SIZE ** (-0.5)
                if head % 2 != parity:
                    q = pltpu.roll(q, HEAD_SIZE, 1)
                q = jnp.where(low == (parity == 0), q, 0.0)
                row = (parity * per + r) * tokens
                q_ref[j, row : row + tokens, :] = q.astype(BF16)


def prepare(groups, span, lengths, request_group, packing, queries, width):
    tokens = queries.shape[0]
    layout = jnp.concatenate([lengths, request_group, packing], axis=0)
    per = queries.shape[1] // width
    vmem = pl.BlockSpec(memory_space=pltpu.VMEM)
    return pl.pallas_call(
        functools.partial(prepare_body, span),
        out_shape=[
            jax.ShapeDtypeStruct((width // LANES, 2 * per * tokens, LANES), BF16),
            jax.ShapeDtypeStruct((tokens, tokens), F32),
            jax.ShapeDtypeStruct((tokens, tokens), F32),
            jax.ShapeDtypeStruct((tokens, groups * span), F32),
        ],
        in_specs=[pl.BlockSpec(memory_space=pltpu.HBM)] * 2,
        out_specs=[vmem] * 4,
        compiler_params=pltpu.CompilerParams(vmem_limit_bytes=8 * 2**20),
        scratch_shapes=[
            pltpu.SMEM(layout.shape, jnp.int32),
            pltpu.VMEM(queries.shape, BF16),
            pltpu.SemaphoreType.DMA((2,)),
        ],
        cost_estimate=cost(3),
        name="prepare",
    )(layout, queries)


def attend_body(first, pieces, refs):
    q_ref, refs = refs[0], refs[1:]
    if not first:
        old_max, old_sum, old_acc = refs[:3]
        refs = refs[3:]
    kv = refs[: 3 * pieces]
    new_max, new_sum, new_acc = refs[-3:]
    pairs, rows = q_ref.shape[0], q_ref.shape[1]
    half = rows // 2
    low = lax.broadcasted_iota(jnp.int32, (half, LANES), 1) < HEAD_SIZE

    def pick(even, odd):
        return jnp.where(low, even, odd)

    for j in range(pairs):
        q = q_ref[j]
        lanes = slice(j * LANES, (j + 1) * LANES)
        scores = []
        for i in range(pieces):
            k_ref, bias_ref = kv[3 * i], kv[3 * i + 2]
            s = dot(q, k_ref[:, lanes], 1)
            keys = s.shape[1]
            bias = bias_ref[...]
            s = s.reshape(rows // bias.shape[0], bias.shape[0], keys) + bias[None]
            scores.append(s.reshape(rows, keys))
        top = functools.reduce(
            jnp.maximum, [jnp.max(s, axis=1, keepdims=True) for s in scores]
        )
        if first:
            row_max = top
            pair_max = pick(row_max[:half], row_max[half:])
        else:
            old = old_max[j]
            pair_max = jnp.maximum(old, pick(top[:half], top[half:]))
            row_max = jnp.concatenate(
                [pair_max[:, :1], pair_max[:, HEAD_SIZE : HEAD_SIZE + 1]], axis=0
            )
        total = None
        for i in range(pieces):
            v_ref = kv[3 * i + 1]
            w = jnp.exp(scores[i] - row_max).astype(BF16)
            v = v_ref[:, lanes]
            v = jnp.concatenate([v, jnp.ones_like(v)], axis=1)
            part = dot(w, v)
            total = part if total is None else total + part
        acc = pick(total[:half, :LANES], total[half:, :LANES])
        summed = pick(total[:half, LANES:], total[half:, LANES:])
        if not first:
            scale = jnp.exp(old - pair_max)
            acc = acc + scale * old_acc[j]
            summed = summed + scale * old_sum[j]
        new_max[j] = pair_max
        new_sum[j] = summed
        new_acc[j] = acc


def block_refs(refs, count):
    return [r for i in range(count) for r in (refs[2 * i].at[0], refs[2 * i].at[1], refs[2 * i + 1])]


def attend(q, state, blocks):
    pairs, rows, lanes = q.shape
    first = state is None

    def kernel(*refs):
        lead = 1 + (0 if first else 3)
        attend_body(first, len(blocks), [*refs[:lead], *block_refs(refs[lead:], len(blocks)), *refs[-3:]])

    shape = jax.ShapeDtypeStruct((pairs, rows // 2, lanes), F32)
    operands = [q] + ([] if first else list(state)) + [a for block in blocks for a in block]
    vmem = pl.BlockSpec(memory_space=pltpu.VMEM)
    return pl.pallas_call(
        kernel,
        out_shape=[shape] * 3,
        in_specs=[vmem] * len(operands),
        out_specs=[vmem] * 3,
        compiler_params=pltpu.CompilerParams(vmem_limit_bytes=(8 + 3 * len(blocks)) * 2**20),
        cost_estimate=cost(1.1 * len(blocks)),
        name="attend",
    )(*operands)


def block_owner(blocks, step):
    chips = blocks // CORES
    me = lax.axis_index("grp")
    x, core = lax.div(me, CORES), lax.rem(me, CORES)
    x = lax.rem(x + chips - step // CORES, chips)
    return x * CORES + lax.rem(core + step % CORES, CORES)


def project_body(
    blocks, sum_ref, acc_ref, weight_ref, residual_ref, gain_ref, hidden_ref, normed_refs, held
):
    pairs, rows, lanes = acc_ref.shape
    tokens = residual_ref.shape[0]
    per = rows // tokens
    hidden = residual_ref[...].astype(F32)
    for j in range(pairs):
        out = (acc_ref[j] / sum_ref[j]).astype(BF16)
        for r in range(0, per, 2):
            left = jnp.concatenate(
                [out[r * tokens : (r + 1) * tokens], out[(r + 1) * tokens : (r + 2) * tokens]], axis=1
            )
            heads = [(2 * j) * per + r, (2 * j + 1) * per + r, (2 * j) * per + r + 1, (2 * j + 1) * per + r + 1]
            right = jnp.concatenate(
                [weight_ref[h * HEAD_SIZE : (h + 1) * HEAD_SIZE, :] for h in heads], axis=0
            )
            hidden = hidden + dot(left, right)
    hidden_ref[...] = hidden
    mean = jnp.mean(hidden * hidden, axis=1, keepdims=True)
    held[...] = hidden * lax.rsqrt(mean + EPSILON) * gain_ref[...]
    width = hidden.shape[1] // blocks
    for b in range(blocks):
        start = pl.multiple_of(block_owner(blocks, b) * width, width)
        half, place = divmod(b, blocks // HALVES)
        normed_refs[half][:, place * width : (place + 1) * width] = held[:, pl.ds(start, width)].astype(BF16)


def attend_project(q, state, blocks, columns, out_weight, residual, gain):
    pairs, rows, lanes = q.shape
    tokens, width = residual.shape
    count = len(blocks)

    def kernel(*refs):
        mine, (weight_ref, residual_ref, gain_ref) = refs[: 4 + 2 * count], refs[4 + 2 * count : 7 + 2 * count]
        hidden_ref, *normed_refs = refs[7 + 2 * count : 8 + 2 * count + HALVES]
        held, top, total, acc = refs[-4:]
        attend_body(False, count, [*mine[:4], *block_refs(mine[4:], count), top, total, acc])
        project_body(
            columns, total, acc, weight_ref, residual_ref, gain_ref, hidden_ref, normed_refs, held
        )

    operands = [q, *state] + [a for block in blocks for a in block]
    vmem = pl.BlockSpec(memory_space=pltpu.VMEM)
    return pl.pallas_call(
        kernel,
        out_shape=[
            jax.ShapeDtypeStruct((tokens, width), F32),
        ]
        + [jax.ShapeDtypeStruct((tokens, width // HALVES), BF16)] * HALVES,
        in_specs=[vmem] * (len(operands) + 3),
        out_specs=[vmem] * (1 + HALVES),
        scratch_shapes=[pltpu.VMEM((tokens, width), F32)]
        + [pltpu.VMEM((pairs, rows // 2, lanes), F32)] * 3,
        compiler_params=pltpu.CompilerParams(vmem_limit_bytes=20 * 2**20),
        cost_estimate=cost(1.1 * count + 2),
        name="attend_project",
    )(*operands, out_weight, residual, gain)


def rise_body(parts, blocks, refs):
    pieces = parts * HALVES
    n_refs, gates, ups = refs[:pieces], refs[pieces : pieces + blocks], refs[pieces + blocks : pieces + 2 * blocks]
    act_ref, x_ref = refs[-2:]
    tokens, width = n_refs[0].shape
    for i in range(parts):
        for half in range(HALVES):
            x_ref[i * tokens : (i + 1) * tokens, half * width : (half + 1) * width] = n_refs[i * HALVES + half][...]
    depth, hidden = gates[0].shape
    tile = math.gcd(hidden, 256)

    @pl.loop(0, hidden // tile)
    def _(t):
        cols = pl.ds(pl.multiple_of(t * tile, tile), tile)
        gate = up = None
        for b in range(blocks):
            x = x_ref[:, b * depth : (b + 1) * depth]
            g, u = dot(x, gates[b][:, cols]), dot(x, ups[b][:, cols])
            gate, up = (g, u) if gate is None else (gate + g, up + u)
        act_ref[:, cols] = (gate / (1.0 + jnp.exp(-gate)) * up).astype(BF16)


def rise(normed, gates, ups):
    parts, blocks = len(normed), len(gates)
    tokens, width = normed[0][0].shape
    hidden = gates[0].shape[1]

    def kernel(*refs):
        rise_body(parts, blocks, refs)

    vmem = pl.BlockSpec(memory_space=pltpu.VMEM)
    return pl.pallas_call(
        kernel,
        out_shape=jax.ShapeDtypeStruct((parts * tokens, hidden), BF16),
        in_specs=[vmem] * (parts * HALVES + 2 * blocks),
        out_specs=vmem,
        scratch_shapes=[pltpu.VMEM((parts * tokens, HALVES * width), BF16)],
        compiler_params=pltpu.CompilerParams(vmem_limit_bytes=12 * 2**20),
        cost_estimate=cost(1.5 * parts),
        name="rise",
    )(*[half for chunk in normed for half in chunk], *gates, *ups)


def fall_body(blocks, refs):
    act_ref, downs, outs = refs[0], refs[1 : 1 + blocks], refs[1 + blocks :]
    rows, width = outs[0].shape[0], downs[0].shape[1]
    tile = math.gcd(width, 256)
    for b in range(blocks):

        @pl.loop(0, width // tile)
        def _(t):
            term = dot(act_ref[...], downs[b][:, pl.ds(pl.multiple_of(t * tile, tile), tile)])
            cols = pl.ds(pl.multiple_of(b * width + t * tile, tile), tile)
            for i, out in enumerate(outs):
                out[:, cols] = term[i * rows : (i + 1) * rows].astype(BF16)


def fall(act, parts, downs):
    blocks = len(downs)
    shape = jax.ShapeDtypeStruct((act.shape[0] // parts, blocks * downs[0].shape[1]), BF16)

    def kernel(*refs):
        fall_body(blocks, refs)

    vmem = pl.BlockSpec(memory_space=pltpu.VMEM)
    return pl.pallas_call(
        kernel,
        out_shape=[shape] * parts,
        in_specs=[vmem] * (1 + blocks),
        out_specs=[vmem] * parts,
        compiler_params=pltpu.CompilerParams(vmem_limit_bytes=12 * 2**20),
        cost_estimate=cost(1.2),
        name="fall",
    )(act, *downs)


def finish_body(blocks, hidden_ref, *refs):
    terms, out_ref = refs[:-1], refs[-1]
    each = len(terms) // HALVES
    width = out_ref.shape[1] // blocks
    for b in range(blocks):
        half, column = divmod(b, blocks // HALVES)
        place = pl.ds(pl.multiple_of(block_owner(blocks, b) * width, width), width)
        total = hidden_ref[:, place]
        for term in terms[half * each : (half + 1) * each]:
            total = total + term[:, column * width : (column + 1) * width].astype(F32)
        out_ref[:, place] = total.astype(BF16)


def finish(blocks, hidden_state, terms):
    vmem = pl.BlockSpec(memory_space=pltpu.VMEM)
    operands = [hidden_state] + [term for half in terms for term in half]
    return pl.pallas_call(
        functools.partial(finish_body, blocks),
        out_shape=jax.ShapeDtypeStruct(hidden_state.shape, BF16),
        in_specs=[vmem] * len(operands),
        out_specs=vmem,
        compiler_params=pltpu.CompilerParams(vmem_limit_bytes=8 * 2**20),
        cost_estimate=cost(1),
        name="finish",
    )(*operands)


def tie(array, *others):
    return lax.optimization_barrier((array, *others))[0] if others else array


def shards(
    grps,
    devs,
    residual,
    queries,
    keys,
    values,
    prefix_keys,
    cached_prefix_values,
    out_weight,
    norm_gain,
    w_gate,
    w_up,
    w_down,
    suffix_lengths,
    request_group,
    placement_order,
):
    depth_z = math.gcd(devs, 4)
    depth_y = devs // depth_z
    cores = CORES
    depth_x = grps // cores
    ring = list(range(0, depth_z, 2)) + list(range(1, depth_z, 2))[::-1]

    def shift(by_z, by_y):
        return [
            (
                ring[i] * depth_y + y,
                ring[(i + by_z) % depth_z] * depth_y + (y + by_y) % depth_y,
            )
            for i in range(depth_z)
            for y in range(depth_y)
        ]

    x_shift = [
        (x * cores + c, (x + 1) % depth_x * cores + c) for x in range(depth_x) for c in range(cores)
    ]
    core_swap = [(x * cores + c, x * cores + 1 - c) for x in range(depth_x) for c in range(cores)]

    def round_z(block, *others):
        return lax.ppermute(tie(block, *others), "dev", shift(1, 0))

    def along_y(block, *others):
        return [lax.ppermute(tie(block, *others), "dev", shift(0, ys)) for ys in range(1, depth_y)]

    def along_x(weight, *others):
        blocks = [weight]
        for _ in range(1, depth_x):
            blocks.append(lax.ppermute(tie(blocks[-1], *others), "grp", x_shift))
        return blocks

    def other_core(block, *others):
        return lax.ppermute(tie(block, *others), "grp", core_swap)

    tokens = queries.shape[0]
    width = keys.shape[1]
    groups, span = prefix_keys.shape[:2]

    prefix = jnp.stack([prefix_keys.reshape(-1, width), cached_prefix_values.reshape(-1, width)])
    other = along_y(prefix)
    arriving = round_z(prefix)
    own = jnp.stack([keys, values])
    before = lax.ppermute(own, "dev", [(i, i + 1) for i in range(devs - 1)])
    gate_rows = along_x(w_gate)
    q, before_mask, within_mask, prefix_mask = prepare(
        groups,
        span,
        suffix_lengths,
        request_group,
        placement_order,
        queries,
        width,
    )
    blocks = [(before, before_mask), (own, within_mask), (prefix, prefix_mask)]
    ready, state = [before], None
    for zs in range(1, depth_z):
        if zs == depth_z - 1:
            state = attend(q, None, blocks)
            blocks, ready = [], [state[0], gate_swap, *gate_rows[1:]]
        here = tie(arriving, *other, *ready)
        if zs < depth_z - 1:
            arriving, ready = round_z(here), [q]
        blocks += [(b, prefix_mask) for b in other + [here]]
        other = along_y(here)
        if zs == 1:
            gate_swap = other_core(w_gate, here)
        elif zs == 2:
            up_swap = other_core(w_up, here)
    state = attend(q, state, blocks)
    down_swap = other_core(w_down, here)
    up_rows = along_x(w_up, *gate_rows[1:], here)
    gates = [w_gate, gate_swap]
    for gate in gate_rows[1:]:
        gates += [gate, other_core(gate, here)]
    hidden_state, *normed = attend_project(
        q,
        state,
        [(b, prefix_mask) for b in other],
        grps,
        out_weight,
        tie(residual, up_swap, down_swap, *gates[2:]),
        norm_gain[None],
    )

    arrived, across = [normed], [[along_y(half) for half in normed]]
    ups, downs, acts = [w_up, up_swap], [w_down, down_swap], {}
    for zs in range(1, depth_z):
        waits = across[zs - 2] if zs > 1 else [[] for _ in normed]
        arrived.append([round_z(half, *wait) for half, wait in zip(arrived[-1], waits)])
        late = arrived[zs][1:]
        if zs == depth_z - 1:
            acts[1] = rise([arrived[1]] + [list(c) for c in zip(*across[1])], gates, ups)
            late = [*late, acts[1]]
        across.append([along_y(half, *late) for half in arrived[zs]])
        if zs == depth_z - 2:
            for up in up_rows[1:]:
                ups += [up, other_core(up, *arrived[zs], *[b for c in across[zs - 1] for b in c])]
            down_cols = along_x(w_down, *up_rows[1:], *arrived[zs], *[b for c in across[zs - 1] for b in c])
    chunks = [[a] + [list(c) for c in zip(*b)] for a, b in zip(arrived, across)]
    each = grps // HALVES
    acts[2] = rise(chunks[2], gates, ups)
    acts[0] = rise(chunks[0], gates, ups)
    soon = [b for c in across[-1] for b in c] + [acts[2], acts[0]]
    sent = [None] * HALVES
    if each <= len(downs):
        sent[0] = round_z(
            fall(acts[1], 1, downs[:each])[0], *arrived[-1], *[b for c in across[-2] for b in c]
        )
        second = fall(acts[2], 1, downs[:each])[0]
        second = (second.astype(F32) + sent[0].astype(F32)).astype(BF16)
        soon.append(second)
        sent[0] = round_z(second)
    final = depth_z - 1
    for down in down_cols[1:]:
        downs += [down, other_core(down, *soon)]

    terms, fallen = [None] * HALVES, {}
    acts[final] = rise(chunks[final], gates, ups)
    fallen[final, 0] = fall(acts[final], depth_y, downs[:each])
    filler = fallen[final, 0][0]
    for zs in list(range(1, depth_z)) + [0]:
        act = acts[zs]
        for half in range(HALVES):
            joint = sent[half] is not None and sent[half].shape[0] > tokens
            if joint and zs < depth_z - 1:
                continue
            parts = fallen.pop((zs, half), None)
            if parts is None:
                parts = fall(act, depth_y, downs[half * each : (half + 1) * each])
            if joint:
                came = [sent[half][i * tokens : (i + 1) * tokens] for i in range(depth_y)]
                parts = [
                    (part.astype(F32) + share.astype(F32)).astype(BF16) if i else part
                    for i, (part, share) in enumerate(zip(parts, came))
                ]
                terms[half] = [parts[0], came[0]]
            else:
                terms[half] = [parts[0]] + ([round_z(sent[half])] if zs != 1 else [])
            if zs == 0:
                parts = [tie(part, sent[0]) for part in parts]
            terms[half] += [
                lax.ppermute(parts[ys], "dev", shift(0, -ys)) for ys in range(1, depth_y)
            ]
            if zs == 1:
                terms[half][0] = tie(terms[half][0], filler)
            if zs:
                sent[half] = functools.reduce(
                    jnp.add, [term.astype(F32) for term in terms[half]]
                ).astype(BF16)
    return finish(grps, hidden_state, terms)


def solution(mesh):
    placed = (
        P(("grp", "dev"), None),
        P(("grp", "dev"), None),
        P(("grp", "dev"), None),
        P(("grp", "dev"), None),
        P("grp", "dev", None),
        P("grp", "dev", None),
        P(),
        P(),
        P("grp", "dev"),
        P("grp", "dev"),
        P("dev", "grp"),
        P("grp", None),
        P("grp", None),
        P("grp", None),
    )
    return jax.shard_map(
        functools.partial(shards, mesh.shape["grp"], mesh.shape["dev"]),
        mesh=mesh,
        in_specs=placed,
        out_specs=P(("grp", "dev"), None),
        check_vma=False,
    )
```

```python
import functools
import math

import jax
import jax.numpy as jnp
from jax import lax
from jax.experimental import pallas as pl
from jax.experimental.pallas import tpu as pltpu
from jax.sharding import PartitionSpec as P

HEAD_SIZE = 64
NEG_FILL = -1e30
EPSILON = 1e-05
F32 = jnp.float32
BF16 = jnp.bfloat16
LANES = 2 * HEAD_SIZE
CORES = 2
HALVES = 2


def cost(microseconds):
    return pl.CostEstimate(flops=0, bytes_accessed=int(microseconds * 3.5e6), transcendentals=0)


def dot(a, b, contract_b=0):
    return lax.dot_general(
        a, b, (((1,), (contract_b,)), ((), ())), preferred_element_type=F32
    )


def prepare_body(
    span,
    layout_hbm,
    queries_hbm,
    *refs,
):
    q_ref, before_ref, within_ref, prefix_ref = refs[:4]
    layout_ref, queries_ref, sems = refs[4:]
    copies = [
        pltpu.make_async_copy(source, target, sems.at[i])
        for i, (source, target) in enumerate(
            [
                (layout_hbm, layout_ref),
                (queries_hbm, queries_ref),
            ]
        )
    ]
    for copy in copies:
        copy.start()
    for copy in copies:
        copy.wait()
    tokens = queries_ref.shape[0]
    pairs, rows = q_ref.shape[0], q_ref.shape[1]
    per = rows // (2 * tokens)
    base = lax.axis_index("dev") * tokens
    own = base + lax.broadcasted_iota(jnp.int32, (tokens, LANES), 0)

    def request(k, carry):
        start, group, first = carry
        j = layout_ref[2, k]
        end = start + layout_ref[0, j]
        inside = (own >= start) & (own < end)
        return (
            end,
            jnp.where(inside, layout_ref[1, j], group),
            jnp.where(inside, start, first),
        )

    zero = jnp.zeros((tokens, LANES), jnp.int32)
    _, group, first = lax.fori_loop(0, layout_ref.shape[1], request, (jnp.int32(0), zero, zero))
    for ref, back in ((before_ref, tokens), (within_ref, 0)):
        for c in range(0, tokens, LANES):
            key = base - back + c + lax.broadcasted_iota(jnp.int32, (tokens, LANES), 1)
            ref[:, c : c + LANES] = jnp.where((key >= first) & (key <= own), 0.0, NEG_FILL)
    for c in range(0, prefix_ref.shape[1], LANES):
        key_group = lax.div(c + lax.broadcasted_iota(jnp.int32, (tokens, LANES), 1), span)
        prefix_ref[:, c : c + LANES] = jnp.where(group == key_group, 0.0, NEG_FILL)
    low = lax.broadcasted_iota(jnp.int32, (tokens, LANES), 1) < HEAD_SIZE
    for j in range(pairs):
        for parity in range(2):
            for r in range(per):
                head = (2 * j + parity) * per + r
                block = head // 2
                q = queries_ref[:, block * LANES : (block + 1) * LANES].astype(F32) * HEAD_SIZE ** (-0.5)
                if head % 2 != parity:
                    q = pltpu.roll(q, HEAD_SIZE, 1)
                q = jnp.where(low == (parity == 0), q, 0.0)
                row = (parity * per + r) * tokens
                q_ref[j, row : row + tokens, :] = q.astype(BF16)


def prepare(groups, span, lengths, request_group, packing, queries, width):
    tokens = queries.shape[0]
    layout = jnp.concatenate([lengths, request_group, packing], axis=0)
    per = queries.shape[1] // width
    vmem = pl.BlockSpec(memory_space=pltpu.VMEM)
    return pl.pallas_call(
        functools.partial(prepare_body, span),
        out_shape=[
            jax.ShapeDtypeStruct((width // LANES, 2 * per * tokens, LANES), BF16),
            jax.ShapeDtypeStruct((tokens, tokens), F32),
            jax.ShapeDtypeStruct((tokens, tokens), F32),
            jax.ShapeDtypeStruct((tokens, groups * span), F32),
        ],
        in_specs=[pl.BlockSpec(memory_space=pltpu.HBM)] * 2,
        out_specs=[vmem] * 4,
        compiler_params=pltpu.CompilerParams(vmem_limit_bytes=8 * 2**20),
        scratch_shapes=[
            pltpu.SMEM(layout.shape, jnp.int32),
            pltpu.VMEM(queries.shape, BF16),
            pltpu.SemaphoreType.DMA((2,)),
        ],
        cost_estimate=cost(3),
        name="prepare",
    )(layout, queries)


def attend_body(first, pieces, refs):
    q_ref, refs = refs[0], refs[1:]
    if not first:
        old_max, old_sum, old_acc = refs[:3]
        refs = refs[3:]
    kv = refs[: 3 * pieces]
    new_max, new_sum, new_acc = refs[-3:]
    pairs, rows = q_ref.shape[0], q_ref.shape[1]
    half = rows // 2
    low = lax.broadcasted_iota(jnp.int32, (half, LANES), 1) < HEAD_SIZE

    def pick(even, odd):
        return jnp.where(low, even, odd)

    for j in range(pairs):
        q = q_ref[j]
        lanes = slice(j * LANES, (j + 1) * LANES)
        scores = []
        for i in range(pieces):
            k_ref, bias_ref = kv[3 * i], kv[3 * i + 2]
            s = dot(q, k_ref[:, lanes], 1)
            keys = s.shape[1]
            bias = bias_ref[...]
            s = s.reshape(rows // bias.shape[0], bias.shape[0], keys) + bias[None]
            scores.append(s.reshape(rows, keys))
        top = functools.reduce(
            jnp.maximum, [jnp.max(s, axis=1, keepdims=True) for s in scores]
        )
        if first:
            row_max = top
            pair_max = pick(row_max[:half], row_max[half:])
        else:
            old = old_max[j]
            pair_max = jnp.maximum(old, pick(top[:half], top[half:]))
            row_max = jnp.concatenate(
                [pair_max[:, :1], pair_max[:, HEAD_SIZE : HEAD_SIZE + 1]], axis=0
            )
        total = None
        for i in range(pieces):
            v_ref = kv[3 * i + 1]
            w = jnp.exp(scores[i] - row_max).astype(BF16)
            v = v_ref[:, lanes]
            v = jnp.concatenate([v, jnp.ones_like(v)], axis=1)
            part = dot(w, v)
            total = part if total is None else total + part
        acc = pick(total[:half, :LANES], total[half:, :LANES])
        summed = pick(total[:half, LANES:], total[half:, LANES:])
        if not first:
            scale = jnp.exp(old - pair_max)
            acc = acc + scale * old_acc[j]
            summed = summed + scale * old_sum[j]
        new_max[j] = pair_max
        new_sum[j] = summed
        new_acc[j] = acc


def block_refs(refs, count):
    return [r for i in range(count) for r in (refs[2 * i].at[0], refs[2 * i].at[1], refs[2 * i + 1])]


def attend(q, state, blocks):
    pairs, rows, lanes = q.shape
    first = state is None

    def kernel(*refs):
        lead = 1 + (0 if first else 3)
        attend_body(first, len(blocks), [*refs[:lead], *block_refs(refs[lead:], len(blocks)), *refs[-3:]])

    shape = jax.ShapeDtypeStruct((pairs, rows // 2, lanes), F32)
    operands = [q] + ([] if first else list(state)) + [a for block in blocks for a in block]
    vmem = pl.BlockSpec(memory_space=pltpu.VMEM)
    return pl.pallas_call(
        kernel,
        out_shape=[shape] * 3,
        in_specs=[vmem] * len(operands),
        out_specs=[vmem] * 3,
        compiler_params=pltpu.CompilerParams(vmem_limit_bytes=(8 + 3 * len(blocks)) * 2**20),
        cost_estimate=cost(1.1 * len(blocks)),
        name="attend",
    )(*operands)


def block_owner(blocks, step):
    chips = blocks // CORES
    me = lax.axis_index("grp")
    x, core = lax.div(me, CORES), lax.rem(me, CORES)
    x = lax.rem(x + chips - step // CORES, chips)
    return x * CORES + lax.rem(core + step % CORES, CORES)


def project_body(
    blocks, sum_ref, acc_ref, weight_ref, residual_ref, gain_ref, hidden_ref, normed_refs, held
):
    pairs, rows, lanes = acc_ref.shape
    tokens = residual_ref.shape[0]
    per = rows // tokens
    hidden = residual_ref[...].astype(F32)
    for j in range(pairs):
        out = (acc_ref[j] / sum_ref[j]).astype(BF16)
        for r in range(0, per, 2):
            left = jnp.concatenate(
                [out[r * tokens : (r + 1) * tokens], out[(r + 1) * tokens : (r + 2) * tokens]], axis=1
            )
            heads = [(2 * j) * per + r, (2 * j + 1) * per + r, (2 * j) * per + r + 1, (2 * j + 1) * per + r + 1]
            right = jnp.concatenate(
                [weight_ref[h * HEAD_SIZE : (h + 1) * HEAD_SIZE, :] for h in heads], axis=0
            )
            hidden = hidden + dot(left, right)
    hidden_ref[...] = hidden
    mean = jnp.mean(hidden * hidden, axis=1, keepdims=True)
    held[...] = hidden * lax.rsqrt(mean + EPSILON) * gain_ref[...]
    width = hidden.shape[1] // blocks
    for b in range(blocks):
        start = pl.multiple_of(block_owner(blocks, b) * width, width)
        half, place = divmod(b, blocks // HALVES)
        normed_refs[half][:, place * width : (place + 1) * width] = held[:, pl.ds(start, width)].astype(BF16)


def attend_project(q, state, blocks, columns, out_weight, residual, gain):
    pairs, rows, lanes = q.shape
    tokens, width = residual.shape
    count = len(blocks)

    def kernel(*refs):
        mine, (weight_ref, residual_ref, gain_ref) = refs[: 4 + 2 * count], refs[4 + 2 * count : 7 + 2 * count]
        hidden_ref, *normed_refs = refs[7 + 2 * count : 8 + 2 * count + HALVES]
        held, top, total, acc = refs[-4:]
        attend_body(False, count, [*mine[:4], *block_refs(mine[4:], count), top, total, acc])
        project_body(
            columns, total, acc, weight_ref, residual_ref, gain_ref, hidden_ref, normed_refs, held
        )

    operands = [q, *state] + [a for block in blocks for a in block]
    vmem = pl.BlockSpec(memory_space=pltpu.VMEM)
    return pl.pallas_call(
        kernel,
        out_shape=[
            jax.ShapeDtypeStruct((tokens, width), F32),
        ]
        + [jax.ShapeDtypeStruct((tokens, width // HALVES), BF16)] * HALVES,
        in_specs=[vmem] * (len(operands) + 3),
        out_specs=[vmem] * (1 + HALVES),
        scratch_shapes=[pltpu.VMEM((tokens, width), F32)]
        + [pltpu.VMEM((pairs, rows // 2, lanes), F32)] * 3,
        compiler_params=pltpu.CompilerParams(vmem_limit_bytes=20 * 2**20),
        cost_estimate=cost(1.1 * count + 2),
        name="attend_project",
    )(*operands, out_weight, residual, gain)


def rise_body(parts, blocks, refs):
    pieces = parts * HALVES
    n_refs, gates, ups = refs[:pieces], refs[pieces : pieces + blocks], refs[pieces + blocks : pieces + 2 * blocks]
    act_ref, x_ref = refs[-2:]
    tokens, width = n_refs[0].shape
    for i in range(parts):
        for half in range(HALVES):
            x_ref[i * tokens : (i + 1) * tokens, half * width : (half + 1) * width] = n_refs[i * HALVES + half][...]
    depth, hidden = gates[0].shape
    tile = math.gcd(hidden, 256)

    @pl.loop(0, hidden // tile)
    def _(t):
        cols = pl.ds(pl.multiple_of(t * tile, tile), tile)
        gate = up = None
        for b in range(blocks):
            x = x_ref[:, b * depth : (b + 1) * depth]
            g, u = dot(x, gates[b][:, cols]), dot(x, ups[b][:, cols])
            gate, up = (g, u) if gate is None else (gate + g, up + u)
        act_ref[:, cols] = (gate / (1.0 + jnp.exp(-gate)) * up).astype(BF16)


def rise(normed, gates, ups):
    parts, blocks = len(normed), len(gates)
    tokens, width = normed[0][0].shape
    hidden = gates[0].shape[1]

    def kernel(*refs):
        rise_body(parts, blocks, refs)

    vmem = pl.BlockSpec(memory_space=pltpu.VMEM)
    return pl.pallas_call(
        kernel,
        out_shape=jax.ShapeDtypeStruct((parts * tokens, hidden), BF16),
        in_specs=[vmem] * (parts * HALVES + 2 * blocks),
        out_specs=vmem,
        scratch_shapes=[pltpu.VMEM((parts * tokens, HALVES * width), BF16)],
        compiler_params=pltpu.CompilerParams(vmem_limit_bytes=12 * 2**20),
        cost_estimate=cost(1.5 * parts),
        name="rise",
    )(*[half for chunk in normed for half in chunk], *gates, *ups)


def fall_body(blocks, refs):
    act_ref, downs, outs = refs[0], refs[1 : 1 + blocks], refs[1 + blocks :]
    rows, width = outs[0].shape[0], downs[0].shape[1]
    tile = math.gcd(width, 256)
    for b in range(blocks):

        @pl.loop(0, width // tile)
        def _(t):
            term = dot(act_ref[...], downs[b][:, pl.ds(pl.multiple_of(t * tile, tile), tile)])
            cols = pl.ds(pl.multiple_of(b * width + t * tile, tile), tile)
            for i, out in enumerate(outs):
                out[:, cols] = term[i * rows : (i + 1) * rows].astype(BF16)


def fall(act, parts, downs):
    blocks = len(downs)
    shape = jax.ShapeDtypeStruct((act.shape[0] // parts, blocks * downs[0].shape[1]), BF16)

    def kernel(*refs):
        fall_body(blocks, refs)

    vmem = pl.BlockSpec(memory_space=pltpu.VMEM)
    return pl.pallas_call(
        kernel,
        out_shape=[shape] * parts,
        in_specs=[vmem] * (1 + blocks),
        out_specs=[vmem] * parts,
        compiler_params=pltpu.CompilerParams(vmem_limit_bytes=12 * 2**20),
        cost_estimate=cost(1.2),
        name="fall",
    )(act, *downs)


def finish_body(blocks, hidden_ref, *refs):
    terms, out_ref = refs[:-1], refs[-1]
    each = len(terms) // HALVES
    width = out_ref.shape[1] // blocks
    for b in range(blocks):
        half, column = divmod(b, blocks // HALVES)
        place = pl.ds(pl.multiple_of(block_owner(blocks, b) * width, width), width)
        total = hidden_ref[:, place]
        for term in terms[half * each : (half + 1) * each]:
            total = total + term[:, column * width : (column + 1) * width].astype(F32)
        out_ref[:, place] = total.astype(BF16)


def finish(blocks, hidden_state, terms):
    vmem = pl.BlockSpec(memory_space=pltpu.VMEM)
    operands = [hidden_state] + [term for half in terms for term in half]
    return pl.pallas_call(
        functools.partial(finish_body, blocks),
        out_shape=jax.ShapeDtypeStruct(hidden_state.shape, BF16),
        in_specs=[vmem] * len(operands),
        out_specs=vmem,
        compiler_params=pltpu.CompilerParams(vmem_limit_bytes=8 * 2**20),
        cost_estimate=cost(1),
        name="finish",
    )(*operands)


def tie(array, *others):
    return lax.optimization_barrier((array, *others))[0] if others else array


def shards(
    grps,
    devs,
    residual,
    queries,
    keys,
    values,
    prefix_keys,
    cached_prefix_values,
    out_weight,
    norm_gain,
    w_gate,
    w_up,
    w_down,
    suffix_lengths,
    request_group,
    placement_order,
):
    depth_z = math.gcd(devs, 4)
    depth_y = devs // depth_z
    cores = CORES
    depth_x = grps // cores
    ring = list(range(0, depth_z, 2)) + list(range(1, depth_z, 2))[::-1]

    def shift(by_z, by_y):
        return [
            (
                ring[i] * depth_y + y,
                ring[(i + by_z) % depth_z] * depth_y + (y + by_y) % depth_y,
            )
            for i in range(depth_z)
            for y in range(depth_y)
        ]

    x_shift = [
        (x * cores + c, (x + 1) % depth_x * cores + c) for x in range(depth_x) for c in range(cores)
    ]
    core_swap = [(x * cores + c, x * cores + 1 - c) for x in range(depth_x) for c in range(cores)]

    def round_z(block, *others):
        return lax.ppermute(tie(block, *others), "dev", shift(1, 0))

    def along_y(block, *others):
        return [lax.ppermute(tie(block, *others), "dev", shift(0, ys)) for ys in range(1, depth_y)]

    def along_x(weight, *others):
        blocks = [weight]
        for _ in range(1, depth_x):
            blocks.append(lax.ppermute(tie(blocks[-1], *others), "grp", x_shift))
        return blocks

    def other_core(block, *others):
        return lax.ppermute(tie(block, *others), "grp", core_swap)

    tokens = queries.shape[0]
    width = keys.shape[1]
    groups, span = prefix_keys.shape[:2]

    prefix = jnp.stack([prefix_keys.reshape(-1, width), cached_prefix_values.reshape(-1, width)])
    other = along_y(prefix)
    arriving = round_z(prefix)
    own = jnp.stack([keys, values])
    before = lax.ppermute(own, "dev", [(i, i + 1) for i in range(devs - 1)])
    gate_rows = along_x(w_gate)
    q, before_mask, within_mask, prefix_mask = prepare(
        groups,
        span,
        suffix_lengths,
        request_group,
        placement_order,
        queries,
        width,
    )
    blocks = [(before, before_mask), (own, within_mask), (prefix, prefix_mask)]
    ready, state = [before], None
    for zs in range(1, depth_z):
        if zs == depth_z - 1:
            state = attend(q, None, blocks)
            blocks, ready = [], [state[0], gate_swap, *gate_rows[1:]]
        here = tie(arriving, *(other if zs != 2 else []), *ready)
        if zs < depth_z - 1:
            arriving, ready = round_z(here), [q]
        blocks += [(b, prefix_mask) for b in other + [here]]
        other = along_y(here)
        if zs == 1:
            gate_swap = other_core(w_gate, here)
        elif zs == 2:
            up_swap = other_core(w_up, here)
    state = attend(q, state, blocks)
    down_swap = other_core(w_down, here)
    up_rows = along_x(w_up, *gate_rows[1:], here)
    gates = [w_gate, gate_swap]
    for gate in gate_rows[1:]:
        gates += [gate, other_core(gate, here)]
    hidden_state, *normed = attend_project(
        q,
        state,
        [(b, prefix_mask) for b in other],
        grps,
        out_weight,
        tie(residual, up_swap, down_swap, *gates[2:]),
        norm_gain[None],
    )

    arrived, across = [normed], [[along_y(half) for half in normed]]
    ups, downs, acts = [w_up, up_swap], [w_down, down_swap], {}
    for zs in range(1, depth_z):
        waits = across[zs - 2] if zs > 1 else [[] for _ in normed]
        arrived.append([round_z(half, *wait) for half, wait in zip(arrived[-1], waits)])
        late = arrived[zs][1:]
        if zs == depth_z - 1:
            acts[1] = rise([arrived[1]] + [list(c) for c in zip(*across[1])], gates, ups)
            late = [*late, acts[1]]
        across.append([along_y(half, *late) for half in arrived[zs]])
        if zs == depth_z - 2:
            for up in up_rows[1:]:
                ups += [up, other_core(up, *arrived[zs], *[b for c in across[zs - 1] for b in c])]
            down_cols = along_x(w_down, *up_rows[1:], *arrived[zs], *[b for c in across[zs - 1] for b in c])
    chunks = [[a] + [list(c) for c in zip(*b)] for a, b in zip(arrived, across)]
    each = grps // HALVES
    acts[2] = rise(chunks[2], gates, ups)
    acts[0] = rise(chunks[0], gates, ups)
    soon = [b for c in across[-1] for b in c] + [acts[2], acts[0]]
    sent = [None] * HALVES
    if each <= len(downs):
        sent[0] = round_z(
            fall(acts[1], 1, downs[:each])[0], *arrived[-1], *[b for c in across[-2] for b in c]
        )
        second = fall(acts[2], 1, downs[:each])[0]
        second = (second.astype(F32) + sent[0].astype(F32)).astype(BF16)
        soon.append(second)
        sent[0] = round_z(second)
    final = depth_z - 1
    for down in down_cols[1:]:
        downs += [down, other_core(down, *soon)]

    terms, fallen = [None] * HALVES, {}
    acts[final] = rise(chunks[final], gates, ups)
    fallen[final, 0] = fall(acts[final], depth_y, downs[:each])
    filler = fallen[final, 0][0]
    for zs in list(range(1, depth_z)) + [0]:
        act = acts[zs]
        for half in range(HALVES):
            joint = sent[half] is not None and sent[half].shape[0] > tokens
            if joint and zs < depth_z - 1:
                continue
            parts = fallen.pop((zs, half), None)
            if parts is None:
                parts = fall(act, depth_y, downs[half * each : (half + 1) * each])
            if joint:
                came = [sent[half][i * tokens : (i + 1) * tokens] for i in range(depth_y)]
                parts = [
                    (part.astype(F32) + share.astype(F32)).astype(BF16) if i else part
                    for i, (part, share) in enumerate(zip(parts, came))
                ]
                terms[half] = [parts[0], came[0]]
            else:
                terms[half] = [parts[0]] + ([round_z(sent[half])] if zs != 1 else [])
            if zs == 0:
                parts = [tie(part, sent[0]) for part in parts]
            terms[half] += [
                lax.ppermute(parts[ys], "dev", shift(0, -ys)) for ys in range(1, depth_y)
            ]
            if zs == 1:
                terms[half][0] = tie(terms[half][0], filler)
            if zs:
                sent[half] = functools.reduce(
                    jnp.add, [term.astype(F32) for term in terms[half]]
                ).astype(BF16)
    return finish(grps, hidden_state, terms)


def solution(mesh):
    placed = (
        P(("grp", "dev"), None),
        P(("grp", "dev"), None),
        P(("grp", "dev"), None),
        P(("grp", "dev"), None),
        P("grp", "dev", None),
        P("grp", "dev", None),
        P(),
        P(),
        P("grp", "dev"),
        P("grp", "dev"),
        P("dev", "grp"),
        P("grp", None),
        P("grp", None),
        P("grp", None),
    )
    return jax.shard_map(
        functools.partial(shards, mesh.shape["grp"], mesh.shape["dev"]),
        mesh=mesh,
        in_specs=placed,
        out_specs=P(("grp", "dev"), None),
        check_vma=False,
    )
```

```python
import functools
import math

import jax
import jax.numpy as jnp
from jax import lax
from jax.experimental import pallas as pl
from jax.experimental.pallas import tpu as pltpu
from jax.sharding import PartitionSpec as P

HEAD_SIZE = 64
NEG_FILL = -1e30
EPSILON = 1e-05
F32 = jnp.float32
BF16 = jnp.bfloat16
LANES = 2 * HEAD_SIZE
CORES = 2
HALVES = 2


def cost(microseconds):
    return pl.CostEstimate(flops=0, bytes_accessed=int(microseconds * 3.5e6), transcendentals=0)


def dot(a, b, contract_b=0):
    return lax.dot_general(
        a, b, (((1,), (contract_b,)), ((), ())), preferred_element_type=F32
    )


def prepare_body(
    span,
    layout_hbm,
    queries_hbm,
    *refs,
):
    q_ref, before_ref, within_ref, prefix_ref = refs[:4]
    layout_ref, queries_ref, sems = refs[4:]
    copies = [
        pltpu.make_async_copy(source, target, sems.at[i])
        for i, (source, target) in enumerate(
            [
                (layout_hbm, layout_ref),
                (queries_hbm, queries_ref),
            ]
        )
    ]
    for copy in copies:
        copy.start()
    for copy in copies:
        copy.wait()
    tokens = queries_ref.shape[0]
    pairs, rows = q_ref.shape[0], q_ref.shape[1]
    per = rows // (2 * tokens)
    base = lax.axis_index("dev") * tokens
    own = base + lax.broadcasted_iota(jnp.int32, (tokens, LANES), 0)

    def request(k, carry):
        start, group, first = carry
        j = layout_ref[2, k]
        end = start + layout_ref[0, j]
        inside = (own >= start) & (own < end)
        return (
            end,
            jnp.where(inside, layout_ref[1, j], group),
            jnp.where(inside, start, first),
        )

    zero = jnp.zeros((tokens, LANES), jnp.int32)
    _, group, first = lax.fori_loop(0, layout_ref.shape[1], request, (jnp.int32(0), zero, zero))
    for ref, back in ((before_ref, tokens), (within_ref, 0)):
        for c in range(0, tokens, LANES):
            key = base - back + c + lax.broadcasted_iota(jnp.int32, (tokens, LANES), 1)
            ref[:, c : c + LANES] = jnp.where((key >= first) & (key <= own), 0.0, NEG_FILL)
    for c in range(0, prefix_ref.shape[1], LANES):
        key_group = lax.div(c + lax.broadcasted_iota(jnp.int32, (tokens, LANES), 1), span)
        prefix_ref[:, c : c + LANES] = jnp.where(group == key_group, 0.0, NEG_FILL)
    low = lax.broadcasted_iota(jnp.int32, (tokens, LANES), 1) < HEAD_SIZE
    for j in range(pairs):
        for parity in range(2):
            for r in range(per):
                head = (2 * j + parity) * per + r
                block = head // 2
                q = queries_ref[:, block * LANES : (block + 1) * LANES].astype(F32) * HEAD_SIZE ** (-0.5)
                if head % 2 != parity:
                    q = pltpu.roll(q, HEAD_SIZE, 1)
                q = jnp.where(low == (parity == 0), q, 0.0)
                row = (parity * per + r) * tokens
                q_ref[j, row : row + tokens, :] = q.astype(BF16)


def prepare(groups, span, lengths, request_group, packing, queries, width):
    tokens = queries.shape[0]
    layout = jnp.concatenate([lengths, request_group, packing], axis=0)
    per = queries.shape[1] // width
    vmem = pl.BlockSpec(memory_space=pltpu.VMEM)
    return pl.pallas_call(
        functools.partial(prepare_body, span),
        out_shape=[
            jax.ShapeDtypeStruct((width // LANES, 2 * per * tokens, LANES), BF16),
            jax.ShapeDtypeStruct((tokens, tokens), F32),
            jax.ShapeDtypeStruct((tokens, tokens), F32),
            jax.ShapeDtypeStruct((tokens, groups * span), F32),
        ],
        in_specs=[pl.BlockSpec(memory_space=pltpu.HBM)] * 2,
        out_specs=[vmem] * 4,
        compiler_params=pltpu.CompilerParams(vmem_limit_bytes=8 * 2**20),
        scratch_shapes=[
            pltpu.SMEM(layout.shape, jnp.int32),
            pltpu.VMEM(queries.shape, BF16),
            pltpu.SemaphoreType.DMA((2,)),
        ],
        cost_estimate=cost(3),
        name="prepare",
    )(layout, queries)


def attend_body(first, pieces, refs):
    q_ref, refs = refs[0], refs[1:]
    if not first:
        old_max, old_sum, old_acc = refs[:3]
        refs = refs[3:]
    kv = refs[: 3 * pieces]
    new_max, new_sum, new_acc = refs[-3:]
    pairs, rows = q_ref.shape[0], q_ref.shape[1]
    half = rows // 2
    low = lax.broadcasted_iota(jnp.int32, (half, LANES), 1) < HEAD_SIZE

    def pick(even, odd):
        return jnp.where(low, even, odd)

    for j in range(pairs):
        q = q_ref[j]
        lanes = slice(j * LANES, (j + 1) * LANES)
        scores = []
        for i in range(pieces):
            k_ref, bias_ref = kv[3 * i], kv[3 * i + 2]
            s = dot(q, k_ref[:, lanes], 1)
            keys = s.shape[1]
            bias = bias_ref[...]
            s = s.reshape(rows // bias.shape[0], bias.shape[0], keys) + bias[None]
            scores.append(s.reshape(rows, keys))
        top = functools.reduce(
            jnp.maximum, [jnp.max(s, axis=1, keepdims=True) for s in scores]
        )
        if first:
            row_max = top
            pair_max = pick(row_max[:half], row_max[half:])
        else:
            old = old_max[j]
            pair_max = jnp.maximum(old, pick(top[:half], top[half:]))
            row_max = jnp.concatenate(
                [pair_max[:, :1], pair_max[:, HEAD_SIZE : HEAD_SIZE + 1]], axis=0
            )
        total = None
        for i in range(pieces):
            v_ref = kv[3 * i + 1]
            w = jnp.exp(scores[i] - row_max).astype(BF16)
            v = v_ref[:, lanes]
            v = jnp.concatenate([v, jnp.ones_like(v)], axis=1)
            part = dot(w, v)
            total = part if total is None else total + part
        acc = pick(total[:half, :LANES], total[half:, :LANES])
        summed = pick(total[:half, LANES:], total[half:, LANES:])
        if not first:
            scale = jnp.exp(old - pair_max)
            acc = acc + scale * old_acc[j]
            summed = summed + scale * old_sum[j]
        new_max[j] = pair_max
        new_sum[j] = summed
        new_acc[j] = acc


def block_refs(refs, count):
    return [r for i in range(count) for r in (refs[2 * i].at[0], refs[2 * i].at[1], refs[2 * i + 1])]


def attend(q, state, blocks):
    pairs, rows, lanes = q.shape
    first = state is None

    def kernel(*refs):
        lead = 1 + (0 if first else 3)
        attend_body(first, len(blocks), [*refs[:lead], *block_refs(refs[lead:], len(blocks)), *refs[-3:]])

    shape = jax.ShapeDtypeStruct((pairs, rows // 2, lanes), F32)
    operands = [q] + ([] if first else list(state)) + [a for block in blocks for a in block]
    vmem = pl.BlockSpec(memory_space=pltpu.VMEM)
    return pl.pallas_call(
        kernel,
        out_shape=[shape] * 3,
        in_specs=[vmem] * len(operands),
        out_specs=[vmem] * 3,
        compiler_params=pltpu.CompilerParams(vmem_limit_bytes=(8 + 3 * len(blocks)) * 2**20),
        cost_estimate=cost(1.1 * len(blocks)),
        name="attend",
    )(*operands)


def block_owner(blocks, step):
    chips = blocks // CORES
    me = lax.axis_index("grp")
    x, core = lax.div(me, CORES), lax.rem(me, CORES)
    x = lax.rem(x + chips - step // CORES, chips)
    return x * CORES + lax.rem(core + step % CORES, CORES)


def project_body(
    blocks, sum_ref, acc_ref, weight_ref, residual_ref, gain_ref, hidden_ref, normed_refs, held
):
    pairs, rows, lanes = acc_ref.shape
    tokens = residual_ref.shape[0]
    per = rows // tokens
    hidden = residual_ref[...].astype(F32)
    for j in range(pairs):
        out = (acc_ref[j] / sum_ref[j]).astype(BF16)
        for r in range(0, per, 2):
            left = jnp.concatenate(
                [out[r * tokens : (r + 1) * tokens], out[(r + 1) * tokens : (r + 2) * tokens]], axis=1
            )
            heads = [(2 * j) * per + r, (2 * j + 1) * per + r, (2 * j) * per + r + 1, (2 * j + 1) * per + r + 1]
            right = jnp.concatenate(
                [weight_ref[h * HEAD_SIZE : (h + 1) * HEAD_SIZE, :] for h in heads], axis=0
            )
            hidden = hidden + dot(left, right)
    hidden_ref[...] = hidden
    mean = jnp.mean(hidden * hidden, axis=1, keepdims=True)
    held[...] = hidden * lax.rsqrt(mean + EPSILON) * gain_ref[...]
    width = hidden.shape[1] // blocks
    for b in range(blocks):
        start = pl.multiple_of(block_owner(blocks, b) * width, width)
        half, place = divmod(b, blocks // HALVES)
        normed_refs[half][:, place * width : (place + 1) * width] = held[:, pl.ds(start, width)].astype(BF16)


def attend_project(q, state, blocks, columns, out_weight, residual, gain):
    pairs, rows, lanes = q.shape
    tokens, width = residual.shape
    count = len(blocks)

    def kernel(*refs):
        mine, (weight_ref, residual_ref, gain_ref) = refs[: 4 + 2 * count], refs[4 + 2 * count : 7 + 2 * count]
        hidden_ref, *normed_refs = refs[7 + 2 * count : 8 + 2 * count + HALVES]
        held, top, total, acc = refs[-4:]
        attend_body(False, count, [*mine[:4], *block_refs(mine[4:], count), top, total, acc])
        project_body(
            columns, total, acc, weight_ref, residual_ref, gain_ref, hidden_ref, normed_refs, held
        )

    operands = [q, *state] + [a for block in blocks for a in block]
    vmem = pl.BlockSpec(memory_space=pltpu.VMEM)
    return pl.pallas_call(
        kernel,
        out_shape=[
            jax.ShapeDtypeStruct((tokens, width), F32),
        ]
        + [jax.ShapeDtypeStruct((tokens, width // HALVES), BF16)] * HALVES,
        in_specs=[vmem] * (len(operands) + 3),
        out_specs=[vmem] * (1 + HALVES),
        scratch_shapes=[pltpu.VMEM((tokens, width), F32)]
        + [pltpu.VMEM((pairs, rows // 2, lanes), F32)] * 3,
        compiler_params=pltpu.CompilerParams(vmem_limit_bytes=20 * 2**20),
        cost_estimate=cost(1.1 * count + 2),
        name="attend_project",
    )(*operands, out_weight, residual, gain)


def rise_body(parts, blocks, refs):
    pieces = parts * HALVES
    n_refs, gates, ups = refs[:pieces], refs[pieces : pieces + blocks], refs[pieces + blocks : pieces + 2 * blocks]
    act_ref, x_ref = refs[-2:]
    tokens, width = n_refs[0].shape
    for i in range(parts):
        for half in range(HALVES):
            x_ref[i * tokens : (i + 1) * tokens, half * width : (half + 1) * width] = n_refs[i * HALVES + half][...]
    depth, hidden = gates[0].shape
    tile = math.gcd(hidden, 256)

    @pl.loop(0, hidden // tile)
    def _(t):
        cols = pl.ds(pl.multiple_of(t * tile, tile), tile)
        gate = up = None
        for b in range(blocks):
            x = x_ref[:, b * depth : (b + 1) * depth]
            g, u = dot(x, gates[b][:, cols]), dot(x, ups[b][:, cols])
            gate, up = (g, u) if gate is None else (gate + g, up + u)
        act_ref[:, cols] = (gate / (1.0 + jnp.exp(-gate)) * up).astype(BF16)


def rise(normed, gates, ups):
    parts, blocks = len(normed), len(gates)
    tokens, width = normed[0][0].shape
    hidden = gates[0].shape[1]

    def kernel(*refs):
        rise_body(parts, blocks, refs)

    vmem = pl.BlockSpec(memory_space=pltpu.VMEM)
    return pl.pallas_call(
        kernel,
        out_shape=jax.ShapeDtypeStruct((parts * tokens, hidden), BF16),
        in_specs=[vmem] * (parts * HALVES + 2 * blocks),
        out_specs=vmem,
        scratch_shapes=[pltpu.VMEM((parts * tokens, HALVES * width), BF16)],
        compiler_params=pltpu.CompilerParams(vmem_limit_bytes=12 * 2**20),
        cost_estimate=cost(1.5 * parts),
        name="rise",
    )(*[half for chunk in normed for half in chunk], *gates, *ups)


def fall_body(blocks, refs):
    act_ref, downs, outs = refs[0], refs[1 : 1 + blocks], refs[1 + blocks :]
    rows, width = outs[0].shape[0], downs[0].shape[1]
    tile = math.gcd(width, 256)
    for b in range(blocks):

        @pl.loop(0, width // tile)
        def _(t):
            term = dot(act_ref[...], downs[b][:, pl.ds(pl.multiple_of(t * tile, tile), tile)])
            cols = pl.ds(pl.multiple_of(b * width + t * tile, tile), tile)
            for i, out in enumerate(outs):
                out[:, cols] = term[i * rows : (i + 1) * rows].astype(BF16)


def fall(act, parts, downs):
    blocks = len(downs)
    shape = jax.ShapeDtypeStruct((act.shape[0] // parts, blocks * downs[0].shape[1]), BF16)

    def kernel(*refs):
        fall_body(blocks, refs)

    vmem = pl.BlockSpec(memory_space=pltpu.VMEM)
    return pl.pallas_call(
        kernel,
        out_shape=[shape] * parts,
        in_specs=[vmem] * (1 + blocks),
        out_specs=[vmem] * parts,
        compiler_params=pltpu.CompilerParams(vmem_limit_bytes=12 * 2**20),
        cost_estimate=cost(1.2),
        name="fall",
    )(act, *downs)


def finish_body(blocks, hidden_ref, *refs):
    terms, out_ref = refs[:-1], refs[-1]
    each = len(terms) // HALVES
    width = out_ref.shape[1] // blocks
    for b in range(blocks):
        half, column = divmod(b, blocks // HALVES)
        place = pl.ds(pl.multiple_of(block_owner(blocks, b) * width, width), width)
        total = hidden_ref[:, place]
        for term in terms[half * each : (half + 1) * each]:
            total = total + term[:, column * width : (column + 1) * width].astype(F32)
        out_ref[:, place] = total.astype(BF16)


def finish(blocks, hidden_state, terms):
    vmem = pl.BlockSpec(memory_space=pltpu.VMEM)
    operands = [hidden_state] + [term for half in terms for term in half]
    return pl.pallas_call(
        functools.partial(finish_body, blocks),
        out_shape=jax.ShapeDtypeStruct(hidden_state.shape, BF16),
        in_specs=[vmem] * len(operands),
        out_specs=vmem,
        compiler_params=pltpu.CompilerParams(vmem_limit_bytes=8 * 2**20),
        cost_estimate=cost(1),
        name="finish",
    )(*operands)


def tie(array, *others):
    return lax.optimization_barrier((array, *others))[0] if others else array


def shards(
    grps,
    devs,
    residual,
    queries,
    keys,
    values,
    prefix_keys,
    cached_prefix_values,
    out_weight,
    norm_gain,
    w_gate,
    w_up,
    w_down,
    suffix_lengths,
    request_group,
    placement_order,
):
    depth_z = math.gcd(devs, 4)
    depth_y = devs // depth_z
    cores = CORES
    depth_x = grps // cores
    ring = list(range(0, depth_z, 2)) + list(range(1, depth_z, 2))[::-1]

    def shift(by_z, by_y):
        return [
            (
                ring[i] * depth_y + y,
                ring[(i + by_z) % depth_z] * depth_y + (y + by_y) % depth_y,
            )
            for i in range(depth_z)
            for y in range(depth_y)
        ]

    x_shift = [
        (x * cores + c, (x + 1) % depth_x * cores + c) for x in range(depth_x) for c in range(cores)
    ]
    core_swap = [(x * cores + c, x * cores + 1 - c) for x in range(depth_x) for c in range(cores)]

    def round_z(block, *others):
        return lax.ppermute(tie(block, *others), "dev", shift(1, 0))

    def along_y(block, *others):
        return [lax.ppermute(tie(block, *others), "dev", shift(0, ys)) for ys in range(1, depth_y)]

    def along_x(weight, *others):
        blocks = [weight]
        for _ in range(1, depth_x):
            blocks.append(lax.ppermute(tie(blocks[-1], *others), "grp", x_shift))
        return blocks

    def other_core(block, *others):
        return lax.ppermute(tie(block, *others), "grp", core_swap)

    tokens = queries.shape[0]
    width = keys.shape[1]
    groups, span = prefix_keys.shape[:2]

    prefix = jnp.stack([prefix_keys.reshape(-1, width), cached_prefix_values.reshape(-1, width)])
    other = along_y(prefix)
    arriving = round_z(prefix)
    own = jnp.stack([keys, values])
    before = lax.ppermute(own, "dev", [(i, i + 1) for i in range(devs - 1)])
    gate_rows = along_x(w_gate)
    q, before_mask, within_mask, prefix_mask = prepare(
        groups,
        span,
        suffix_lengths,
        request_group,
        placement_order,
        queries,
        width,
    )
    blocks = [(before, before_mask), (own, within_mask), (prefix, prefix_mask)]
    ready, state = [before], None
    for zs in range(1, depth_z):
        if zs == depth_z - 1:
            state = attend(q, None, blocks)
            blocks, ready = [], [state[0], gate_swap, *gate_rows[1:]]
        here = tie(arriving, *(other if zs != 2 else []), *ready)
        if zs < depth_z - 1:
            arriving, ready = round_z(here), [q]
        blocks += [(b, prefix_mask) for b in other + [here]]
        other = along_y(here)
        if zs == 1:
            gate_swap = other_core(w_gate, here)
        elif zs == 2:
            up_swap = other_core(w_up, here)
    state = attend(q, state, blocks)
    down_swap = other_core(w_down, here)
    up_rows = along_x(w_up, *gate_rows[1:], here)
    gates = [w_gate, gate_swap]
    for gate in gate_rows[1:]:
        gates += [gate, other_core(gate, here)]
    hidden_state, *normed = attend_project(
        q,
        state,
        [(b, prefix_mask) for b in other],
        grps,
        out_weight,
        tie(residual, up_swap, down_swap, *gates[2:]),
        norm_gain[None],
    )

    arrived, across = [normed], [[along_y(half) for half in normed]]
    ups, downs, acts = [w_up, up_swap], [w_down, down_swap], {}
    for zs in range(1, depth_z):
        waits = across[zs - 2] if zs > 1 else [[] for _ in normed]
        arrived.append([round_z(half, *wait) for half, wait in zip(arrived[-1], waits)])
        late = arrived[zs][1:]
        if zs == depth_z - 1:
            acts[1] = rise([arrived[1]] + [list(c) for c in zip(*across[1])], gates, ups)
            late = [*late, acts[1]]
        across.append([along_y(half, *late) for half in arrived[zs]])
        if zs == depth_z - 2:
            for up in up_rows[1:]:
                ups += [up, other_core(up, *arrived[zs], *[b for c in across[zs - 1] for b in c])]
            down_cols = along_x(w_down, *up_rows[1:], *arrived[zs], *[b for c in across[zs - 1] for b in c])
    chunks = [[a] + [list(c) for c in zip(*b)] for a, b in zip(arrived, across)]
    each = grps // HALVES
    acts[2] = rise(chunks[2], gates, ups)
    acts[0] = rise(chunks[0], gates, ups)
    soon = [b for c in across[-1] for b in c] + [acts[2], acts[0]]
    sent = [None] * HALVES
    if each <= len(downs):
        sent[0] = round_z(
            fall(acts[1], 1, downs[:each])[0], *arrived[-1], *[b for c in across[-2] for b in c]
        )
        second = fall(acts[2], 1, downs[:each])[0]
        second = (second.astype(F32) + sent[0].astype(F32)).astype(BF16)
        soon.append(second)
        sent[0] = round_z(second)
    final = depth_z - 1
    for down in down_cols[1:]:
        downs += [down, other_core(down, *soon)]

    terms, fallen = [None] * HALVES, {}
    fallen[2, 1] = fall(acts[2], depth_y, downs[each:])
    chunks[final][0][0] = tie(chunks[final][0][0], fallen[2, 1][0])
    acts[final] = rise(chunks[final], gates, ups)
    fallen[final, 0] = fall(acts[final], depth_y, downs[:each])
    filler = fallen[final, 0][0]
    for zs in list(range(1, depth_z)) + [0]:
        act = acts[zs]
        for half in range(HALVES):
            joint = sent[half] is not None and sent[half].shape[0] > tokens
            if joint and zs < depth_z - 1:
                continue
            parts = fallen.pop((zs, half), None)
            if parts is None:
                parts = fall(act, depth_y, downs[half * each : (half + 1) * each])
            if joint:
                came = [sent[half][i * tokens : (i + 1) * tokens] for i in range(depth_y)]
                parts = [
                    (part.astype(F32) + share.astype(F32)).astype(BF16) if i else part
                    for i, (part, share) in enumerate(zip(parts, came))
                ]
                terms[half] = [parts[0], came[0]]
            else:
                terms[half] = [parts[0]] + ([round_z(sent[half])] if zs != 1 else [])
            if zs == 0:
                parts = [tie(part, sent[0]) for part in parts]
            terms[half] += [
                lax.ppermute(parts[ys], "dev", shift(0, -ys)) for ys in range(1, depth_y)
            ]
            if zs == 1:
                terms[half][0] = tie(terms[half][0], filler)
            if zs:
                sent[half] = functools.reduce(
                    jnp.add, [term.astype(F32) for term in terms[half]]
                ).astype(BF16)
    return finish(grps, hidden_state, terms)


def solution(mesh):
    placed = (
        P(("grp", "dev"), None),
        P(("grp", "dev"), None),
        P(("grp", "dev"), None),
        P(("grp", "dev"), None),
        P("grp", "dev", None),
        P("grp", "dev", None),
        P(),
        P(),
        P("grp", "dev"),
        P("grp", "dev"),
        P("dev", "grp"),
        P("grp", None),
        P("grp", None),
        P("grp", None),
    )
    return jax.shard_map(
        functools.partial(shards, mesh.shape["grp"], mesh.shape["dev"]),
        mesh=mesh,
        in_specs=placed,
        out_specs=P(("grp", "dev"), None),
        check_vma=False,
    )
```
